32 devices in a mesh: dp: 2 (over x), seq: 16 (over z, y, core).
Axes of the slice: x: 2, y: 2, z: 4, core: 2. Of those that a mesh axis runs over, the one named last changes fastest.
Arguments:
- tokens: bfloat16 [2, 2048, 1024], P('dp', 'seq'), may hold values from -6 to 6
- cotangent: bfloat16 [2, 2048, 1024], P('dp', 'seq'), may hold values from -6 to 6
- first_gain: float32 [1024], replicated, may hold values from 0.5 to 1.5
- first_shift: float32 [1024], replicated, may hold values from -1 to 1
- input_weight: bfloat16 [1024, 3072], P(('dp', 'seq')), may hold values from -0.1875 to 0.1875
- input_bias: float32 [3072], replicated, may hold values from -1 to 1
- short_weight: float32 [3, 3072], replicated, may hold values from -3 to 3
- short_bias: float32 [3072], replicated, may hold values from -1 to 1
- feat_weight: float32 [33, 64], replicated, may hold values from -1 to 1
- feat_bias: float32 [64], replicated, may hold values from -3 to 3
- feat_freq: float32 [64], replicated, may hold values from 1 to 8
- inner_weight: float32 [64, 64], replicated, may hold values from -0.75 to 0.75
- inner_bias: float32 [64], replicated, may hold values from -3 to 3
- inner_freq: float32 [64], replicated, may hold values from 1 to 8
- filter_weight: float32 [64, 1024], replicated, may hold values from -0.0625 to 0.0625
- skip_gain: float32 [1024], replicated, may hold values from -4 to 4
- decay_rates: float32 [1024], replicated, may hold values from 1 to 32
- output_weight: bfloat16 [1024, 1024], P(('dp', 'seq')), may hold values from -0.1875 to 0.1875
- output_bias: float32 [1024], replicated, may hold values from -1 to 1
- second_gain: float32 [1024], replicated, may hold values from 0.5 to 1.5
- second_shift: float32 [1024], replicated, may hold values from -1 to 1
- up_weight: bfloat16 [1024, 4096], P(('dp', 'seq')), may hold values from -0.1875 to 0.1875
- up_bias: float32 [4096], replicated, may hold values from -1 to 1
- down_weight: bfloat16 [4096, 1024], P(('dp', 'seq')), may hold values from -0.09375 to 0.09375
- down_bias: float32 [1024], replicated, may hold values from -1 to 1
Outputs:
- block_out: bfloat16 [2, 2048, 1024], P('dp', 'seq')
- tokens_grad: bfloat16 [2, 2048, 1024], P('dp', 'seq')
- first_gain_grad: float32 [1024], replicated
- first_shift_grad: float32 [1024], replicated
- input_weight_grad: float32 [1024, 3072], P(('dp', 'seq'))
- input_bias_grad: float32 [3072], replicated
- short_weight_grad: float32 [3, 3072], replicated
- short_bias_grad: float32 [3072], replicated
- feat_weight_grad: float32 [33, 64], replicated
- feat_bias_grad: float32 [64], replicated
- feat_freq_grad: float32 [64], replicated
- inner_weight_grad: float32 [64, 64], replicated
- inner_bias_grad: float32 [64], replicated
- inner_freq_grad: float32 [64], replicated
- filter_weight_grad: float32 [64, 1024], replicated
- skip_gain_grad: float32 [1024], replicated
- output_weight_grad: float32 [1024, 1024], P(('dp', 'seq'))
- output_bias_grad: float32 [1024], replicated
- second_gain_grad: float32 [1024], replicated
- second_shift_grad: float32 [1024], replicated
- up_weight_grad: float32 [1024, 4096], P(('dp', 'seq'))
- up_bias_grad: float32 [4096], replicated
- down_weight_grad: float32 [4096, 1024], P(('dp', 'seq'))
- down_bias_grad: float32 [1024], replicated
The draws below stay inside these ranges and needn't reach their ends.
All inputs are finite; a program needn't handle non-finite values.
Results may differ from the reference program's by a relative error of at most 0.014.
Values may be sent and summed in bfloat16 or wider, within the bound.
A program may use at most 192 MiB of HBM per device.

```python
import math
from functools import partial
import jax
import jax.numpy as jnp
from jax import lax

D = 1024
FF = 4096
FILT = 64
FEAT = 33
LENGTH = 2048
SEQS = 2


def block_scale(rng, dims, shards, low, largest):
    def one(axis_at, blocks):
        steps = jax.random.uniform(jax.random.fold_in(jax.random.fold_in(rng, 6), axis_at), (blocks,), jnp.float32, low / len(shards), largest / len(shards))
        return jnp.repeat(jnp.exp(steps), dims[axis_at] // blocks).reshape((-1,) + (1,) * (len(dims) - axis_at - 1))

    factor_of = one(*shards[0])
    for cut in shards[1:]:
        factor_of = factor_of * one(*cut)
    return factor_of


def scatter_about(own_key, dims, scale, bound, split=(), held_as=jnp.bfloat16):
    loudness = block_scale(own_key, dims, split, -0.22, 0.18) if split else 1.0
    values = jax.random.normal(own_key, dims, jnp.float32) * scale * loudness
    return jnp.minimum(jnp.maximum(values, -bound), bound).astype(held_as)


def setup_inputs(seed: int = 0) -> dict:
    key_of = jax.random.split(jax.random.key(seed), 26)
    tokens = scatter_about(key_of[0], (SEQS, LENGTH, D), 1.0, 6.0, ((0, 2), (1, 16)))
    cotangent = scatter_about(key_of[1], (SEQS, LENGTH, D), 1.0, 6.0, ((0, 2), (1, 16)))
    first_gain = jnp.clip(1.0 + 0.1 * jax.random.normal(key_of[2], (D,), jnp.float32), 0.5, 1.5)
    first_shift = scatter_about(key_of[3], (D,), 0.2, 1.0, (), jnp.float32)
    input_weight = scatter_about(key_of[4], (D, 3 * D), D ** -0.5, 0.1875, ((0, 32),))
    input_bias = scatter_about(key_of[5], (3 * D,), 0.2, 1.0, (), jnp.float32)
    short_weight = scatter_about(key_of[6], (3, 3 * D), 0.6, 3.0, (), jnp.float32)
    short_bias = scatter_about(key_of[7], (3 * D,), 0.2, 1.0, (), jnp.float32)
    feat_weight = scatter_about(key_of[8], (FEAT, FILT), FEAT ** -0.5, 1.0, (), jnp.float32)
    feat_bias = scatter_about(key_of[9], (FILT,), 1.0, 3.0, (), jnp.float32)
    feat_freq = jnp.clip(jnp.exp(jax.random.uniform(key_of[10], (FILT,), jnp.float32, math.log(1.0), math.log(8.0))), 1.0, 8.0)
    inner_weight = scatter_about(key_of[11], (FILT, FILT), FILT ** -0.5, 0.75, (), jnp.float32)
    inner_bias = scatter_about(key_of[12], (FILT,), 1.0, 3.0, (), jnp.float32)
    inner_freq = jnp.clip(jnp.exp(jax.random.uniform(key_of[13], (FILT,), jnp.float32, math.log(1.0), math.log(8.0))), 1.0, 8.0)
    filter_weight = scatter_about(key_of[14], (FILT, D), (4 * LENGTH) ** -0.5, 0.0625, (), jnp.float32)
    skip_gain = scatter_about(key_of[15], (D,), 1.0, 4.0, (), jnp.float32)
    decay_rates = jnp.clip(jnp.exp(jax.random.uniform(key_of[16], (D,), jnp.float32, math.log(1.0), math.log(32.0))), 1.0, 32.0)
    output_weight = scatter_about(key_of[17], (D, D), D ** -0.5, 0.1875, ((0, 32),))
    output_bias = scatter_about(key_of[18], (D,), 0.2, 1.0, (), jnp.float32)
    second_gain = jnp.clip(1.0 + 0.1 * jax.random.normal(key_of[19], (D,), jnp.float32), 0.5, 1.5)
    second_shift = scatter_about(key_of[20], (D,), 0.2, 1.0, (), jnp.float32)
    up_weight = scatter_about(key_of[21], (D, FF), D ** -0.5, 0.1875, ((0, 32),))
    up_bias = scatter_about(key_of[22], (FF,), 0.2, 1.0, (), jnp.float32)
    down_weight = scatter_about(key_of[23], (FF, D), FF ** -0.5, 0.09375, ((0, 32),))
    down_bias = scatter_about(key_of[24], (D,), 0.2, 1.0, (), jnp.float32)
    return {"tokens": tokens, "cotangent": cotangent, "first_gain": first_gain, "first_shift": first_shift, "input_weight": input_weight, "input_bias": input_bias, "short_weight": short_weight, "short_bias": short_bias, "feat_weight": feat_weight, "feat_bias": feat_bias, "feat_freq": feat_freq, "inner_weight": inner_weight, "inner_bias": inner_bias, "inner_freq": inner_freq, "filter_weight": filter_weight, "skip_gain": skip_gain, "decay_rates": decay_rates, "output_weight": output_weight, "output_bias": output_bias, "second_gain": second_gain, "second_shift": second_shift, "up_weight": up_weight, "up_bias": up_bias, "down_weight": down_weight, "down_bias": down_bias}


@jax.custom_vjp
def low(v):
    return lax.optimization_barrier(v.astype(jnp.bfloat16)).astype(jnp.float32)

@jax.custom_vjp
def low_back(v):
    return v

def low_keep(v):
    return (low(v), None)

def low_pass(kept, grad):
    return (grad,)

def back_keep(v):
    return (v, None)

def back_low(kept, grad):
    return (low(grad),)
low.defvjp(low_keep, low_pass)
low_back.defvjp(back_keep, back_low)
exact_precision = lax.Precision.HIGHEST

def layer_norm(values, gain_vec, offset):
    center = values - lax.optimization_barrier(jnp.mean(values, -1, keepdims=True))
    spread = lax.optimization_barrier(jnp.mean(center * center, -1, keepdims=True))
    return center * lax.rsqrt(spread + 1e-05) * gain_vec + offset

def position_features(stamps, length):
    stamp_float = stamps.astype(jnp.float32)
    linear_ramp = stamp_float / (length - 1)
    band_rates = 0.0001 + jnp.arange((FEAT - 1) // 2).astype(jnp.float32) * ((15.0 - 0.0001) / 15.0)
    phase_angle = (stamp_float * (2.0 * math.pi / length))[:, None] * band_rates[None, :]
    return jnp.concatenate([linear_ramp[:, None], jnp.cos(phase_angle), -jnp.sin(phase_angle)], 1)

def filter_net(feat_weight, feat_bias, feat_freq, inner_weight, inner_bias, inner_freq, filter_weight, feature_rows, modulate):
    hidden = jnp.sin(feat_freq * (jnp.dot(feature_rows, feat_weight, precision=exact_precision) + feat_bias))
    hidden = jnp.sin(inner_freq * (jnp.dot(hidden, inner_weight, precision=exact_precision) + inner_bias))
    raw_filter = lax.dot_general(filter_weight, hidden, (((0,), (1,)), ((), ())), precision=exact_precision)
    return raw_filter * modulate

def project(activation_list, weight_matrix):
    return jnp.einsum('mfj,jk->mfk', activation_list, weight_matrix, precision=exact_precision)

def block_forward(decay_rates, tokens, first_gain, first_shift, input_weight, input_bias, short_weight, short_bias, feat_weight, feat_bias, feat_freq, inner_weight, inner_bias, inner_freq, filter_weight, skip_gain, output_weight, output_bias, second_gain, second_shift, up_weight, up_bias, down_weight, down_bias):
    length = tokens.shape[1]
    model_width = tokens.shape[2]
    act_one = low(layer_norm(tokens, first_gain, first_shift))
    projected = low_back(project(act_one, input_weight) + input_bias)
    padded = jnp.pad(projected, ((0, 0), (2, 0), (0, 0)))
    conv_out = short_bias + short_weight[0] * padded[:, :length] + short_weight[1] * padded[:, 1:length + 1] + short_weight[2] * padded[:, 2:]
    leading_gate = conv_out[:, :, :model_width]
    second_gate = conv_out[:, :, model_width:2 * model_width]
    value_part = conv_out[:, :, 2 * model_width:]
    carried = leading_gate * value_part
    stamps = jnp.arange(length).astype(jnp.int32)
    modulate = jnp.exp(-decay_rates[:, None] * (stamps.astype(jnp.float32) / (length - 1))[None, :])
    filters = filter_net(feat_weight, feat_bias, feat_freq, inner_weight, inner_bias, inner_freq, filter_weight, position_features(stamps, length), modulate)
    period = 2 * length
    spectrum = jnp.fft.rfft(carried, n=period, axis=1) * jnp.fft.rfft(filters, n=period, axis=1).T[None]
    long_out = jnp.fft.irfft(spectrum, n=period, axis=1)[:, :length] + skip_gain * carried
    act_pre = low(second_gate * long_out)
    residual = tokens + low_back(project(act_pre, output_weight) + output_bias)
    act_two = low(layer_norm(residual, second_gain, second_shift))
    upper = low_back(project(act_two, up_weight) + up_bias)
    act_three = low(jax.nn.gelu(upper))
    return residual + low_back(project(act_three, down_weight) + down_bias)

def reference(tokens, cotangent, first_gain, first_shift, input_weight, input_bias, short_weight, short_bias, feat_weight, feat_bias, feat_freq, inner_weight, inner_bias, inner_freq, filter_weight, skip_gain, decay_rates, output_weight, output_bias, second_gain, second_shift, up_weight, up_bias, down_weight, down_bias):
    weights = (first_gain, first_shift, input_weight.astype(jnp.float32), input_bias, short_weight, short_bias, feat_weight, feat_bias, feat_freq, inner_weight, inner_bias, inner_freq, filter_weight, skip_gain, output_weight.astype(jnp.float32), output_bias, second_gain, second_shift, up_weight.astype(jnp.float32), up_bias, down_weight.astype(jnp.float32), down_bias)
    result, pullback = jax.vjp(partial(block_forward, decay_rates), tokens.astype(jnp.float32), *weights)
    tokens_grad, first_gain_grad, first_shift_grad, input_weight_grad, input_bias_grad, short_weight_grad, short_bias_grad, feat_weight_grad, feat_bias_grad, feat_freq_grad, inner_weight_grad, inner_bias_grad, inner_freq_grad, filter_weight_grad, skip_gain_grad, output_weight_grad, output_bias_grad, second_gain_grad, second_shift_grad, up_weight_grad, up_bias_grad, down_weight_grad, down_bias_grad = pullback(cotangent.astype(jnp.float32))
    return (result.astype(jnp.bfloat16), tokens_grad.astype(jnp.bfloat16), first_gain_grad, first_shift_grad, input_weight_grad, input_bias_grad, short_weight_grad, short_bias_grad, feat_weight_grad, feat_bias_grad, feat_freq_grad, inner_weight_grad, inner_bias_grad, inner_freq_grad, filter_weight_grad, skip_gain_grad, output_weight_grad, output_bias_grad, second_gain_grad, second_shift_grad, up_weight_grad, up_bias_grad, down_weight_grad, down_bias_grad)
```

```python
import functools
import math
import types
from typing import NamedTuple

import jax
import jax.numpy as jnp
import ml_dtypes
import numpy as np
from jax import lax
from jax.experimental import pallas as pl
from jax.experimental.pallas import tpu as pltpu
from jax.sharding import PartitionSpec as P

FEAT = 33
FILT = 64


exact_precision = lax.Precision.HIGHEST


def from_behind(x, axis, by):
    size = lax.axis_size(axis)
    pairs = [(i, i + by) for i in range(size) if 0 <= i + by < size]
    return lax.ppermute(x, axis, pairs)


def layer_norm(values, gain_vec, offset):
    center = values - jnp.mean(values, -1, keepdims=True)
    spread = jnp.mean(center * center, -1, keepdims=True)
    return center * lax.rsqrt(spread + 1e-05) * gain_vec + offset


def position_features(stamps, length):
    stamp_float = stamps.astype(jnp.float32)
    linear_ramp = stamp_float / (length - 1)
    band_rates = 0.0001 + jnp.arange((FEAT - 1) // 2).astype(jnp.float32) * ((15.0 - 0.0001) / 15.0)
    phase_angle = (stamp_float * (2.0 * math.pi / length))[:, None] * band_rates[None, :]
    return jnp.concatenate([linear_ramp[:, None], jnp.cos(phase_angle), -jnp.sin(phase_angle)], 1)


def filter_net(
    feat_weight,
    feat_bias,
    feat_freq,
    inner_weight,
    inner_bias,
    inner_freq,
    filter_weight,
    feature_rows,
    modulate,
):
    hidden = jnp.sin(
        feat_freq * (jnp.dot(feature_rows, feat_weight, precision=exact_precision) + feat_bias)
    )
    hidden = jnp.sin(
        inner_freq * (jnp.dot(hidden, inner_weight, precision=exact_precision) + inner_bias)
    )
    raw_filter = lax.dot_general(
        filter_weight, hidden, (((0,), (1,)), ((), ())), precision=exact_precision
    )
    return raw_filter * modulate


def short_conv(padded, kernel, offset):
    col_count = padded.shape[1] - 2
    return (
        offset[:, None]
        + kernel[0][:, None] * padded[:, :col_count]
        + kernel[1][:, None] * padded[:, 1 : col_count + 1]
        + kernel[2][:, None] * padded[:, 2:]
    )


def unit_angles(rows, cols, period):
    row_index = lax.broadcasted_iota(jnp.int32, (rows, cols), 0)
    col_index = lax.broadcasted_iota(jnp.int32, (rows, cols), 1)
    phase_angle = (row_index * col_index % period).astype(jnp.float32) * (2.0 * math.pi / period)
    return (jnp.cos(phase_angle), jnp.sin(phase_angle))


def forward_frequency_domain(signal, outer_size, period):
    block_count = signal.shape[1]
    row_count = signal.shape[2]
    cos_first, sin_first = unit_angles(outer_size, block_count, outer_size)
    real_first = jnp.einsum("dn,cnt->cdt", cos_first, signal, precision=exact_precision)
    imag_first = -jnp.einsum("dn,cnt->cdt", sin_first, signal, precision=exact_precision)
    cos_turn, sin_turn = unit_angles(outer_size, row_count, period)
    real_turned = real_first * cos_turn + imag_first * sin_turn
    imag_turned = imag_first * cos_turn - real_first * sin_turn
    cos_last, sin_last = unit_angles(row_count, row_count, row_count)
    real_out = jnp.einsum(
        "cdb,bk->cdk", real_turned, cos_last, precision=exact_precision
    ) + jnp.einsum("cdb,bk->cdk", imag_turned, sin_last, precision=exact_precision)
    imag_out = jnp.einsum(
        "cdb,bk->cdk", imag_turned, cos_last, precision=exact_precision
    ) - jnp.einsum("cdb,bk->cdk", real_turned, sin_last, precision=exact_precision)
    return (real_out, imag_out)


def inverse_spectrum(real_part, imag_part, block_count, period):
    outer_size = real_part.shape[1]
    row_count = real_part.shape[2]
    cos_last, sin_last = unit_angles(row_count, row_count, row_count)
    real_back = jnp.einsum(
        "cdk,kb->cdb", real_part, cos_last, precision=exact_precision
    ) - jnp.einsum("cdk,kb->cdb", imag_part, sin_last, precision=exact_precision)
    imag_back = jnp.einsum(
        "cdk,kb->cdb", real_part, sin_last, precision=exact_precision
    ) + jnp.einsum("cdk,kb->cdb", imag_part, cos_last, precision=exact_precision)
    cos_turn, sin_turn = unit_angles(outer_size, row_count, period)
    real_turned = real_back * cos_turn - imag_back * sin_turn
    imag_turned = real_back * sin_turn + imag_back * cos_turn
    cos_first, sin_first = unit_angles(block_count, outer_size, outer_size)
    summed = jnp.einsum(
        "nd,cdt->cnt", cos_first, real_turned, precision=exact_precision
    ) - jnp.einsum("nd,cdt->cnt", sin_first, imag_turned, precision=exact_precision)
    return summed / period


def on_device(
    tokens,
    cotangent,
    first_gain,
    first_shift,
    input_weight,
    input_bias,
    short_weight,
    short_bias,
    feat_weight,
    feat_bias,
    feat_freq,
    inner_weight,
    inner_bias,
    inner_freq,
    filter_weight,
    skip_gain,
    decay_rates,
    output_weight,
    output_bias,
    second_gain,
    second_shift,
    up_weight,
    up_bias,
    down_weight,
    down_bias,
):
    sequence_count = lax.axis_size("seq")
    seq_index = lax.axis_index("seq")
    row_count = tokens.shape[1]
    model_width = tokens.shape[2]
    length = row_count * sequence_count
    period = 2 * length
    outer_size = 2 * sequence_count
    narrow = model_width // sequence_count
    inputs = tokens[0].astype(jnp.float32)
    cotan_rows = cotangent[0].astype(jnp.float32)
    w_in, w_out, w_up, w_down = (
        lax.all_gather(input_weight, ("dp", "seq"), axis=0, tiled=True),
        lax.all_gather(output_weight, ("dp", "seq"), axis=0, tiled=True),
        lax.all_gather(up_weight, ("dp", "seq"), axis=0, tiled=True),
        lax.all_gather(down_weight, ("dp", "seq"), axis=0, tiled=True),
    )
    normed_one, norm_one_back = jax.vjp(layer_norm, inputs, first_gain, first_shift)
    act_one = normed_one.astype(jnp.bfloat16)
    projected = lax.dot_general(
        w_in, act_one, (((0,), (1,)), ((), ())), preferred_element_type=jnp.float32
    )
    projected = projected + input_bias[:, None]
    rim_rows = from_behind(projected[:, row_count - 2 :], "seq", 1)
    padded = jnp.concatenate([rim_rows, projected], 1)
    conv_out, short_back = jax.vjp(short_conv, padded, short_weight, short_bias)
    leading_gate = conv_out[:model_width]
    second_gate = conv_out[model_width : 2 * model_width]
    value_part = conv_out[2 * model_width :]
    carried = leading_gate * value_part
    stamps = seq_index * row_count + lax.iota(jnp.int32, row_count)
    modulate = jnp.exp(-decay_rates[:, None] * (stamps.astype(jnp.float32) / (length - 1))[None, :])
    filter_fixed = functools.partial(
        filter_net, feature_rows=position_features(stamps, length), modulate=modulate
    )
    filters, filter_back = jax.vjp(
        filter_fixed,
        feat_weight,
        feat_bias,
        feat_freq,
        inner_weight,
        inner_bias,
        inner_freq,
        filter_weight,
    )
    carried_blocks = carried.reshape(sequence_count, narrow, row_count)
    filter_blocks = filters.reshape(sequence_count, narrow, row_count)
    carried_chan, filter_chan = (
        lax.all_to_all(
            carried_blocks.astype(jnp.bfloat16), "seq", split_axis=0, concat_axis=2, tiled=True
        ).astype(carried_blocks.dtype),
        lax.all_to_all(
            filter_blocks.astype(jnp.bfloat16), "seq", split_axis=0, concat_axis=2, tiled=True
        ).astype(filter_blocks.dtype),
    )
    carried_chan = carried_chan.reshape(narrow, sequence_count, row_count)
    filter_chan = filter_chan.reshape(narrow, sequence_count, row_count)
    carried_real, carried_imag = forward_frequency_domain(carried_chan, outer_size, period)
    filter_real, filter_imag = forward_frequency_domain(filter_chan, outer_size, period)
    conv_chan = inverse_spectrum(
        carried_real * filter_real - carried_imag * filter_imag,
        carried_real * filter_imag + carried_imag * filter_real,
        sequence_count,
        period,
    )
    conv_rows = lax.all_to_all(
        conv_chan.reshape(1, narrow, length).astype(jnp.bfloat16),
        "seq",
        split_axis=2,
        concat_axis=0,
        tiled=True,
    ).astype(jnp.float32)
    long_out = conv_rows.reshape(model_width, row_count) + skip_gain[:, None] * carried
    act_pre = (second_gate * long_out).astype(jnp.bfloat16)
    branch_out = lax.dot_general(
        act_pre, w_out, (((0,), (0,)), ((), ())), preferred_element_type=jnp.float32
    )
    residual = inputs + branch_out + output_bias
    normed_two, norm_two_back = jax.vjp(layer_norm, residual, second_gain, second_shift)
    act_two = normed_two.astype(jnp.bfloat16)
    upper = jnp.dot(act_two, w_up, preferred_element_type=jnp.float32) + up_bias
    gelu_out, gelu_back = jax.vjp(jax.nn.gelu, upper)
    act_three = gelu_out.astype(jnp.bfloat16)
    result = residual + jnp.dot(act_three, w_down, preferred_element_type=jnp.float32) + down_bias
    block_out = result.astype(jnp.bfloat16)[None]
    grad_final = cotan_rows.astype(jnp.bfloat16)
    down_grad = lax.dot_general(
        act_three, grad_final, (((0,), (0,)), ((), ())), preferred_element_type=jnp.float32
    )
    down_bias_grad = jnp.sum(grad_final, 0, dtype=jnp.float32)
    grad_act_three = lax.dot_general(
        grad_final, w_down, (((1,), (1,)), ((), ())), preferred_element_type=jnp.float32
    )
    (grad_upper,) = gelu_back(grad_act_three)
    grad_upper = grad_upper.astype(jnp.bfloat16)
    up_grad = lax.dot_general(
        act_two, grad_upper, (((0,), (0,)), ((), ())), preferred_element_type=jnp.float32
    )
    up_bias_grad = jnp.sum(grad_upper, 0, dtype=jnp.float32)
    grad_norm_two = lax.dot_general(
        grad_upper, w_up, (((1,), (1,)), ((), ())), preferred_element_type=jnp.float32
    )
    grad_resid_norm, second_gain_grad, second_shift_grad = norm_two_back(grad_norm_two)
    grad_residual = cotan_rows + grad_resid_norm
    grad_branch = grad_residual.astype(jnp.bfloat16)
    output_grad = jnp.dot(act_pre, grad_branch, preferred_element_type=jnp.float32)
    output_bias_grad = jnp.sum(grad_branch, 0, dtype=jnp.float32)
    grad_pre = lax.dot_general(
        w_out, grad_branch, (((1,), (1,)), ((), ())), preferred_element_type=jnp.float32
    )
    grad_second = grad_pre * long_out
    grad_long = grad_pre * second_gate
    skip_gain_grad = jnp.sum(grad_long * carried, 1)
    grad_long_blocks = grad_long.reshape(sequence_count, narrow, row_count)
    grad_chan, carried_again, filter_again = (
        lax.all_to_all(
            grad_long_blocks.astype(jnp.bfloat16), "seq", split_axis=0, concat_axis=2, tiled=True
        ).astype(grad_long_blocks.dtype),
        lax.all_to_all(
            carried_blocks.astype(jnp.bfloat16), "seq", split_axis=0, concat_axis=2, tiled=True
        ).astype(carried_blocks.dtype),
        lax.all_to_all(
            filter_blocks.astype(jnp.bfloat16), "seq", split_axis=0, concat_axis=2, tiled=True
        ).astype(filter_blocks.dtype),
    )
    carried_real, carried_imag = forward_frequency_domain(
        carried_again.reshape(narrow, sequence_count, row_count), outer_size, period
    )
    filter_real, filter_imag = forward_frequency_domain(
        filter_again.reshape(narrow, sequence_count, row_count), outer_size, period
    )
    grad_real, grad_imag = forward_frequency_domain(
        grad_chan.reshape(narrow, sequence_count, row_count), outer_size, period
    )
    carried_back = inverse_spectrum(
        filter_real * grad_real + filter_imag * grad_imag,
        filter_real * grad_imag - filter_imag * grad_real,
        sequence_count,
        period,
    )
    filter_grad_chan = inverse_spectrum(
        carried_real * grad_real + carried_imag * grad_imag,
        carried_real * grad_imag - carried_imag * grad_real,
        sequence_count,
        period,
    )
    carried_got, filters_got = (
        lax.all_to_all(
            carried_back.reshape(1, narrow, length).astype(jnp.bfloat16),
            "seq",
            split_axis=2,
            concat_axis=0,
            tiled=True,
        ).astype(jnp.float32),
        lax.all_to_all(
            filter_grad_chan.reshape(1, narrow, length).astype(jnp.bfloat16),
            "seq",
            split_axis=2,
            concat_axis=0,
            tiled=True,
        ).astype(jnp.float32),
    )
    grad_carried = carried_got.reshape(model_width, row_count) + skip_gain[:, None] * grad_long
    grad_filters = filters_got.reshape(model_width, row_count)
    (
        feat_weight_grad,
        feat_bias_grad,
        feat_freq_grad,
        inner_weight_grad,
        inner_bias_grad,
        inner_freq_grad,
        filter_weight_grad,
    ) = filter_back(grad_filters)
    grad_conv = jnp.concatenate(
        [grad_carried * value_part, grad_second, grad_carried * leading_gate], 0
    )
    grad_padded, short_weight_grad, short_bias_grad = short_back(grad_conv)
    rim_grad = from_behind(grad_padded[:, :2], "seq", -1)
    grad_projected = jnp.concatenate(
        [grad_padded[:, 2:row_count], grad_padded[:, row_count:] + rim_grad], 1
    )
    grad_projected = grad_projected.astype(jnp.bfloat16)
    input_grad = lax.dot_general(
        act_one, grad_projected, (((0,), (1,)), ((), ())), preferred_element_type=jnp.float32
    )
    input_bias_grad = jnp.sum(grad_projected, 1, dtype=jnp.float32)
    first_norm_gradient = lax.dot_general(
        grad_projected, w_in, (((0,), (1,)), ((), ())), preferred_element_type=jnp.float32
    )
    grad_inputs, first_gain_grad, first_shift_grad = norm_one_back(first_norm_gradient)
    tokens_grad = (grad_inputs + grad_residual).astype(jnp.bfloat16)[None]
    input_weight_grad, output_weight_grad, up_weight_grad, down_weight_grad = (
        lax.psum_scatter(input_grad, ("dp", "seq"), scatter_dimension=0, tiled=True),
        lax.psum_scatter(output_grad, ("dp", "seq"), scatter_dimension=0, tiled=True),
        lax.psum_scatter(up_grad, ("dp", "seq"), scatter_dimension=0, tiled=True),
        lax.psum_scatter(down_grad, ("dp", "seq"), scatter_dimension=0, tiled=True),
    )
    (
        first_gain_grad,
        first_shift_grad,
        input_bias_grad,
        short_weight_grad,
        short_bias_grad,
        feat_weight_grad,
        feat_bias_grad,
        feat_freq_grad,
        inner_weight_grad,
        inner_bias_grad,
        inner_freq_grad,
        filter_weight_grad,
        skip_gain_grad,
        output_bias_grad,
        second_gain_grad,
        second_shift_grad,
        up_bias_grad,
        down_bias_grad,
    ) = lax.psum(
        (
            first_gain_grad,
            first_shift_grad,
            input_bias_grad,
            short_weight_grad,
            short_bias_grad,
            feat_weight_grad,
            feat_bias_grad,
            feat_freq_grad,
            inner_weight_grad,
            inner_bias_grad,
            inner_freq_grad,
            filter_weight_grad,
            skip_gain_grad,
            output_bias_grad,
            second_gain_grad,
            second_shift_grad,
            up_bias_grad,
            down_bias_grad,
        ),
        ("dp", "seq"),
    )
    return (
        block_out,
        tokens_grad,
        first_gain_grad,
        first_shift_grad,
        input_weight_grad,
        input_bias_grad,
        short_weight_grad,
        short_bias_grad,
        feat_weight_grad,
        feat_bias_grad,
        feat_freq_grad,
        inner_weight_grad,
        inner_bias_grad,
        inner_freq_grad,
        filter_weight_grad,
        skip_gain_grad,
        output_weight_grad,
        output_bias_grad,
        second_gain_grad,
        second_shift_grad,
        up_weight_grad,
        up_bias_grad,
        down_weight_grad,
        down_bias_grad,
    )


f32 = jnp.float32
bf16 = jnp.bfloat16
ON_MESH = pl.DeviceIdType.MESH
INNER = 4
LANES = 128
CT_FILTER = 64
PS_ROWS = 256
AT_VECTOR = 64
AT_SECOND_GAIN = 96
AT_SECOND_SHIFT = 104
AT_OUTPUT_BIAS = 112
AT_DOWN_BIAS = 120
AT_FIRST_GAIN = 128
AT_FIRST_SHIFT = 136
AT_UP_BIAS = 144
AT_FEAT = 176


def dot_nn(a, b, precision=None):
    return lax.dot_general(
        a, b, (((1,), (0,)), ((), ())), precision=precision, preferred_element_type=f32
    )


def dot_nt(a, b, precision=None):
    return lax.dot_general(
        a, b, (((1,), (1,)), ((), ())), precision=precision, preferred_element_type=f32
    )


def step_at(index, size):
    return pl.ds(pl.multiple_of(index * size, size), size)


def times_unit(value, turns):
    re, im = value
    c, s = math.cos(2 * math.pi * turns), math.sin(2 * math.pi * turns)
    if abs(s) < 1e-12:
        return (re, im) if c > 0 else (-re, -im)
    if abs(c) < 1e-12:
        return (-im, re) if s > 0 else (im, -re)
    return re * c - im * s, re * s + im * c


def small_transform(values, sign):
    size = len(values)
    if size == 1:
        return values
    even = small_transform(values[0::2], sign)
    odd = small_transform(values[1::2], sign)
    turned = [times_unit(odd[k], sign * k / size) for k in range(size // 2)]
    return [(e[0] + t[0], e[1] + t[1]) for e, t in zip(even, turned)] + [
        (e[0] - t[0], e[1] - t[1]) for e, t in zip(even, turned)
    ]


@functools.lru_cache(None)
def constant_tables(blocks, lanes):
    length = blocks * lanes
    n2 = np.arange(lanes)
    angle = 2 * np.pi * np.outer(n2, n2) / lanes
    c, s = np.cos(angle), np.sin(angle)
    forth = np.block([[c, -s], [s, c]])
    back = np.block([[c, s], [-s, c]])

    def split(x):
        high = x.astype(ml_dtypes.bfloat16)
        return high, (x - high.astype(np.float64)).astype(ml_dtypes.bfloat16)

    turn = 2 * np.pi * np.outer(np.arange(blocks) + 0.25, n2) / length
    turns = np.concatenate([np.cos(turn), np.sin(turn)], 1).astype(np.float32)
    rates = 1e-4 + np.arange((FEAT - 1) // 2) * ((15.0 - 1e-4) / 15.0)
    phase = (2 * np.pi * np.arange(length) / length)[None, :] * rates[:, None]
    ramp = (np.arange(length) / (length - 1))[None, :]
    features = np.concatenate([ramp, np.cos(phase), -np.sin(phase)], 0)
    features = np.pad(features, ((0, -FEAT % 8), (0, 0))).astype(np.float32)
    return split(forth) + split(back) + (turns, features)


def split_dot(x, high, low):
    head = x.astype(bf16)
    tail = (x - head.astype(f32)).astype(bf16)
    return dot_nn(head, high) + dot_nn(tail, high) + dot_nn(head, low)


def sin_cos(x):
    count = jnp.floor(x * (2 / math.pi) + 0.5)
    r = x - count * 1.5703125
    r = r - count * 4.837512969970703e-4
    r = r - count * 7.549789948768648e-8
    r2 = r * r
    s = r + r * r2 * (-1.6666654611e-1 + r2 * (8.3321608736e-3 + r2 * -1.9515295891e-4))
    c = 1.0 - 0.5 * r2 + r2 * r2 * (
        4.166664568298827e-2 + r2 * (-1.388731625493765e-3 + r2 * 2.443315711809948e-5)
    )
    quarter = count - 4.0 * jnp.floor(count * 0.25)
    odd = (quarter == 1.0) | (quarter == 3.0)
    sine = jnp.where(odd, c, s)
    cosine = jnp.where(odd, s, c)
    sine = jnp.where(quarter >= 2.0, -sine, sine)
    cosine = jnp.where((quarter == 1.0) | (quarter == 2.0), -cosine, cosine)
    return sine, cosine


class Inputs(NamedTuple):
    tokens: jax.Array
    cotangent: jax.Array
    first_gain: jax.Array
    first_shift: jax.Array
    input_weight: jax.Array
    input_bias: jax.Array
    short_weight: jax.Array
    short_bias: jax.Array
    feat_weight: jax.Array
    feat_bias: jax.Array
    feat_freq: jax.Array
    inner_weight: jax.Array
    inner_bias: jax.Array
    inner_freq: jax.Array
    filter_weight: jax.Array
    skip_gain: jax.Array
    decay_rates: jax.Array
    output_weight: jax.Array
    output_bias: jax.Array
    second_gain: jax.Array
    second_shift: jax.Array
    up_weight: jax.Array
    up_bias: jax.Array
    down_weight: jax.Array
    down_bias: jax.Array
    forth_high: jax.Array
    forth_low: jax.Array
    back_high: jax.Array
    back_low: jax.Array
    turns: jax.Array
    features: jax.Array


def scratch_buffers(g):
    tok, width, pt, ch = g.tok, g.width, g.plane_tokens, g.chan
    ff, blocks = g.ff_part, g.blocks
    return dict(
        w_in=((width, 3 * LANES), bf16),
        w_in_send=((g.members * g.rows, 3 * LANES), bf16),
        w_up_send=((g.members * g.rows, ff), bf16),
        w_in_t=((3 * LANES, width), bf16),
        w_out=((width, width), bf16),
        w_up=((width, ff), bf16),
        w_down=((ff, width), bf16),
        act_one=((pt, width), bf16),
        act_two=((pt, width), bf16),
        cotan=((pt, width), bf16),
        proj_send=((3 * LANES, pt), bf16),
        proj_recv=((3 * LANES, pt), bf16),
        square=((LANES, LANES), f32),
        param_cols=((LANES, LANES), f32),
        taps=((4, 3 * ch, LANES), f32),
        skip=((ch, LANES), f32),
        decay=((ch, LANES), f32),
        net_weights=((4, LANES, LANES), f32),
        net_cols=((LANES, LANES), f32),
        p_one=((FILT, g.length), f32),
        hid_one=((FILT, g.length), f32),
        cos_one=((FILT, g.length), f32),
        p_two=((FILT, g.length), f32),
        hid_two=((LANES, g.length), f32),
        cos_two=((FILT, g.length), f32),
        filt=((blocks, ch, LANES), f32),
        padded=((2, blocks + 1, 3 * ch, LANES), f32),
        conv=((2 * blocks, 3 * ch, LANES), f32),
        carried=((blocks, 2 * ch, LANES), f32),
        long=((blocks, 2 * ch, LANES), f32),
        grad_long=((blocks, 2 * ch, LANES), f32),
        grad_conv=((2, blocks + 1, 3 * ch, LANES), f32),
        stage=((blocks, 2 * ch, 2 * LANES), f32),
        stage_filt=((blocks, ch, 2 * LANES), f32),
        spec_filt=((blocks, ch, 2 * LANES), f32),
        spec_car=((blocks, 2 * ch, 2 * LANES), f32),
        spec_grad=((blocks, 2 * ch, 2 * LANES), f32),
        back_sig=((blocks, 2 * ch, LANES), f32),
        back_filt=((blocks, ch, LANES), f32),
        sums=((6, 3 * ch, LANES), f32),
        pre_send=((width, tok), bf16),
        pre_recv=((width, tok), bf16),
        gpre_send=((width, tok), bf16),
        gpre_recv=((width, tok), bf16),
        residual=((tok, width), f32),
        xhat_two=((tok, width), f32),
        xhat_one=((tok, width), f32),
        grad_res=((tok, width), f32),
        grad_branch=((tok, width), bf16),
        act_three=((pt, ff), bf16),
        grad_up=((pt, ff), bf16),
        up_send=((width, ff), bf16),
        down_send=((ff, width), bf16),
        in_send=((width, 3 * LANES), bf16),
        out_sum=((LANES, width), bf16),
        gproj_send=((3 * LANES, pt), bf16),
        gproj_recv=((3 * LANES, pt), bf16),
        ct=((width, LANES), f32),
        ps=((PS_ROWS, LANES), f32),
        ps_recv=((PS_ROWS, LANES), f32),
        ps_all=((PS_ROWS, LANES), f32),
        gn_two_own=((pt, width), bf16),
        gn_two_send=((pt // 2, width), bf16),
        gn_two_sib=((pt // 2, width), bf16),
        gn_two_recv=((3 * tok, width), bf16),
        result_own=((pt, width), bf16),
        result_send=((pt // 2, width), bf16),
        result_sib=((pt // 2, width), bf16),
        result_recv=((3 * tok, width), bf16),
        w_out_grad_sib=((pt // 2, width), bf16),
        w_out_grad_recv=((3 * tok, width), bf16),
        gn_one_sib=((pt // 2, width), bf16),
        gn_one_recv=((3 * tok, width), bf16),
    )


SEMAPHORES = dict(
    w_in=32,
    w_up=32,
    up_grad=32,
    in_grad=32,
    pre=32,
    gpre=32,
    ps=32,
    ps_back=32,
    w_down=8,
    w_out_z=8,
    proj=8,
    gproj=8,
    down_grad=8,
    out_grad=8,
    ct_z=8,
    act_one=8,
    act_two=8,
    cotan=8,
    w_out=32,
    ct=8,
    gn_two=8,
    result=8,
    w_out_grad=8,
    gn_one=8,
)


class Geometry:
    def __init__(self, n_dp, n_seq, tok, width, hidden, rows, down_rows):
        self.n_dp, self.n_seq = n_dp, n_seq
        self.devices = n_dp * n_seq
        self.planes = n_seq // INNER
        self.members = n_dp * INNER
        self.chips = self.members // 2
        self.tok, self.width, self.hidden = tok, width, hidden
        self.rows, self.down_rows = rows, down_rows
        self.plane_tokens = self.members * tok
        self.length = n_seq * tok
        self.blocks = n_seq
        self.ff_part = hidden // self.members
        self.chan = LANES // max(self.planes, 1)

    def fits(self):
        return (
            self.n_dp == 2
            and self.n_seq % INNER == 0
            and self.tok == LANES
            and self.width == self.members * LANES
            and self.down_rows % LANES == 0
            and self.rows % 16 == 0
            and self.chan % 16 == 0
            and self.down_rows * self.planes == self.ff_part
        )


class Net:
    def __init__(self, g):
        self.g = g
        self.x, self.s = lax.axis_index("dp"), lax.axis_index("seq")
        self.z, self.q = self.s // INNER, self.s % INNER
        self.m = self.x * INNER + self.q
        self.p, self.c = self.m // 2, self.m % 2
        self.flat = self.x * g.n_seq + self.s
        self.sib = 2 * self.p + 1 - self.c
        self.chan_block = self.m * g.planes + self.z
        self.ends = []

    def device(self, flat):
        return (flat // self.g.n_seq, flat % self.g.n_seq)

    def member(self, m):
        return (m // INNER, self.z * INNER + m % INNER)

    def in_plane(self, z):
        return (self.x, z * INNER + self.q)

    def copy(self, src, dst, sems, k, device, sent=None):
        send, recv = sems
        return pltpu.make_async_remote_copy(
            src_ref=src,
            dst_ref=dst,
            send_sem=send.at[k if sent is None else sent],
            recv_sem=recv.at[k],
            device_id=device,
            device_id_type=ON_MESH,
        )

    def finish(self):
        for end in self.ends:
            end()


class ToAll:
    def __init__(self, net, sems, src, dst):
        self.net, self.sems, self.src, self.dst = net, sems, src, dst
        net.ends.append(self.wait_send)

    def one(self, j):
        net = self.net
        target = lax.rem(net.flat + j, net.g.devices)
        return net.copy(self.src(target), self.dst, self.sems, j, net.device(target))

    def each(self, act):
        @pl.loop(1, self.net.g.devices)
        def _(j):
            act(self.one(j))

    def start(self):
        self.each(lambda copy: copy.start())

    def wait(self):
        self.each(lambda copy: copy.wait_recv())

    def wait_send(self):
        self.each(lambda copy: copy.wait_send())


class AlongPlanes:
    def __init__(self, net, sems, src, dst):
        self.net, self.sems, self.src, self.dst = net, sems, src, dst
        net.ends.append(self.wait_send)

    def each(self, act):
        net = self.net
        for j in range(1, net.g.planes):
            z = lax.rem(net.z + j, net.g.planes)
            act(net.copy(self.src(z), self.dst, self.sems, j, net.in_plane(z)))

    def start(self):
        self.each(lambda copy: copy.start())

    def wait(self):
        self.each(lambda copy: copy.wait_recv())

    def wait_send(self):
        self.each(lambda copy: copy.wait_send())


class PlaneGather:
    def __init__(self, net, sems, piece, base=0):
        self.net, self.sems, self.piece, self.base = net, sems, piece, base
        net.ends.append(self.wait_send)

    def peer(self, j):
        return 2 * lax.rem(self.net.p + j, self.net.g.chips) + self.net.c

    def source(self, j):
        return 2 * lax.rem(self.net.p + self.net.g.chips - j, self.net.g.chips) + self.net.c

    def across(self, j):
        net = self.net
        mine = self.piece(net.m)
        return net.copy(mine, mine, self.sems, self.base + j, net.member(self.peer(j)))

    def beside(self, j):
        net = self.net
        held = self.piece(self.source(j) if j else net.m)
        return net.copy(held, held, self.sems, self.base + net.g.chips + j, net.member(net.sib))

    def start(self):
        for j in range(1, self.net.g.chips):
            self.across(j).start()
        self.beside(0).start()

    def forward(self, j):
        self.across(j).wait_recv()
        self.beside(j).start()

    def wait(self, j):
        self.beside(j).wait_recv()

    def forward_all(self):
        for j in range(1, self.net.g.chips):
            self.forward(j)

    def wait_all(self):
        for j in range(self.net.g.chips):
            self.wait(j)

    def wait_send(self):
        for j in range(1, self.net.g.chips):
            self.across(j).wait_send()
        for j in range(self.net.g.chips):
            self.beside(j).wait_send()


class PlaneSum:
    def __init__(self, net, sems, sib, recv, own=None, send=None, after=None):
        self.net, self.sems, self.sib, self.recv = net, sems, sib, recv
        if after is None:
            self.own, self.send = own, send
        else:
            self.own, self.send = after.own, after.send
            after.wait_send()
            net.ends.remove(after.wait_send)
        net.ends.append(self.wait_send)

    def block(self, ref, k):
        return ref.at[step_at(k, self.net.g.tok)]

    def beside(self, chip):
        net = self.net
        return net.copy(
            self.block(self.own, 2 * chip + 1 - net.c), self.block(self.sib, chip), self.sems, chip, net.member(net.sib)
        )

    def across(self, j):
        net = self.net
        chip = lax.rem(net.p + j, net.g.chips)
        return net.copy(
            self.block(self.send, chip),
            self.block(self.recv, j - 1),
            self.sems,
            net.g.chips + j,
            net.member(2 * chip + net.c),
        )

    def start(self, chip):
        self.beside(chip).start()

    def pair(self, chip):
        self.beside(chip).wait_recv()
        mine = self.own[step_at(2 * chip + self.net.c, self.net.g.tok), :].astype(f32)
        return mine + self.sib[step_at(chip, self.net.g.tok), :].astype(f32)

    def relay(self, j):
        chip = lax.rem(self.net.p + j, self.net.g.chips)
        self.send[step_at(chip, self.net.g.tok), :] = self.pair(chip).astype(bf16)
        self.across(j).start()

    def result(self):
        total = self.pair(self.net.p)
        tok = self.net.g.tok
        for j in range(1, self.net.g.chips):
            self.across(j).wait_recv()
            total = total + self.recv[(j - 1) * tok : j * tok, :].astype(f32)
        return total

    def wait_send(self):
        for chip in range(self.net.g.chips):
            self.beside(chip).wait_send()
        for j in range(1, self.net.g.chips):
            self.across(j).wait_send()


def to_rows(ref, at, row):
    for k in range(row.shape[1] // LANES):
        ref[at + k : at + k + 1, :] = row[:, k * LANES : (k + 1) * LANES]


def column_sum(x):
    return jnp.sum(x, 0, keepdims=True)


def normalized(x):
    center = x - jnp.mean(x, -1, keepdims=True)
    inverse = lax.rsqrt(jnp.mean(center * center, -1, keepdims=True) + 1e-5)
    return center * inverse, inverse


def norm_back(grad, xhat, inverse, gain):
    e = grad * gain
    return (e - jnp.mean(e, -1, keepdims=True) - xhat * jnp.mean(e * xhat, -1, keepdims=True)) * inverse


def gelu_pair(v):
    scale = math.sqrt(2 / math.pi)
    v2 = v * v
    t = jnp.tanh(scale * v * (1.0 + 0.044715 * v2))
    half = 0.5 * (1.0 + t)
    return v * half, half + 0.5 * v * (1.0 - t * t) * (scale * (1.0 + 3 * 0.044715 * v2))


def to_spectrum(g, signal, rows, stage, turns, high, low, out):
    @pl.loop(0, rows // 8)
    def _(step):
        at = step_at(step, 8)
        first = []
        for n in range(g.blocks):
            block = signal[n, at, :]
            angle = -2 * math.pi * n / (4 * g.blocks)
            first.append((block * math.cos(angle), block * math.sin(angle)))
        for k, (re, im) in enumerate(small_transform(first, -1)):
            c, s = turns[k : k + 1, :LANES], turns[k : k + 1, LANES:]
            stage[k, at, :LANES] = re * c + im * s
            stage[k, at, LANES:] = im * c - re * s

    group = 256 // rows

    @pl.loop(0, g.blocks // group)
    def _(step):
        at = step_at(step, group)
        x = stage[at].reshape(group * rows, 2 * LANES)
        out[at] = split_dot(x, high[...], low[...]).reshape(group, rows, 2 * LANES)


def from_spectrum(g, product, rows, stage, turns, high, low, signal):
    group = 256 // rows

    @pl.loop(0, g.blocks // group)
    def _(step):
        at = step_at(step, group)
        re, im = product(at)
        x = jnp.concatenate([re, im], -1).reshape(group * rows, 2 * LANES)
        stage[at] = split_dot(x, high[...], low[...]).reshape(group, rows, 2 * LANES)

    @pl.loop(0, rows // 8)
    def _(step):
        at = step_at(step, 8)
        values = []
        for k in range(g.blocks):
            re, im = stage[k, at, :LANES], stage[k, at, LANES:]
            c, s = turns[k : k + 1, :LANES], turns[k : k + 1, LANES:]
            values.append((re * c - im * s, re * s + im * c))
        for n, (re, im) in enumerate(small_transform(values, 1)):
            angle = 2 * math.pi * n / (4 * g.blocks)
            signal[n, at, :] = (re * math.cos(angle) - im * math.sin(angle)) * (1.0 / g.length)


def halves(x):
    return x[..., :LANES], x[..., LANES:]


def later(here, before, by):
    lane = lax.broadcasted_iota(jnp.int32, here.shape, 1)
    return jnp.where(lane < by, pltpu.roll(before, by, 1), pltpu.roll(here, by, 1))


def sooner(here, after, by):
    lane = lax.broadcasted_iota(jnp.int32, here.shape, 1)
    back = LANES - by
    return jnp.where(lane >= back, pltpu.roll(after, back, 1), pltpu.roll(here, back, 1))


def block_kernel(g, *refs):
    refs = list(refs)
    r = Inputs(*(refs.pop(0) for _ in Inputs._fields))
    block_out, tokens_grad, ct_out, ps_out, in_recv, up_recv, down_recv, out_recv = (refs.pop(0) for _ in range(8))
    w = types.SimpleNamespace(**{name: refs.pop(0) for name in scratch_buffers(g)})
    sems = types.SimpleNamespace(**{name: (refs.pop(0), refs.pop(0)) for name in SEMAPHORES})
    local_sem = refs.pop(0)
    net = Net(g)
    tok, width, pt, ch, ff = g.tok, g.width, g.plane_tokens, g.chan, g.ff_part
    rows, planes, members, chips, blocks = g.rows, g.planes, g.members, g.chips, g.blocks
    part = g.down_rows
    exact = lax.Precision.HIGHEST

    barrier = pltpu.get_barrier_semaphore()

    @pl.loop(1, g.devices)
    def _(j):
        there = net.device(lax.rem(net.flat + j, g.devices))
        pl.semaphore_signal(barrier, inc=1, device_id=there, device_id_type=ON_MESH)

    xhat_one, inverse_one = normalized(r.tokens[...].astype(f32))
    w.xhat_one[...] = xhat_one
    mine = step_at(net.m, tok)
    w.act_one[mine, :] = (xhat_one * r.first_gain[...] + r.first_shift[...]).astype(bf16)
    w.cotan[mine, :] = r.cotangent[...]
    for m in range(members):
        for b in range(3):
            at = b * width + m * LANES
            w.w_in_send[m * rows : (m + 1) * rows, b * LANES : (b + 1) * LANES] = r.input_weight[:, at : at + LANES]
        for z in range(planes):
            at = ((m // INNER) * g.n_seq + z * INNER + m % INNER) * part
            w.w_up_send[m * rows : (m + 1) * rows, z * part : (z + 1) * part] = r.up_weight[:, at : at + part]
    w.w_in[step_at(net.flat, rows), :] = w.w_in_send[step_at(net.m, rows), :]
    w.w_up[step_at(net.flat, rows), :] = w.w_up_send[step_at(net.m, rows), :]
    w.w_down[step_at(net.z, part), :] = r.down_weight[...]
    w.w_out[step_at(net.flat, rows), :] = r.output_weight[...]

    pl.semaphore_wait(barrier, g.devices - 1)

    def member_of(target):
        x, s = net.device(target)
        return x * INNER + s % INNER

    move_in = ToAll(
        net, sems.w_in, lambda t: w.w_in_send.at[step_at(member_of(t), rows)], w.w_in.at[step_at(net.flat, rows)]
    )
    move_up = ToAll(
        net, sems.w_up, lambda t: w.w_up_send.at[step_at(member_of(t), rows)], w.w_up.at[step_at(net.flat, rows)]
    )
    move_down = AlongPlanes(net, sems.w_down, lambda z: r.down_weight, w.w_down.at[step_at(net.z, part)])
    gather_one = PlaneGather(net, sems.act_one, lambda m: w.act_one.at[step_at(m, tok)])
    gather_cotan = PlaneGather(net, sems.cotan, lambda m: w.cotan.at[step_at(m, tok)])
    out_z = AlongPlanes(
        net, sems.w_out_z, lambda z: w.w_out.at[step_at(net.flat, rows)], w.w_out.at[step_at(net.flat, rows)]
    )

    def out_rows(z):
        return lambda m: w.w_out.at[step_at((m // INNER) * g.n_seq + z * INNER + m % INNER, rows)]

    gather_out = [PlaneGather(net, sems.w_out, out_rows(z), 8 * z) for z in range(planes)]

    gather_one.start()
    move_in.start()

    w.square[...] = jnp.zeros_like(w.square)
    lane_of = step_at(net.m, LANES)

    def param(row, ref, k, at):
        w.square[row : row + 1, :] = ref[k : k + 1, pl.ds(pl.multiple_of(at + net.m * LANES, LANES), LANES)]

    for b in range(3):
        param(b, r.input_bias, 0, b * width)
        for i in range(3):
            param(3 + 3 * i + b, r.short_weight, i, b * width)
        param(12 + b, r.short_bias, 0, b * width)
    param(15, r.skip_gain, 0, 0)
    param(16, r.decay_rates, 0, 0)
    w.param_cols[...] = w.square[...].T
    here = step_at(net.z, ch)

    def spread(col):
        return jnp.broadcast_to(w.param_cols[here, col : col + 1], (ch, LANES))

    for b in range(3):
        for i in range(3):
            w.taps[i, b * ch : (b + 1) * ch, :] = spread(3 + 3 * i + b)
        w.taps[3, b * ch : (b + 1) * ch, :] = spread(12 + b)
    w.skip[...] = spread(15)
    w.decay[...] = spread(16)

    w.square[...] = jnp.zeros_like(w.square)
    for k, ref in enumerate((r.feat_bias, r.feat_freq, r.inner_bias, r.inner_freq)):
        w.square[k : k + 1, :FILT] = ref[...]
    w.net_cols[...] = w.square[...].T
    w.square[...] = jnp.zeros_like(w.square)
    w.square[:FEAT, :FILT] = r.feat_weight[...]
    w.net_weights[0] = w.square[...].T
    w.square[...] = jnp.zeros_like(w.square)
    w.square[:FILT, :FILT] = r.inner_weight[...]
    w.net_weights[1] = w.square[...].T
    w.square[...] = jnp.zeros_like(w.square)
    w.square[:FILT, :] = r.filter_weight[:, lane_of]
    w.net_weights[3] = w.square[...].T
    w.square[...] = jnp.zeros_like(w.square)
    w.square[:ch, :] = w.net_weights[3, here, :]
    w.net_weights[2] = w.square[...]
    w.net_weights[3] = w.square[...].T
    w.hid_two[...] = jnp.zeros_like(w.hid_two)

    span = 4 * LANES
    col = lambda k: w.net_cols[:FILT, k : k + 1]
    features_rows = r.features.shape[0]

    @pl.loop(0, g.length // span)
    def _(step):
        at = step_at(step, span)
        feats = r.features[:, at]
        p_one = dot_nn(w.net_weights[0, :FILT, :features_rows], feats, exact) + col(0)
        hid_one, cos_one = sin_cos(col(1) * p_one)
        p_two = dot_nn(w.net_weights[1, :FILT, :FILT], hid_one, exact) + col(2)
        hid_two, cos_two = sin_cos(col(3) * p_two)
        w.p_one[:, at], w.hid_one[:, at], w.cos_one[:, at] = p_one, hid_one, cos_one
        w.p_two[:, at], w.hid_two[:FILT, at], w.cos_two[:, at] = p_two, hid_two, cos_two
        filters = dot_nn(w.net_weights[2, :ch, :FILT], hid_two, exact)
        for k in range(span // LANES):
            cut = slice(k * LANES, (k + 1) * LANES)
            w.filt[step * (span // LANES) + k] = filters[:, cut] * jnp.exp(-w.decay[...] * feats[:1, cut])

    to_spectrum(g, w.filt, ch, w.stage_filt, r.turns, r.forth_high, r.forth_low, w.spec_filt)

    gather_one.forward_all()
    move_in.wait()
    for b in range(3):
        turned = w.w_in[:, b * LANES : (b + 1) * LANES].astype(f32).T.astype(bf16)
        for z in range(planes):
            at = z * 3 * ch + b * ch
            w.w_in_t[at : at + ch, :] = turned[z * ch : (z + 1) * ch, :]
    gather_one.wait_all()
    biases = jnp.concatenate(
        [w.param_cols[z * ch : (z + 1) * ch, b : b + 1] for z in range(planes) for b in range(3)], 0
    )

    @pl.loop(0, members // 2)
    def _(step):
        at = step_at(step, 2 * tok)
        w.proj_send[:, at] = (dot_nt(w.w_in_t[...], w.act_one[at, :]) + biases).astype(bf16)

    move_proj = AlongPlanes(
        net, sems.proj, lambda z: w.proj_send.at[step_at(z, 3 * ch)], w.proj_recv.at[step_at(net.z, 3 * ch)]
    )
    move_proj.start()
    w.proj_recv[step_at(net.z, 3 * ch), :] = w.proj_send[step_at(net.z, 3 * ch), :]
    gather_cotan.start()
    out_z.start()
    gather_cotan.forward_all()
    out_z.wait()
    for k in gather_out:
        k.start()
    move_proj.wait()
    move_up.start()

    def place(d):
        a, n = d // blocks, d % blocks
        return a, n, step_at(n // INNER, 3 * ch), step_at(a * INNER + n % INNER, LANES)

    for a in range(2):
        w.padded[a, 0] = jnp.zeros((3 * ch, LANES), f32)
        w.grad_conv[a, blocks] = jnp.zeros((3 * ch, LANES), f32)

    @pl.loop(0, 2 * blocks)
    def _(d):
        a, n, from_rows, from_lanes = place(d)
        w.padded[a, n + 1] = w.proj_recv[from_rows, from_lanes].astype(f32)

    @pl.loop(0, 2 * blocks)
    def _(d):
        a, n, _, _ = place(d)
        now, before = w.padded[a, n + 1], w.padded[a, n]
        conv = w.taps[3] + w.taps[2] * now + w.taps[1] * later(now, before, 1) + w.taps[0] * later(now, before, 2)
        w.conv[d] = conv
        w.carried[n, step_at(a, ch), :] = conv[:ch] * conv[2 * ch :]

    def both(filt):
        return jnp.concatenate([filt, filt], 1)

    to_spectrum(g, w.carried, 2 * ch, w.stage, r.turns, r.forth_high, r.forth_low, w.spec_car)

    def forth_product(at):
        (hr, hi), (xr, xi) = halves(both(w.spec_filt[at])), halves(w.spec_car[at])
        return xr * hr - xi * hi, xr * hi + xi * hr

    from_spectrum(g, forth_product, 2 * ch, w.stage, r.turns, r.back_high, r.back_low, w.back_sig)

    @pl.loop(0, 2 * blocks)
    def _(d):
        a, n, _, _ = place(d)
        at = step_at(a, ch)
        long_out = w.back_sig[n, at, :] + w.skip[...] * w.carried[n, at, :]
        w.long[n, at, :] = long_out
        w.pre_send[step_at(d, ch), :] = (w.conv[d, ch : 2 * ch, :] * long_out).astype(bf16)

    own_block, own_slot = step_at(net.chan_block, ch), step_at(net.flat, ch)

    def chan_block_of(target):
        x, s = net.device(target)
        return (x * INNER + s % INNER) * planes + s // INNER

    move_pre = ToAll(net, sems.pre, lambda t: w.pre_send.at[step_at(t, ch)], w.pre_recv.at[own_block])
    move_pre.start()
    w.pre_recv[own_block, :] = w.pre_send[own_slot, :]
    for k in gather_out:
        k.forward_all()
    for k in gather_out:
        k.wait_all()
    move_pre.wait()
    move_down.start()

    pre_rows = w.pre_recv[...].astype(f32).T.astype(bf16)
    branch = dot_nn(pre_rows, w.w_out[...])
    residual = r.tokens[...].astype(f32) + branch + r.output_bias[...]
    w.residual[...] = residual
    xhat_two, inverse_two = normalized(residual)
    w.xhat_two[...] = xhat_two
    w.act_two[mine, :] = (xhat_two * r.second_gain[...] + r.second_shift[...]).astype(bf16)
    gather_two = PlaneGather(net, sems.act_two, lambda m: w.act_two.at[step_at(m, tok)])
    gather_two.start()

    gather_cotan.wait_all()
    move_up.wait()
    sum_two = PlaneSum(net, sems.gn_two, w.gn_two_sib, w.gn_two_recv, w.gn_two_own, w.gn_two_send)
    w.ps[...] = jnp.zeros_like(w.ps)
    hidden_block = [net.x * g.n_seq + z * INNER + net.q for z in range(planes)]
    up_bias = jnp.concatenate([r.up_bias[:, step_at(k, part)] for k in hidden_block], 1)
    bias_sum = jnp.zeros((1, ff), f32)
    for j in range(chips):
        if j == 1:
            gather_two.forward_all()
        gather_two.wait(j)
        chip = lax.rem(net.p + chips - j, chips)
        at = step_at(chip, 2 * tok)
        upper = dot_nn(w.act_two[at, :], w.w_up[...]) + up_bias
        gelu, slope = gelu_pair(upper)
        w.act_three[at, :] = gelu.astype(bf16)
        if j == 0:
            move_down.wait()
        grad_upper = (dot_nt(w.cotan[at, :], w.w_down[...]) * slope).astype(bf16)
        w.grad_up[at, :] = grad_upper
        bias_sum = bias_sum + column_sum(grad_upper.astype(f32))
        sum_two.own[at, :] = dot_nt(grad_upper, w.w_up[...]).astype(bf16)
        sum_two.start(chip)
    for z, k in enumerate(hidden_block):
        w.ps[pl.ds(AT_UP_BIAS + k, 1), :] = bias_sum[:, z * part : (z + 1) * part]
    for j in range(1, chips):
        sum_two.relay(j)

    def to_local(src, dst):
        copy = pltpu.make_async_copy(src, dst, local_sem)
        copy.start()
        copy.wait()

    own_rows = step_at(net.flat, rows)
    move_up_grad = ToAll(net, sems.up_grad, lambda t: w.up_send.at[step_at(t, rows)], up_recv.at[own_rows])
    @pl.loop(0, width // LANES)
    def _(step):
        at = step_at(step, LANES)
        turned = w.act_two[:, at].astype(f32).T.astype(bf16)
        w.up_send[at, :] = dot_nn(turned, w.grad_up[...]).astype(bf16)

    move_up_grad.start()
    to_local(w.up_send.at[own_rows], up_recv.at[own_rows])
    sum_result = PlaneSum(net, sems.result, w.result_sib, w.result_recv, w.result_own, w.result_send)
    for j in range(1, chips + 1):
        chip = lax.rem(net.p + j, chips)
        at = step_at(chip, 2 * tok)
        sum_result.own[at, :] = dot_nn(w.act_three[at, :], w.w_down[...]).astype(bf16)
    grad_two = sum_two.result()

    xhat_two = w.xhat_two[...]
    to_rows(w.ps, AT_SECOND_GAIN, column_sum(grad_two * xhat_two))
    to_rows(w.ps, AT_SECOND_SHIFT, column_sum(grad_two))
    cotan = r.cotangent[...].astype(f32)
    to_rows(w.ps, AT_DOWN_BIAS, column_sum(cotan))
    grad_res = cotan + norm_back(grad_two, xhat_two, inverse_two, r.second_gain[...])
    w.grad_res[...] = grad_res
    grad_branch = grad_res.astype(bf16)
    w.grad_branch[...] = grad_branch
    to_rows(w.ps, AT_OUTPUT_BIAS, column_sum(grad_branch.astype(f32)))

    @pl.loop(0, width // 256)
    def _(step):
        at = step_at(step, 256)
        w.gpre_send[at, :] = dot_nt(w.w_out[at, :], w.grad_branch[...]).astype(bf16)

    move_gpre = ToAll(net, sems.gpre, lambda t: w.gpre_send.at[step_at(chan_block_of(t), ch)], w.gpre_recv.at[own_slot])
    move_gpre.start()
    w.gpre_recv[own_slot, :] = w.gpre_send[own_block, :]

    for j in range(1, chips + 1):
        sum_result.start(lax.rem(net.p + j, chips))

    @pl.loop(0, ff // LANES)
    def _(step):
        at = step_at(step, LANES)
        turned = w.act_three[:, at].astype(f32).T.astype(bf16)
        w.down_send[at, :] = dot_nn(turned, w.cotan[...]).astype(bf16)

    move_gpre.wait()
    move_down_grad = AlongPlanes(
        net, sems.down_grad, lambda z: w.down_send.at[step_at(z, part)], down_recv.at[step_at(net.z, part)]
    )
    move_down_grad.start()
    to_local(w.down_send.at[step_at(net.z, part)], down_recv.at[step_at(net.z, part)])

    w.sums[...] = jnp.zeros_like(w.sums)

    @pl.loop(0, 2 * blocks)
    def _(d):
        a, n, _, _ = place(d)
        at = step_at(a, ch)
        grad_pre = w.gpre_recv[step_at(d, ch), :].astype(f32)
        grad_long = grad_pre * w.conv[d, ch : 2 * ch, :]
        w.grad_long[n, at, :] = grad_long
        w.grad_conv[a, n, ch : 2 * ch, :] = grad_pre * w.long[n, at, :]
        w.sums[5, :ch, :] += grad_long * w.carried[n, at, :]

    to_spectrum(g, w.grad_long, 2 * ch, w.stage, r.turns, r.forth_high, r.forth_low, w.spec_grad)

    def back_product(at):
        (hr, hi), (gr, gi) = halves(both(w.spec_filt[at])), halves(w.spec_grad[at])
        return hr * gr + hi * gi, hr * gi - hi * gr

    from_spectrum(g, back_product, 2 * ch, w.stage, r.turns, r.back_high, r.back_low, w.back_sig)

    @pl.loop(0, 2 * blocks)
    def _(d):
        a, n, _, _ = place(d)
        at = step_at(a, ch)
        grad_car = w.back_sig[n, at, :] + w.skip[...] * w.grad_long[n, at, :]
        w.grad_conv[a, n, :ch, :] = grad_car * w.conv[d, 2 * ch :, :]
        w.grad_conv[a, n, 2 * ch :, :] = grad_car * w.conv[d, :ch, :]

    @pl.loop(0, 2 * blocks)
    def _(d):
        a, n, to_row, to_lane = place(d)
        now, after = w.grad_conv[a, n], w.grad_conv[a, n + 1]
        grad = w.taps[2] * now + w.taps[1] * sooner(now, after, 1) + w.taps[0] * sooner(now, after, 2)
        grad = grad.astype(bf16)
        w.gproj_send[to_row, to_lane] = grad
        w.sums[4] += grad.astype(f32)

    move_gproj = AlongPlanes(
        net, sems.gproj, lambda z: w.gproj_send.at[step_at(z, 3 * ch)], w.gproj_recv.at[step_at(net.z, 3 * ch)]
    )
    move_gproj.start()
    w.gproj_recv[step_at(net.z, 3 * ch), :] = w.gproj_send[step_at(net.z, 3 * ch), :]

    for j in range(1, chips):
        sum_result.relay(j)

    sum_out = PlaneSum(net, sems.w_out_grad, w.w_out_grad_sib, w.w_out_grad_recv, after=sum_two)
    for j in range(1, chips + 1):
        chip = lax.rem(net.p + j, chips)
        at = step_at(chip, 2 * tok)
        sum_out.own[at, :] = dot_nn(w.pre_recv[at, :], w.grad_branch[...]).astype(bf16)
        sum_out.start(chip)

    @pl.loop(0, 2 * blocks)
    def _(d):
        a, n, _, _ = place(d)
        grad, now, before = w.grad_conv[a, n], w.padded[a, n + 1], w.padded[a, n]
        w.sums[3] += grad
        w.sums[2] += grad * now
        w.sums[1] += grad * later(now, before, 1)
        w.sums[0] += grad * later(now, before, 2)

    for j in range(1, chips):
        sum_out.relay(j)

    def filt_product(at):
        out = []
        for a in range(2):
            cut = slice(a * ch, (a + 1) * ch)
            (xr, xi), (gr, gi) = halves(w.spec_car[at, cut, :]), halves(w.spec_grad[at, cut, :])
            out.append((xr * gr + xi * gi, xr * gi - xi * gr))
        return out[0][0] + out[1][0], out[0][1] + out[1][1]

    from_spectrum(g, filt_product, ch, w.stage_filt, r.turns, r.back_high, r.back_low, w.back_filt)

    ones = jnp.ones((8, span), f32)
    chan_rows = step_at(net.chan_block, ch)
    w.ct[chan_rows, :] = jnp.zeros((ch, LANES), f32)

    @pl.loop(0, g.length // span)
    def _(step):
        at = step_at(step, span)
        feats = r.features[:, at]
        gate = []
        for k in range(span // LANES):
            fade = jnp.exp(-w.decay[...] * feats[:1, k * LANES : (k + 1) * LANES])
            gate.append(w.back_filt[step * (span // LANES) + k] * fade)
        gate = jnp.concatenate(gate, 1)
        w.ct[chan_rows, :] += dot_nt(gate, w.hid_two[:, at], exact)
        q_two = dot_nn(w.net_weights[3, :FILT, :ch], gate, exact)
        slope_two = q_two * w.cos_two[:, at]
        r_two = slope_two * col(3)
        w.ps[:FILT, :FILT] += dot_nt(w.hid_one[:, at], r_two, exact)
        q_one = dot_nn(r.inner_weight[...], r_two, exact)
        slope_one = q_one * w.cos_one[:, at]
        r_one = slope_one * col(1)
        w.ps[AT_FEAT : AT_FEAT + features_rows, :FILT] += dot_nt(feats, r_one, exact)
        for k, x in enumerate((r_one, slope_one * w.p_one[:, at], r_two, slope_two * w.p_two[:, at])):
            w.ps[AT_VECTOR + 8 * k : AT_VECTOR + 8 * k + 8, :FILT] += dot_nt(ones, x, exact)

    lane = lax.broadcasted_iota(jnp.int32, (ch, LANES), 1)
    tile = w.ct[chan_rows, :]

    def put(tile, k, x):
        return jnp.where(lane == CT_FILTER + k, jnp.sum(x, 1, keepdims=True), tile)

    for b in range(3):
        cut = slice(b * ch, (b + 1) * ch)
        tile = put(tile, b, w.sums[4, cut, :])
        for i in range(3):
            tile = put(tile, 3 + 3 * i + b, w.sums[i, cut, :])
        tile = put(tile, 12 + b, w.sums[3, cut, :])
    tile = put(tile, 15, w.sums[5, :ch, :])
    w.ct[chan_rows, :] = tile
    ct_z = AlongPlanes(net, sems.ct_z, lambda z: w.ct.at[chan_rows], w.ct.at[chan_rows])
    ct_z.start()

    w.out_sum[...] = sum_out.result().astype(bf16)
    own_part = LANES // rows

    def out_grad_copy(k):
        return net.copy(
            w.out_sum.at[k * rows : (k + 1) * rows],
            out_recv.at[step_at(net.z, rows)],
            sems.out_grad,
            net.z,
            net.device(net.m * own_part + k),
            k,
        )

    def out_grad_send(k, act):
        @pl.when(net.m * own_part + k != net.flat)
        def _():
            act(out_grad_copy(k))

    for k in range(own_part):
        out_grad_send(k, lambda copy: copy.start())

        @pl.when(net.m * own_part + k == net.flat)
        def _():
            to_local(w.out_sum.at[k * rows : (k + 1) * rows], out_recv.at[step_at(net.z, rows)])

    def out_grad_end():
        for k in range(own_part):
            out_grad_send(k, lambda copy: copy.wait_send())
        for z in range(planes):

            @pl.when((net.flat // own_part != net.m) | (net.z != z))
            def _():
                here = out_recv.at[z * rows : (z + 1) * rows]
                net.copy(here, here, sems.out_grad, z, net.member(net.sib)).wait_recv()

    block_out[...] = (w.residual[...] + sum_result.result() + r.down_bias[...]).astype(bf16)
    move_gproj.wait()
    sum_one = PlaneSum(net, sems.gn_one, w.gn_one_sib, w.gn_one_recv, after=sum_result)
    shift_sum = gain_sum = jnp.zeros((1, width), f32)
    for j in range(1, chips + 1):
        chip = lax.rem(net.p + j, chips)
        at = step_at(chip, 2 * tok)
        turned = w.gproj_recv[:, at].astype(f32).T.astype(bf16)
        partial = dot_nn(turned, w.w_in_t[...])
        sum_one.own[at, :] = partial.astype(bf16)
        sum_one.start(chip)
        shift_sum = shift_sum + column_sum(partial)
        gain_sum = gain_sum + column_sum(partial * w.act_one[at, :].astype(f32))
    to_rows(w.ps, AT_FIRST_GAIN, (gain_sum - r.first_shift[...] * shift_sum) / r.first_gain[...])
    to_rows(w.ps, AT_FIRST_SHIFT, shift_sum)
    share = PS_ROWS // g.devices
    own_share = step_at(net.flat, share)
    move_ps = ToAll(net, sems.ps, lambda t: w.ps.at[step_at(t, share)], w.ps_recv.at[own_share])
    move_ps.start()
    w.ps_recv[own_share, :] = w.ps[own_share, :]

    @pl.loop(0, width // LANES)
    def _(step):
        at = step_at(step, LANES)
        grad = dot_nn(w.gproj_recv[...], w.act_one[:, at])
        for b in range(3):
            piece = [grad[z * 3 * ch + b * ch : z * 3 * ch + (b + 1) * ch] for z in range(planes)]
            w.in_send[at, b * LANES : (b + 1) * LANES] = jnp.concatenate(piece, 0).T.astype(bf16)

    move_in_grad = ToAll(net, sems.in_grad, lambda t: w.in_send.at[step_at(t, rows)], in_recv.at[own_rows])
    move_in_grad.start()
    to_local(w.in_send.at[own_rows], in_recv.at[own_rows])
    for j in range(1, chips):
        sum_one.relay(j)
    ct_z.wait()
    gather_ct = PlaneGather(net, sems.ct, lambda m: w.ct.at[step_at(m, LANES)])
    gather_ct.start()
    move_ps.wait()
    total = w.ps_recv[:share, :]
    for k in range(1, g.devices):
        total = total + w.ps_recv[k * share : (k + 1) * share, :]
    w.ps_all[own_share, :] = total
    move_back = ToAll(net, sems.ps_back, lambda t: w.ps_all.at[own_share], w.ps_all.at[own_share])
    move_back.start()
    gather_ct.forward_all()
    grad_one = sum_one.result()

    grad_tokens = norm_back(grad_one, w.xhat_one[...], inverse_one, r.first_gain[...])
    tokens_grad[...] = (w.grad_res[...] + grad_tokens).astype(bf16)
    gather_ct.wait_all()
    ct_out[...] = w.ct[...]
    move_back.wait()
    ps_out[...] = w.ps_all[...]
    move_in_grad.wait()
    move_up_grad.wait()
    move_down_grad.wait()
    out_grad_end()
    net.finish()


def finish_kernel(g, *refs):
    ins, outs = refs[:8], refs[8:]
    block_in, tokens_in, ct, ps, in_recv, up_recv, down_recv, out_recv = ins
    (
        block_out, tokens_grad, first_gain, first_shift, input_weight, input_bias, short_weight, short_bias, feat_weight,
        feat_bias, feat_freq, inner_weight, inner_bias, inner_freq, filter_weight, skip_gain, output_weight, output_bias,
        second_gain, second_shift, up_weight, up_bias, down_weight, down_bias,
    ) = outs
    rows, planes, width, ff = g.rows, g.planes, g.width, g.ff_part
    block_out[...] = block_in[...]
    tokens_grad[...] = tokens_in[...]
    for m in range(g.members):
        x, q = m // INNER, m % INNER
        parts = [x * g.n_seq + z * INNER + q for z in range(planes)]
        total = sum(in_recv[k * rows : (k + 1) * rows, :].astype(f32) for k in parts)
        for b in range(3):
            input_weight[:, b * width + m * LANES : b * width + (m + 1) * LANES] = total[:, b * LANES : (b + 1) * LANES]
        total = sum(up_recv[k * rows : (k + 1) * rows, :].astype(f32) for k in parts)
        for z, k in enumerate(parts):
            cut = slice(z * g.down_rows, (z + 1) * g.down_rows)
            up_weight[:, k * g.down_rows : (k + 1) * g.down_rows] = total[:, cut]
    down_weight[...] = sum(down_recv[z * g.down_rows : (z + 1) * g.down_rows, :].astype(f32) for z in range(planes))
    output_weight[...] = sum(out_recv[z * rows : (z + 1) * rows, :].astype(f32) for z in range(planes))
    for m in range(g.members):
        cut = slice(m * LANES, (m + 1) * LANES)
        turned = ct[cut, :].T
        filter_weight[:, cut] = turned[:FILT, :]
        line = lambda k: turned[CT_FILTER + k : CT_FILTER + k + 1, :]
        for b in range(3):
            at = b * g.members + m
            input_bias[at : at + 1, :] = line(b)
            for i in range(3):
                short_weight[i : i + 1, b * width + m * LANES : b * width + (m + 1) * LANES] = line(3 + 3 * i + b)
            short_bias[at : at + 1, :] = line(12 + b)
        skip_gain[m : m + 1, :] = line(15)
    for out, at in (
        (first_gain, AT_FIRST_GAIN), (first_shift, AT_FIRST_SHIFT), (second_gain, AT_SECOND_GAIN), (up_bias, AT_UP_BIAS),
        (second_shift, AT_SECOND_SHIFT), (output_bias, AT_OUTPUT_BIAS), (down_bias, AT_DOWN_BIAS),
    ):
        out[...] = ps[at : at + out.shape[0], :]
    feat_weight[...] = ps[AT_FEAT : AT_FEAT + FEAT, :FILT]
    inner_weight[...] = ps[:FILT, :FILT]
    for k, out in enumerate((feat_bias, feat_freq, inner_bias, inner_freq)):
        out[...] = ps[AT_VECTOR + 8 * k : AT_VECTOR + 8 * k + 1, :FILT]


def on_device_in_kernels(g, *args):
    operands = [a[0] if a.ndim == 3 else a[None] if a.ndim == 1 else a for a in args]
    operands += [jnp.asarray(table) for table in constant_tables(g.blocks, LANES)]
    tok, width = g.tok, g.width
    in_vmem = pl.BlockSpec(memory_space=pltpu.VMEM)
    anywhere = pl.BlockSpec(memory_space=pl.ANY)
    S = jax.ShapeDtypeStruct
    parts = pl.pallas_call(
        functools.partial(block_kernel, g),
        out_shape=[
            S((tok, width), bf16),
            S((tok, width), bf16),
            S((width, LANES), f32),
            S((PS_ROWS, LANES), f32),
            S((g.devices * g.rows, 3 * LANES), bf16),
            S((g.devices * g.rows, g.ff_part), bf16),
            S((g.planes * g.down_rows, width), bf16),
            S((g.planes * g.rows, width), bf16),
        ],
        in_specs=[in_vmem] * len(operands),
        out_specs=[in_vmem] * 4 + [anywhere] * 4,
        scratch_shapes=[pltpu.VMEM(shape, dtype) for shape, dtype in scratch_buffers(g).values()]
        + [pltpu.SemaphoreType.DMA((count,)) for count in SEMAPHORES.values() for _ in range(2)]
        + [pltpu.SemaphoreType.DMA],
        compiler_params=pltpu.CompilerParams(
            collective_id=0, has_side_effects=True, vmem_limit_bytes=63 * 1024 * 1024
        ),
        name="block",
    )(*operands)

    def out_shape(a):
        if a.ndim == 3:
            return S(a.shape[1:], bf16)
        if a.ndim == 1:
            return S((a.shape[0] // LANES, LANES) if a.shape[0] % LANES == 0 else (1, a.shape[0]), f32)
        return S(a.shape, f32)

    named = Inputs(*args, *operands[len(args) :])
    wanted = [a for a in args if a is not named.cotangent and a is not named.decay_rates]
    wanted = [named.tokens] + wanted
    outs = pl.pallas_call(
        functools.partial(finish_kernel, g),
        out_shape=[out_shape(a) for a in wanted],
        in_specs=[in_vmem] * 8,
        out_specs=[in_vmem] * len(wanted),
        compiler_params=pltpu.CompilerParams(vmem_limit_bytes=63 * 1024 * 1024),
        name="finish",
    )(*parts)
    return tuple(o.reshape(a.shape) for o, a in zip(outs, wanted))


def on_device_by_size(tokens, cotangent, *args):
    named = Inputs(tokens, cotangent, *args, *[None] * 6)
    g = Geometry(
        lax.axis_size("dp"),
        lax.axis_size("seq"),
        tokens.shape[1],
        tokens.shape[2],
        named.up_weight.shape[1],
        named.input_weight.shape[0],
        named.down_weight.shape[0],
    )
    if g.fits():
        return on_device_in_kernels(g, tokens, cotangent, *args)
    return on_device(tokens, cotangent, *args)


def solution(mesh):
    placed = (
        P("dp", "seq", None),
        P("dp", "seq", None),
        P(),
        P(),
        P(("dp", "seq"), None),
        P(),
        P(),
        P(),
        P(),
        P(),
        P(),
        P(),
        P(),
        P(),
        P(),
        P(),
        P(),
        P(("dp", "seq"), None),
        P(),
        P(),
        P(),
        P(("dp", "seq"), None),
        P(),
        P(("dp", "seq"), None),
        P(),
    )
    return jax.shard_map(
        on_device_by_size,
        mesh=mesh,
        in_specs=placed,
        out_specs=(
            P("dp", "seq", None),
            P("dp", "seq", None),
            P(),
            P(),
            P(("dp", "seq"), None),
            P(),
            P(),
            P(),
            P(),
            P(),
            P(),
            P(),
            P(),
            P(),
            P(),
            P(),
            P(("dp", "seq"), None),
            P(),
            P(),
            P(),
            P(("dp", "seq"), None),
            P(),
            P(("dp", "seq"), None),
            P(),
        ),
        check_vma=False,
    )
```

```python
import functools
import math
import types
from typing import NamedTuple

import jax
import jax.numpy as jnp
import ml_dtypes
import numpy as np
from jax import lax
from jax.experimental import pallas as pl
from jax.experimental.pallas import tpu as pltpu
from jax.sharding import PartitionSpec as P

FEAT = 33
FILT = 64


exact_precision = lax.Precision.HIGHEST


def from_behind(x, axis, by):
    size = lax.axis_size(axis)
    pairs = [(i, i + by) for i in range(size) if 0 <= i + by < size]
    return lax.ppermute(x, axis, pairs)


def layer_norm(values, gain_vec, offset):
    center = values - jnp.mean(values, -1, keepdims=True)
    spread = jnp.mean(center * center, -1, keepdims=True)
    return center * lax.rsqrt(spread + 1e-05) * gain_vec + offset


def position_features(stamps, length):
    stamp_float = stamps.astype(jnp.float32)
    linear_ramp = stamp_float / (length - 1)
    band_rates = 0.0001 + jnp.arange((FEAT - 1) // 2).astype(jnp.float32) * ((15.0 - 0.0001) / 15.0)
    phase_angle = (stamp_float * (2.0 * math.pi / length))[:, None] * band_rates[None, :]
    return jnp.concatenate([linear_ramp[:, None], jnp.cos(phase_angle), -jnp.sin(phase_angle)], 1)


def filter_net(
    feat_weight,
    feat_bias,
    feat_freq,
    inner_weight,
    inner_bias,
    inner_freq,
    filter_weight,
    feature_rows,
    modulate,
):
    hidden = jnp.sin(
        feat_freq * (jnp.dot(feature_rows, feat_weight, precision=exact_precision) + feat_bias)
    )
    hidden = jnp.sin(
        inner_freq * (jnp.dot(hidden, inner_weight, precision=exact_precision) + inner_bias)
    )
    raw_filter = lax.dot_general(
        filter_weight, hidden, (((0,), (1,)), ((), ())), precision=exact_precision
    )
    return raw_filter * modulate


def short_conv(padded, kernel, offset):
    col_count = padded.shape[1] - 2
    return (
        offset[:, None]
        + kernel[0][:, None] * padded[:, :col_count]
        + kernel[1][:, None] * padded[:, 1 : col_count + 1]
        + kernel[2][:, None] * padded[:, 2:]
    )


def unit_angles(rows, cols, period):
    row_index = lax.broadcasted_iota(jnp.int32, (rows, cols), 0)
    col_index = lax.broadcasted_iota(jnp.int32, (rows, cols), 1)
    phase_angle = (row_index * col_index % period).astype(jnp.float32) * (2.0 * math.pi / period)
    return (jnp.cos(phase_angle), jnp.sin(phase_angle))


def forward_frequency_domain(signal, outer_size, period):
    block_count = signal.shape[1]
    row_count = signal.shape[2]
    cos_first, sin_first = unit_angles(outer_size, block_count, outer_size)
    real_first = jnp.einsum("dn,cnt->cdt", cos_first, signal, precision=exact_precision)
    imag_first = -jnp.einsum("dn,cnt->cdt", sin_first, signal, precision=exact_precision)
    cos_turn, sin_turn = unit_angles(outer_size, row_count, period)
    real_turned = real_first * cos_turn + imag_first * sin_turn
    imag_turned = imag_first * cos_turn - real_first * sin_turn
    cos_last, sin_last = unit_angles(row_count, row_count, row_count)
    real_out = jnp.einsum(
        "cdb,bk->cdk", real_turned, cos_last, precision=exact_precision
    ) + jnp.einsum("cdb,bk->cdk", imag_turned, sin_last, precision=exact_precision)
    imag_out = jnp.einsum(
        "cdb,bk->cdk", imag_turned, cos_last, precision=exact_precision
    ) - jnp.einsum("cdb,bk->cdk", real_turned, sin_last, precision=exact_precision)
    return (real_out, imag_out)


def inverse_spectrum(real_part, imag_part, block_count, period):
    outer_size = real_part.shape[1]
    row_count = real_part.shape[2]
    cos_last, sin_last = unit_angles(row_count, row_count, row_count)
    real_back = jnp.einsum(
        "cdk,kb->cdb", real_part, cos_last, precision=exact_precision
    ) - jnp.einsum("cdk,kb->cdb", imag_part, sin_last, precision=exact_precision)
    imag_back = jnp.einsum(
        "cdk,kb->cdb", real_part, sin_last, precision=exact_precision
    ) + jnp.einsum("cdk,kb->cdb", imag_part, cos_last, precision=exact_precision)
    cos_turn, sin_turn = unit_angles(outer_size, row_count, period)
    real_turned = real_back * cos_turn - imag_back * sin_turn
    imag_turned = real_back * sin_turn + imag_back * cos_turn
    cos_first, sin_first = unit_angles(block_count, outer_size, outer_size)
    summed = jnp.einsum(
        "nd,cdt->cnt", cos_first, real_turned, precision=exact_precision
    ) - jnp.einsum("nd,cdt->cnt", sin_first, imag_turned, precision=exact_precision)
    return summed / period


def on_device(
    tokens,
    cotangent,
    first_gain,
    first_shift,
    input_weight,
    input_bias,
    short_weight,
    short_bias,
    feat_weight,
    feat_bias,
    feat_freq,
    inner_weight,
    inner_bias,
    inner_freq,
    filter_weight,
    skip_gain,
    decay_rates,
    output_weight,
    output_bias,
    second_gain,
    second_shift,
    up_weight,
    up_bias,
    down_weight,
    down_bias,
):
    sequence_count = lax.axis_size("seq")
    seq_index = lax.axis_index("seq")
    row_count = tokens.shape[1]
    model_width = tokens.shape[2]
    length = row_count * sequence_count
    period = 2 * length
    outer_size = 2 * sequence_count
    narrow = model_width // sequence_count
    inputs = tokens[0].astype(jnp.float32)
    cotan_rows = cotangent[0].astype(jnp.float32)
    w_in, w_out, w_up, w_down = (
        lax.all_gather(input_weight, ("dp", "seq"), axis=0, tiled=True),
        lax.all_gather(output_weight, ("dp", "seq"), axis=0, tiled=True),
        lax.all_gather(up_weight, ("dp", "seq"), axis=0, tiled=True),
        lax.all_gather(down_weight, ("dp", "seq"), axis=0, tiled=True),
    )
    normed_one, norm_one_back = jax.vjp(layer_norm, inputs, first_gain, first_shift)
    act_one = normed_one.astype(jnp.bfloat16)
    projected = lax.dot_general(
        w_in, act_one, (((0,), (1,)), ((), ())), preferred_element_type=jnp.float32
    )
    projected = projected + input_bias[:, None]
    rim_rows = from_behind(projected[:, row_count - 2 :], "seq", 1)
    padded = jnp.concatenate([rim_rows, projected], 1)
    conv_out, short_back = jax.vjp(short_conv, padded, short_weight, short_bias)
    leading_gate = conv_out[:model_width]
    second_gate = conv_out[model_width : 2 * model_width]
    value_part = conv_out[2 * model_width :]
    carried = leading_gate * value_part
    stamps = seq_index * row_count + lax.iota(jnp.int32, row_count)
    modulate = jnp.exp(-decay_rates[:, None] * (stamps.astype(jnp.float32) / (length - 1))[None, :])
    filter_fixed = functools.partial(
        filter_net, feature_rows=position_features(stamps, length), modulate=modulate
    )
    filters, filter_back = jax.vjp(
        filter_fixed,
        feat_weight,
        feat_bias,
        feat_freq,
        inner_weight,
        inner_bias,
        inner_freq,
        filter_weight,
    )
    carried_blocks = carried.reshape(sequence_count, narrow, row_count)
    filter_blocks = filters.reshape(sequence_count, narrow, row_count)
    carried_chan, filter_chan = (
        lax.all_to_all(
            carried_blocks.astype(jnp.bfloat16), "seq", split_axis=0, concat_axis=2, tiled=True
        ).astype(carried_blocks.dtype),
        lax.all_to_all(
            filter_blocks.astype(jnp.bfloat16), "seq", split_axis=0, concat_axis=2, tiled=True
        ).astype(filter_blocks.dtype),
    )
    carried_chan = carried_chan.reshape(narrow, sequence_count, row_count)
    filter_chan = filter_chan.reshape(narrow, sequence_count, row_count)
    carried_real, carried_imag = forward_frequency_domain(carried_chan, outer_size, period)
    filter_real, filter_imag = forward_frequency_domain(filter_chan, outer_size, period)
    conv_chan = inverse_spectrum(
        carried_real * filter_real - carried_imag * filter_imag,
        carried_real * filter_imag + carried_imag * filter_real,
        sequence_count,
        period,
    )
    conv_rows = lax.all_to_all(
        conv_chan.reshape(1, narrow, length).astype(jnp.bfloat16),
        "seq",
        split_axis=2,
        concat_axis=0,
        tiled=True,
    ).astype(jnp.float32)
    long_out = conv_rows.reshape(model_width, row_count) + skip_gain[:, None] * carried
    act_pre = (second_gate * long_out).astype(jnp.bfloat16)
    branch_out = lax.dot_general(
        act_pre, w_out, (((0,), (0,)), ((), ())), preferred_element_type=jnp.float32
    )
    residual = inputs + branch_out + output_bias
    normed_two, norm_two_back = jax.vjp(layer_norm, residual, second_gain, second_shift)
    act_two = normed_two.astype(jnp.bfloat16)
    upper = jnp.dot(act_two, w_up, preferred_element_type=jnp.float32) + up_bias
    gelu_out, gelu_back = jax.vjp(jax.nn.gelu, upper)
    act_three = gelu_out.astype(jnp.bfloat16)
    result = residual + jnp.dot(act_three, w_down, preferred_element_type=jnp.float32) + down_bias
    block_out = result.astype(jnp.bfloat16)[None]
    grad_final = cotan_rows.astype(jnp.bfloat16)
    down_grad = lax.dot_general(
        act_three, grad_final, (((0,), (0,)), ((), ())), preferred_element_type=jnp.float32
    )
    down_bias_grad = jnp.sum(grad_final, 0, dtype=jnp.float32)
    grad_act_three = lax.dot_general(
        grad_final, w_down, (((1,), (1,)), ((), ())), preferred_element_type=jnp.float32
    )
    (grad_upper,) = gelu_back(grad_act_three)
    grad_upper = grad_upper.astype(jnp.bfloat16)
    up_grad = lax.dot_general(
        act_two, grad_upper, (((0,), (0,)), ((), ())), preferred_element_type=jnp.float32
    )
    up_bias_grad = jnp.sum(grad_upper, 0, dtype=jnp.float32)
    grad_norm_two = lax.dot_general(
        grad_upper, w_up, (((1,), (1,)), ((), ())), preferred_element_type=jnp.float32
    )
    grad_resid_norm, second_gain_grad, second_shift_grad = norm_two_back(grad_norm_two)
    grad_residual = cotan_rows + grad_resid_norm
    grad_branch = grad_residual.astype(jnp.bfloat16)
    output_grad = jnp.dot(act_pre, grad_branch, preferred_element_type=jnp.float32)
    output_bias_grad = jnp.sum(grad_branch, 0, dtype=jnp.float32)
    grad_pre = lax.dot_general(
        w_out, grad_branch, (((1,), (1,)), ((), ())), preferred_element_type=jnp.float32
    )
    grad_second = grad_pre * long_out
    grad_long = grad_pre * second_gate
    skip_gain_grad = jnp.sum(grad_long * carried, 1)
    grad_long_blocks = grad_long.reshape(sequence_count, narrow, row_count)
    grad_chan, carried_again, filter_again = (
        lax.all_to_all(
            grad_long_blocks.astype(jnp.bfloat16), "seq", split_axis=0, concat_axis=2, tiled=True
        ).astype(grad_long_blocks.dtype),
        lax.all_to_all(
            carried_blocks.astype(jnp.bfloat16), "seq", split_axis=0, concat_axis=2, tiled=True
        ).astype(carried_blocks.dtype),
        lax.all_to_all(
            filter_blocks.astype(jnp.bfloat16), "seq", split_axis=0, concat_axis=2, tiled=True
        ).astype(filter_blocks.dtype),
    )
    carried_real, carried_imag = forward_frequency_domain(
        carried_again.reshape(narrow, sequence_count, row_count), outer_size, period
    )
    filter_real, filter_imag = forward_frequency_domain(
        filter_again.reshape(narrow, sequence_count, row_count), outer_size, period
    )
    grad_real, grad_imag = forward_frequency_domain(
        grad_chan.reshape(narrow, sequence_count, row_count), outer_size, period
    )
    carried_back = inverse_spectrum(
        filter_real * grad_real + filter_imag * grad_imag,
        filter_real * grad_imag - filter_imag * grad_real,
        sequence_count,
        period,
    )
    filter_grad_chan = inverse_spectrum(
        carried_real * grad_real + carried_imag * grad_imag,
        carried_real * grad_imag - carried_imag * grad_real,
        sequence_count,
        period,
    )
    carried_got, filters_got = (
        lax.all_to_all(
            carried_back.reshape(1, narrow, length).astype(jnp.bfloat16),
            "seq",
            split_axis=2,
            concat_axis=0,
            tiled=True,
        ).astype(jnp.float32),
        lax.all_to_all(
            filter_grad_chan.reshape(1, narrow, length).astype(jnp.bfloat16),
            "seq",
            split_axis=2,
            concat_axis=0,
            tiled=True,
        ).astype(jnp.float32),
    )
    grad_carried = carried_got.reshape(model_width, row_count) + skip_gain[:, None] * grad_long
    grad_filters = filters_got.reshape(model_width, row_count)
    (
        feat_weight_grad,
        feat_bias_grad,
        feat_freq_grad,
        inner_weight_grad,
        inner_bias_grad,
        inner_freq_grad,
        filter_weight_grad,
    ) = filter_back(grad_filters)
    grad_conv = jnp.concatenate(
        [grad_carried * value_part, grad_second, grad_carried * leading_gate], 0
    )
    grad_padded, short_weight_grad, short_bias_grad = short_back(grad_conv)
    rim_grad = from_behind(grad_padded[:, :2], "seq", -1)
    grad_projected = jnp.concatenate(
        [grad_padded[:, 2:row_count], grad_padded[:, row_count:] + rim_grad], 1
    )
    grad_projected = grad_projected.astype(jnp.bfloat16)
    input_grad = lax.dot_general(
        act_one, grad_projected, (((0,), (1,)), ((), ())), preferred_element_type=jnp.float32
    )
    input_bias_grad = jnp.sum(grad_projected, 1, dtype=jnp.float32)
    first_norm_gradient = lax.dot_general(
        grad_projected, w_in, (((0,), (1,)), ((), ())), preferred_element_type=jnp.float32
    )
    grad_inputs, first_gain_grad, first_shift_grad = norm_one_back(first_norm_gradient)
    tokens_grad = (grad_inputs + grad_residual).astype(jnp.bfloat16)[None]
    input_weight_grad, output_weight_grad, up_weight_grad, down_weight_grad = (
        lax.psum_scatter(input_grad, ("dp", "seq"), scatter_dimension=0, tiled=True),
        lax.psum_scatter(output_grad, ("dp", "seq"), scatter_dimension=0, tiled=True),
        lax.psum_scatter(up_grad, ("dp", "seq"), scatter_dimension=0, tiled=True),
        lax.psum_scatter(down_grad, ("dp", "seq"), scatter_dimension=0, tiled=True),
    )
    (
        first_gain_grad,
        first_shift_grad,
        input_bias_grad,
        short_weight_grad,
        short_bias_grad,
        feat_weight_grad,
        feat_bias_grad,
        feat_freq_grad,
        inner_weight_grad,
        inner_bias_grad,
        inner_freq_grad,
        filter_weight_grad,
        skip_gain_grad,
        output_bias_grad,
        second_gain_grad,
        second_shift_grad,
        up_bias_grad,
        down_bias_grad,
    ) = lax.psum(
        (
            first_gain_grad,
            first_shift_grad,
            input_bias_grad,
            short_weight_grad,
            short_bias_grad,
            feat_weight_grad,
            feat_bias_grad,
            feat_freq_grad,
            inner_weight_grad,
            inner_bias_grad,
            inner_freq_grad,
            filter_weight_grad,
            skip_gain_grad,
            output_bias_grad,
            second_gain_grad,
            second_shift_grad,
            up_bias_grad,
            down_bias_grad,
        ),
        ("dp", "seq"),
    )
    return (
        block_out,
        tokens_grad,
        first_gain_grad,
        first_shift_grad,
        input_weight_grad,
        input_bias_grad,
        short_weight_grad,
        short_bias_grad,
        feat_weight_grad,
        feat_bias_grad,
        feat_freq_grad,
        inner_weight_grad,
        inner_bias_grad,
        inner_freq_grad,
        filter_weight_grad,
        skip_gain_grad,
        output_weight_grad,
        output_bias_grad,
        second_gain_grad,
        second_shift_grad,
        up_weight_grad,
        up_bias_grad,
        down_weight_grad,
        down_bias_grad,
    )


f32 = jnp.float32
bf16 = jnp.bfloat16
ON_MESH = pl.DeviceIdType.MESH
INNER = 4
LANES = 128
PS_ROWS = 320
AT_VECTOR = 64
AT_SECOND_GAIN = 72
AT_SECOND_SHIFT = 80
AT_OUTPUT_BIAS = 88
AT_DOWN_BIAS = 96
AT_FIRST_GAIN = 104
AT_FIRST_SHIFT = 112
AT_UP_BIAS = 120
AT_FEAT = 152
AT_CHANNEL = 192


def dot_nn(a, b, precision=None):
    return lax.dot_general(
        a, b, (((1,), (0,)), ((), ())), precision=precision, preferred_element_type=f32
    )


def dot_nt(a, b, precision=None):
    return lax.dot_general(
        a, b, (((1,), (1,)), ((), ())), precision=precision, preferred_element_type=f32
    )


def step_at(index, size):
    return pl.ds(pl.multiple_of(index * size, size), size)


def times_unit(value, turns):
    re, im = value
    c, s = math.cos(2 * math.pi * turns), math.sin(2 * math.pi * turns)
    if abs(s) < 1e-12:
        return (re, im) if c > 0 else (-re, -im)
    if abs(c) < 1e-12:
        return (-im, re) if s > 0 else (im, -re)
    return re * c - im * s, re * s + im * c


def small_transform(values, sign):
    size = len(values)
    if size == 1:
        return values
    even = small_transform(values[0::2], sign)
    odd = small_transform(values[1::2], sign)
    turned = [times_unit(odd[k], sign * k / size) for k in range(size // 2)]
    return [(e[0] + t[0], e[1] + t[1]) for e, t in zip(even, turned)] + [
        (e[0] - t[0], e[1] - t[1]) for e, t in zip(even, turned)
    ]


@functools.lru_cache(None)
def constant_tables(blocks, lanes):
    length = blocks * lanes
    n2 = np.arange(lanes)
    angle = 2 * np.pi * np.outer(n2, n2) / lanes
    c, s = np.cos(angle), np.sin(angle)
    forth = np.block([[c, -s], [s, c]])
    back = np.block([[c, s], [-s, c]])

    def split(x):
        high = x.astype(ml_dtypes.bfloat16)
        return high, (x - high.astype(np.float64)).astype(ml_dtypes.bfloat16)

    turn = 2 * np.pi * np.outer(np.arange(blocks) + 0.25, n2) / length
    turns = np.concatenate([np.cos(turn), np.sin(turn)], 1).astype(np.float32)
    rates = 1e-4 + np.arange((FEAT - 1) // 2) * ((15.0 - 1e-4) / 15.0)
    phase = (2 * np.pi * np.arange(length) / length)[None, :] * rates[:, None]
    ramp = (np.arange(length) / (length - 1))[None, :]
    features = np.concatenate([ramp, np.cos(phase), -np.sin(phase)], 0)
    features = np.pad(features, ((0, -FEAT % 8), (0, 0))).astype(np.float32)
    return split(forth) + split(back) + (turns, features)


def split_dot(x, high, low):
    head = x.astype(bf16)
    tail = (x - head.astype(f32)).astype(bf16)
    return dot_nn(head, high) + dot_nn(tail, high) + dot_nn(head, low)


def sin_cos(x):
    count = jnp.floor(x * (2 / math.pi) + 0.5)
    r = x - count * 1.5703125
    r = r - count * 4.837512969970703e-4
    r = r - count * 7.549789948768648e-8
    r2 = r * r
    s = r + r * r2 * (-1.6666654611e-1 + r2 * (8.3321608736e-3 + r2 * -1.9515295891e-4))
    c = 1.0 - 0.5 * r2 + r2 * r2 * (
        4.166664568298827e-2 + r2 * (-1.388731625493765e-3 + r2 * 2.443315711809948e-5)
    )
    quarter = count - 4.0 * jnp.floor(count * 0.25)
    odd = (quarter == 1.0) | (quarter == 3.0)
    sine = jnp.where(odd, c, s)
    cosine = jnp.where(odd, s, c)
    sine = jnp.where(quarter >= 2.0, -sine, sine)
    cosine = jnp.where((quarter == 1.0) | (quarter == 2.0), -cosine, cosine)
    return sine, cosine


class Inputs(NamedTuple):
    tokens: jax.Array
    cotangent: jax.Array
    first_gain: jax.Array
    first_shift: jax.Array
    input_weight: jax.Array
    input_bias: jax.Array
    short_weight: jax.Array
    short_bias: jax.Array
    feat_weight: jax.Array
    feat_bias: jax.Array
    feat_freq: jax.Array
    inner_weight: jax.Array
    inner_bias: jax.Array
    inner_freq: jax.Array
    filter_weight: jax.Array
    skip_gain: jax.Array
    decay_rates: jax.Array
    output_weight: jax.Array
    output_bias: jax.Array
    second_gain: jax.Array
    second_shift: jax.Array
    up_weight: jax.Array
    up_bias: jax.Array
    down_weight: jax.Array
    down_bias: jax.Array
    forth_high: jax.Array
    forth_low: jax.Array
    back_high: jax.Array
    back_low: jax.Array
    turns: jax.Array
    features: jax.Array


def scratch_buffers(g):
    tok, width, pt, ch = g.tok, g.width, g.plane_tokens, g.chan
    ff, blocks = g.ff_part, g.blocks
    return dict(
        w_in=((width, 3 * LANES), bf16),
        w_in_send=((g.members * g.rows, 3 * LANES), bf16),
        w_up_send=((g.members * g.rows, ff), bf16),
        w_in_t=((3 * LANES, width), bf16),
        w_out=((width, width), bf16),
        w_up=((width, ff), bf16),
        w_down=((ff, width), bf16),
        act_one=((pt, width), bf16),
        act_two=((pt, width), bf16),
        cotan=((pt, width), bf16),
        proj=((3 * LANES, pt), bf16),
        conv=((3 * LANES, pt), f32),
        grad_conv=((3 * LANES, pt), f32),
        carried=((LANES, pt), f32),
        long=((LANES, pt), f32),
        grad_long=((LANES, pt), f32),
        car_send=((LANES, pt), bf16),
        car_recv=((LANES, pt), bf16),
        y_send=((LANES, pt), bf16),
        y_recv=((LANES, pt), bf16),
        gl_send=((LANES, pt), bf16),
        gl_recv=((LANES, pt), bf16),
        gc_send=((LANES, pt), bf16),
        gc_recv=((LANES, pt), bf16),
        act_pre=((LANES, pt), bf16),
        gpre=((LANES, pt), bf16),
        gproj=((3 * LANES, pt), bf16),
        signal=((blocks, 2 * ch, LANES), f32),
        taps=((4, 3 * LANES, LANES), f32),
        skip=((LANES, LANES), f32),
        edge_send=((16, 3 * LANES), f32),
        edge_recv=((16, 3 * LANES), f32),
        back_edge_send=((16, 3 * LANES), f32),
        back_edge_recv=((16, 3 * LANES), f32),
        edge=((2, 3 * LANES, LANES), f32),
        back_edge=((2, 3 * LANES, LANES), f32),
        ps_recv=((PS_ROWS, LANES), f32),
        ps_line=((PS_ROWS // g.members * g.planes, LANES), f32),
        square=((LANES, LANES), f32),
        param_cols=((LANES, LANES), f32),
        decay=((ch, LANES), f32),
        net_weights=((4, LANES, LANES), f32),
        net_cols=((LANES, LANES), f32),
        p_one=((FILT, g.length), f32),
        hid_one=((FILT, g.length), f32),
        cos_one=((FILT, g.length), f32),
        p_two=((FILT, g.length), f32),
        hid_two=((LANES, g.length), f32),
        cos_two=((FILT, g.length), f32),
        filt=((blocks, ch, LANES), f32),
        stage=((blocks, 2 * ch, 2 * LANES), f32),
        stage_filt=((blocks, ch, 2 * LANES), f32),
        spec_filt=((blocks, ch, 2 * LANES), f32),
        spec_car=((blocks, 2 * ch, 2 * LANES), f32),
        spec_grad=((blocks, 2 * ch, 2 * LANES), f32),
        back_sig=((blocks, 2 * ch, LANES), f32),
        back_filt=((blocks, ch, LANES), f32),
        pre_recv=((width, tok), bf16),
        pre_line=((width, tok), bf16),
        gpre_send=((width, tok), bf16),
        residual=((tok, width), f32),
        xhat_two=((tok, width), f32),
        xhat_one=((tok, width), f32),
        grad_res=((tok, width), f32),
        grad_branch=((tok, width), bf16),
        act_three=((pt, ff), bf16),
        grad_up=((pt, ff), bf16),
        up_send=((width, ff), bf16),
        up_parts=((width, ff), bf16),
        up_pre=((width // g.planes, ff), bf16),
        up_mid=((width // g.planes, ff), bf16),
        down_parts=((ff, width), bf16),
        down_pre=((g.down_rows, width), bf16),
        down_total=((g.down_rows, width), f32),
        down_send=((ff, width), bf16),
        in_mid=((width // g.planes, 3 * LANES), bf16),
        in_send=((width, 3 * LANES), bf16),
        out_sum=((LANES, width), bf16),
        out_parts=((LANES, width), bf16),
        out_pre=((g.rows, width), bf16),
        out_total=((g.rows, width), f32),
        ct=((width, LANES), f32),
        ps=((PS_ROWS, LANES), f32),
        ps_all=((PS_ROWS, LANES), f32),
        gn_two_own=((pt, width), bf16),
        gn_two_send=((pt // 2, width), bf16),
        gn_two_sib=((pt // 2, width), bf16),
        gn_two_recv=((3 * tok, width), bf16),
        result_send=((pt // 2, width), bf16),
        result_sib=((pt // 2, width), bf16),
        result_recv=((3 * tok, width), bf16),
        w_out_grad_sib=((pt // 2, width), bf16),
        w_out_grad_recv=((3 * tok, width), bf16),
        gn_one_sib=((pt // 2, width), bf16),
        gn_one_recv=((3 * tok, width), bf16),
    )


def semaphore_counts(g):
    plane, line, n, far = g.members - 1, g.planes - 1, g.planes, g.n_dp
    gather, add = (n + 1, n), (n, n + 1)
    both = lambda counts: (counts[0] * far, counts[1] * far)
    chips = (2 * g.chips - 1,) * 2
    return dict(
        w_in=(plane,) * 2,
        w_up=(plane,) * 2,
        pre=(plane,) * 2,
        ps=(plane,) * 2,
        ps_back=(plane,) * 2,
        car=(line,) * 2,
        y=(line,) * 2,
        ps_line=(line,) * 2,
        ct_z=(line,) * 2,
        edge=(1, 1),
        back_edge=(1, 1),
        act_one=chips,
        act_two=chips,
        cotan=chips,
        w_out=chips,
        gn_two=chips,
        result=chips,
        w_out_grad=chips,
        w_in_line=both(gather),
        w_up_line=both(gather),
        w_down=gather,
        w_out_line=gather,
        up_grad=both(add),
        in_grad=both(add),
        down_grad=add,
        out_grad=add,
    )


class Geometry:
    def __init__(self, n_dp, n_seq, tok, width, hidden, rows, down_rows):
        self.n_dp, self.n_seq = n_dp, n_seq
        self.devices = n_dp * n_seq
        self.planes = n_seq // INNER
        self.members = n_dp * INNER
        self.chips = self.members // 2
        self.tok, self.width, self.hidden = tok, width, hidden
        self.rows, self.down_rows = rows, down_rows
        self.plane_tokens = self.members * tok
        self.length = n_seq * tok
        self.blocks = n_seq
        self.ff_part = hidden // self.members
        self.chan = LANES // max(self.planes, 1)

    def fits(self):
        return (
            self.n_dp == 2
            and self.n_seq % INNER == 0
            and self.tok == LANES
            and self.width == self.members * LANES
            and self.down_rows % LANES == 0
            and self.rows % 16 == 0
            and self.chan % 16 == 0
            and self.down_rows * self.planes == self.ff_part
        )


class Net:
    def __init__(self, g):
        self.g = g
        self.x, self.s = lax.axis_index("dp"), lax.axis_index("seq")
        self.z, self.q = self.s // INNER, self.s % INNER
        self.m = self.x * INNER + self.q
        self.p, self.c = self.m // 2, self.m % 2
        self.flat = self.x * g.n_seq + self.s
        self.sib = 2 * self.p + 1 - self.c
        self.chan_block = self.m * g.planes + self.z
        self.ends = []

    def device(self, flat):
        return (flat // self.g.n_seq, flat % self.g.n_seq)

    def member(self, m):
        return (m // INNER, self.z * INNER + m % INNER)

    def in_plane(self, z):
        return (self.x, z * INNER + self.q)

    def copy(self, src, dst, sems, k, device, sent=None):
        send, recv = sems
        return pltpu.make_async_remote_copy(
            src_ref=src,
            dst_ref=dst,
            send_sem=send.at[k if sent is None else sent],
            recv_sem=recv.at[k],
            device_id=device,
            device_id_type=ON_MESH,
        )

    def sent(self, *moves):
        for move in moves:
            move.wait_send()
            self.ends.remove(move.wait_send)

    def finish(self):
        for end in self.ends:
            end()


class AlongPlanes:
    def __init__(self, net, sems, src, dst):
        self.net, self.sems, self.src, self.dst = net, sems, src, dst
        net.ends.append(self.wait_send)

    def each(self, act):
        net = self.net
        for j in range(1, net.g.planes):
            z = lax.rem(net.z + j, net.g.planes)
            act(net.copy(self.src(z), self.dst, self.sems, j - 1, net.in_plane(z)))

    def start(self):
        self.each(lambda copy: copy.start())

    def wait(self):
        self.each(lambda copy: copy.wait_recv())

    def wait_send(self):
        self.each(lambda copy: copy.wait_send())


class ToMembers:
    def __init__(self, net, sems, src, dst):
        self.net, self.sems, self.src, self.dst = net, sems, src, dst
        net.ends.append(self.wait_send)

    def each(self, act):
        net = self.net
        for j in range(1, net.g.members):
            m = lax.rem(net.m + j, net.g.members)
            act(net.copy(self.src(m), self.dst, self.sems, j - 1, net.member(m)))

    def start(self):
        self.each(lambda copy: copy.start())

    def wait(self):
        self.each(lambda copy: copy.wait_recv())

    def wait_send(self):
        self.each(lambda copy: copy.wait_send())


def relays(planes):
    return [(2, 1, 0), (planes - 3, planes - 2, planes - 1)] if planes > 3 else []


class LineGather:
    def __init__(self, net, sems, pieces):
        self.net, self.sems, self.pieces = net, sems, pieces
        net.ends.append(self.wait_send)

    def copies(self, source, target, handed):
        n = len(self.pieces(0))
        for k, piece in enumerate(self.pieces(source)):
            sent = (self.net.g.planes if handed else target) * n + k
            yield self.net.copy(piece, piece, self.sems, source * n + k, self.net.in_plane(target), sent)

    def to_plane(self, target, act):
        z = self.net.z
        away = z != target
        for source, _, end in relays(self.net.g.planes):
            if end == target:
                away = away & (z != source)

        @pl.when(away)
        def _():
            for copy in self.copies(z, target, 0):
                act(copy)

    def start(self, far):
        for target in range(self.net.g.planes):
            near = (self.net.z == target - 1) | (self.net.z == target + 1)

            @pl.when((near if not far else jnp.logical_not(near)))
            def _():
                self.to_plane(target, lambda copy: copy.start())

    def hand_on(self):
        for source, through, target in relays(self.net.g.planes):

            @pl.when(self.net.z == through)
            def _():
                for copy in self.copies(source, target, 1):
                    copy.wait_recv()
                    copy.start()

    def wait(self):
        for source in range(self.net.g.planes):
            due = self.net.z != source
            for held, through, _ in relays(self.net.g.planes):
                if held == source:
                    due = due & (self.net.z != through)

            @pl.when(due)
            def _():
                for copy in self.copies(source, 0, 0):
                    copy.wait_recv()

    def wait_send(self):
        for target in range(self.net.g.planes):
            self.to_plane(target, lambda copy: copy.wait_send())
        for source, through, target in relays(self.net.g.planes):

            @pl.when(self.net.z == through)
            def _():
                for copy in self.copies(source, target, 1):
                    copy.wait_send()


class LineSum:
    def __init__(self, net, sems, own, slots, pre):
        self.net, self.sems, self.own, self.slots, self.pre = net, sems, own, slots, pre
        self.ends = [(t, through, 0 if t else net.g.planes - 1) for _, through, t in relays(net.g.planes)]
        net.ends.append(self.wait_send)

    def copies(self, target):
        for k, (piece, slot) in enumerate(zip(self.own(target), self.slots(self.net.z))):
            n = len(self.own(0))
            yield self.net.copy(piece, slot, self.sems, self.net.z * n + k, self.net.in_plane(target), target * n + k)

    def early(self, target, through):
        n = len(self.own(0))
        for k, (piece, held) in enumerate(zip(self.own(target), self.pre)):
            at = self.net.g.planes * n + k
            yield self.net.copy(piece, held, self.sems, at, self.net.in_plane(through), target * n + k)

    def direct(self, target, act):
        away = self.net.z != target
        for end, through, far in self.ends:
            if end == target:
                away = away & (self.net.z != through) & (self.net.z != far)

        @pl.when(away)
        def _():
            for copy in self.copies(target):
                act(copy)

    def start_early(self):
        for target, through, far in self.ends:

            @pl.when(self.net.z == far)
            def _():
                for copy in self.early(target, through):
                    copy.start()

    def start(self, far):
        for target in range(self.net.g.planes):
            near = (self.net.z == target - 1) | (self.net.z == target + 1)

            @pl.when(jnp.logical_not(near) if far else near)
            def _():
                self.direct(target, lambda copy: copy.start())

    def clear(self):
        for target, _, far in self.ends:

            @pl.when(self.net.z == target)
            def _():
                for slot in self.slots(far):
                    slot[...] = jnp.zeros(slot.shape, slot.dtype)

    def add_up(self):
        for target, through, _ in self.ends:

            @pl.when(self.net.z == through)
            def _():
                for copy in self.early(target, through):
                    copy.wait_recv()
                for piece, held in zip(self.own(target), self.pre):
                    piece[...] = (piece[...].astype(f32) + held[...].astype(f32)).astype(bf16)
                for copy in self.copies(target):
                    copy.start()

    def wait(self):
        for source in range(self.net.g.planes):
            due = self.net.z != source
            for target, _, far in self.ends:
                if far == source:
                    due = due & (self.net.z != target)

            @pl.when(due)
            def _():
                n = len(self.own(0))
                for k, slot in enumerate(self.slots(source)):
                    self.net.copy(slot, slot, self.sems, source * n + k, self.net.in_plane(source)).wait_recv()

    def wait_send(self):
        for target, through, far in self.ends:

            @pl.when(self.net.z == far)
            def _():
                for copy in self.early(target, through):
                    copy.wait_send()

            @pl.when(self.net.z == through)
            def _():
                for copy in self.copies(target):
                    copy.wait_send()

        for target in range(self.net.g.planes):
            self.direct(target, lambda copy: copy.wait_send())


class PlaneGather:
    def __init__(self, net, sems, piece):
        self.net, self.sems, self.piece = net, sems, piece
        net.ends.append(self.wait_send)

    def peer(self, j):
        return 2 * lax.rem(self.net.p + j, self.net.g.chips) + self.net.c

    def source(self, j):
        return 2 * lax.rem(self.net.p + self.net.g.chips - j, self.net.g.chips) + self.net.c

    def across(self, j):
        net = self.net
        mine = self.piece(net.m)
        return net.copy(mine, mine, self.sems, j - 1, net.member(self.peer(j)))

    def beside(self, j):
        net = self.net
        held = self.piece(self.source(j) if j else net.m)
        return net.copy(held, held, self.sems, net.g.chips - 1 + j, net.member(net.sib))

    def start(self):
        for j in range(1, self.net.g.chips):
            self.across(j).start()
        self.beside(0).start()

    def forward(self, j):
        self.across(j).wait_recv()
        self.beside(j).start()

    def wait(self, j):
        self.beside(j).wait_recv()

    def forward_all(self):
        for j in range(1, self.net.g.chips):
            self.forward(j)

    def wait_all(self):
        for j in range(self.net.g.chips):
            self.wait(j)

    def wait_send(self):
        for j in range(1, self.net.g.chips):
            self.across(j).wait_send()
        for j in range(self.net.g.chips):
            self.beside(j).wait_send()


class PlaneSum:
    def __init__(self, net, sems, sib, recv, own=None, send=None, after=None):
        self.net, self.sems, self.sib, self.recv = net, sems, sib, recv
        if after is None:
            self.own, self.send = own, send
        else:
            self.own, self.send = after.own, after.send
            net.sent(after)
        net.ends.append(self.wait_send)

    def block(self, ref, k):
        return ref.at[step_at(k, self.net.g.tok)]

    def beside(self, chip):
        net = self.net
        return net.copy(
            self.block(self.own, 2 * chip + 1 - net.c), self.block(self.sib, chip), self.sems, chip, net.member(net.sib)
        )

    def across(self, j):
        net = self.net
        chip = lax.rem(net.p + j, net.g.chips)
        return net.copy(
            self.block(self.send, chip),
            self.block(self.recv, j - 1),
            self.sems,
            net.g.chips - 1 + j,
            net.member(2 * chip + net.c),
        )

    def start(self, chip):
        self.beside(chip).start()

    def pair(self, chip):
        self.beside(chip).wait_recv()
        mine = self.own[step_at(2 * chip + self.net.c, self.net.g.tok), :].astype(f32)
        return mine + self.sib[step_at(chip, self.net.g.tok), :].astype(f32)

    def relay(self, j):
        chip = lax.rem(self.net.p + j, self.net.g.chips)
        self.send[step_at(chip, self.net.g.tok), :] = self.pair(chip).astype(bf16)
        self.across(j).start()

    def result(self):
        total = self.pair(self.net.p)
        tok = self.net.g.tok
        for j in range(1, self.net.g.chips):
            self.across(j).wait_recv()
            total = total + self.recv[(j - 1) * tok : j * tok, :].astype(f32)
        return total

    def wait_send(self):
        for chip in range(self.net.g.chips):
            self.beside(chip).wait_send()
        for j in range(1, self.net.g.chips):
            self.across(j).wait_send()


def to_rows(ref, at, row):
    for k in range(row.shape[1] // LANES):
        ref[at + k : at + k + 1, :] = row[:, k * LANES : (k + 1) * LANES]


def column_sum(x):
    return jnp.sum(x, 0, keepdims=True)


def normalized(x):
    center = x - jnp.mean(x, -1, keepdims=True)
    inverse = lax.rsqrt(jnp.mean(center * center, -1, keepdims=True) + 1e-5)
    return center * inverse, inverse


def norm_back(grad, xhat, inverse, gain):
    e = grad * gain
    return (e - jnp.mean(e, -1, keepdims=True) - xhat * jnp.mean(e * xhat, -1, keepdims=True)) * inverse


def gelu_pair(v):
    scale = math.sqrt(2 / math.pi)
    v2 = v * v
    t = jnp.tanh(scale * v * (1.0 + 0.044715 * v2))
    half = 0.5 * (1.0 + t)
    return v * half, half + 0.5 * v * (1.0 - t * t) * (scale * (1.0 + 3 * 0.044715 * v2))


def to_spectrum(g, signal, rows, stage, turns, high, low, out):
    @pl.loop(0, rows // 8)
    def _(step):
        at = step_at(step, 8)
        first = []
        for n in range(g.blocks):
            block = signal[n, at, :]
            angle = -2 * math.pi * n / (4 * g.blocks)
            first.append((block * math.cos(angle), block * math.sin(angle)))
        for k, (re, im) in enumerate(small_transform(first, -1)):
            c, s = turns[k : k + 1, :LANES], turns[k : k + 1, LANES:]
            stage[k, at, :LANES] = re * c + im * s
            stage[k, at, LANES:] = im * c - re * s

    group = 256 // rows

    @pl.loop(0, g.blocks // group)
    def _(step):
        at = step_at(step, group)
        x = stage[at].reshape(group * rows, 2 * LANES)
        out[at] = split_dot(x, high[...], low[...]).reshape(group, rows, 2 * LANES)


def from_spectrum(g, product, rows, stage, turns, high, low, signal):
    group = 256 // rows

    @pl.loop(0, g.blocks // group)
    def _(step):
        at = step_at(step, group)
        re, im = product(at)
        x = jnp.concatenate([re, im], -1).reshape(group * rows, 2 * LANES)
        stage[at] = split_dot(x, high[...], low[...]).reshape(group, rows, 2 * LANES)

    @pl.loop(0, rows // 8)
    def _(step):
        at = step_at(step, 8)
        values = []
        for k in range(g.blocks):
            re, im = stage[k, at, :LANES], stage[k, at, LANES:]
            c, s = turns[k : k + 1, :LANES], turns[k : k + 1, LANES:]
            values.append((re * c - im * s, re * s + im * c))
        for n, (re, im) in enumerate(small_transform(values, 1)):
            angle = 2 * math.pi * n / (4 * g.blocks)
            signal[n, at, :] = (re * math.cos(angle) - im * math.sin(angle)) * (1.0 / g.length)


def halves(x):
    return x[..., :LANES], x[..., LANES:]


def block_kernel(g, *refs):
    refs = list(refs)
    r = Inputs(*(refs.pop(0) for _ in Inputs._fields))
    block_out, tokens_grad, ct_out, ps_out, in_recv, up_recv, down_recv, out_recv = (refs.pop(0) for _ in range(8))
    w = types.SimpleNamespace(**{name: refs.pop(0) for name in scratch_buffers(g)})
    sems = types.SimpleNamespace(**{name: (refs.pop(0), refs.pop(0)) for name in semaphore_counts(g)})
    local_sem = refs.pop(0)
    net = Net(g)
    tok, width, pt, ch, ff = g.tok, g.width, g.plane_tokens, g.chan, g.ff_part
    rows, planes, members, chips, blocks = g.rows, g.planes, g.members, g.chips, g.blocks
    part = g.down_rows
    exact = lax.Precision.HIGHEST

    barrier = pltpu.get_barrier_semaphore()
    partners = [net.member(lax.rem(net.m + j, members)) for j in range(1, members)]
    partners += [net.in_plane(lax.rem(net.z + j, planes)) for j in range(1, planes)]
    for there in partners:
        pl.semaphore_signal(barrier, inc=1, device_id=there, device_id_type=ON_MESH)

    for m in range(members):
        for b in range(3):
            at = b * width + m * LANES
            w.w_in_send[m * rows : (m + 1) * rows, b * LANES : (b + 1) * LANES] = r.input_weight[:, at : at + LANES]

    own_rows = step_at(net.flat, rows)

    def plane_rows(ref, z):
        return [ref.at[step_at(x * planes + z, INNER * rows)] for x in range(g.n_dp)]

    move_in = ToMembers(net, sems.w_in, lambda m: w.w_in_send.at[step_at(m, rows)], w.w_in.at[own_rows])
    line_in = LineGather(net, sems.w_in_line, lambda z: plane_rows(w.w_in, z))
    w.w_down[step_at(net.z, part), :] = r.down_weight[...]
    w.w_out[step_at(net.m * planes + net.z, rows), :] = r.output_weight[...]
    line_down = LineGather(net, sems.w_down, lambda z: [w.w_down.at[step_at(z, part)]])
    line_out = LineGather(net, sems.w_out_line, lambda z: [w.w_out.at[step_at(net.m * planes + z, rows)]])
    pl.semaphore_wait(barrier, len(partners))
    move_in.start()
    line_out.start(far=False)

    xhat_one, inverse_one = normalized(r.tokens[...].astype(f32))
    w.xhat_one[...] = xhat_one
    mine = step_at(net.m, tok)
    w.act_one[mine, :] = (xhat_one * r.first_gain[...] + r.first_shift[...]).astype(bf16)
    gather_one = PlaneGather(net, sems.act_one, lambda m: w.act_one.at[step_at(m, tok)])
    gather_one.start()

    for m in range(members):
        for z in range(planes):
            at = ((m // INNER) * g.n_seq + z * INNER + m % INNER) * part
            w.w_up_send[m * rows : (m + 1) * rows, z * part : (z + 1) * part] = r.up_weight[:, at : at + part]
    w.w_in[own_rows, :] = w.w_in_send[step_at(net.m, rows), :]
    w.w_up[own_rows, :] = w.w_up_send[step_at(net.m, rows), :]
    w.cotan[mine, :] = r.cotangent[...]
    move_up = ToMembers(net, sems.w_up, lambda m: w.w_up_send.at[step_at(m, rows)], w.w_up.at[own_rows])
    line_up = LineGather(net, sems.w_up_line, lambda z: plane_rows(w.w_up, z))
    gather_cotan = PlaneGather(net, sems.cotan, lambda m: w.cotan.at[step_at(m, tok)])

    gather_out = PlaneGather(net, sems.w_out, lambda m: w.w_out.at[step_at(m, LANES)])
    move_up.start()
    line_out.start(far=True)
    move_in.wait()
    line_in.start(far=False)
    line_in.start(far=True)

    w.square[...] = jnp.zeros_like(w.square)
    lane_of = step_at(net.m, LANES)

    def param(row, ref, k, at):
        w.square[row : row + 1, :] = ref[k : k + 1, pl.ds(pl.multiple_of(at + net.m * LANES, LANES), LANES)]

    for b in range(3):
        param(b, r.input_bias, 0, b * width)
        for i in range(3):
            param(3 + 3 * i + b, r.short_weight, i, b * width)
        param(12 + b, r.short_bias, 0, b * width)
    param(15, r.skip_gain, 0, 0)
    param(16, r.decay_rates, 0, 0)
    w.param_cols[...] = w.square[...].T
    here = step_at(net.z, ch)

    def spread(col, rows=slice(None)):
        cols = w.param_cols[rows, col : col + 1]
        return jnp.broadcast_to(cols, (cols.shape[0], LANES))

    for b in range(3):
        for i in range(3):
            w.taps[i, b * LANES : (b + 1) * LANES, :] = spread(3 + 3 * i + b)
        w.taps[3, b * LANES : (b + 1) * LANES, :] = spread(12 + b)
    w.skip[...] = spread(15)
    w.decay[...] = spread(16, here)

    w.square[...] = jnp.zeros_like(w.square)
    for k, ref in enumerate((r.feat_bias, r.feat_freq, r.inner_bias, r.inner_freq)):
        w.square[k : k + 1, :FILT] = ref[...]
    w.net_cols[...] = w.square[...].T
    w.square[...] = jnp.zeros_like(w.square)
    w.square[:FEAT, :FILT] = r.feat_weight[...]
    w.net_weights[0] = w.square[...].T
    w.square[...] = jnp.zeros_like(w.square)
    w.square[:FILT, :FILT] = r.inner_weight[...]
    w.net_weights[1] = w.square[...].T
    w.square[...] = jnp.zeros_like(w.square)
    w.square[:FILT, :] = r.filter_weight[:, lane_of]
    w.net_weights[3] = w.square[...].T
    w.square[...] = jnp.zeros_like(w.square)
    w.square[:ch, :] = w.net_weights[3, here, :]
    w.net_weights[2] = w.square[...]
    w.net_weights[3] = w.square[...].T
    w.hid_two[...] = jnp.zeros_like(w.hid_two)

    span = 4 * LANES
    col = lambda k: w.net_cols[:FILT, k : k + 1]
    features_rows = r.features.shape[0]

    @pl.loop(0, g.length // span)
    def _(step):
        at = step_at(step, span)
        feats = r.features[:, at]
        p_one = dot_nn(w.net_weights[0, :FILT, :features_rows], feats, exact) + col(0)
        hid_one, cos_one = sin_cos(col(1) * p_one)
        p_two = dot_nn(w.net_weights[1, :FILT, :FILT], hid_one, exact) + col(2)
        hid_two, cos_two = sin_cos(col(3) * p_two)
        w.p_one[:, at], w.hid_one[:, at], w.cos_one[:, at] = p_one, hid_one, cos_one
        w.p_two[:, at], w.hid_two[:FILT, at], w.cos_two[:, at] = p_two, hid_two, cos_two
        filters = dot_nn(w.net_weights[2, :ch, :FILT], hid_two, exact)
        for k in range(span // LANES):
            cut = slice(k * LANES, (k + 1) * LANES)
            w.filt[step * (span // LANES) + k] = filters[:, cut] * jnp.exp(-w.decay[...] * feats[:1, cut])

    to_spectrum(g, w.filt, ch, w.stage_filt, r.turns, r.forth_high, r.forth_low, w.spec_filt)

    line_out.hand_on()
    line_in.hand_on()
    gather_one.forward_all()
    line_out.wait()
    gather_out.start()
    line_in.wait()
    move_up.wait()
    for b in range(3):
        turned = w.w_in[:, b * LANES : (b + 1) * LANES].astype(f32).T.astype(bf16)
        w.w_in_t[b * LANES : (b + 1) * LANES, :] = turned
    gather_one.wait_all()
    biases = jnp.concatenate([w.param_cols[:, b : b + 1] for b in range(3)], 0)

    def project(step):
        at = slice(step * 2 * tok, (step + 1) * 2 * tok)
        w.proj[:, at] = (dot_nt(w.w_in_t[...], w.act_one[at, :]) + biases).astype(bf16)

    def columns(a, n):
        return slice((a * INNER + n) * tok, (a * INNER + n + 1) * tok)

    def share_edge(values, n, rows, to_plane, from_plane, send, recv, sem, edge):
        for a in range(2):
            for b in range(3):
                block = values[b * LANES : (b + 1) * LANES, columns(a, n)].astype(f32)
                send[a * 8 : (a + 1) * 8, b * LANES : (b + 1) * LANES] = block.T[rows, :]
        there = lax.rem(to_plane + planes, planes)
        has_next = (to_plane >= 0) & (to_plane < planes)
        has_before = (from_plane >= 0) & (from_plane < planes)

        def copy():
            return net.copy(send, recv, sem, 0, net.in_plane(there))

        @pl.when(has_next)
        def _():
            copy().start()

        @pl.when(jnp.logical_not(has_before))
        def _():
            recv[...] = jnp.zeros_like(recv)

        def end():
            @pl.when(has_next)
            def _():
                copy().wait_send()

        net.ends.append(end)

        def wait():
            @pl.when(has_before)
            def _():
                copy().wait_recv()

            w.square[...] = jnp.zeros_like(w.square)
            for a in range(2):
                for b in range(3):
                    w.square[rows, :] = recv[a * 8 : (a + 1) * 8, b * LANES : (b + 1) * LANES]
                    edge[a, b * LANES : (b + 1) * LANES, :] = w.square[...].T

        return wait

    for half in range(INNER // 2)[::-1]:
        for a in range(2):
            project(a * INNER // 2 + half)
        if half == INNER // 2 - 1:
            wait_edge = share_edge(
                w.proj, INNER - 1, slice(LANES - 8, LANES), net.z + 1, net.z - 1, w.edge_send, w.edge_recv, sems.edge, w.edge
            )
            line_up.start(far=False)

    net.sent(move_in, line_in, move_up, gather_one)

    group = 32
    lane = lax.broadcasted_iota(jnp.int32, (group, LANES), 1)

    def rows_of(b, step):
        return pl.ds(pl.multiple_of(b * LANES + step * group, group), group)

    def rolled(x, by):
        return pltpu.roll(x, by, 1), pltpu.roll(x, (2 * by) % LANES, 1)

    def shifted(here, there, edge):
        return jnp.where(edge(1), there[0], here[0]), jnp.where(edge(2), there[1], here[1])

    from_left, from_right = (lambda k: lane < k), (lambda k: lane >= LANES - k)

    def filter_blocks(step, which):
        for a in range(2):
            conv = {}
            for b in range(3):
                at = rows_of(b, step)
                taps = [w.taps[i, at, :] for i in range(4)]
                before = rolled(w.edge[a, at, :], 1) if 0 in which else None
                for n in range(max(which) + 1):
                    now = w.proj[at, columns(a, n)].astype(f32)
                    turned = rolled(now, 1)
                    if n in which:
                        one, two = shifted(turned, before, from_left)
                        conv[b, n] = taps[3] + taps[2] * now + taps[1] * one + taps[0] * two
                        w.conv[at, columns(a, n)] = conv[b, n]
                    before = turned
            for n in which:
                carried = conv[0, n] * conv[2, n]
                w.carried[rows_of(0, step), columns(a, n)] = carried
                w.car_send[rows_of(0, step), columns(a, n)] = carried.astype(bf16)

    @pl.loop(0, LANES // group)
    def _(step):
        filter_blocks(step, range(1, INNER))

    wait_edge()

    @pl.loop(0, LANES // group)
    def _(step):
        filter_blocks(step, range(1))

    own_z = step_at(net.z, ch)

    def along(sem, send, recv):
        move = AlongPlanes(net, sem, lambda z: send.at[step_at(z, ch)], recv.at[own_z])
        move.start()
        recv[own_z, :] = send[own_z, :]
        return move

    def place(d):
        a, n = d // blocks, d % blocks
        return n, step_at(a, ch), step_at(n // INNER, ch), step_at(a * INNER + n % INNER, LANES)

    def to_signal(recv):
        @pl.loop(0, 2 * blocks)
        def _(d):
            n, at, from_rows, from_lanes = place(d)
            w.signal[n, at, :] = recv[from_rows, from_lanes].astype(f32)

    def to_planes(send):
        @pl.loop(0, 2 * blocks)
        def _(d):
            n, at, to_row, to_lane = place(d)
            send[to_row, to_lane] = w.back_sig[n, at, :].astype(bf16)

    move_car = along(sems.car, w.car_send, w.car_recv)
    gather_cotan.start()
    line_up.hand_on()
    move_car.wait()
    line_down.start(far=False)
    to_signal(w.car_recv)

    def both(filt):
        return jnp.concatenate([filt, filt], 1)

    to_spectrum(g, w.signal, 2 * ch, w.stage, r.turns, r.forth_high, r.forth_low, w.spec_car)

    def forth_product(at):
        (hr, hi), (xr, xi) = halves(both(w.spec_filt[at])), halves(w.spec_car[at])
        return xr * hr - xi * hi, xr * hi + xi * hr

    from_spectrum(g, forth_product, 2 * ch, w.stage, r.turns, r.back_high, r.back_low, w.back_sig)
    to_planes(w.y_send)
    move_y = along(sems.y, w.y_send, w.y_recv)
    gather_out.forward_all()
    move_y.wait()
    line_up.start(far=True)
    line_down.start(far=True)

    @pl.loop(0, LANES // group)
    def _(step):
        at = rows_of(0, step)
        long_out = w.y_recv[at, :].astype(f32) + jnp.tile(w.skip[at, :], (1, members)) * w.carried[at, :]
        w.long[at, :] = long_out
        w.act_pre[at, :] = (w.conv[rows_of(1, step), :] * long_out).astype(bf16)

    own_block = step_at(net.m, LANES)
    move_pre = ToMembers(net, sems.pre, lambda m: w.act_pre.at[:, step_at(m, tok)], w.pre_recv.at[own_block])
    move_pre.start()
    w.pre_recv[own_block, :] = w.act_pre[:, mine]
    gather_cotan.forward_all()
    gather_out.wait_all()
    move_pre.wait()

    def by_line(piece):
        m, z = divmod(piece, planes)
        return (m // INNER) * g.n_seq + z * INNER + m % INNER

    for k in range(members * planes):
        at = by_line(k) * rows
        w.pre_line[k * rows : (k + 1) * rows, :] = w.pre_recv[at : at + rows, :]
    pre_rows = w.pre_line[...].astype(f32).T.astype(bf16)
    branch = dot_nn(pre_rows, w.w_out[...])
    residual = r.tokens[...].astype(f32) + branch + r.output_bias[...]
    w.residual[...] = residual
    xhat_two, inverse_two = normalized(residual)
    w.xhat_two[...] = xhat_two
    w.act_two[mine, :] = (xhat_two * r.second_gain[...] + r.second_shift[...]).astype(bf16)
    gather_two = PlaneGather(net, sems.act_two, lambda m: w.act_two.at[step_at(m, tok)])
    gather_two.start()
    net.sent(move_car, move_y, move_pre)

    gather_cotan.wait_all()
    line_up.wait()
    sum_two = PlaneSum(net, sems.gn_two, w.gn_two_sib, w.gn_two_recv, w.gn_two_own, w.gn_two_send)
    w.ps[...] = jnp.zeros_like(w.ps)
    hidden_block = [net.x * g.n_seq + z * INNER + net.q for z in range(planes)]
    up_bias = jnp.concatenate([r.up_bias[:, step_at(k, part)] for k in hidden_block], 1)
    bias_sum = jnp.zeros((1, ff), f32)
    slopes = []
    for j in range(chips):
        if j == 1:
            gather_two.forward_all()
            line_down.hand_on()
        gather_two.wait(j)
        at = step_at(lax.rem(net.p + chips - j, chips), 2 * tok)
        gelu, slope = gelu_pair(dot_nn(w.act_two[at, :], w.w_up[...]) + up_bias)
        w.act_three[at, :] = gelu.astype(bf16)
        slopes.append(slope)
    def to_local(src, dst):
        copy = pltpu.make_async_copy(src, dst, local_sem.at[0])
        copy.start()
        copy.wait()

    plane_part = INNER * rows

    def parts_of(ref, z):
        at = z * g.n_dp * plane_part
        return [ref.at[pl.ds(at + x * plane_part, plane_part)] for x in range(g.n_dp)]

    def added(ref):
        group_rows = g.n_dp * plane_part
        return sum(ref[z * group_rows : (z + 1) * group_rows, :].astype(f32) for z in range(planes)).astype(bf16)

    def to_owners(sem, mid, out):
        move = ToMembers(net, sem, lambda m: mid.at[step_at(m, rows)], out.at[step_at(net.m, rows)])
        move.start()
        to_local(mid.at[step_at(net.m, rows)], out.at[step_at(net.m, rows)])
        return move

    sum_up = LineSum(
        net,
        sems.up_grad,
        lambda z: plane_rows(w.up_send, z),
        lambda z: parts_of(w.up_parts, z),
        [w.up_pre.at[x * plane_part : (x + 1) * plane_part] for x in range(g.n_dp)],
    )
    sum_down = LineSum(
        net, sems.down_grad, lambda z: [w.down_send.at[step_at(z, part)]], lambda z: [w.down_parts.at[step_at(z, part)]], [w.down_pre]
    )
    @pl.loop(0, ff // 256)
    def _(step):
        at = step_at(step, 256)
        turned = w.act_three[:, at].astype(f32).T.astype(bf16)
        w.down_send[at, :] = dot_nn(turned, w.cotan[...]).astype(bf16)

    sum_down.start_early()
    line_down.wait()
    sum_down.start(far=False)
    sum_down.clear()
    w.down_parts[step_at(net.z, part), :] = w.down_send[step_at(net.z, part), :]
    for j in range(1, chips + 1):
        chip = lax.rem(net.p + j, chips)
        at = step_at(chip, 2 * tok)
        grad_upper = (dot_nt(w.cotan[at, :], w.w_down[...]) * slopes[-j]).astype(bf16)
        w.grad_up[at, :] = grad_upper
        bias_sum = bias_sum + column_sum(grad_upper.astype(f32))
        sum_two.own[at, :] = dot_nt(grad_upper, w.w_up[...]).astype(bf16)
        sum_two.start(chip)
    for z, k in enumerate(hidden_block):
        w.ps[pl.ds(AT_UP_BIAS + k, 1), :] = bias_sum[:, z * part : (z + 1) * part]
    for j in range(1, chips):
        sum_two.relay(j)

    @pl.loop(0, width // 256)
    def _(step):
        at = step_at(step, 256)
        turned = w.act_two[:, at].astype(f32).T.astype(bf16)
        w.up_send[at, :] = dot_nn(turned, w.grad_up[...]).astype(bf16)

    sum_up.start_early()
    sum_down.add_up()
    sum_down.start(far=True)
    for slot, piece in zip(parts_of(w.up_parts, net.z), plane_rows(w.up_send, net.z)):
        slot[...] = piece[...]
    net.sent(gather_cotan)
    sum_result = PlaneSum(net, sems.result, w.result_sib, w.result_recv, w.cotan, w.result_send)
    for j in range(1, chips + 1):
        chip = lax.rem(net.p + j, chips)
        at = step_at(chip, 2 * tok)
        sum_result.own[at, :] = dot_nn(w.act_three[at, :], w.w_down[...]).astype(bf16)
    sum_up.clear()
    sum_up.start(far=False)
    grad_two = sum_two.result()

    xhat_two = w.xhat_two[...]
    to_rows(w.ps, AT_SECOND_GAIN, column_sum(grad_two * xhat_two))
    to_rows(w.ps, AT_SECOND_SHIFT, column_sum(grad_two))
    cotan = r.cotangent[...].astype(f32)
    to_rows(w.ps, AT_DOWN_BIAS, column_sum(cotan))
    grad_res = cotan + norm_back(grad_two, xhat_two, inverse_two, r.second_gain[...])
    w.grad_res[...] = grad_res
    grad_branch = grad_res.astype(bf16)
    w.grad_branch[...] = grad_branch
    to_rows(w.ps, AT_OUTPUT_BIAS, column_sum(grad_branch.astype(f32)))

    per_step = 256 // rows
    for step in range(width // 256):
        grad = dot_nt(w.w_out[step * 256 : (step + 1) * 256, :], w.grad_branch[...]).astype(bf16)
        for k in range(per_step):
            at = by_line(step * per_step + k) * rows
            w.gpre_send[at : at + rows, :] = grad[k * rows : (k + 1) * rows, :]

    move_gpre = ToMembers(net, sems.w_in, lambda m: w.gpre_send.at[step_at(m, LANES)], w.gpre.at[:, mine])
    move_gpre.start()
    w.gpre[:, mine] = w.gpre_send[own_block, :]

    sum_out = PlaneSum(net, sems.w_out_grad, w.w_out_grad_sib, w.w_out_grad_recv, after=sum_two)
    for m in range(members):
        at = slice(m * LANES, (m + 1) * LANES)
        sum_out.own[at, :] = dot_nn(w.pre_line[at, :], w.grad_branch[...]).astype(bf16)
    sum_up.add_up()
    move_gpre.wait()
    for total in (sum_out, sum_result):
        for j in range(1, chips + 1):
            total.start(lax.rem(net.p + j, chips))

    @pl.loop(0, LANES // group)
    def _(step):
        at, second = rows_of(0, step), rows_of(1, step)
        grad_pre = w.gpre[at, :].astype(f32)
        grad_long = grad_pre * w.conv[second, :]
        w.grad_long[at, :] = grad_long
        w.gl_send[at, :] = grad_long.astype(bf16)
        w.grad_conv[second, :] = grad_pre * w.long[at, :]

    move_gl = along(sems.car, w.gl_send, w.gl_recv)
    for j in range(1, chips):
        sum_out.relay(j)
    move_gl.wait()
    sum_up.start(far=True)
    to_signal(w.gl_recv)
    to_spectrum(g, w.signal, 2 * ch, w.stage, r.turns, r.forth_high, r.forth_low, w.spec_grad)

    def back_product(at):
        (hr, hi), (gr, gi) = halves(both(w.spec_filt[at])), halves(w.spec_grad[at])
        return hr * gr + hi * gi, hr * gi - hi * gr

    from_spectrum(g, back_product, 2 * ch, w.stage, r.turns, r.back_high, r.back_low, w.back_sig)
    to_planes(w.gc_send)
    move_gc = along(sems.y, w.gc_send, w.gc_recv)
    for j in range(1, chips):
        sum_result.relay(j)

    def filt_product(at):
        out = []
        for a in range(2):
            cut = slice(a * ch, (a + 1) * ch)
            (xr, xi), (gr, gi) = halves(w.spec_car[at, cut, :]), halves(w.spec_grad[at, cut, :])
            out.append((xr * gr + xi * gi, xr * gi - xi * gr))
        return out[0][0] + out[1][0], out[0][1] + out[1][1]

    from_spectrum(g, filt_product, ch, w.stage_filt, r.turns, r.back_high, r.back_low, w.back_filt)

    ones = jnp.ones((8, span), f32)
    chan_rows = step_at(net.chan_block, ch)
    w.ct[chan_rows, :] = jnp.zeros((ch, LANES), f32)

    @pl.loop(0, g.length // span)
    def _(step):
        at = step_at(step, span)
        feats = r.features[:, at]
        gate = []
        for k in range(span // LANES):
            fade = jnp.exp(-w.decay[...] * feats[:1, k * LANES : (k + 1) * LANES])
            gate.append(w.back_filt[step * (span // LANES) + k] * fade)
        gate = jnp.concatenate(gate, 1)
        w.ct[chan_rows, :] += dot_nt(gate, w.hid_two[:, at], exact)
        q_two = dot_nn(w.net_weights[3, :FILT, :ch], gate, exact)
        slope_two = q_two * w.cos_two[:, at]
        r_two = slope_two * col(3)
        w.ps[:FILT, :FILT] += dot_nt(w.hid_one[:, at], r_two, exact)
        q_one = dot_nn(r.inner_weight[...], r_two, exact)
        slope_one = q_one * w.cos_one[:, at]
        r_one = slope_one * col(1)
        w.ps[AT_FEAT : AT_FEAT + features_rows, :FILT] += dot_nt(feats, r_one, exact)
        for k, x in enumerate((r_one, slope_one * w.p_one[:, at], r_two, slope_two * w.p_two[:, at])):
            w.ps[AT_VECTOR + k : AT_VECTOR + k + 1, :FILT] += dot_nt(ones, x, exact)[:1, :]

    ct_z = AlongPlanes(net, sems.ct_z, lambda z: w.ct.at[chan_rows], w.ct.at[chan_rows])
    ct_z.start()
    sum_up.wait()
    w.up_mid[...] = added(w.up_parts)
    move_up_grad = to_owners(sems.w_up, w.up_mid, up_recv)
    move_gc.wait()

    @pl.loop(0, LANES // group)
    def _(step):
        at, last = rows_of(0, step), rows_of(2, step)
        grad = w.gc_recv[at, :].astype(f32) + jnp.tile(w.skip[at, :], (1, members)) * w.grad_long[at, :]
        w.grad_conv[at, :] = grad * w.conv[last, :]
        w.grad_conv[last, :] = grad * w.conv[at, :]

    wait_back_edge = share_edge(
        w.grad_conv, 0, slice(0, 8), net.z - 1, net.z + 1, w.back_edge_send, w.back_edge_recv, sems.back_edge, w.back_edge
    )

    line_out_grad = LineSum(
        net,
        sems.out_grad,
        lambda z: [w.out_sum.at[step_at(z, rows)]],
        lambda z: [w.out_parts.at[step_at(z, rows)]],
        [w.out_pre],
    )
    w.out_sum[...] = sum_out.result().astype(bf16)
    line_out_grad.start_early()
    line_out_grad.clear()
    line_out_grad.start(far=False)
    line_out_grad.start(far=True)
    w.out_parts[step_at(net.z, rows), :] = w.out_sum[step_at(net.z, rows), :]


    def filter_blocks_back(step, which):
        for a in range(2):
            for b in range(3):
                at = rows_of(b, step)
                taps = [w.taps[i, at, :] for i in range(3)]
                after = rolled(w.back_edge[a, at, :], LANES - 1) if INNER - 1 in which else None
                for n in range(min(which), INNER)[::-1]:
                    now = w.grad_conv[at, columns(a, n)]
                    turned = rolled(now, LANES - 1)
                    if n in which:
                        one, two = shifted(turned, after, from_right)
                        w.gproj[at, columns(a, n)] = (taps[2] * now + taps[1] * one + taps[0] * two).astype(bf16)
                    after = turned

    @pl.loop(0, LANES // group)
    def _(step):
        filter_blocks_back(step, range(INNER - 1))

    wait_back_edge()

    @pl.loop(0, LANES // group)
    def _(step):
        filter_blocks_back(step, range(INNER - 1, INNER))

    @pl.loop(0, width // 256)
    def _(step):
        at = step_at(step, 256)
        grad = dot_nn(w.gproj[...], w.act_one[:, at])
        for b in range(3):
            cut = slice(b * LANES, (b + 1) * LANES)
            w.in_send[at, cut] = grad[cut].T.astype(bf16)

    sum_in = LineSum(
        net,
        sems.in_grad,
        lambda z: plane_rows(w.in_send, z),
        lambda z: parts_of(w.w_in, z),
        [w.w_in_send.at[x * plane_part : (x + 1) * plane_part] for x in range(g.n_dp)],
    )
    line_out_grad.add_up()
    sum_in.start_early()
    sum_in.clear()
    sum_in.start(far=False)
    sum_in.start(far=True)
    for slot, piece in zip(parts_of(w.w_in, net.z), plane_rows(w.in_send, net.z)):
        slot[...] = piece[...]
    ct_z.wait()
    gather_ct = PlaneGather(net, sems.act_one, lambda m: w.ct.at[step_at(m, LANES)])
    gather_ct.start()
    block_out[...] = (w.residual[...] + sum_result.result() + r.down_bias[...]).astype(bf16)
    sum_one = PlaneSum(net, sems.gn_two, w.gn_one_sib, w.gn_one_recv, after=sum_result)
    shift_sum = gain_sum = jnp.zeros((1, width), f32)
    for j in range(1, chips + 1):
        chip = lax.rem(net.p + j, chips)
        at = step_at(chip, 2 * tok)
        turned = w.gproj[:, at].astype(f32).T.astype(bf16)
        partial = dot_nn(turned, w.w_in_t[...])
        sum_one.own[at, :] = partial.astype(bf16)
        sum_one.start(chip)
        shift_sum = shift_sum + column_sum(partial)
        gain_sum = gain_sum + column_sum(partial * w.act_one[at, :].astype(f32))
    to_rows(w.ps, AT_FIRST_GAIN, (gain_sum - r.first_shift[...] * shift_sum) / r.first_gain[...])
    to_rows(w.ps, AT_FIRST_SHIFT, shift_sum)

    kept = w.conv

    @pl.loop(0, LANES // group)
    def _(step):
        for b in range(3):
            at = rows_of(b, step)
            sums = [jnp.zeros((group, LANES), f32)] * 5
            for a in range(2):
                before = rolled(w.edge[a, at, :], 1)
                for n in range(INNER):
                    grad, now = w.grad_conv[at, columns(a, n)], w.proj[at, columns(a, n)].astype(f32)
                    turned = rolled(now, 1)
                    one, two = shifted(turned, before, from_left)
                    terms = (grad * two, grad * one, grad * now, grad, w.gproj[at, columns(a, n)].astype(f32))
                    sums = [x + y for x, y in zip(sums, terms)]
                    before = turned
            for k in range(5):
                kept[at, k * LANES : (k + 1) * LANES] = sums[k]
        at = rows_of(0, step)
        product = w.grad_long[at, :] * w.carried[at, :]
        kept[at, 5 * LANES : 6 * LANES] = sum(product[:, k * LANES : (k + 1) * LANES] for k in range(members))

    which_lane = lax.broadcasted_iota(jnp.int32, (LANES, LANES), 1)
    tile = jnp.zeros((LANES, LANES), f32)
    for k, (kind, b) in enumerate(
        [(4, b) for b in range(3)] + [(i, b) for i in range(3) for b in range(3)] + [(3, b) for b in range(3)] + [(5, 0)]
    ):
        part_sums = kept[b * LANES : (b + 1) * LANES, kind * LANES : (kind + 1) * LANES]
        tile = jnp.where(which_lane == k, jnp.sum(part_sums, 1, keepdims=True), tile)
    w.ps[pl.ds(pl.multiple_of(AT_CHANNEL + net.m * 16, 16), 16), :] = tile.T[:16, :]

    share = PS_ROWS // members
    own_share = step_at(net.m, share)
    move_ps = ToMembers(net, sems.ps, lambda m: w.ps.at[step_at(m, share)], w.ps_recv.at[own_share])
    move_ps.start()
    w.ps_recv[own_share, :] = w.ps[own_share, :]
    for j in range(1, chips):
        sum_one.relay(j)
    sum_in.add_up()
    move_ps.wait()

    def shares_added(ref, count):
        return sum(ref[k * share : (k + 1) * share, :] for k in range(count))

    own_line = step_at(net.z, share)
    w.ps_line[own_line, :] = shares_added(w.ps_recv, members)
    line_ps = AlongPlanes(net, sems.ps_line, lambda z: w.ps_line.at[own_line], w.ps_line.at[own_line])
    line_ps.start()
    sum_down.wait()
    w.down_total[...] = sum(w.down_parts[z * part : (z + 1) * part, :].astype(f32) for z in range(planes))
    down_out = pltpu.make_async_copy(w.down_total, down_recv, local_sem.at[1])
    down_out.start()
    net.ends.append(down_out.wait)
    gather_ct.forward_all()
    line_ps.wait()
    w.ps_all[own_share, :] = shares_added(w.ps_line, planes)
    move_back = ToMembers(net, sems.ps_back, lambda m: w.ps_all.at[own_share], w.ps_all.at[own_share])
    move_back.start()
    sum_in.wait()
    w.in_mid[...] = added(w.w_in)
    move_in_grad = to_owners(sems.pre, w.in_mid, in_recv)
    grad_one = sum_one.result()

    grad_tokens = norm_back(grad_one, w.xhat_one[...], inverse_one, r.first_gain[...])
    tokens_grad[...] = (w.grad_res[...] + grad_tokens).astype(bf16)
    gather_ct.wait_all()
    ct_out[...] = w.ct[...]
    line_out_grad.wait()
    w.out_total[...] = sum(w.out_parts[z * rows : (z + 1) * rows, :].astype(f32) for z in range(planes))
    out_out = pltpu.make_async_copy(w.out_total, out_recv, local_sem.at[2])
    out_out.start()
    net.ends.append(out_out.wait)
    move_back.wait()
    ps_out[...] = w.ps_all[...]
    move_in_grad.wait()
    move_up_grad.wait()
    net.finish()


def finish_kernel(g, *refs):
    ins, outs = refs[:8], refs[8:]
    block_in, tokens_in, ct, ps, in_recv, up_recv, down_recv, out_recv = ins
    (
        block_out, tokens_grad, first_gain, first_shift, input_weight, input_bias, short_weight, short_bias, feat_weight,
        feat_bias, feat_freq, inner_weight, inner_bias, inner_freq, filter_weight, skip_gain, output_weight, output_bias,
        second_gain, second_shift, up_weight, up_bias, down_weight, down_bias,
    ) = outs
    rows, planes, width, ff = g.rows, g.planes, g.width, g.ff_part
    block_out[...] = block_in[...]
    tokens_grad[...] = tokens_in[...]
    for m in range(g.members):
        x, q = m // INNER, m % INNER
        parts = [x * g.n_seq + z * INNER + q for z in range(planes)]
        total = in_recv[m * rows : (m + 1) * rows, :].astype(f32)
        for b in range(3):
            input_weight[:, b * width + m * LANES : b * width + (m + 1) * LANES] = total[:, b * LANES : (b + 1) * LANES]
        total = up_recv[m * rows : (m + 1) * rows, :].astype(f32)
        for z, k in enumerate(parts):
            cut = slice(z * g.down_rows, (z + 1) * g.down_rows)
            up_weight[:, k * g.down_rows : (k + 1) * g.down_rows] = total[:, cut]
    down_weight[...] = down_recv[...]
    output_weight[...] = out_recv[...]
    for m in range(g.members):
        cut = slice(m * LANES, (m + 1) * LANES)
        turned = ct[cut, :].T
        filter_weight[:, cut] = turned[:FILT, :]
        line = lambda k: ps[AT_CHANNEL + 16 * m + k : AT_CHANNEL + 16 * m + k + 1, :]
        for b in range(3):
            at = b * g.members + m
            input_bias[at : at + 1, :] = line(b)
            for i in range(3):
                short_weight[i : i + 1, b * width + m * LANES : b * width + (m + 1) * LANES] = line(3 + 3 * i + b)
            short_bias[at : at + 1, :] = line(12 + b)
        skip_gain[m : m + 1, :] = line(15)
    for out, at in (
        (first_gain, AT_FIRST_GAIN), (first_shift, AT_FIRST_SHIFT), (second_gain, AT_SECOND_GAIN), (up_bias, AT_UP_BIAS),
        (second_shift, AT_SECOND_SHIFT), (output_bias, AT_OUTPUT_BIAS), (down_bias, AT_DOWN_BIAS),
    ):
        out[...] = ps[at : at + out.shape[0], :]
    feat_weight[...] = ps[AT_FEAT : AT_FEAT + FEAT, :FILT]
    inner_weight[...] = ps[:FILT, :FILT]
    for k, out in enumerate((feat_bias, feat_freq, inner_bias, inner_freq)):
        out[...] = ps[AT_VECTOR + k : AT_VECTOR + k + 1, :FILT]


def on_device_in_kernels(g, *args):
    operands = [a[0] if a.ndim == 3 else a[None] if a.ndim == 1 else a for a in args]
    operands += [jnp.asarray(table) for table in constant_tables(g.blocks, LANES)]
    tok, width = g.tok, g.width
    in_vmem = pl.BlockSpec(memory_space=pltpu.VMEM)
    anywhere = pl.BlockSpec(memory_space=pl.ANY)
    S = jax.ShapeDtypeStruct
    parts = pl.pallas_call(
        functools.partial(block_kernel, g),
        out_shape=[
            S((tok, width), bf16),
            S((tok, width), bf16),
            S((width, LANES), f32),
            S((PS_ROWS, LANES), f32),
            S((g.members * g.rows, 3 * LANES), bf16),
            S((g.members * g.rows, g.ff_part), bf16),
            S((g.down_rows, width), f32),
            S((g.rows, width), f32),
        ],
        in_specs=[in_vmem] * len(operands),
        out_specs=[in_vmem] * 4 + [anywhere] * 4,
        scratch_shapes=[pltpu.VMEM(shape, dtype) for shape, dtype in scratch_buffers(g).values()]
        + [pltpu.SemaphoreType.DMA((count,)) for pair in semaphore_counts(g).values() for count in pair]
        + [pltpu.SemaphoreType.DMA((3,))],
        compiler_params=pltpu.CompilerParams(
            collective_id=0, has_side_effects=True, vmem_limit_bytes=63 * 1024 * 1024
        ),
        name="block",
    )(*operands)

    def out_shape(a):
        if a.ndim == 3:
            return S(a.shape[1:], bf16)
        if a.ndim == 1:
            return S((a.shape[0] // LANES, LANES) if a.shape[0] % LANES == 0 else (1, a.shape[0]), f32)
        return S(a.shape, f32)

    named = Inputs(*args, *operands[len(args) :])
    wanted = [a for a in args if a is not named.cotangent and a is not named.decay_rates]
    wanted = [named.tokens] + wanted
    outs = pl.pallas_call(
        functools.partial(finish_kernel, g),
        out_shape=[out_shape(a) for a in wanted],
        in_specs=[in_vmem] * 8,
        out_specs=[in_vmem] * len(wanted),
        compiler_params=pltpu.CompilerParams(vmem_limit_bytes=63 * 1024 * 1024),
        name="finish",
    )(*parts)
    return tuple(o.reshape(a.shape) for o, a in zip(outs, wanted))


def on_device_by_size(tokens, cotangent, *args):
    named = Inputs(tokens, cotangent, *args, *[None] * 6)
    g = Geometry(
        lax.axis_size("dp"),
        lax.axis_size("seq"),
        tokens.shape[1],
        tokens.shape[2],
        named.up_weight.shape[1],
        named.input_weight.shape[0],
        named.down_weight.shape[0],
    )
    if g.fits():
        return on_device_in_kernels(g, tokens, cotangent, *args)
    return on_device(tokens, cotangent, *args)


def solution(mesh):
    placed = (
        P("dp", "seq", None),
        P("dp", "seq", None),
        P(),
        P(),
        P(("dp", "seq"), None),
        P(),
        P(),
        P(),
        P(),
        P(),
        P(),
        P(),
        P(),
        P(),
        P(),
        P(),
        P(),
        P(("dp", "seq"), None),
        P(),
        P(),
        P(),
        P(("dp", "seq"), None),
        P(),
        P(("dp", "seq"), None),
        P(),
    )
    return jax.shard_map(
        on_device_by_size,
        mesh=mesh,
        in_specs=placed,
        out_specs=(
            P("dp", "seq", None),
            P("dp", "seq", None),
            P(),
            P(),
            P(("dp", "seq"), None),
            P(),
            P(),
            P(),
            P(),
            P(),
            P(),
            P(),
            P(),
            P(),
            P(),
            P(),
            P(("dp", "seq"), None),
            P(),
            P(),
            P(),
            P(("dp", "seq"), None),
            P(),
            P(("dp", "seq"), None),
            P(),
        ),
        check_vma=False,
    )
```

```python
import functools
import math
import types
from typing import NamedTuple

import jax
import jax.numpy as jnp
import ml_dtypes
import numpy as np
from jax import lax
from jax.experimental import pallas as pl
from jax.experimental.pallas import tpu as pltpu
from jax.sharding import PartitionSpec as P

FEAT = 33
FILT = 64


exact_precision = lax.Precision.HIGHEST


def from_behind(x, axis, by):
    size = lax.axis_size(axis)
    pairs = [(i, i + by) for i in range(size) if 0 <= i + by < size]
    return lax.ppermute(x, axis, pairs)


def layer_norm(values, gain_vec, offset):
    center = values - jnp.mean(values, -1, keepdims=True)
    spread = jnp.mean(center * center, -1, keepdims=True)
    return center * lax.rsqrt(spread + 1e-05) * gain_vec + offset


def position_features(stamps, length):
    stamp_float = stamps.astype(jnp.float32)
    linear_ramp = stamp_float / (length - 1)
    band_rates = 0.0001 + jnp.arange((FEAT - 1) // 2).astype(jnp.float32) * ((15.0 - 0.0001) / 15.0)
    phase_angle = (stamp_float * (2.0 * math.pi / length))[:, None] * band_rates[None, :]
    return jnp.concatenate([linear_ramp[:, None], jnp.cos(phase_angle), -jnp.sin(phase_angle)], 1)


def filter_net(
    feat_weight,
    feat_bias,
    feat_freq,
    inner_weight,
    inner_bias,
    inner_freq,
    filter_weight,
    feature_rows,
    modulate,
):
    hidden = jnp.sin(
        feat_freq * (jnp.dot(feature_rows, feat_weight, precision=exact_precision) + feat_bias)
    )
    hidden = jnp.sin(
        inner_freq * (jnp.dot(hidden, inner_weight, precision=exact_precision) + inner_bias)
    )
    raw_filter = lax.dot_general(
        filter_weight, hidden, (((0,), (1,)), ((), ())), precision=exact_precision
    )
    return raw_filter * modulate


def short_conv(padded, kernel, offset):
    col_count = padded.shape[1] - 2
    return (
        offset[:, None]
        + kernel[0][:, None] * padded[:, :col_count]
        + kernel[1][:, None] * padded[:, 1 : col_count + 1]
        + kernel[2][:, None] * padded[:, 2:]
    )


def unit_angles(rows, cols, period):
    row_index = lax.broadcasted_iota(jnp.int32, (rows, cols), 0)
    col_index = lax.broadcasted_iota(jnp.int32, (rows, cols), 1)
    phase_angle = (row_index * col_index % period).astype(jnp.float32) * (2.0 * math.pi / period)
    return (jnp.cos(phase_angle), jnp.sin(phase_angle))


def forward_frequency_domain(signal, outer_size, period):
    block_count = signal.shape[1]
    row_count = signal.shape[2]
    cos_first, sin_first = unit_angles(outer_size, block_count, outer_size)
    real_first = jnp.einsum("dn,cnt->cdt", cos_first, signal, precision=exact_precision)
    imag_first = -jnp.einsum("dn,cnt->cdt", sin_first, signal, precision=exact_precision)
    cos_turn, sin_turn = unit_angles(outer_size, row_count, period)
    real_turned = real_first * cos_turn + imag_first * sin_turn
    imag_turned = imag_first * cos_turn - real_first * sin_turn
    cos_last, sin_last = unit_angles(row_count, row_count, row_count)
    real_out = jnp.einsum(
        "cdb,bk->cdk", real_turned, cos_last, precision=exact_precision
    ) + jnp.einsum("cdb,bk->cdk", imag_turned, sin_last, precision=exact_precision)
    imag_out = jnp.einsum(
        "cdb,bk->cdk", imag_turned, cos_last, precision=exact_precision
    ) - jnp.einsum("cdb,bk->cdk", real_turned, sin_last, precision=exact_precision)
    return (real_out, imag_out)


def inverse_spectrum(real_part, imag_part, block_count, period):
    outer_size = real_part.shape[1]
    row_count = real_part.shape[2]
    cos_last, sin_last = unit_angles(row_count, row_count, row_count)
    real_back = jnp.einsum(
        "cdk,kb->cdb", real_part, cos_last, precision=exact_precision
    ) - jnp.einsum("cdk,kb->cdb", imag_part, sin_last, precision=exact_precision)
    imag_back = jnp.einsum(
        "cdk,kb->cdb", real_part, sin_last, precision=exact_precision
    ) + jnp.einsum("cdk,kb->cdb", imag_part, cos_last, precision=exact_precision)
    cos_turn, sin_turn = unit_angles(outer_size, row_count, period)
    real_turned = real_back * cos_turn - imag_back * sin_turn
    imag_turned = real_back * sin_turn + imag_back * cos_turn
    cos_first, sin_first = unit_angles(block_count, outer_size, outer_size)
    summed = jnp.einsum(
        "nd,cdt->cnt", cos_first, real_turned, precision=exact_precision
    ) - jnp.einsum("nd,cdt->cnt", sin_first, imag_turned, precision=exact_precision)
    return summed / period


def on_device(
    tokens,
    cotangent,
    first_gain,
    first_shift,
    input_weight,
    input_bias,
    short_weight,
    short_bias,
    feat_weight,
    feat_bias,
    feat_freq,
    inner_weight,
    inner_bias,
    inner_freq,
    filter_weight,
    skip_gain,
    decay_rates,
    output_weight,
    output_bias,
    second_gain,
    second_shift,
    up_weight,
    up_bias,
    down_weight,
    down_bias,
):
    sequence_count = lax.axis_size("seq")
    seq_index = lax.axis_index("seq")
    row_count = tokens.shape[1]
    model_width = tokens.shape[2]
    length = row_count * sequence_count
    period = 2 * length
    outer_size = 2 * sequence_count
    narrow = model_width // sequence_count
    inputs = tokens[0].astype(jnp.float32)
    cotan_rows = cotangent[0].astype(jnp.float32)
    w_in, w_out, w_up, w_down = (
        lax.all_gather(input_weight, ("dp", "seq"), axis=0, tiled=True),
        lax.all_gather(output_weight, ("dp", "seq"), axis=0, tiled=True),
        lax.all_gather(up_weight, ("dp", "seq"), axis=0, tiled=True),
        lax.all_gather(down_weight, ("dp", "seq"), axis=0, tiled=True),
    )
    normed_one, norm_one_back = jax.vjp(layer_norm, inputs, first_gain, first_shift)
    act_one = normed_one.astype(jnp.bfloat16)
    projected = lax.dot_general(
        w_in, act_one, (((0,), (1,)), ((), ())), preferred_element_type=jnp.float32
    )
    projected = projected + input_bias[:, None]
    rim_rows = from_behind(projected[:, row_count - 2 :], "seq", 1)
    padded = jnp.concatenate([rim_rows, projected], 1)
    conv_out, short_back = jax.vjp(short_conv, padded, short_weight, short_bias)
    leading_gate = conv_out[:model_width]
    second_gate = conv_out[model_width : 2 * model_width]
    value_part = conv_out[2 * model_width :]
    carried = leading_gate * value_part
    stamps = seq_index * row_count + lax.iota(jnp.int32, row_count)
    modulate = jnp.exp(-decay_rates[:, None] * (stamps.astype(jnp.float32) / (length - 1))[None, :])
    filter_fixed = functools.partial(
        filter_net, feature_rows=position_features(stamps, length), modulate=modulate
    )
    filters, filter_back = jax.vjp(
        filter_fixed,
        feat_weight,
        feat_bias,
        feat_freq,
        inner_weight,
        inner_bias,
        inner_freq,
        filter_weight,
    )
    carried_blocks = carried.reshape(sequence_count, narrow, row_count)
    filter_blocks = filters.reshape(sequence_count, narrow, row_count)
    carried_chan, filter_chan = (
        lax.all_to_all(
            carried_blocks.astype(jnp.bfloat16), "seq", split_axis=0, concat_axis=2, tiled=True
        ).astype(carried_blocks.dtype),
        lax.all_to_all(
            filter_blocks.astype(jnp.bfloat16), "seq", split_axis=0, concat_axis=2, tiled=True
        ).astype(filter_blocks.dtype),
    )
    carried_chan = carried_chan.reshape(narrow, sequence_count, row_count)
    filter_chan = filter_chan.reshape(narrow, sequence_count, row_count)
    carried_real, carried_imag = forward_frequency_domain(carried_chan, outer_size, period)
    filter_real, filter_imag = forward_frequency_domain(filter_chan, outer_size, period)
    conv_chan = inverse_spectrum(
        carried_real * filter_real - carried_imag * filter_imag,
        carried_real * filter_imag + carried_imag * filter_real,
        sequence_count,
        period,
    )
    conv_rows = lax.all_to_all(
        conv_chan.reshape(1, narrow, length).astype(jnp.bfloat16),
        "seq",
        split_axis=2,
        concat_axis=0,
        tiled=True,
    ).astype(jnp.float32)
    long_out = conv_rows.reshape(model_width, row_count) + skip_gain[:, None] * carried
    act_pre = (second_gate * long_out).astype(jnp.bfloat16)
    branch_out = lax.dot_general(
        act_pre, w_out, (((0,), (0,)), ((), ())), preferred_element_type=jnp.float32
    )
    residual = inputs + branch_out + output_bias
    normed_two, norm_two_back = jax.vjp(layer_norm, residual, second_gain, second_shift)
    act_two = normed_two.astype(jnp.bfloat16)
    upper = jnp.dot(act_two, w_up, preferred_element_type=jnp.float32) + up_bias
    gelu_out, gelu_back = jax.vjp(jax.nn.gelu, upper)
    act_three = gelu_out.astype(jnp.bfloat16)
    result = residual + jnp.dot(act_three, w_down, preferred_element_type=jnp.float32) + down_bias
    block_out = result.astype(jnp.bfloat16)[None]
    grad_final = cotan_rows.astype(jnp.bfloat16)
    down_grad = lax.dot_general(
        act_three, grad_final, (((0,), (0,)), ((), ())), preferred_element_type=jnp.float32
    )
    down_bias_grad = jnp.sum(grad_final, 0, dtype=jnp.float32)
    grad_act_three = lax.dot_general(
        grad_final, w_down, (((1,), (1,)), ((), ())), preferred_element_type=jnp.float32
    )
    (grad_upper,) = gelu_back(grad_act_three)
    grad_upper = grad_upper.astype(jnp.bfloat16)
    up_grad = lax.dot_general(
        act_two, grad_upper, (((0,), (0,)), ((), ())), preferred_element_type=jnp.float32
    )
    up_bias_grad = jnp.sum(grad_upper, 0, dtype=jnp.float32)
    grad_norm_two = lax.dot_general(
        grad_upper, w_up, (((1,), (1,)), ((), ())), preferred_element_type=jnp.float32
    )
    grad_resid_norm, second_gain_grad, second_shift_grad = norm_two_back(grad_norm_two)
    grad_residual = cotan_rows + grad_resid_norm
    grad_branch = grad_residual.astype(jnp.bfloat16)
    output_grad = jnp.dot(act_pre, grad_branch, preferred_element_type=jnp.float32)
    output_bias_grad = jnp.sum(grad_branch, 0, dtype=jnp.float32)
    grad_pre = lax.dot_general(
        w_out, grad_branch, (((1,), (1,)), ((), ())), preferred_element_type=jnp.float32
    )
    grad_second = grad_pre * long_out
    grad_long = grad_pre * second_gate
    skip_gain_grad = jnp.sum(grad_long * carried, 1)
    grad_long_blocks = grad_long.reshape(sequence_count, narrow, row_count)
    grad_chan, carried_again, filter_again = (
        lax.all_to_all(
            grad_long_blocks.astype(jnp.bfloat16), "seq", split_axis=0, concat_axis=2, tiled=True
        ).astype(grad_long_blocks.dtype),
        lax.all_to_all(
            carried_blocks.astype(jnp.bfloat16), "seq", split_axis=0, concat_axis=2, tiled=True
        ).astype(carried_blocks.dtype),
        lax.all_to_all(
            filter_blocks.astype(jnp.bfloat16), "seq", split_axis=0, concat_axis=2, tiled=True
        ).astype(filter_blocks.dtype),
    )
    carried_real, carried_imag = forward_frequency_domain(
        carried_again.reshape(narrow, sequence_count, row_count), outer_size, period
    )
    filter_real, filter_imag = forward_frequency_domain(
        filter_again.reshape(narrow, sequence_count, row_count), outer_size, period
    )
    grad_real, grad_imag = forward_frequency_domain(
        grad_chan.reshape(narrow, sequence_count, row_count), outer_size, period
    )
    carried_back = inverse_spectrum(
        filter_real * grad_real + filter_imag * grad_imag,
        filter_real * grad_imag - filter_imag * grad_real,
        sequence_count,
        period,
    )
    filter_grad_chan = inverse_spectrum(
        carried_real * grad_real + carried_imag * grad_imag,
        carried_real * grad_imag - carried_imag * grad_real,
        sequence_count,
        period,
    )
    carried_got, filters_got = (
        lax.all_to_all(
            carried_back.reshape(1, narrow, length).astype(jnp.bfloat16),
            "seq",
            split_axis=2,
            concat_axis=0,
            tiled=True,
        ).astype(jnp.float32),
        lax.all_to_all(
            filter_grad_chan.reshape(1, narrow, length).astype(jnp.bfloat16),
            "seq",
            split_axis=2,
            concat_axis=0,
            tiled=True,
        ).astype(jnp.float32),
    )
    grad_carried = carried_got.reshape(model_width, row_count) + skip_gain[:, None] * grad_long
    grad_filters = filters_got.reshape(model_width, row_count)
    (
        feat_weight_grad,
        feat_bias_grad,
        feat_freq_grad,
        inner_weight_grad,
        inner_bias_grad,
        inner_freq_grad,
        filter_weight_grad,
    ) = filter_back(grad_filters)
    grad_conv = jnp.concatenate(
        [grad_carried * value_part, grad_second, grad_carried * leading_gate], 0
    )
    grad_padded, short_weight_grad, short_bias_grad = short_back(grad_conv)
    rim_grad = from_behind(grad_padded[:, :2], "seq", -1)
    grad_projected = jnp.concatenate(
        [grad_padded[:, 2:row_count], grad_padded[:, row_count:] + rim_grad], 1
    )
    grad_projected = grad_projected.astype(jnp.bfloat16)
    input_grad = lax.dot_general(
        act_one, grad_projected, (((0,), (1,)), ((), ())), preferred_element_type=jnp.float32
    )
    input_bias_grad = jnp.sum(grad_projected, 1, dtype=jnp.float32)
    first_norm_gradient = lax.dot_general(
        grad_projected, w_in, (((0,), (1,)), ((), ())), preferred_element_type=jnp.float32
    )
    grad_inputs, first_gain_grad, first_shift_grad = norm_one_back(first_norm_gradient)
    tokens_grad = (grad_inputs + grad_residual).astype(jnp.bfloat16)[None]
    input_weight_grad, output_weight_grad, up_weight_grad, down_weight_grad = (
        lax.psum_scatter(input_grad, ("dp", "seq"), scatter_dimension=0, tiled=True),
        lax.psum_scatter(output_grad, ("dp", "seq"), scatter_dimension=0, tiled=True),
        lax.psum_scatter(up_grad, ("dp", "seq"), scatter_dimension=0, tiled=True),
        lax.psum_scatter(down_grad, ("dp", "seq"), scatter_dimension=0, tiled=True),
    )
    (
        first_gain_grad,
        first_shift_grad,
        input_bias_grad,
        short_weight_grad,
        short_bias_grad,
        feat_weight_grad,
        feat_bias_grad,
        feat_freq_grad,
        inner_weight_grad,
        inner_bias_grad,
        inner_freq_grad,
        filter_weight_grad,
        skip_gain_grad,
        output_bias_grad,
        second_gain_grad,
        second_shift_grad,
        up_bias_grad,
        down_bias_grad,
    ) = lax.psum(
        (
            first_gain_grad,
            first_shift_grad,
            input_bias_grad,
            short_weight_grad,
            short_bias_grad,
            feat_weight_grad,
            feat_bias_grad,
            feat_freq_grad,
            inner_weight_grad,
            inner_bias_grad,
            inner_freq_grad,
            filter_weight_grad,
            skip_gain_grad,
            output_bias_grad,
            second_gain_grad,
            second_shift_grad,
            up_bias_grad,
            down_bias_grad,
        ),
        ("dp", "seq"),
    )
    return (
        block_out,
        tokens_grad,
        first_gain_grad,
        first_shift_grad,
        input_weight_grad,
        input_bias_grad,
        short_weight_grad,
        short_bias_grad,
        feat_weight_grad,
        feat_bias_grad,
        feat_freq_grad,
        inner_weight_grad,
        inner_bias_grad,
        inner_freq_grad,
        filter_weight_grad,
        skip_gain_grad,
        output_weight_grad,
        output_bias_grad,
        second_gain_grad,
        second_shift_grad,
        up_weight_grad,
        up_bias_grad,
        down_weight_grad,
        down_bias_grad,
    )


f32 = jnp.float32
bf16 = jnp.bfloat16
ON_MESH = pl.DeviceIdType.MESH
INNER = 4
LANES = 128
PS_ROWS = 320
AT_VECTOR = 64
AT_SECOND_GAIN = 72
AT_SECOND_SHIFT = 80
AT_OUTPUT_BIAS = 88
AT_DOWN_BIAS = 96
AT_FIRST_GAIN = 104
AT_FIRST_SHIFT = 112
AT_UP_BIAS = 120
AT_FEAT = 152
AT_CHANNEL = 192


def dot_nn(a, b, precision=None):
    return lax.dot_general(
        a, b, (((1,), (0,)), ((), ())), precision=precision, preferred_element_type=f32
    )


def dot_nt(a, b, precision=None):
    return lax.dot_general(
        a, b, (((1,), (1,)), ((), ())), precision=precision, preferred_element_type=f32
    )


def step_at(index, size):
    return pl.ds(pl.multiple_of(index * size, size), size)


def times_unit(value, turns):
    re, im = value
    c, s = math.cos(2 * math.pi * turns), math.sin(2 * math.pi * turns)
    if abs(s) < 1e-12:
        return (re, im) if c > 0 else (-re, -im)
    if abs(c) < 1e-12:
        return (-im, re) if s > 0 else (im, -re)
    return re * c - im * s, re * s + im * c


def small_transform(values, sign):
    size = len(values)
    if size == 1:
        return values
    even = small_transform(values[0::2], sign)
    odd = small_transform(values[1::2], sign)
    turned = [times_unit(odd[k], sign * k / size) for k in range(size // 2)]
    return [(e[0] + t[0], e[1] + t[1]) for e, t in zip(even, turned)] + [
        (e[0] - t[0], e[1] - t[1]) for e, t in zip(even, turned)
    ]


@functools.lru_cache(None)
def constant_tables(blocks, lanes):
    length = blocks * lanes
    n2 = np.arange(lanes)
    angle = 2 * np.pi * np.outer(n2, n2) / lanes
    c, s = np.cos(angle), np.sin(angle)
    forth = np.block([[c, -s], [s, c]])
    back = np.block([[c, s], [-s, c]])

    def split(x):
        high = x.astype(ml_dtypes.bfloat16)
        return high, (x - high.astype(np.float64)).astype(ml_dtypes.bfloat16)

    turn = 2 * np.pi * np.outer(np.arange(blocks) + 0.25, n2) / length
    turns = np.concatenate([np.cos(turn), np.sin(turn)], 1).astype(np.float32)
    rates = 1e-4 + np.arange((FEAT - 1) // 2) * ((15.0 - 1e-4) / 15.0)
    phase = (2 * np.pi * np.arange(length) / length)[None, :] * rates[:, None]
    ramp = (np.arange(length) / (length - 1))[None, :]
    features = np.concatenate([ramp, np.cos(phase), -np.sin(phase)], 0)
    features = np.pad(features, ((0, -FEAT % 8), (0, 0))).astype(np.float32)
    return split(forth) + split(back) + (turns, features)


def split_dot(x, high, low):
    head = x.astype(bf16)
    tail = (x - head.astype(f32)).astype(bf16)
    return dot_nn(head, high) + dot_nn(tail, high) + dot_nn(head, low)


def sin_cos(x):
    count = jnp.floor(x * (2 / math.pi) + 0.5)
    r = x - count * 1.5703125
    r = r - count * 4.837512969970703e-4
    r = r - count * 7.549789948768648e-8
    r2 = r * r
    s = r + r * r2 * (-1.6666654611e-1 + r2 * (8.3321608736e-3 + r2 * -1.9515295891e-4))
    c = 1.0 - 0.5 * r2 + r2 * r2 * (
        4.166664568298827e-2 + r2 * (-1.388731625493765e-3 + r2 * 2.443315711809948e-5)
    )
    quarter = count - 4.0 * jnp.floor(count * 0.25)
    odd = (quarter == 1.0) | (quarter == 3.0)
    sine = jnp.where(odd, c, s)
    cosine = jnp.where(odd, s, c)
    sine = jnp.where(quarter >= 2.0, -sine, sine)
    cosine = jnp.where((quarter == 1.0) | (quarter == 2.0), -cosine, cosine)
    return sine, cosine


class Inputs(NamedTuple):
    tokens: jax.Array
    cotangent: jax.Array
    first_gain: jax.Array
    first_shift: jax.Array
    input_weight: jax.Array
    input_bias: jax.Array
    short_weight: jax.Array
    short_bias: jax.Array
    feat_weight: jax.Array
    feat_bias: jax.Array
    feat_freq: jax.Array
    inner_weight: jax.Array
    inner_bias: jax.Array
    inner_freq: jax.Array
    filter_weight: jax.Array
    skip_gain: jax.Array
    decay_rates: jax.Array
    output_weight: jax.Array
    output_bias: jax.Array
    second_gain: jax.Array
    second_shift: jax.Array
    up_weight: jax.Array
    up_bias: jax.Array
    down_weight: jax.Array
    down_bias: jax.Array
    forth_high: jax.Array
    forth_low: jax.Array
    back_high: jax.Array
    back_low: jax.Array
    turns: jax.Array
    features: jax.Array


def scratch_buffers(g):
    tok, width, pt, ch = g.tok, g.width, g.plane_tokens, g.chan
    ff, blocks = g.ff_part, g.blocks
    return dict(
        up_weight=((g.rows, g.hidden), bf16),
        down_weight=((g.down_rows, width), bf16),
        cotangent=((tok, width), bf16),
        filter_weight=((FILT, width), f32),
        features=((FEAT + -FEAT % 8, g.length), f32),
        forth_high=((2 * LANES, 2 * LANES), bf16),
        forth_low=((2 * LANES, 2 * LANES), bf16),
        back_high=((2 * LANES, 2 * LANES), bf16),
        back_low=((2 * LANES, 2 * LANES), bf16),
        block_out=((tok, width), bf16),
        tokens_grad=((tok, width), bf16),
        w_in=((width, 3 * LANES), bf16),
        w_in_send=((g.members * g.rows, 3 * LANES), bf16),
        w_up_send=((g.members * g.rows, ff), bf16),
        w_in_t=((3 * LANES, width), bf16),
        w_out=((width, width), bf16),
        w_up=((width, ff), bf16),
        w_down=((ff, width), bf16),
        act_one=((pt, width), bf16),
        act_two=((pt, width), bf16),
        cotan=((pt, width), bf16),
        proj=((3 * LANES, pt), bf16),
        conv=((3 * LANES, pt), f32),
        grad_conv=((3 * LANES, pt), f32),
        carried=((LANES, pt), f32),
        long=((LANES, pt), f32),
        grad_long=((LANES, pt), f32),
        car_send=((LANES, pt), bf16),
        car_recv=((LANES, pt), bf16),
        y_send=((LANES, pt), bf16),
        y_recv=((LANES, pt), bf16),
        gl_send=((LANES, pt), bf16),
        gl_recv=((LANES, pt), bf16),
        gc_send=((LANES, pt), bf16),
        gc_recv=((LANES, pt), bf16),
        act_pre=((LANES, pt), bf16),
        gpre=((LANES, pt), bf16),
        gproj=((3 * LANES, pt), bf16),
        signal=((blocks, 2 * ch, LANES), f32),
        taps=((4, 3 * LANES, LANES), f32),
        skip=((LANES, LANES), f32),
        edge_send=((16, 3 * LANES), f32),
        edge_recv=((16, 3 * LANES), f32),
        back_edge_send=((16, 3 * LANES), f32),
        back_edge_recv=((16, 3 * LANES), f32),
        edge=((2, 3 * LANES, LANES), f32),
        back_edge=((2, 3 * LANES, LANES), f32),
        ps_recv=((PS_ROWS, LANES), f32),
        ps_line=((PS_ROWS // g.members * g.planes, LANES), f32),
        square=((LANES, LANES), f32),
        param_cols=((LANES, LANES), f32),
        decay=((ch, LANES), f32),
        net_weights=((4, LANES, LANES), f32),
        net_cols=((LANES, LANES), f32),
        p_one=((FILT, g.length), f32),
        hid_one=((FILT, g.length), f32),
        cos_one=((FILT, g.length), f32),
        p_two=((FILT, g.length), f32),
        hid_two=((LANES, g.length), f32),
        cos_two=((FILT, g.length), f32),
        filt=((blocks, ch, LANES), f32),
        stage=((blocks, 2 * ch, 2 * LANES), f32),
        stage_filt=((blocks, ch, 2 * LANES), f32),
        spec_filt=((blocks, ch, 2 * LANES), f32),
        spec_car=((blocks, 2 * ch, 2 * LANES), f32),
        spec_grad=((blocks, 2 * ch, 2 * LANES), f32),
        back_sig=((blocks, 2 * ch, LANES), f32),
        back_filt=((blocks, ch, LANES), f32),
        pre_recv=((width, tok), bf16),
        pre_line=((width, tok), bf16),
        gpre_send=((width, tok), bf16),
        residual=((tok, width), f32),
        xhat_two=((tok, width), f32),
        xhat_one=((tok, width), f32),
        grad_res=((tok, width), f32),
        grad_branch=((tok, width), bf16),
        act_three=((pt, ff), bf16),
        grad_up=((pt, ff), bf16),
        up_send=((width, ff), bf16),
        up_parts=((width, ff), bf16),
        up_pre=((width // g.planes, ff), bf16),
        up_mid=((width // g.planes, ff), bf16),
        down_parts=((ff, width), bf16),
        down_pre=((g.down_rows, width), bf16),
        down_total=((g.down_rows, width), f32),
        down_send=((ff, width), bf16),
        in_mid=((width // g.planes, 3 * LANES), bf16),
        in_send=((width, 3 * LANES), bf16),
        out_sum=((LANES, width), bf16),
        out_parts=((LANES, width), bf16),
        out_pre=((g.rows, width), bf16),
        out_total=((g.rows, width), f32),
        ct=((width, LANES), f32),
        gain_sum=((1, width), f32),
        ps=((PS_ROWS, LANES), f32),
        ps_all=((PS_ROWS, LANES), f32),
        gn_two_own=((pt, width), bf16),
        gn_two_send=((pt // 2, width), bf16),
        gn_two_sib=((pt // 2, width), bf16),
        gn_two_recv=((3 * tok, width), bf16),
        result_send=((pt // 2, width), bf16),
        result_sib=((pt // 2, width), bf16),
        result_recv=((3 * tok, width), bf16),
        w_out_grad_sib=((pt // 2, width), bf16),
        w_out_grad_recv=((3 * tok, width), bf16),
        gn_one_sib=((pt // 2, width), bf16),
        gn_one_recv=((3 * tok, width), bf16),
    )


def semaphore_counts(g):
    plane, line = (g.members - 1,) * 2, (g.planes - 1,) * 2
    chips = (2 * g.chips - 1,) * 2
    along, along_twice = (g.planes + 1,) * 2, (2 * g.planes + 2,) * 2
    return dict(
        w_in=plane,
        w_up=plane,
        pre=plane,
        ps_back=plane,
        car=line,
        y=line,
        ps_line=line,
        ct_z=line,
        edge=(1, 1),
        back_edge=(1, 1),
        act_one=chips,
        act_two=chips,
        cotan=chips,
        w_out=chips,
        gn_two=chips,
        w_in_line=along_twice,
        w_up_line=along_twice,
        w_out_line=along_twice,
        w_down=along,
    )


class Geometry:
    def __init__(self, n_dp, n_seq, tok, width, hidden, rows, down_rows):
        self.n_dp, self.n_seq = n_dp, n_seq
        self.devices = n_dp * n_seq
        self.planes = n_seq // INNER
        self.members = n_dp * INNER
        self.chips = self.members // 2
        self.tok, self.width, self.hidden = tok, width, hidden
        self.rows, self.down_rows = rows, down_rows
        self.plane_tokens = self.members * tok
        self.length = n_seq * tok
        self.blocks = n_seq
        self.ff_part = hidden // self.members
        self.chan = LANES // max(self.planes, 1)

    def fits(self):
        return (
            self.n_dp == 2
            and self.n_seq % INNER == 0
            and self.tok == LANES
            and self.width == self.members * LANES
            and self.down_rows % LANES == 0
            and self.rows % 16 == 0
            and self.chan % 16 == 0
            and self.down_rows * self.planes == self.ff_part
        )


class Net:
    def __init__(self, g):
        self.g = g
        self.x, self.s = lax.axis_index("dp"), lax.axis_index("seq")
        self.z, self.q = self.s // INNER, self.s % INNER
        self.m = self.x * INNER + self.q
        self.p, self.c = self.m // 2, self.m % 2
        self.flat = self.x * g.n_seq + self.s
        self.sib = 2 * self.p + 1 - self.c
        self.chan_block = self.m * g.planes + self.z
        self.ends = []

    def device(self, flat):
        return (flat // self.g.n_seq, flat % self.g.n_seq)

    def member(self, m):
        return (m // INNER, self.z * INNER + m % INNER)

    def in_plane(self, z):
        return (self.x, z * INNER + self.q)

    def copy(self, src, dst, sems, k, device, sent=None):
        send, recv = sems
        return pltpu.make_async_remote_copy(
            src_ref=src,
            dst_ref=dst,
            send_sem=send.at[k if sent is None else sent],
            recv_sem=recv.at[k],
            device_id=device,
            device_id_type=ON_MESH,
        )

    def sent(self, *moves):
        for move in moves:
            move.wait_send()
            self.ends.remove(move.wait_send)

    def finish(self):
        for end in self.ends:
            end()


class AlongPlanes:
    def __init__(self, net, sems, src, dst):
        self.net, self.sems, self.src, self.dst = net, sems, src, dst
        net.ends.append(self.wait_send)

    def each(self, act):
        net = self.net
        for j in range(1, net.g.planes):
            z = lax.rem(net.z + j, net.g.planes)
            act(net.copy(self.src(z), self.dst, self.sems, j - 1, net.in_plane(z)))

    def start(self):
        self.each(lambda copy: copy.start())

    def wait(self):
        self.each(lambda copy: copy.wait_recv())

    def wait_send(self):
        self.each(lambda copy: copy.wait_send())


class ToMembers:
    def __init__(self, net, sems, src, dst):
        self.net, self.sems, self.src, self.dst = net, sems, src, dst
        net.ends.append(self.wait_send)

    def each(self, act):
        net = self.net
        for j in range(1, net.g.members):
            m = lax.rem(net.m + j, net.g.members)
            act(net.copy(self.src(m), self.dst, self.sems, j - 1, net.member(m)))

    def start(self):
        self.each(lambda copy: copy.start())

    def wait(self):
        self.each(lambda copy: copy.wait_recv())

    def wait_send(self):
        self.each(lambda copy: copy.wait_send())


def relays(planes):
    return [(2, 1, 0), (planes - 3, planes - 2, planes - 1)] if planes > 3 else []


class LineGather:
    def __init__(self, net, sems, pieces):
        self.net, self.sems, self.pieces = net, sems, pieces
        net.ends.append(self.wait_send)

    def copies(self, source, target, handed):
        n = len(self.pieces(0))
        for k, piece in enumerate(self.pieces(source)):
            sent = (self.net.g.planes if handed else target) * n + k
            yield self.net.copy(piece, piece, self.sems, source * n + k, self.net.in_plane(target), sent)

    def to_plane(self, target, act):
        z = self.net.z
        away = z != target
        for source, _, end in relays(self.net.g.planes):
            if end == target:
                away = away & (z != source)

        @pl.when(away)
        def _():
            for copy in self.copies(z, target, 0):
                act(copy)

    def start(self, far):
        for target in range(self.net.g.planes):
            near = (self.net.z == target - 1) | (self.net.z == target + 1)

            @pl.when((near if not far else jnp.logical_not(near)))
            def _():
                self.to_plane(target, lambda copy: copy.start())

    def hand_on(self):
        for source, through, target in relays(self.net.g.planes):

            @pl.when(self.net.z == through)
            def _():
                for copy in self.copies(source, target, 1):
                    copy.wait_recv()
                    copy.start()

    def wait(self):
        for source in range(self.net.g.planes):
            due = self.net.z != source
            for held, through, _ in relays(self.net.g.planes):
                if held == source:
                    due = due & (self.net.z != through)

            @pl.when(due)
            def _():
                for copy in self.copies(source, 0, 0):
                    copy.wait_recv()

    def wait_send(self):
        for target in range(self.net.g.planes):
            self.to_plane(target, lambda copy: copy.wait_send())
        for source, through, target in relays(self.net.g.planes):

            @pl.when(self.net.z == through)
            def _():
                for copy in self.copies(source, target, 1):
                    copy.wait_send()


class LineSum:
    def __init__(self, net, sems, own, slots, pre):
        self.net, self.sems, self.own, self.slots, self.pre = net, sems, own, slots, pre
        self.ends = [(t, through, 0 if t else net.g.planes - 1) for _, through, t in relays(net.g.planes)]
        net.ends.append(self.wait_send)

    def copies(self, target):
        for k, (piece, slot) in enumerate(zip(self.own(target), self.slots(self.net.z))):
            n = len(self.own(0))
            yield self.net.copy(piece, slot, self.sems, self.net.z * n + k, self.net.in_plane(target), target * n + k)

    def early(self, target, through):
        n = len(self.own(0))
        for k, (piece, held) in enumerate(zip(self.own(target), self.pre)):
            at = self.net.g.planes * n + k
            yield self.net.copy(piece, held, self.sems, at, self.net.in_plane(through), target * n + k)

    def direct(self, target, act):
        away = self.net.z != target
        for end, through, far in self.ends:
            if end == target:
                away = away & (self.net.z != through) & (self.net.z != far)

        @pl.when(away)
        def _():
            for copy in self.copies(target):
                act(copy)

    def start_early(self):
        for target, through, far in self.ends:

            @pl.when(self.net.z == far)
            def _():
                for copy in self.early(target, through):
                    copy.start()

    def start(self, far):
        for target in range(self.net.g.planes):
            near = (self.net.z == target - 1) | (self.net.z == target + 1)

            @pl.when(jnp.logical_not(near) if far else near)
            def _():
                self.direct(target, lambda copy: copy.start())

    def clear(self):
        for target, _, far in self.ends:

            @pl.when(self.net.z == target)
            def _():
                for slot in self.slots(far):
                    slot[...] = jnp.zeros(slot.shape, slot.dtype)

    def add_up(self):
        for target, through, _ in self.ends:

            @pl.when(self.net.z == through)
            def _():
                arriving, leaving = self.early(target, through), self.copies(target)
                for piece, held, come, go in zip(self.own(target), self.pre, arriving, leaving):
                    come.wait_recv()
                    piece[...] = (piece[...].astype(f32) + held[...].astype(f32)).astype(bf16)
                    go.start()

    def wait(self):
        for source in range(self.net.g.planes):
            due = self.net.z != source
            for target, _, far in self.ends:
                if far == source:
                    due = due & (self.net.z != target)

            @pl.when(due)
            def _():
                n = len(self.own(0))
                for k, slot in enumerate(self.slots(source)):
                    self.net.copy(slot, slot, self.sems, source * n + k, self.net.in_plane(source)).wait_recv()

    def wait_send(self):
        for target, through, far in self.ends:

            @pl.when(self.net.z == far)
            def _():
                for copy in self.early(target, through):
                    copy.wait_send()

            @pl.when(self.net.z == through)
            def _():
                for copy in self.copies(target):
                    copy.wait_send()

        for target in range(self.net.g.planes):
            self.direct(target, lambda copy: copy.wait_send())


class PlaneGather:
    def __init__(self, net, sems, piece):
        self.net, self.sems, self.piece = net, sems, piece
        net.ends.append(self.wait_send)

    def peer(self, j):
        return 2 * lax.rem(self.net.p + j, self.net.g.chips) + self.net.c

    def source(self, j):
        return 2 * lax.rem(self.net.p + self.net.g.chips - j, self.net.g.chips) + self.net.c

    def across(self, j):
        net = self.net
        mine = self.piece(net.m)
        return net.copy(mine, mine, self.sems, j - 1, net.member(self.peer(j)))

    def beside(self, j):
        net = self.net
        held = self.piece(self.source(j) if j else net.m)
        return net.copy(held, held, self.sems, net.g.chips - 1 + j, net.member(net.sib))

    def start(self):
        for j in range(1, self.net.g.chips):
            self.across(j).start()
        self.beside(0).start()

    def forward(self, j):
        self.across(j).wait_recv()
        self.beside(j).start()

    def wait(self, j):
        self.beside(j).wait_recv()

    def forward_all(self):
        for j in range(1, self.net.g.chips):
            self.forward(j)

    def wait_all(self):
        for j in range(self.net.g.chips):
            self.wait(j)

    def wait_send(self):
        for j in range(1, self.net.g.chips):
            self.across(j).wait_send()
        for j in range(self.net.g.chips):
            self.beside(j).wait_send()


class PlaneSum:
    def __init__(self, net, sems, sib, recv, own=None, send=None, after=None):
        self.net, self.sems, self.sib, self.recv = net, sems, sib, recv
        if after is None:
            self.own, self.send = own, send
        else:
            self.own, self.send = after.own, after.send
            net.sent(after)
        net.ends.append(self.wait_send)

    def block(self, ref, k):
        return ref.at[step_at(k, self.net.g.tok)]

    def beside(self, chip):
        net = self.net
        return net.copy(
            self.block(self.own, 2 * chip + 1 - net.c), self.block(self.sib, chip), self.sems, chip, net.member(net.sib)
        )

    def across(self, j):
        net = self.net
        chip = lax.rem(net.p + j, net.g.chips)
        return net.copy(
            self.block(self.send, chip),
            self.block(self.recv, j - 1),
            self.sems,
            net.g.chips - 1 + j,
            net.member(2 * chip + net.c),
        )

    def start(self, chip):
        self.beside(chip).start()

    def pair(self, chip):
        self.beside(chip).wait_recv()
        mine = self.own[step_at(2 * chip + self.net.c, self.net.g.tok), :].astype(f32)
        return mine + self.sib[step_at(chip, self.net.g.tok), :].astype(f32)

    def relay(self, j):
        chip = lax.rem(self.net.p + j, self.net.g.chips)
        self.send[step_at(chip, self.net.g.tok), :] = self.pair(chip).astype(bf16)
        self.across(j).start()

    def result(self):
        total = self.pair(self.net.p)
        tok = self.net.g.tok
        for j in range(1, self.net.g.chips):
            self.across(j).wait_recv()
            total = total + self.recv[(j - 1) * tok : j * tok, :].astype(f32)
        return total

    def wait_send(self):
        for chip in range(self.net.g.chips):
            self.beside(chip).wait_send()
        for j in range(1, self.net.g.chips):
            self.across(j).wait_send()


def to_rows(ref, at, row):
    for k in range(row.shape[1] // LANES):
        ref[at + k : at + k + 1, :] = row[:, k * LANES : (k + 1) * LANES]


def column_sum(x):
    return jnp.sum(x, 0, keepdims=True)


def normalized(x):
    center = x - jnp.mean(x, -1, keepdims=True)
    inverse = lax.rsqrt(jnp.mean(center * center, -1, keepdims=True) + 1e-5)
    return center * inverse, inverse


def norm_back(grad, xhat, inverse, gain):
    e = grad * gain
    return (e - jnp.mean(e, -1, keepdims=True) - xhat * jnp.mean(e * xhat, -1, keepdims=True)) * inverse


def gelu_pair(v):
    scale = math.sqrt(2 / math.pi)
    v2 = v * v
    t = jnp.tanh(scale * v * (1.0 + 0.044715 * v2))
    half = 0.5 * (1.0 + t)
    return v * half, half + 0.5 * v * (1.0 - t * t) * (scale * (1.0 + 3 * 0.044715 * v2))


def to_spectrum(g, signal, rows, stage, turns, high, low, out):
    @pl.loop(0, rows // 8)
    def _(step):
        at = step_at(step, 8)
        first = []
        for n in range(g.blocks):
            block = signal[n, at, :]
            angle = -2 * math.pi * n / (4 * g.blocks)
            first.append((block * math.cos(angle), block * math.sin(angle)))
        for k, (re, im) in enumerate(small_transform(first, -1)):
            c, s = turns[k : k + 1, :LANES], turns[k : k + 1, LANES:]
            stage[k, at, :LANES] = re * c + im * s
            stage[k, at, LANES:] = im * c - re * s

    group = 256 // rows

    @pl.loop(0, g.blocks // group)
    def _(step):
        at = step_at(step, group)
        x = stage[at].reshape(group * rows, 2 * LANES)
        out[at] = split_dot(x, high[...], low[...]).reshape(group, rows, 2 * LANES)


def from_spectrum(g, product, rows, stage, turns, high, low, signal):
    group = 256 // rows

    @pl.loop(0, g.blocks // group)
    def _(step):
        at = step_at(step, group)
        re, im = product(at)
        x = jnp.concatenate([re, im], -1).reshape(group * rows, 2 * LANES)
        stage[at] = split_dot(x, high[...], low[...]).reshape(group, rows, 2 * LANES)

    @pl.loop(0, rows // 8)
    def _(step):
        at = step_at(step, 8)
        values = []
        for k in range(g.blocks):
            re, im = stage[k, at, :LANES], stage[k, at, LANES:]
            c, s = turns[k : k + 1, :LANES], turns[k : k + 1, LANES:]
            values.append((re * c - im * s, re * s + im * c))
        for n, (re, im) in enumerate(small_transform(values, 1)):
            angle = 2 * math.pi * n / (4 * g.blocks)
            signal[n, at, :] = (re * math.cos(angle) - im * math.sin(angle)) * (1.0 / g.length)


def halves(x):
    return x[..., :LANES], x[..., LANES:]


def block_kernel(g, *refs):
    refs = list(refs)
    r = Inputs(*(refs.pop(0) for _ in Inputs._fields))
    block_out, tokens_grad, ct_out, ps_out, in_recv, up_recv, down_recv, out_recv = (refs.pop(0) for _ in range(8))
    w = types.SimpleNamespace(**{name: refs.pop(0) for name in scratch_buffers(g)})
    sems = types.SimpleNamespace(**{name: (refs.pop(0), refs.pop(0)) for name in semaphore_counts(g)})
    local_sem = refs.pop(0)
    net = Net(g)
    local_count = [0]

    def to_local(src, dst):
        copy = pltpu.make_async_copy(src, dst, local_sem.at[local_count[0]])
        local_count[0] += 1
        copy.start()
        return copy

    def to_output(src, dst):
        net.ends.append(to_local(src, dst).wait)

    coming = {
        name: to_local(getattr(r, name), getattr(w, name))
        for name in w.__dict__
        if name in Inputs._fields
    }
    r = r._replace(**{name: getattr(w, name) for name in coming})

    def arrive(*refs):
        for name in list(coming):
            if any(getattr(w, name) is ref for ref in refs):
                coming.pop(name).wait()
    tok, width, pt, ch, ff = g.tok, g.width, g.plane_tokens, g.chan, g.ff_part
    rows, planes, members, chips, blocks = g.rows, g.planes, g.members, g.chips, g.blocks
    part = g.down_rows
    exact = lax.Precision.HIGHEST

    barrier = pltpu.get_barrier_semaphore()
    partners = [net.member(lax.rem(net.m + j, members)) for j in range(1, members)]
    partners += [net.in_plane(lax.rem(net.z + j, planes)) for j in range(1, planes)]
    for there in partners:
        pl.semaphore_signal(barrier, inc=1, device_id=there, device_id_type=ON_MESH)

    for m in range(members):
        for b in range(3):
            at = b * width + m * LANES
            w.w_in_send[m * rows : (m + 1) * rows, b * LANES : (b + 1) * LANES] = r.input_weight[:, at : at + LANES]

    own_rows = step_at(net.flat, rows)

    def plane_rows(ref, z):
        return [ref.at[step_at(x * planes + z, INNER * rows)] for x in range(g.n_dp)]

    move_in = ToMembers(net, sems.w_in, lambda m: w.w_in_send.at[step_at(m, rows)], w.w_in.at[own_rows])
    line_in = LineGather(net, sems.w_in_line, lambda z: plane_rows(w.w_in, z))
    arrive(r.down_weight)
    w.w_down[step_at(net.z, part), :] = r.down_weight[...]
    w.w_out[step_at(net.m * planes + net.z, rows), :] = r.output_weight[...]
    line_down = LineGather(net, sems.w_down, lambda z: [w.w_down.at[step_at(z, part)]])
    line_out = LineGather(net, sems.w_out_line, lambda z: [w.w_out.at[step_at(net.m * planes + z, rows)]])
    pl.semaphore_wait(barrier, len(partners))
    move_in.start()
    line_out.start(far=False)
    line_down.start(far=False)

    xhat_one, inverse_one = normalized(r.tokens[...].astype(f32))
    w.xhat_one[...] = xhat_one
    mine = step_at(net.m, tok)
    w.act_one[mine, :] = (xhat_one * r.first_gain[...] + r.first_shift[...]).astype(bf16)
    gather_one = PlaneGather(net, sems.act_one, lambda m: w.act_one.at[step_at(m, tok)])
    gather_one.start()

    arrive(r.up_weight)
    for m in range(members):
        for z in range(planes):
            at = ((m // INNER) * g.n_seq + z * INNER + m % INNER) * part
            w.w_up_send[m * rows : (m + 1) * rows, z * part : (z + 1) * part] = r.up_weight[:, at : at + part]
    w.w_in[own_rows, :] = w.w_in_send[step_at(net.m, rows), :]
    w.w_up[own_rows, :] = w.w_up_send[step_at(net.m, rows), :]
    arrive(r.cotangent)
    w.cotan[mine, :] = r.cotangent[...]
    move_up = ToMembers(net, sems.w_up, lambda m: w.w_up_send.at[step_at(m, rows)], w.w_up.at[own_rows])
    line_up = LineGather(net, sems.w_up_line, lambda z: plane_rows(w.w_up, z))
    gather_cotan = PlaneGather(net, sems.cotan, lambda m: w.cotan.at[step_at(m, tok)])

    gather_out = PlaneGather(net, sems.w_out, lambda m: w.w_out.at[step_at(m, LANES)])
    move_up.start()
    line_out.start(far=True)
    move_in.wait()
    line_in.start(far=False)
    line_in.start(far=True)

    w.square[...] = jnp.zeros_like(w.square)
    lane_of = step_at(net.m, LANES)

    def param(row, ref, k, at):
        w.square[row : row + 1, :] = ref[k : k + 1, pl.ds(pl.multiple_of(at + net.m * LANES, LANES), LANES)]

    for b in range(3):
        param(b, r.input_bias, 0, b * width)
        for i in range(3):
            param(3 + 3 * i + b, r.short_weight, i, b * width)
        param(12 + b, r.short_bias, 0, b * width)
    param(15, r.skip_gain, 0, 0)
    param(16, r.decay_rates, 0, 0)
    w.param_cols[...] = w.square[...].T
    here = step_at(net.z, ch)

    def spread(col, rows=slice(None)):
        cols = w.param_cols[rows, col : col + 1]
        return jnp.broadcast_to(cols, (cols.shape[0], LANES))

    for b in range(3):
        for i in range(3):
            w.taps[i, b * LANES : (b + 1) * LANES, :] = spread(3 + 3 * i + b)
        w.taps[3, b * LANES : (b + 1) * LANES, :] = spread(12 + b)
    w.skip[...] = spread(15)
    w.decay[...] = spread(16, here)

    arrive(r.filter_weight, r.features, r.forth_high, r.forth_low, r.back_high, r.back_low)
    w.square[...] = jnp.zeros_like(w.square)
    for k, ref in enumerate((r.feat_bias, r.feat_freq, r.inner_bias, r.inner_freq)):
        w.square[k : k + 1, :FILT] = ref[...]
    w.net_cols[...] = w.square[...].T
    w.square[...] = jnp.zeros_like(w.square)
    w.square[:FEAT, :FILT] = r.feat_weight[...]
    w.net_weights[0] = w.square[...].T
    w.square[...] = jnp.zeros_like(w.square)
    w.square[:FILT, :FILT] = r.inner_weight[...]
    w.net_weights[1] = w.square[...].T
    w.square[...] = jnp.zeros_like(w.square)
    w.square[:FILT, :] = r.filter_weight[:, lane_of]
    w.net_weights[3] = w.square[...].T
    w.square[...] = jnp.zeros_like(w.square)
    w.square[:ch, :] = w.net_weights[3, here, :]
    w.net_weights[2] = w.square[...]
    w.net_weights[3] = w.square[...].T
    w.hid_two[...] = jnp.zeros_like(w.hid_two)

    span = 4 * LANES
    col = lambda k: w.net_cols[:FILT, k : k + 1]
    features_rows = r.features.shape[0]

    @pl.loop(0, g.length // span)
    def _(step):
        at = step_at(step, span)
        feats = r.features[:, at]
        p_one = dot_nn(w.net_weights[0, :FILT, :features_rows], feats, exact) + col(0)
        hid_one, cos_one = sin_cos(col(1) * p_one)
        p_two = dot_nn(w.net_weights[1, :FILT, :FILT], hid_one, exact) + col(2)
        hid_two, cos_two = sin_cos(col(3) * p_two)
        w.p_one[:, at], w.hid_one[:, at], w.cos_one[:, at] = p_one, hid_one, cos_one
        w.p_two[:, at], w.hid_two[:FILT, at], w.cos_two[:, at] = p_two, hid_two, cos_two
        filters = dot_nn(w.net_weights[2, :ch, :FILT], hid_two, exact)
        for k in range(span // LANES):
            cut = slice(k * LANES, (k + 1) * LANES)
            w.filt[step * (span // LANES) + k] = filters[:, cut] * jnp.exp(-w.decay[...] * feats[:1, cut])

    to_spectrum(g, w.filt, ch, w.stage_filt, r.turns, r.forth_high, r.forth_low, w.spec_filt)

    line_out.hand_on()
    line_in.hand_on()
    gather_one.forward_all()
    line_out.wait()
    gather_out.start()
    line_in.wait()
    move_up.wait()
    for b in range(3):
        turned = w.w_in[:, b * LANES : (b + 1) * LANES].astype(f32).T.astype(bf16)
        w.w_in_t[b * LANES : (b + 1) * LANES, :] = turned
    gather_one.wait_all()
    biases = jnp.concatenate([w.param_cols[:, b : b + 1] for b in range(3)], 0)

    def project(step):
        at = slice(step * 2 * tok, (step + 1) * 2 * tok)
        w.proj[:, at] = (dot_nt(w.w_in_t[...], w.act_one[at, :]) + biases).astype(bf16)

    def columns(a, n):
        return slice((a * INNER + n) * tok, (a * INNER + n + 1) * tok)

    def share_edge(values, n, rows, to_plane, from_plane, send, recv, sem, edge):
        for a in range(2):
            for b in range(3):
                block = values[b * LANES : (b + 1) * LANES, columns(a, n)].astype(f32)
                send[a * 8 : (a + 1) * 8, b * LANES : (b + 1) * LANES] = block.T[rows, :]
        there = lax.rem(to_plane + planes, planes)
        has_next = (to_plane >= 0) & (to_plane < planes)
        has_before = (from_plane >= 0) & (from_plane < planes)

        def copy():
            return net.copy(send, recv, sem, 0, net.in_plane(there))

        @pl.when(has_next)
        def _():
            copy().start()

        @pl.when(jnp.logical_not(has_before))
        def _():
            recv[...] = jnp.zeros_like(recv)

        def end():
            @pl.when(has_next)
            def _():
                copy().wait_send()

        net.ends.append(end)

        def wait():
            @pl.when(has_before)
            def _():
                copy().wait_recv()

            w.square[...] = jnp.zeros_like(w.square)
            for a in range(2):
                for b in range(3):
                    w.square[rows, :] = recv[a * 8 : (a + 1) * 8, b * LANES : (b + 1) * LANES]
                    edge[a, b * LANES : (b + 1) * LANES, :] = w.square[...].T

        return wait

    for half in range(INNER // 2)[::-1]:
        for a in range(2):
            project(a * INNER // 2 + half)
        if half == INNER // 2 - 1:
            wait_edge = share_edge(
                w.proj, INNER - 1, slice(LANES - 8, LANES), net.z + 1, net.z - 1, w.edge_send, w.edge_recv, sems.edge, w.edge
            )
            line_up.start(far=False)

    net.sent(move_in, line_in, line_out, move_up, gather_one)

    group = 32
    lane = lax.broadcasted_iota(jnp.int32, (group, LANES), 1)

    def rows_of(b, step):
        return pl.ds(pl.multiple_of(b * LANES + step * group, group), group)

    def rolled(x, by):
        return pltpu.roll(x, by, 1), pltpu.roll(x, (2 * by) % LANES, 1)

    def shifted(here, there, edge):
        return jnp.where(edge(1), there[0], here[0]), jnp.where(edge(2), there[1], here[1])

    from_left, from_right = (lambda k: lane < k), (lambda k: lane >= LANES - k)

    def filter_blocks(step, which):
        for a in range(2):
            conv = {}
            for b in range(3):
                at = rows_of(b, step)
                taps = [w.taps[i, at, :] for i in range(4)]
                before = rolled(w.edge[a, at, :], 1) if 0 in which else None
                for n in range(max(which) + 1):
                    now = w.proj[at, columns(a, n)].astype(f32)
                    turned = rolled(now, 1)
                    if n in which:
                        one, two = shifted(turned, before, from_left)
                        conv[b, n] = taps[3] + taps[2] * now + taps[1] * one + taps[0] * two
                        w.conv[at, columns(a, n)] = conv[b, n]
                    before = turned
            for n in which:
                carried = conv[0, n] * conv[2, n]
                w.carried[rows_of(0, step), columns(a, n)] = carried
                w.car_send[rows_of(0, step), columns(a, n)] = carried.astype(bf16)

    @pl.loop(0, LANES // group)
    def _(step):
        filter_blocks(step, range(1, INNER))

    wait_edge()

    @pl.loop(0, LANES // group)
    def _(step):
        filter_blocks(step, range(1))

    own_z = step_at(net.z, ch)

    def along(sem, send, recv):
        move = AlongPlanes(net, sem, lambda z: send.at[step_at(z, ch)], recv.at[own_z])
        move.start()
        recv[own_z, :] = send[own_z, :]
        return move

    def place(d):
        a, n = d // blocks, d % blocks
        return n, step_at(a, ch), step_at(n // INNER, ch), step_at(a * INNER + n % INNER, LANES)

    def to_signal(recv):
        @pl.loop(0, 2 * blocks)
        def _(d):
            n, at, from_rows, from_lanes = place(d)
            w.signal[n, at, :] = recv[from_rows, from_lanes].astype(f32)

    def to_planes(send):
        @pl.loop(0, 2 * blocks)
        def _(d):
            n, at, to_row, to_lane = place(d)
            send[to_row, to_lane] = w.back_sig[n, at, :].astype(bf16)

    move_car = along(sems.car, w.car_send, w.car_recv)
    gather_cotan.start()
    line_up.hand_on()
    move_car.wait()
    to_signal(w.car_recv)

    def both(filt):
        return jnp.concatenate([filt, filt], 1)

    to_spectrum(g, w.signal, 2 * ch, w.stage, r.turns, r.forth_high, r.forth_low, w.spec_car)

    def forth_product(at):
        (hr, hi), (xr, xi) = halves(both(w.spec_filt[at])), halves(w.spec_car[at])
        return xr * hr - xi * hi, xr * hi + xi * hr

    from_spectrum(g, forth_product, 2 * ch, w.stage, r.turns, r.back_high, r.back_low, w.back_sig)
    to_planes(w.y_send)
    move_y = along(sems.y, w.y_send, w.y_recv)
    gather_out.forward_all()
    move_y.wait()
    line_up.start(far=True)
    line_down.hand_on()
    line_down.start(far=True)

    @pl.loop(0, LANES // group)
    def _(step):
        at = rows_of(0, step)
        long_out = w.y_recv[at, :].astype(f32) + jnp.tile(w.skip[at, :], (1, members)) * w.carried[at, :]
        w.long[at, :] = long_out
        w.act_pre[at, :] = (w.conv[rows_of(1, step), :] * long_out).astype(bf16)

    own_block = step_at(net.m, LANES)
    move_pre = ToMembers(net, sems.pre, lambda m: w.act_pre.at[:, step_at(m, tok)], w.pre_recv.at[own_block])
    move_pre.start()
    w.pre_recv[own_block, :] = w.act_pre[:, mine]
    gather_cotan.forward_all()
    gather_out.wait_all()
    move_pre.wait()

    def by_line(piece):
        m, z = divmod(piece, planes)
        return (m // INNER) * g.n_seq + z * INNER + m % INNER

    for k in range(members * planes):
        at = by_line(k) * rows
        w.pre_line[k * rows : (k + 1) * rows, :] = w.pre_recv[at : at + rows, :]
    pre_rows = w.pre_line[...].astype(f32).T.astype(bf16)
    branch = dot_nn(pre_rows, w.w_out[...])
    residual = r.tokens[...].astype(f32) + branch + r.output_bias[...]
    w.residual[...] = residual
    xhat_two, inverse_two = normalized(residual)
    w.xhat_two[...] = xhat_two
    w.act_two[mine, :] = (xhat_two * r.second_gain[...] + r.second_shift[...]).astype(bf16)
    gather_two = PlaneGather(net, sems.act_two, lambda m: w.act_two.at[step_at(m, tok)])
    gather_two.start()
    net.sent(move_car, move_y, move_pre)

    gather_cotan.wait_all()
    line_up.wait()
    sum_two = PlaneSum(net, sems.gn_two, w.gn_two_sib, w.gn_two_recv, w.gn_two_own, w.gn_two_send)
    w.ps[...] = jnp.zeros_like(w.ps)
    hidden_block = [net.x * g.n_seq + z * INNER + net.q for z in range(planes)]
    up_bias = jnp.concatenate([r.up_bias[:, step_at(k, part)] for k in hidden_block], 1)
    bias_sum = jnp.zeros((1, ff), f32)
    slopes = []
    for j in range(chips):
        if j == 1:
            gather_two.forward_all()
        gather_two.wait(j)
        at = step_at(lax.rem(net.p + chips - j, chips), 2 * tok)
        gelu, slope = gelu_pair(dot_nn(w.act_two[at, :], w.w_up[...]) + up_bias)
        w.act_three[at, :] = gelu.astype(bf16)
        slopes.append(slope)
    plane_part = INNER * rows

    def parts_of(ref, z):
        at = z * g.n_dp * plane_part
        return [ref.at[pl.ds(at + x * plane_part, plane_part)] for x in range(g.n_dp)]

    def added(ref):
        group_rows = g.n_dp * plane_part
        return sum(ref[z * group_rows : (z + 1) * group_rows, :].astype(f32) for z in range(planes)).astype(bf16)

    def to_owners(sem, mid, out):
        move = ToMembers(net, sem, lambda m: mid.at[step_at(m, rows)], out.at[step_at(net.m, rows)])
        move.start()
        to_output(mid.at[step_at(net.m, rows)], out.at[step_at(net.m, rows)])
        return move

    sum_up = LineSum(
        net,
        sems.w_in_line,
        lambda z: plane_rows(w.up_send, z),
        lambda z: parts_of(w.up_parts, z),
        [w.up_pre.at[x * plane_part : (x + 1) * plane_part] for x in range(g.n_dp)],
    )
    half = part // 2

    def halves_of(ref, z):
        return [ref.at[step_at(2 * z + k, half)] for k in range(2)]

    sum_down = LineSum(
        net,
        sems.w_out_line,
        lambda z: halves_of(w.down_send, z),
        lambda z: halves_of(w.down_parts, z),
        [w.down_pre.at[k * half : (k + 1) * half] for k in range(2)],
    )
    @pl.loop(0, ff // 256)
    def _(step):
        at = step_at(step, 256)
        turned = w.act_three[:, at].astype(f32).T.astype(bf16)
        w.down_send[at, :] = dot_nn(turned, w.cotan[...]).astype(bf16)

    sum_down.start_early()
    line_down.wait()
    sum_down.start(far=False)
    sum_down.clear()
    w.down_parts[step_at(net.z, part), :] = w.down_send[step_at(net.z, part), :]
    for j in range(1, chips + 1):
        chip = lax.rem(net.p + j, chips)
        at = step_at(chip, 2 * tok)
        grad_upper = (dot_nt(w.cotan[at, :], w.w_down[...]) * slopes[-j]).astype(bf16)
        w.grad_up[at, :] = grad_upper
        bias_sum = bias_sum + column_sum(grad_upper.astype(f32))
        sum_two.own[at, :] = dot_nt(grad_upper, w.w_up[...]).astype(bf16)
        sum_two.start(chip)
    for z, k in enumerate(hidden_block):
        w.ps[pl.ds(AT_UP_BIAS + k, 1), :] = bias_sum[:, z * part : (z + 1) * part]
    for j in range(1, chips):
        sum_two.relay(j)

    @pl.loop(0, width // 256)
    def _(step):
        at = step_at(step, 256)
        turned = w.act_two[:, at].astype(f32).T.astype(bf16)
        w.up_send[at, :] = dot_nn(turned, w.grad_up[...]).astype(bf16)

    sum_up.start_early()
    sum_down.add_up()
    sum_down.start(far=True)
    for slot, piece in zip(parts_of(w.up_parts, net.z), plane_rows(w.up_send, net.z)):
        slot[...] = piece[...]
    net.sent(gather_cotan, gather_two, line_up, line_down)
    sum_result = PlaneSum(net, sems.cotan, w.result_sib, w.result_recv, w.cotan, w.result_send)
    for j in range(1, chips + 1):
        chip = lax.rem(net.p + j, chips)
        at = step_at(chip, 2 * tok)
        sum_result.own[at, :] = dot_nn(w.act_three[at, :], w.w_down[...]).astype(bf16)
    sum_up.clear()
    grad_two = sum_two.result()

    xhat_two = w.xhat_two[...]
    to_rows(w.ps, AT_SECOND_GAIN, column_sum(grad_two * xhat_two))
    to_rows(w.ps, AT_SECOND_SHIFT, column_sum(grad_two))
    cotan = r.cotangent[...].astype(f32)
    to_rows(w.ps, AT_DOWN_BIAS, column_sum(cotan))
    grad_res = cotan + norm_back(grad_two, xhat_two, inverse_two, r.second_gain[...])
    w.grad_res[...] = grad_res
    grad_branch = grad_res.astype(bf16)
    w.grad_branch[...] = grad_branch
    to_rows(w.ps, AT_OUTPUT_BIAS, column_sum(grad_branch.astype(f32)))

    per_step = 256 // rows
    for step in range(width // 256):
        grad = dot_nt(w.w_out[step * 256 : (step + 1) * 256, :], w.grad_branch[...]).astype(bf16)
        for k in range(per_step):
            at = by_line(step * per_step + k) * rows
            w.gpre_send[at : at + rows, :] = grad[k * rows : (k + 1) * rows, :]

    move_gpre = ToMembers(net, sems.w_in, lambda m: w.gpre_send.at[step_at(m, LANES)], w.gpre.at[:, mine])
    move_gpre.start()
    w.gpre[:, mine] = w.gpre_send[own_block, :]

    sum_out = PlaneSum(net, sems.act_two, w.w_out_grad_sib, w.w_out_grad_recv, after=sum_two)
    for m in range(members):
        at = slice(m * LANES, (m + 1) * LANES)
        sum_out.own[at, :] = dot_nn(w.pre_line[at, :], w.grad_branch[...]).astype(bf16)
    sum_up.add_up()
    move_gpre.wait()
    for total in (sum_out, sum_result):
        for j in range(1, chips + 1):
            total.start(lax.rem(net.p + j, chips))

    @pl.loop(0, LANES // group)
    def _(step):
        at, second = rows_of(0, step), rows_of(1, step)
        grad_pre = w.gpre[at, :].astype(f32)
        grad_long = grad_pre * w.conv[second, :]
        w.grad_long[at, :] = grad_long
        w.gl_send[at, :] = grad_long.astype(bf16)
        w.grad_conv[second, :] = grad_pre * w.long[at, :]

    move_gl = along(sems.car, w.gl_send, w.gl_recv)
    sum_up.start(far=False)
    for j in range(1, chips):
        sum_out.relay(j)
    move_gl.wait()
    to_signal(w.gl_recv)
    to_spectrum(g, w.signal, 2 * ch, w.stage, r.turns, r.forth_high, r.forth_low, w.spec_grad)

    def back_product(at):
        (hr, hi), (gr, gi) = halves(both(w.spec_filt[at])), halves(w.spec_grad[at])
        return hr * gr + hi * gi, hr * gi - hi * gr

    from_spectrum(g, back_product, 2 * ch, w.stage, r.turns, r.back_high, r.back_low, w.back_sig)
    to_planes(w.gc_send)
    move_gc = along(sems.y, w.gc_send, w.gc_recv)
    for j in range(1, chips):
        sum_result.relay(j)

    def filt_product(at):
        out = []
        for a in range(2):
            cut = slice(a * ch, (a + 1) * ch)
            (xr, xi), (gr, gi) = halves(w.spec_car[at, cut, :]), halves(w.spec_grad[at, cut, :])
            out.append((xr * gr + xi * gi, xr * gi - xi * gr))
        return out[0][0] + out[1][0], out[0][1] + out[1][1]

    from_spectrum(g, filt_product, ch, w.stage_filt, r.turns, r.back_high, r.back_low, w.back_filt)

    ones = jnp.ones((8, span), f32)
    chan_rows = step_at(net.chan_block, ch)
    w.ct[chan_rows, :] = jnp.zeros((ch, LANES), f32)

    @pl.loop(0, g.length // span)
    def _(step):
        at = step_at(step, span)
        feats = r.features[:, at]
        gate = []
        for k in range(span // LANES):
            fade = jnp.exp(-w.decay[...] * feats[:1, k * LANES : (k + 1) * LANES])
            gate.append(w.back_filt[step * (span // LANES) + k] * fade)
        gate = jnp.concatenate(gate, 1)
        w.ct[chan_rows, :] += dot_nt(gate, w.hid_two[:, at], exact)
        q_two = dot_nn(w.net_weights[3, :FILT, :ch], gate, exact)
        slope_two = q_two * w.cos_two[:, at]
        r_two = slope_two * col(3)
        w.ps[:FILT, :FILT] += dot_nt(w.hid_one[:, at], r_two, exact)
        q_one = dot_nn(r.inner_weight[...], r_two, exact)
        slope_one = q_one * w.cos_one[:, at]
        r_one = slope_one * col(1)
        w.ps[AT_FEAT : AT_FEAT + features_rows, :FILT] += dot_nt(feats, r_one, exact)
        for k, x in enumerate((r_one, slope_one * w.p_one[:, at], r_two, slope_two * w.p_two[:, at])):
            w.ps[AT_VECTOR + k : AT_VECTOR + k + 1, :FILT] += dot_nt(ones, x, exact)[:1, :]

    ct_z = AlongPlanes(net, sems.ct_z, lambda z: w.ct.at[chan_rows], w.ct.at[chan_rows])
    ct_z.start()
    move_gc.wait()

    @pl.loop(0, LANES // group)
    def _(step):
        at, last = rows_of(0, step), rows_of(2, step)
        grad = w.gc_recv[at, :].astype(f32) + jnp.tile(w.skip[at, :], (1, members)) * w.grad_long[at, :]
        w.grad_conv[at, :] = grad * w.conv[last, :]
        w.grad_conv[last, :] = grad * w.conv[at, :]

    wait_back_edge = share_edge(
        w.grad_conv, 0, slice(0, 8), net.z - 1, net.z + 1, w.back_edge_send, w.back_edge_recv, sems.back_edge, w.back_edge
    )
    sum_up.start(far=True)

    line_out_grad = LineSum(
        net,
        sems.w_down,
        lambda z: [w.out_sum.at[step_at(z, rows)]],
        lambda z: [w.out_parts.at[step_at(z, rows)]],
        [w.out_pre],
    )
    w.out_sum[...] = sum_out.result().astype(bf16)
    def filter_blocks_back(step, which):
        for a in range(2):
            for b in range(3):
                at = rows_of(b, step)
                taps = [w.taps[i, at, :] for i in range(3)]
                after = rolled(w.back_edge[a, at, :], LANES - 1) if INNER - 1 in which else None
                for n in range(min(which), INNER)[::-1]:
                    now = w.grad_conv[at, columns(a, n)]
                    turned = rolled(now, LANES - 1)
                    if n in which:
                        one, two = shifted(turned, after, from_right)
                        w.gproj[at, columns(a, n)] = (taps[2] * now + taps[1] * one + taps[0] * two).astype(bf16)
                    after = turned

    @pl.loop(0, LANES // group)
    def _(step):
        filter_blocks_back(step, range(INNER - 1))

    wait_back_edge()

    @pl.loop(0, LANES // group)
    def _(step):
        filter_blocks_back(step, range(INNER - 1, INNER))

    @pl.loop(0, width // 256)
    def _(step):
        at = step_at(step, 256)
        grad = dot_nn(w.gproj[...], w.act_one[:, at])
        w.gain_sum[:, at] = column_sum(grad * w.w_in_t[:, at].astype(f32))
        for b in range(3):
            cut = slice(b * LANES, (b + 1) * LANES)
            w.in_send[at, cut] = grad[cut].T.astype(bf16)

    sum_in = LineSum(
        net,
        sems.w_up_line,
        lambda z: plane_rows(w.in_send, z),
        lambda z: parts_of(w.w_in, z),
        [w.w_in_send.at[x * plane_part : (x + 1) * plane_part] for x in range(g.n_dp)],
    )
    sum_in.start_early()
    sum_in.clear()
    sum_in.start(far=False)
    for slot, piece in zip(parts_of(w.w_in, net.z), plane_rows(w.in_send, net.z)):
        slot[...] = piece[...]
    ct_z.wait()
    gather_ct = PlaneGather(net, sems.act_one, lambda m: w.ct.at[step_at(m, LANES)])
    gather_ct.start()
    w.block_out[...] = (w.residual[...] + sum_result.result() + r.down_bias[...]).astype(bf16)
    to_output(w.block_out, block_out)
    kept = w.conv

    @pl.loop(0, LANES // group)
    def _(step):
        for b in range(3):
            at = rows_of(b, step)
            sums = [jnp.zeros((group, LANES), f32)] * 5
            for a in range(2):
                before = rolled(w.edge[a, at, :], 1)
                for n in range(INNER):
                    grad, now = w.grad_conv[at, columns(a, n)], w.proj[at, columns(a, n)].astype(f32)
                    turned = rolled(now, 1)
                    one, two = shifted(turned, before, from_left)
                    terms = (grad * two, grad * one, grad * now, grad, w.gproj[at, columns(a, n)].astype(f32))
                    sums = [x + y for x, y in zip(sums, terms)]
                    before = turned
            for k in range(5):
                kept[at, k * LANES : (k + 1) * LANES] = sums[k]
        at = rows_of(0, step)
        product = w.grad_long[at, :] * w.carried[at, :]
        kept[at, 5 * LANES : 6 * LANES] = sum(product[:, k * LANES : (k + 1) * LANES] for k in range(members))

    which_lane = lax.broadcasted_iota(jnp.int32, (LANES, LANES), 1)
    tile = jnp.zeros((LANES, LANES), f32)
    for k, (kind, b) in enumerate(
        [(4, b) for b in range(3)] + [(i, b) for i in range(3) for b in range(3)] + [(3, b) for b in range(3)] + [(5, 0)]
    ):
        part_sums = kept[b * LANES : (b + 1) * LANES, kind * LANES : (kind + 1) * LANES]
        tile = jnp.where(which_lane == k, jnp.sum(part_sums, 1, keepdims=True), tile)
    channel_sum = jnp.sum(kept[:, 4 * LANES : 5 * LANES], 1, keepdims=True)
    shift_sum = column_sum(channel_sum * w.w_in_t[...].astype(f32))
    to_rows(w.ps, AT_FIRST_GAIN, (w.gain_sum[...] - r.first_shift[...] * shift_sum) / r.first_gain[...])
    to_rows(w.ps, AT_FIRST_SHIFT, shift_sum)
    w.ps[pl.ds(pl.multiple_of(AT_CHANNEL + net.m * 16, 16), 16), :] = tile.T[:16, :]

    share = PS_ROWS // members
    own_share = step_at(net.m, share)
    move_ps = ToMembers(net, sems.w_in, lambda m: w.ps.at[step_at(m, share)], w.ps_recv.at[own_share])
    net.sent(move_gpre)
    move_ps.start()
    w.ps_recv[own_share, :] = w.ps[own_share, :]
    sum_one = PlaneSum(net, sems.gn_two, w.gn_one_sib, w.gn_one_recv, after=sum_result)
    for j in range(1, chips + 1):
        chip = lax.rem(net.p + j, chips)
        at = step_at(chip, 2 * tok)
        turned = w.gproj[:, at].astype(f32).T.astype(bf16)
        sum_one.own[at, :] = dot_nn(turned, w.w_in_t[...]).astype(bf16)
        sum_one.start(chip)
    sum_in.add_up()
    for j in range(1, chips):
        sum_one.relay(j)
    move_ps.wait()

    def shares_added(ref, count):
        return sum(ref[k * share : (k + 1) * share, :] for k in range(count))

    own_line = step_at(net.z, share)
    w.ps_line[own_line, :] = shares_added(w.ps_recv, members)
    line_ps = AlongPlanes(net, sems.ps_line, lambda z: w.ps_line.at[own_line], w.ps_line.at[own_line])
    line_ps.start()
    sum_in.start(far=True)
    line_out_grad.start_early()
    line_out_grad.clear()
    line_out_grad.start(far=False)
    line_out_grad.start(far=True)
    w.out_parts[step_at(net.z, rows), :] = w.out_sum[step_at(net.z, rows), :]
    line_out_grad.add_up()
    sum_up.wait()
    w.up_mid[...] = added(w.up_parts)
    move_up_grad = to_owners(sems.w_up, w.up_mid, up_recv)
    sum_down.wait()
    w.down_total[...] = sum(w.down_parts[z * part : (z + 1) * part, :].astype(f32) for z in range(planes))
    to_output(w.down_total, down_recv)
    gather_ct.forward_all()
    line_ps.wait()
    w.ps_all[own_share, :] = shares_added(w.ps_line, planes)
    move_back = ToMembers(net, sems.ps_back, lambda m: w.ps_all.at[own_share], w.ps_all.at[own_share])
    move_back.start()
    sum_in.wait()
    w.in_mid[...] = added(w.w_in)
    move_in_grad = to_owners(sems.pre, w.in_mid, in_recv)
    grad_one = sum_one.result()

    grad_tokens = norm_back(grad_one, w.xhat_one[...], inverse_one, r.first_gain[...])
    w.tokens_grad[...] = (w.grad_res[...] + grad_tokens).astype(bf16)
    to_output(w.tokens_grad, tokens_grad)
    gather_ct.wait_all()
    to_output(w.ct, ct_out)
    line_out_grad.wait()
    w.out_total[...] = sum(w.out_parts[z * rows : (z + 1) * rows, :].astype(f32) for z in range(planes))
    to_output(w.out_total, out_recv)
    move_back.wait()
    to_output(w.ps_all, ps_out)
    move_in_grad.wait()
    move_up_grad.wait()
    net.finish()


def finish_kernel(g, *refs):
    ins, outs = refs[:8], refs[8:]
    block_in, tokens_in, ct, ps, in_recv, up_recv, down_recv, out_recv = ins
    (
        block_out, tokens_grad, first_gain, first_shift, input_weight, input_bias, short_weight, short_bias, feat_weight,
        feat_bias, feat_freq, inner_weight, inner_bias, inner_freq, filter_weight, skip_gain, output_weight, output_bias,
        second_gain, second_shift, up_weight, up_bias, down_weight, down_bias,
    ) = outs
    rows, planes, width, ff = g.rows, g.planes, g.width, g.ff_part
    for src, dst in ((block_in, block_out), (tokens_in, tokens_grad), (down_recv, down_weight), (out_recv, output_weight)):
        dst[...] = src[...]
    for m in range(g.members):
        x, q = m // INNER, m % INNER
        parts = [x * g.n_seq + z * INNER + q for z in range(planes)]
        total = in_recv[m * rows : (m + 1) * rows, :].astype(f32)
        for b in range(3):
            input_weight[:, b * width + m * LANES : b * width + (m + 1) * LANES] = total[:, b * LANES : (b + 1) * LANES]
        total = up_recv[m * rows : (m + 1) * rows, :].astype(f32)
        for z, k in enumerate(parts):
            cut = slice(z * g.down_rows, (z + 1) * g.down_rows)
            up_weight[:, k * g.down_rows : (k + 1) * g.down_rows] = total[:, cut]
    for m in range(g.members):
        cut = slice(m * LANES, (m + 1) * LANES)
        turned = ct[cut, :].T
        filter_weight[:, cut] = turned[:FILT, :]
        line = lambda k: ps[AT_CHANNEL + 16 * m + k : AT_CHANNEL + 16 * m + k + 1, :]
        for b in range(3):
            at = b * g.members + m
            input_bias[at : at + 1, :] = line(b)
            for i in range(3):
                short_weight[i : i + 1, b * width + m * LANES : b * width + (m + 1) * LANES] = line(3 + 3 * i + b)
            short_bias[at : at + 1, :] = line(12 + b)
        skip_gain[m : m + 1, :] = line(15)
    for out, at in (
        (first_gain, AT_FIRST_GAIN), (first_shift, AT_FIRST_SHIFT), (second_gain, AT_SECOND_GAIN), (up_bias, AT_UP_BIAS),
        (second_shift, AT_SECOND_SHIFT), (output_bias, AT_OUTPUT_BIAS), (down_bias, AT_DOWN_BIAS),
    ):
        out[...] = ps[at : at + out.shape[0], :]
    feat_weight[...] = ps[AT_FEAT : AT_FEAT + FEAT, :FILT]
    inner_weight[...] = ps[:FILT, :FILT]
    for k, out in enumerate((feat_bias, feat_freq, inner_bias, inner_freq)):
        out[...] = ps[AT_VECTOR + k : AT_VECTOR + k + 1, :FILT]


def on_device_in_kernels(g, *args):
    operands = [a[0] if a.ndim == 3 else a[None] if a.ndim == 1 else a for a in args]
    operands += [jnp.asarray(table) for table in constant_tables(g.blocks, LANES)]
    tok, width = g.tok, g.width
    in_vmem = pl.BlockSpec(memory_space=pltpu.VMEM)
    anywhere = pl.BlockSpec(memory_space=pl.ANY)
    S = jax.ShapeDtypeStruct
    buffers = scratch_buffers(g)
    parts = pl.pallas_call(
        functools.partial(block_kernel, g),
        out_shape=[
            S((tok, width), bf16),
            S((tok, width), bf16),
            S((width, LANES), f32),
            S((PS_ROWS, LANES), f32),
            S((g.members * g.rows, 3 * LANES), bf16),
            S((g.members * g.rows, g.ff_part), bf16),
            S((g.down_rows, width), f32),
            S((g.rows, width), f32),
        ],
        in_specs=[anywhere if name in buffers else in_vmem for name in Inputs._fields],
        out_specs=[anywhere] * 8,
        scratch_shapes=[pltpu.VMEM(shape, dtype) for shape, dtype in buffers.values()]
        + [pltpu.SemaphoreType.DMA((count,)) for pair in semaphore_counts(g).values() for count in pair]
        + [pltpu.SemaphoreType.DMA((len(set(Inputs._fields) & set(buffers)) + 8,))],
        compiler_params=pltpu.CompilerParams(
            collective_id=0, has_side_effects=True, vmem_limit_bytes=63 * 1024 * 1024
        ),
        name="block",
    )(*operands)

    def out_shape(a):
        if a.ndim == 3:
            return S(a.shape[1:], bf16)
        if a.ndim == 1:
            return S((a.shape[0] // LANES, LANES) if a.shape[0] % LANES == 0 else (1, a.shape[0]), f32)
        return S(a.shape, f32)

    named = Inputs(*args, *operands[len(args) :])
    wanted = [a for a in args if a is not named.cotangent and a is not named.decay_rates]
    wanted = [named.tokens] + wanted
    outs = pl.pallas_call(
        functools.partial(finish_kernel, g),
        out_shape=[out_shape(a) for a in wanted],
        in_specs=[in_vmem] * 8,
        out_specs=[in_vmem] * len(wanted),
        compiler_params=pltpu.CompilerParams(vmem_limit_bytes=63 * 1024 * 1024),
        name="finish",
    )(*parts)
    return tuple(o.reshape(a.shape) for o, a in zip(outs, wanted))


def on_device_by_size(tokens, cotangent, *args):
    named = Inputs(tokens, cotangent, *args, *[None] * 6)
    g = Geometry(
        lax.axis_size("dp"),
        lax.axis_size("seq"),
        tokens.shape[1],
        tokens.shape[2],
        named.up_weight.shape[1],
        named.input_weight.shape[0],
        named.down_weight.shape[0],
    )
    if g.fits():
        return on_device_in_kernels(g, tokens, cotangent, *args)
    return on_device(tokens, cotangent, *args)


def solution(mesh):
    placed = (
        P("dp", "seq", None),
        P("dp", "seq", None),
        P(),
        P(),
        P(("dp", "seq"), None),
        P(),
        P(),
        P(),
        P(),
        P(),
        P(),
        P(),
        P(),
        P(),
        P(),
        P(),
        P(),
        P(("dp", "seq"), None),
        P(),
        P(),
        P(),
        P(("dp", "seq"), None),
        P(),
        P(("dp", "seq"), None),
        P(),
    )
    return jax.shard_map(
        on_device_by_size,
        mesh=mesh,
        in_specs=placed,
        out_specs=(
            P("dp", "seq", None),
            P("dp", "seq", None),
            P(),
            P(),
            P(("dp", "seq"), None),
            P(),
            P(),
            P(),
            P(),
            P(),
            P(),
            P(),
            P(),
            P(),
            P(),
            P(),
            P(("dp", "seq"), None),
            P(),
            P(),
            P(),
            P(("dp", "seq"), None),
            P(),
            P(("dp", "seq"), None),
            P(),
        ),
        check_vma=False,
    )
```

```python
import functools
import math
import types
from typing import NamedTuple

import jax
import jax.numpy as jnp
import ml_dtypes
import numpy as np
from jax import lax
from jax.experimental import pallas as pl
from jax.experimental.pallas import tpu as pltpu
from jax.sharding import PartitionSpec as P

FEAT = 33
FILT = 64


exact_precision = lax.Precision.HIGHEST


def from_behind(x, axis, by):
    size = lax.axis_size(axis)
    pairs = [(i, i + by) for i in range(size) if 0 <= i + by < size]
    return lax.ppermute(x, axis, pairs)


def layer_norm(values, gain_vec, offset):
    center = values - jnp.mean(values, -1, keepdims=True)
    spread = jnp.mean(center * center, -1, keepdims=True)
    return center * lax.rsqrt(spread + 1e-05) * gain_vec + offset


def position_features(stamps, length):
    stamp_float = stamps.astype(jnp.float32)
    linear_ramp = stamp_float / (length - 1)
    band_rates = 0.0001 + jnp.arange((FEAT - 1) // 2).astype(jnp.float32) * ((15.0 - 0.0001) / 15.0)
    phase_angle = (stamp_float * (2.0 * math.pi / length))[:, None] * band_rates[None, :]
    return jnp.concatenate([linear_ramp[:, None], jnp.cos(phase_angle), -jnp.sin(phase_angle)], 1)


def filter_net(
    feat_weight,
    feat_bias,
    feat_freq,
    inner_weight,
    inner_bias,
    inner_freq,
    filter_weight,
    feature_rows,
    modulate,
):
    hidden = jnp.sin(
        feat_freq * (jnp.dot(feature_rows, feat_weight, precision=exact_precision) + feat_bias)
    )
    hidden = jnp.sin(
        inner_freq * (jnp.dot(hidden, inner_weight, precision=exact_precision) + inner_bias)
    )
    raw_filter = lax.dot_general(
        filter_weight, hidden, (((0,), (1,)), ((), ())), precision=exact_precision
    )
    return raw_filter * modulate


def short_conv(padded, kernel, offset):
    col_count = padded.shape[1] - 2
    return (
        offset[:, None]
        + kernel[0][:, None] * padded[:, :col_count]
        + kernel[1][:, None] * padded[:, 1 : col_count + 1]
        + kernel[2][:, None] * padded[:, 2:]
    )


def unit_angles(rows, cols, period):
    row_index = lax.broadcasted_iota(jnp.int32, (rows, cols), 0)
    col_index = lax.broadcasted_iota(jnp.int32, (rows, cols), 1)
    phase_angle = (row_index * col_index % period).astype(jnp.float32) * (2.0 * math.pi / period)
    return (jnp.cos(phase_angle), jnp.sin(phase_angle))


def forward_frequency_domain(signal, outer_size, period):
    block_count = signal.shape[1]
    row_count = signal.shape[2]
    cos_first, sin_first = unit_angles(outer_size, block_count, outer_size)
    real_first = jnp.einsum("dn,cnt->cdt", cos_first, signal, precision=exact_precision)
    imag_first = -jnp.einsum("dn,cnt->cdt", sin_first, signal, precision=exact_precision)
    cos_turn, sin_turn = unit_angles(outer_size, row_count, period)
    real_turned = real_first * cos_turn + imag_first * sin_turn
    imag_turned = imag_first * cos_turn - real_first * sin_turn
    cos_last, sin_last = unit_angles(row_count, row_count, row_count)
    real_out = jnp.einsum(
        "cdb,bk->cdk", real_turned, cos_last, precision=exact_precision
    ) + jnp.einsum("cdb,bk->cdk", imag_turned, sin_last, precision=exact_precision)
    imag_out = jnp.einsum(
        "cdb,bk->cdk", imag_turned, cos_last, precision=exact_precision
    ) - jnp.einsum("cdb,bk->cdk", real_turned, sin_last, precision=exact_precision)
    return (real_out, imag_out)


def inverse_spectrum(real_part, imag_part, block_count, period):
    outer_size = real_part.shape[1]
    row_count = real_part.shape[2]
    cos_last, sin_last = unit_angles(row_count, row_count, row_count)
    real_back = jnp.einsum(
        "cdk,kb->cdb", real_part, cos_last, precision=exact_precision
    ) - jnp.einsum("cdk,kb->cdb", imag_part, sin_last, precision=exact_precision)
    imag_back = jnp.einsum(
        "cdk,kb->cdb", real_part, sin_last, precision=exact_precision
    ) + jnp.einsum("cdk,kb->cdb", imag_part, cos_last, precision=exact_precision)
    cos_turn, sin_turn = unit_angles(outer_size, row_count, period)
    real_turned = real_back * cos_turn - imag_back * sin_turn
    imag_turned = real_back * sin_turn + imag_back * cos_turn
    cos_first, sin_first = unit_angles(block_count, outer_size, outer_size)
    summed = jnp.einsum(
        "nd,cdt->cnt", cos_first, real_turned, precision=exact_precision
    ) - jnp.einsum("nd,cdt->cnt", sin_first, imag_turned, precision=exact_precision)
    return summed / period


def on_device(
    tokens,
    cotangent,
    first_gain,
    first_shift,
    input_weight,
    input_bias,
    short_weight,
    short_bias,
    feat_weight,
    feat_bias,
    feat_freq,
    inner_weight,
    inner_bias,
    inner_freq,
    filter_weight,
    skip_gain,
    decay_rates,
    output_weight,
    output_bias,
    second_gain,
    second_shift,
    up_weight,
    up_bias,
    down_weight,
    down_bias,
):
    sequence_count = lax.axis_size("seq")
    seq_index = lax.axis_index("seq")
    row_count = tokens.shape[1]
    model_width = tokens.shape[2]
    length = row_count * sequence_count
    period = 2 * length
    outer_size = 2 * sequence_count
    narrow = model_width // sequence_count
    inputs = tokens[0].astype(jnp.float32)
    cotan_rows = cotangent[0].astype(jnp.float32)
    w_in, w_out, w_up, w_down = (
        lax.all_gather(input_weight, ("dp", "seq"), axis=0, tiled=True),
        lax.all_gather(output_weight, ("dp", "seq"), axis=0, tiled=True),
        lax.all_gather(up_weight, ("dp", "seq"), axis=0, tiled=True),
        lax.all_gather(down_weight, ("dp", "seq"), axis=0, tiled=True),
    )
    normed_one, norm_one_back = jax.vjp(layer_norm, inputs, first_gain, first_shift)
    act_one = normed_one.astype(jnp.bfloat16)
    projected = lax.dot_general(
        w_in, act_one, (((0,), (1,)), ((), ())), preferred_element_type=jnp.float32
    )
    projected = projected + input_bias[:, None]
    rim_rows = from_behind(projected[:, row_count - 2 :], "seq", 1)
    padded = jnp.concatenate([rim_rows, projected], 1)
    conv_out, short_back = jax.vjp(short_conv, padded, short_weight, short_bias)
    leading_gate = conv_out[:model_width]
    second_gate = conv_out[model_width : 2 * model_width]
    value_part = conv_out[2 * model_width :]
    carried = leading_gate * value_part
    stamps = seq_index * row_count + lax.iota(jnp.int32, row_count)
    modulate = jnp.exp(-decay_rates[:, None] * (stamps.astype(jnp.float32) / (length - 1))[None, :])
    filter_fixed = functools.partial(
        filter_net, feature_rows=position_features(stamps, length), modulate=modulate
    )
    filters, filter_back = jax.vjp(
        filter_fixed,
        feat_weight,
        feat_bias,
        feat_freq,
        inner_weight,
        inner_bias,
        inner_freq,
        filter_weight,
    )
    carried_blocks = carried.reshape(sequence_count, narrow, row_count)
    filter_blocks = filters.reshape(sequence_count, narrow, row_count)
    carried_chan, filter_chan = (
        lax.all_to_all(
            carried_blocks.astype(jnp.bfloat16), "seq", split_axis=0, concat_axis=2, tiled=True
        ).astype(carried_blocks.dtype),
        lax.all_to_all(
            filter_blocks.astype(jnp.bfloat16), "seq", split_axis=0, concat_axis=2, tiled=True
        ).astype(filter_blocks.dtype),
    )
    carried_chan = carried_chan.reshape(narrow, sequence_count, row_count)
    filter_chan = filter_chan.reshape(narrow, sequence_count, row_count)
    carried_real, carried_imag = forward_frequency_domain(carried_chan, outer_size, period)
    filter_real, filter_imag = forward_frequency_domain(filter_chan, outer_size, period)
    conv_chan = inverse_spectrum(
        carried_real * filter_real - carried_imag * filter_imag,
        carried_real * filter_imag + carried_imag * filter_real,
        sequence_count,
        period,
    )
    conv_rows = lax.all_to_all(
        conv_chan.reshape(1, narrow, length).astype(jnp.bfloat16),
        "seq",
        split_axis=2,
        concat_axis=0,
        tiled=True,
    ).astype(jnp.float32)
    long_out = conv_rows.reshape(model_width, row_count) + skip_gain[:, None] * carried
    act_pre = (second_gate * long_out).astype(jnp.bfloat16)
    branch_out = lax.dot_general(
        act_pre, w_out, (((0,), (0,)), ((), ())), preferred_element_type=jnp.float32
    )
    residual = inputs + branch_out + output_bias
    normed_two, norm_two_back = jax.vjp(layer_norm, residual, second_gain, second_shift)
    act_two = normed_two.astype(jnp.bfloat16)
    upper = jnp.dot(act_two, w_up, preferred_element_type=jnp.float32) + up_bias
    gelu_out, gelu_back = jax.vjp(jax.nn.gelu, upper)
    act_three = gelu_out.astype(jnp.bfloat16)
    result = residual + jnp.dot(act_three, w_down, preferred_element_type=jnp.float32) + down_bias
    block_out = result.astype(jnp.bfloat16)[None]
    grad_final = cotan_rows.astype(jnp.bfloat16)
    down_grad = lax.dot_general(
        act_three, grad_final, (((0,), (0,)), ((), ())), preferred_element_type=jnp.float32
    )
    down_bias_grad = jnp.sum(grad_final, 0, dtype=jnp.float32)
    grad_act_three = lax.dot_general(
        grad_final, w_down, (((1,), (1,)), ((), ())), preferred_element_type=jnp.float32
    )
    (grad_upper,) = gelu_back(grad_act_three)
    grad_upper = grad_upper.astype(jnp.bfloat16)
    up_grad = lax.dot_general(
        act_two, grad_upper, (((0,), (0,)), ((), ())), preferred_element_type=jnp.float32
    )
    up_bias_grad = jnp.sum(grad_upper, 0, dtype=jnp.float32)
    grad_norm_two = lax.dot_general(
        grad_upper, w_up, (((1,), (1,)), ((), ())), preferred_element_type=jnp.float32
    )
    grad_resid_norm, second_gain_grad, second_shift_grad = norm_two_back(grad_norm_two)
    grad_residual = cotan_rows + grad_resid_norm
    grad_branch = grad_residual.astype(jnp.bfloat16)
    output_grad = jnp.dot(act_pre, grad_branch, preferred_element_type=jnp.float32)
    output_bias_grad = jnp.sum(grad_branch, 0, dtype=jnp.float32)
    grad_pre = lax.dot_general(
        w_out, grad_branch, (((1,), (1,)), ((), ())), preferred_element_type=jnp.float32
    )
    grad_second = grad_pre * long_out
    grad_long = grad_pre * second_gate
    skip_gain_grad = jnp.sum(grad_long * carried, 1)
    grad_long_blocks = grad_long.reshape(sequence_count, narrow, row_count)
    grad_chan, carried_again, filter_again = (
        lax.all_to_all(
            grad_long_blocks.astype(jnp.bfloat16), "seq", split_axis=0, concat_axis=2, tiled=True
        ).astype(grad_long_blocks.dtype),
        lax.all_to_all(
            carried_blocks.astype(jnp.bfloat16), "seq", split_axis=0, concat_axis=2, tiled=True
        ).astype(carried_blocks.dtype),
        lax.all_to_all(
            filter_blocks.astype(jnp.bfloat16), "seq", split_axis=0, concat_axis=2, tiled=True
        ).astype(filter_blocks.dtype),
    )
    carried_real, carried_imag = forward_frequency_domain(
        carried_again.reshape(narrow, sequence_count, row_count), outer_size, period
    )
    filter_real, filter_imag = forward_frequency_domain(
        filter_again.reshape(narrow, sequence_count, row_count), outer_size, period
    )
    grad_real, grad_imag = forward_frequency_domain(
        grad_chan.reshape(narrow, sequence_count, row_count), outer_size, period
    )
    carried_back = inverse_spectrum(
        filter_real * grad_real + filter_imag * grad_imag,
        filter_real * grad_imag - filter_imag * grad_real,
        sequence_count,
        period,
    )
    filter_grad_chan = inverse_spectrum(
        carried_real * grad_real + carried_imag * grad_imag,
        carried_real * grad_imag - carried_imag * grad_real,
        sequence_count,
        period,
    )
    carried_got, filters_got = (
        lax.all_to_all(
            carried_back.reshape(1, narrow, length).astype(jnp.bfloat16),
            "seq",
            split_axis=2,
            concat_axis=0,
            tiled=True,
        ).astype(jnp.float32),
        lax.all_to_all(
            filter_grad_chan.reshape(1, narrow, length).astype(jnp.bfloat16),
            "seq",
            split_axis=2,
            concat_axis=0,
            tiled=True,
        ).astype(jnp.float32),
    )
    grad_carried = carried_got.reshape(model_width, row_count) + skip_gain[:, None] * grad_long
    grad_filters = filters_got.reshape(model_width, row_count)
    (
        feat_weight_grad,
        feat_bias_grad,
        feat_freq_grad,
        inner_weight_grad,
        inner_bias_grad,
        inner_freq_grad,
        filter_weight_grad,
    ) = filter_back(grad_filters)
    grad_conv = jnp.concatenate(
        [grad_carried * value_part, grad_second, grad_carried * leading_gate], 0
    )
    grad_padded, short_weight_grad, short_bias_grad = short_back(grad_conv)
    rim_grad = from_behind(grad_padded[:, :2], "seq", -1)
    grad_projected = jnp.concatenate(
        [grad_padded[:, 2:row_count], grad_padded[:, row_count:] + rim_grad], 1
    )
    grad_projected = grad_projected.astype(jnp.bfloat16)
    input_grad = lax.dot_general(
        act_one, grad_projected, (((0,), (1,)), ((), ())), preferred_element_type=jnp.float32
    )
    input_bias_grad = jnp.sum(grad_projected, 1, dtype=jnp.float32)
    first_norm_gradient = lax.dot_general(
        grad_projected, w_in, (((0,), (1,)), ((), ())), preferred_element_type=jnp.float32
    )
    grad_inputs, first_gain_grad, first_shift_grad = norm_one_back(first_norm_gradient)
    tokens_grad = (grad_inputs + grad_residual).astype(jnp.bfloat16)[None]
    input_weight_grad, output_weight_grad, up_weight_grad, down_weight_grad = (
        lax.psum_scatter(input_grad, ("dp", "seq"), scatter_dimension=0, tiled=True),
        lax.psum_scatter(output_grad, ("dp", "seq"), scatter_dimension=0, tiled=True),
        lax.psum_scatter(up_grad, ("dp", "seq"), scatter_dimension=0, tiled=True),
        lax.psum_scatter(down_grad, ("dp", "seq"), scatter_dimension=0, tiled=True),
    )
    (
        first_gain_grad,
        first_shift_grad,
        input_bias_grad,
        short_weight_grad,
        short_bias_grad,
        feat_weight_grad,
        feat_bias_grad,
        feat_freq_grad,
        inner_weight_grad,
        inner_bias_grad,
        inner_freq_grad,
        filter_weight_grad,
        skip_gain_grad,
        output_bias_grad,
        second_gain_grad,
        second_shift_grad,
        up_bias_grad,
        down_bias_grad,
    ) = lax.psum(
        (
            first_gain_grad,
            first_shift_grad,
            input_bias_grad,
            short_weight_grad,
            short_bias_grad,
            feat_weight_grad,
            feat_bias_grad,
            feat_freq_grad,
            inner_weight_grad,
            inner_bias_grad,
            inner_freq_grad,
            filter_weight_grad,
            skip_gain_grad,
            output_bias_grad,
            second_gain_grad,
            second_shift_grad,
            up_bias_grad,
            down_bias_grad,
        ),
        ("dp", "seq"),
    )
    return (
        block_out,
        tokens_grad,
        first_gain_grad,
        first_shift_grad,
        input_weight_grad,
        input_bias_grad,
        short_weight_grad,
        short_bias_grad,
        feat_weight_grad,
        feat_bias_grad,
        feat_freq_grad,
        inner_weight_grad,
        inner_bias_grad,
        inner_freq_grad,
        filter_weight_grad,
        skip_gain_grad,
        output_weight_grad,
        output_bias_grad,
        second_gain_grad,
        second_shift_grad,
        up_weight_grad,
        up_bias_grad,
        down_weight_grad,
        down_bias_grad,
    )


f32 = jnp.float32
bf16 = jnp.bfloat16
ON_MESH = pl.DeviceIdType.MESH
INNER = 4
LANES = 128
PS_ROWS = 320
AT_VECTOR = 64
AT_SECOND_GAIN = 72
AT_SECOND_SHIFT = 80
AT_OUTPUT_BIAS = 88
AT_DOWN_BIAS = 96
AT_FIRST_GAIN = 104
AT_FIRST_SHIFT = 112
AT_UP_BIAS = 120
AT_FEAT = 152
AT_CHANNEL = 192


def dot_nn(a, b, precision=None):
    return lax.dot_general(
        a, b, (((1,), (0,)), ((), ())), precision=precision, preferred_element_type=f32
    )


def dot_nt(a, b, precision=None):
    return lax.dot_general(
        a, b, (((1,), (1,)), ((), ())), precision=precision, preferred_element_type=f32
    )


def step_at(index, size):
    return pl.ds(pl.multiple_of(index * size, size), size)


def times_unit(value, turns):
    re, im = value
    c, s = math.cos(2 * math.pi * turns), math.sin(2 * math.pi * turns)
    if abs(s) < 1e-12:
        return (re, im) if c > 0 else (-re, -im)
    if abs(c) < 1e-12:
        return (-im, re) if s > 0 else (im, -re)
    return re * c - im * s, re * s + im * c


def small_transform(values, sign):
    size = len(values)
    if size == 1:
        return values
    even = small_transform(values[0::2], sign)
    odd = small_transform(values[1::2], sign)
    turned = [times_unit(odd[k], sign * k / size) for k in range(size // 2)]
    return [(e[0] + t[0], e[1] + t[1]) for e, t in zip(even, turned)] + [
        (e[0] - t[0], e[1] - t[1]) for e, t in zip(even, turned)
    ]


@functools.lru_cache(None)
def constant_tables(blocks, lanes):
    length = blocks * lanes
    n2 = np.arange(lanes)
    angle = 2 * np.pi * np.outer(n2, n2) / lanes
    c, s = np.cos(angle), np.sin(angle)
    forth = np.block([[c, -s], [s, c]])
    back = np.block([[c, s], [-s, c]])

    def split(x):
        high = x.astype(ml_dtypes.bfloat16)
        return high, (x - high.astype(np.float64)).astype(ml_dtypes.bfloat16)

    turn = 2 * np.pi * np.outer(np.arange(blocks) + 0.25, n2) / length
    turns = np.concatenate([np.cos(turn), np.sin(turn)], 1).astype(np.float32)
    rates = 1e-4 + np.arange((FEAT - 1) // 2) * ((15.0 - 1e-4) / 15.0)
    phase = (2 * np.pi * np.arange(length) / length)[None, :] * rates[:, None]
    ramp = (np.arange(length) / (length - 1))[None, :]
    features = np.concatenate([ramp, np.cos(phase), -np.sin(phase)], 0)
    features = np.pad(features, ((0, -FEAT % 8), (0, 0))).astype(np.float32)
    return split(forth) + split(back) + (turns, features)


def split_dot(x, high, low):
    head = x.astype(bf16)
    tail = (x - head.astype(f32)).astype(bf16)
    return dot_nn(head, high) + dot_nn(tail, high) + dot_nn(head, low)


def sin_cos(x):
    count = jnp.floor(x * (2 / math.pi) + 0.5)
    r = x - count * 1.5703125
    r = r - count * 4.837512969970703e-4
    r = r - count * 7.549789948768648e-8
    r2 = r * r
    s = r + r * r2 * (-1.6666654611e-1 + r2 * (8.3321608736e-3 + r2 * -1.9515295891e-4))
    c = 1.0 - 0.5 * r2 + r2 * r2 * (
        4.166664568298827e-2 + r2 * (-1.388731625493765e-3 + r2 * 2.443315711809948e-5)
    )
    quarter = count - 4.0 * jnp.floor(count * 0.25)
    odd = (quarter == 1.0) | (quarter == 3.0)
    sine = jnp.where(odd, c, s)
    cosine = jnp.where(odd, s, c)
    sine = jnp.where(quarter >= 2.0, -sine, sine)
    cosine = jnp.where((quarter == 1.0) | (quarter == 2.0), -cosine, cosine)
    return sine, cosine


class Inputs(NamedTuple):
    tokens: jax.Array
    cotangent: jax.Array
    first_gain: jax.Array
    first_shift: jax.Array
    input_weight: jax.Array
    input_bias: jax.Array
    short_weight: jax.Array
    short_bias: jax.Array
    feat_weight: jax.Array
    feat_bias: jax.Array
    feat_freq: jax.Array
    inner_weight: jax.Array
    inner_bias: jax.Array
    inner_freq: jax.Array
    filter_weight: jax.Array
    skip_gain: jax.Array
    decay_rates: jax.Array
    output_weight: jax.Array
    output_bias: jax.Array
    second_gain: jax.Array
    second_shift: jax.Array
    up_weight: jax.Array
    up_bias: jax.Array
    down_weight: jax.Array
    down_bias: jax.Array
    forth_high: jax.Array
    forth_low: jax.Array
    back_high: jax.Array
    back_low: jax.Array
    turns: jax.Array
    features: jax.Array


def scratch_buffers(g):
    tok, width, pt, ch = g.tok, g.width, g.plane_tokens, g.chan
    ff, blocks = g.ff_part, g.blocks
    return dict(
        up_weight=((g.rows, g.hidden), bf16),
        down_weight=((g.down_rows, width), bf16),
        cotangent=((tok, width), bf16),
        filter_weight=((FILT, width), f32),
        features=((FEAT + -FEAT % 8, g.length), f32),
        forth_high=((2 * LANES, 2 * LANES), bf16),
        forth_low=((2 * LANES, 2 * LANES), bf16),
        back_high=((2 * LANES, 2 * LANES), bf16),
        back_low=((2 * LANES, 2 * LANES), bf16),
        block_out=((tok, width), bf16),
        tokens_grad=((tok, width), bf16),
        w_in=((width, 3 * LANES), bf16),
        w_in_send=((g.members * g.rows, 3 * LANES), bf16),
        w_up_send=((g.members * g.rows, ff), bf16),
        w_in_t=((3 * LANES, width), bf16),
        w_out=((width, width), bf16),
        w_up=((width, ff), bf16),
        w_down=((ff, width), bf16),
        act_one=((pt, width), bf16),
        act_two=((pt, width), bf16),
        cotan=((pt, width), bf16),
        proj=((3 * LANES, pt), bf16),
        conv=((3 * LANES, pt), f32),
        grad_conv=((3 * LANES, pt), f32),
        carried=((LANES, pt), f32),
        long=((LANES, pt), f32),
        grad_long=((LANES, pt), f32),
        car_send=((LANES, pt), bf16),
        car_recv=((LANES, pt), bf16),
        y_send=((LANES, pt), bf16),
        y_recv=((LANES, pt), bf16),
        gl_send=((LANES, pt), bf16),
        gl_recv=((LANES, pt), bf16),
        gc_send=((LANES, pt), bf16),
        gc_recv=((LANES, pt), bf16),
        act_pre=((LANES, pt), bf16),
        gpre=((LANES, pt), bf16),
        gproj=((3 * LANES, pt), bf16),
        taps=((4, 3 * LANES, LANES), f32),
        skip=((LANES, LANES), f32),
        edge_send=((16, 3 * LANES), f32),
        edge_recv=((16, 3 * LANES), f32),
        back_edge_send=((16, 3 * LANES), f32),
        back_edge_recv=((16, 3 * LANES), f32),
        edge=((2, 3 * LANES, LANES), f32),
        back_edge=((2, 3 * LANES, LANES), f32),
        ps_recv=((PS_ROWS, LANES), f32),
        ps_line=((PS_ROWS // g.members * g.planes, LANES), f32),
        square=((LANES, LANES), f32),
        param_cols=((LANES, LANES), f32),
        decay=((ch, LANES), f32),
        net_weights=((4, LANES, LANES), f32),
        net_cols=((LANES, LANES), f32),
        p_one=((FILT, g.length), f32),
        hid_one=((FILT, g.length), f32),
        cos_one=((FILT, g.length), f32),
        p_two=((FILT, g.length), f32),
        hid_two=((LANES, g.length), f32),
        cos_two=((FILT, g.length), f32),
        filt=((blocks, ch, LANES), f32),
        stage=((blocks, 2 * ch, 2 * LANES), f32),
        stage_filt=((blocks, ch, 2 * LANES), f32),
        spec_filt=((blocks, ch, 2 * LANES), f32),
        spec_car=((blocks, 2 * ch, 2 * LANES), f32),
        spec_grad=((blocks, 2 * ch, 2 * LANES), f32),
        back_filt=((blocks, ch, LANES), f32),
        pre_recv=((width, tok), bf16),
        pre_line=((width, tok), bf16),
        gpre_send=((width, tok), bf16),
        residual=((tok, width), f32),
        xhat_two=((tok, width), f32),
        xhat_one=((tok, width), f32),
        grad_res=((tok, width), f32),
        grad_branch=((tok, width), bf16),
        act_three=((pt, ff), bf16),
        grad_up=((pt, ff), bf16),
        up_send=((width, ff), bf16),
        up_parts=((width, ff), bf16),
        up_pre=((width // g.planes, ff), bf16),
        up_mid=((width // g.planes, ff), bf16),
        down_parts=((ff, width), bf16),
        down_pre=((g.down_rows, width), bf16),
        down_total=((g.down_rows, width), f32),
        down_send=((ff, width), bf16),
        in_mid=((width // g.planes, 3 * LANES), bf16),
        in_send=((width, 3 * LANES), bf16),
        out_sum=((LANES, width), bf16),
        out_parts=((LANES, width), bf16),
        out_total=((g.rows, width), f32),
        ct=((width, LANES), f32),
        gain_sum=((1, width), f32),
        ps=((PS_ROWS, LANES), f32),
        ps_all=((PS_ROWS, LANES), f32),
        gn_two_own=((pt, width), bf16),
        gn_two_send=((pt // 2, width), bf16),
        gn_two_sib=((pt // 2, width), bf16),
        gn_two_recv=((3 * tok, width), bf16),
        result_send=((pt // 2, width), bf16),
        result_sib=((pt // 2, width), bf16),
        result_recv=((3 * tok, width), bf16),
        w_out_grad_sib=((pt // 2, width), bf16),
        w_out_grad_recv=((3 * tok, width), bf16),
        gn_one_sib=((pt // 2, width), bf16),
        gn_one_recv=((3 * tok, width), bf16),
    )


def semaphore_counts(g):
    plane, line = (g.members - 1,) * 2, (g.planes - 1,) * 2
    chips = (2 * g.chips - 1,) * 2
    along, along_twice = (g.planes + 1,) * 2, (2 * g.planes + 2,) * 2
    return dict(
        w_in=plane,
        w_up=plane,
        pre=plane,
        ps_back=plane,
        car=line,
        y=line,
        ps_line=line,
        ct_z=line,
        edge=(1, 1),
        back_edge=(1, 1),
        act_one=chips,
        act_two=chips,
        cotan=chips,
        w_out=chips,
        gn_two=chips,
        w_in_line=along_twice,
        w_up_line=along_twice,
        w_out_line=along_twice,
        w_down=along,
    )


class Geometry:
    def __init__(self, n_dp, n_seq, tok, width, hidden, rows, down_rows):
        self.n_dp, self.n_seq = n_dp, n_seq
        self.devices = n_dp * n_seq
        self.planes = n_seq // INNER
        self.members = n_dp * INNER
        self.chips = self.members // 2
        self.tok, self.width, self.hidden = tok, width, hidden
        self.rows, self.down_rows = rows, down_rows
        self.plane_tokens = self.members * tok
        self.length = n_seq * tok
        self.blocks = n_seq
        self.ff_part = hidden // self.members
        self.chan = LANES // max(self.planes, 1)

    def fits(self):
        return (
            self.n_dp == 2
            and self.n_seq % INNER == 0
            and self.tok == LANES
            and self.width == self.members * LANES
            and self.down_rows % LANES == 0
            and self.rows % 16 == 0
            and self.chan % 16 == 0
            and self.down_rows * self.planes == self.ff_part
        )


class Net:
    def __init__(self, g):
        self.g = g
        self.x, self.s = lax.axis_index("dp"), lax.axis_index("seq")
        self.z, self.q = self.s // INNER, self.s % INNER
        self.m = self.x * INNER + self.q
        self.p, self.c = self.m // 2, self.m % 2
        self.flat = self.x * g.n_seq + self.s
        self.sib = 2 * self.p + 1 - self.c
        self.chan_block = self.m * g.planes + self.z
        self.ends = []

    def device(self, flat):
        return (flat // self.g.n_seq, flat % self.g.n_seq)

    def member(self, m):
        return (m // INNER, self.z * INNER + m % INNER)

    def in_plane(self, z):
        return (self.x, z * INNER + self.q)

    def copy(self, src, dst, sems, k, device, sent=None):
        send, recv = sems
        return pltpu.make_async_remote_copy(
            src_ref=src,
            dst_ref=dst,
            send_sem=send.at[k if sent is None else sent],
            recv_sem=recv.at[k],
            device_id=device,
            device_id_type=ON_MESH,
        )

    def sent(self, *moves):
        for move in moves:
            move.wait_send()
            self.ends.remove(move.wait_send)

    def finish(self):
        for end in self.ends:
            end()


class AlongPlanes:
    def __init__(self, net, sems, src, dst):
        self.net, self.sems, self.src, self.dst = net, sems, src, dst
        net.ends.append(self.wait_send)

    def each(self, act):
        net = self.net
        for j in range(1, net.g.planes):
            z = lax.rem(net.z + j, net.g.planes)
            act(net.copy(self.src(z), self.dst, self.sems, j - 1, net.in_plane(z)))

    def start(self):
        self.each(lambda copy: copy.start())

    def wait(self):
        self.each(lambda copy: copy.wait_recv())

    def wait_send(self):
        self.each(lambda copy: copy.wait_send())


class ToMembers:
    def __init__(self, net, sems, src, dst):
        self.net, self.sems, self.src, self.dst = net, sems, src, dst
        net.ends.append(self.wait_send)

    def each(self, act):
        net = self.net
        for j in range(1, net.g.members):
            m = lax.rem(net.m + j, net.g.members)
            act(net.copy(self.src(m), self.dst, self.sems, j - 1, net.member(m)))

    def start(self):
        self.each(lambda copy: copy.start())

    def wait(self):
        self.each(lambda copy: copy.wait_recv())

    def wait_send(self):
        self.each(lambda copy: copy.wait_send())


def relays(planes):
    return [(2, 1, 0), (planes - 3, planes - 2, planes - 1)] if planes > 3 else []


class LineGather:
    def __init__(self, net, sems, pieces):
        self.net, self.sems, self.pieces = net, sems, pieces
        net.ends.append(self.wait_send)

    def copies(self, source, target, handed):
        n = len(self.pieces(0))
        for k, piece in enumerate(self.pieces(source)):
            sent = (self.net.g.planes if handed else target) * n + k
            yield self.net.copy(piece, piece, self.sems, source * n + k, self.net.in_plane(target), sent)

    def to_plane(self, target, act):
        z = self.net.z
        away = z != target
        for source, _, end in relays(self.net.g.planes):
            if end == target:
                away = away & (z != source)

        @pl.when(away)
        def _():
            for copy in self.copies(z, target, 0):
                act(copy)

    def start(self, far):
        for target in range(self.net.g.planes):
            near = (self.net.z == target - 1) | (self.net.z == target + 1)

            @pl.when((near if not far else jnp.logical_not(near)))
            def _():
                self.to_plane(target, lambda copy: copy.start())

    def hand_on(self):
        for source, through, target in relays(self.net.g.planes):

            @pl.when(self.net.z == through)
            def _():
                for copy in self.copies(source, target, 1):
                    copy.wait_recv()
                    copy.start()

    def wait(self):
        for source in range(self.net.g.planes):
            due = self.net.z != source
            for held, through, _ in relays(self.net.g.planes):
                if held == source:
                    due = due & (self.net.z != through)

            @pl.when(due)
            def _():
                for copy in self.copies(source, 0, 0):
                    copy.wait_recv()

    def wait_send(self):
        for target in range(self.net.g.planes):
            self.to_plane(target, lambda copy: copy.wait_send())
        for source, through, target in relays(self.net.g.planes):

            @pl.when(self.net.z == through)
            def _():
                for copy in self.copies(source, target, 1):
                    copy.wait_send()


class LineSum:
    def __init__(self, net, sems, own, slots, pre=()):
        self.net, self.sems, self.own, self.slots, self.pre = net, sems, own, slots, pre
        passing = relays(net.g.planes) if pre else []
        self.ends = [(t, through, 0 if t else net.g.planes - 1) for _, through, t in passing]
        net.ends.append(self.wait_send)

    def copies(self, target):
        for k, (piece, slot) in enumerate(zip(self.own(target), self.slots(self.net.z))):
            n = len(self.own(0))
            yield self.net.copy(piece, slot, self.sems, self.net.z * n + k, self.net.in_plane(target), target * n + k)

    def early(self, target, through):
        n = len(self.own(0))
        for k, (piece, held) in enumerate(zip(self.own(target), self.pre)):
            at = self.net.g.planes * n + k
            yield self.net.copy(piece, held, self.sems, at, self.net.in_plane(through), target * n + k)

    def direct(self, target, act):
        away = self.net.z != target
        for end, through, far in self.ends:
            if end == target:
                away = away & (self.net.z != through) & (self.net.z != far)

        @pl.when(away)
        def _():
            for copy in self.copies(target):
                act(copy)

    def start_early(self):
        for target, through, far in self.ends:

            @pl.when(self.net.z == far)
            def _():
                for copy in self.early(target, through):
                    copy.start()

    def start(self, far):
        for target in range(self.net.g.planes):
            near = (self.net.z == target - 1) | (self.net.z == target + 1)

            @pl.when(jnp.logical_not(near) if far else near)
            def _():
                self.direct(target, lambda copy: copy.start())

    def clear(self):
        for target, _, far in self.ends:

            @pl.when(self.net.z == target)
            def _():
                for slot in self.slots(far):
                    slot[...] = jnp.zeros(slot.shape, slot.dtype)

    def add_up(self):
        for target, through, _ in self.ends:

            @pl.when(self.net.z == through)
            def _():
                arriving, leaving = self.early(target, through), self.copies(target)
                for piece, held, come, go in zip(self.own(target), self.pre, arriving, leaving):
                    come.wait_recv()
                    piece[...] = (piece[...].astype(f32) + held[...].astype(f32)).astype(bf16)
                    go.start()

    def wait(self):
        for source in range(self.net.g.planes):
            due = self.net.z != source
            for target, _, far in self.ends:
                if far == source:
                    due = due & (self.net.z != target)

            @pl.when(due)
            def _():
                n = len(self.own(0))
                for k, slot in enumerate(self.slots(source)):
                    self.net.copy(slot, slot, self.sems, source * n + k, self.net.in_plane(source)).wait_recv()

    def wait_send(self):
        for target, through, far in self.ends:

            @pl.when(self.net.z == far)
            def _():
                for copy in self.early(target, through):
                    copy.wait_send()

            @pl.when(self.net.z == through)
            def _():
                for copy in self.copies(target):
                    copy.wait_send()

        for target in range(self.net.g.planes):
            self.direct(target, lambda copy: copy.wait_send())


class PlaneGather:
    def __init__(self, net, sems, piece):
        self.net, self.sems, self.piece = net, sems, piece
        net.ends.append(self.wait_send)

    def peer(self, j):
        return 2 * lax.rem(self.net.p + j, self.net.g.chips) + self.net.c

    def source(self, j):
        return 2 * lax.rem(self.net.p + self.net.g.chips - j, self.net.g.chips) + self.net.c

    def across(self, j):
        net = self.net
        mine = self.piece(net.m)
        return net.copy(mine, mine, self.sems, j - 1, net.member(self.peer(j)))

    def beside(self, j):
        net = self.net
        held = self.piece(self.source(j) if j else net.m)
        return net.copy(held, held, self.sems, net.g.chips - 1 + j, net.member(net.sib))

    def start(self):
        for j in range(1, self.net.g.chips):
            self.across(j).start()
        self.beside(0).start()

    def forward(self, j):
        self.across(j).wait_recv()
        self.beside(j).start()

    def wait(self, j):
        self.beside(j).wait_recv()

    def forward_all(self):
        for j in range(1, self.net.g.chips):
            self.forward(j)

    def wait_all(self):
        for j in range(self.net.g.chips):
            self.wait(j)

    def wait_send(self):
        for j in range(1, self.net.g.chips):
            self.across(j).wait_send()
        for j in range(self.net.g.chips):
            self.beside(j).wait_send()


class PlaneSum:
    def __init__(self, net, sems, sib, recv, own=None, send=None, after=None):
        self.net, self.sems, self.sib, self.recv = net, sems, sib, recv
        if after is None:
            self.own, self.send = own, send
        else:
            self.own, self.send = after.own, after.send
            net.sent(after)
        net.ends.append(self.wait_send)

    def block(self, ref, k):
        return ref.at[step_at(k, self.net.g.tok)]

    def beside(self, chip):
        net = self.net
        return net.copy(
            self.block(self.own, 2 * chip + 1 - net.c), self.block(self.sib, chip), self.sems, chip, net.member(net.sib)
        )

    def across(self, j):
        net = self.net
        chip = lax.rem(net.p + j, net.g.chips)
        return net.copy(
            self.block(self.send, chip),
            self.block(self.recv, j - 1),
            self.sems,
            net.g.chips - 1 + j,
            net.member(2 * chip + net.c),
        )

    def start(self, chip):
        self.beside(chip).start()

    def pair(self, chip):
        self.beside(chip).wait_recv()
        mine = self.own[step_at(2 * chip + self.net.c, self.net.g.tok), :].astype(f32)
        return mine + self.sib[step_at(chip, self.net.g.tok), :].astype(f32)

    def relay(self, j):
        chip = lax.rem(self.net.p + j, self.net.g.chips)
        self.send[step_at(chip, self.net.g.tok), :] = self.pair(chip).astype(bf16)
        self.across(j).start()

    def result(self):
        total = self.pair(self.net.p)
        tok = self.net.g.tok
        for j in range(1, self.net.g.chips):
            self.across(j).wait_recv()
            total = total + self.recv[(j - 1) * tok : j * tok, :].astype(f32)
        return total

    def wait_send(self):
        for chip in range(self.net.g.chips):
            self.beside(chip).wait_send()
        for j in range(1, self.net.g.chips):
            self.across(j).wait_send()


def to_rows(ref, at, row):
    for k in range(row.shape[1] // LANES):
        ref[at + k : at + k + 1, :] = row[:, k * LANES : (k + 1) * LANES]


def column_sum(x):
    return jnp.sum(x, 0, keepdims=True)


def normalized(x):
    center = x - jnp.mean(x, -1, keepdims=True)
    inverse = lax.rsqrt(jnp.mean(center * center, -1, keepdims=True) + 1e-5)
    return center * inverse, inverse


def norm_back(grad, xhat, inverse, gain):
    e = grad * gain
    return (e - jnp.mean(e, -1, keepdims=True) - xhat * jnp.mean(e * xhat, -1, keepdims=True)) * inverse


def gelu_pair(v):
    scale = math.sqrt(2 / math.pi)
    v2 = v * v
    t = jnp.tanh(scale * v * (1.0 + 0.044715 * v2))
    half = 0.5 * (1.0 + t)
    return v * half, half + 0.5 * v * (1.0 - t * t) * (scale * (1.0 + 3 * 0.044715 * v2))


def to_spectrum(g, load, rows, stage, turns, high, low, out):
    @pl.loop(0, rows // 16)
    def _(step):
        at = step_at(step, 16)
        first = []
        for n in range(g.blocks):
            block = load(n, step)
            angle = -2 * math.pi * n / (4 * g.blocks)
            first.append((block * math.cos(angle), block * math.sin(angle)))
        for k, (re, im) in enumerate(small_transform(first, -1)):
            c, s = turns[k : k + 1, :LANES], turns[k : k + 1, LANES:]
            stage[k, at, :LANES] = re * c + im * s
            stage[k, at, LANES:] = im * c - re * s

    group = 256 // rows

    @pl.loop(0, g.blocks // group)
    def _(step):
        at = step_at(step, group)
        x = stage[at].reshape(group * rows, 2 * LANES)
        out[at] = split_dot(x, high[...], low[...]).reshape(group, rows, 2 * LANES)


def from_spectrum(g, product, rows, stage, turns, high, low, store):
    group = 256 // rows

    @pl.loop(0, g.blocks // group)
    def _(step):
        at = step_at(step, group)
        re, im = product(at)
        x = jnp.concatenate([re, im], -1).reshape(group * rows, 2 * LANES)
        stage[at] = split_dot(x, high[...], low[...]).reshape(group, rows, 2 * LANES)

    @pl.loop(0, rows // 16)
    def _(step):
        at = step_at(step, 16)
        values = []
        for k in range(g.blocks):
            re, im = stage[k, at, :LANES], stage[k, at, LANES:]
            c, s = turns[k : k + 1, :LANES], turns[k : k + 1, LANES:]
            values.append((re * c - im * s, re * s + im * c))
        for n, (re, im) in enumerate(small_transform(values, 1)):
            angle = 2 * math.pi * n / (4 * g.blocks)
            store(n, step, (re * math.cos(angle) - im * math.sin(angle)) * (1.0 / g.length))


def halves(x):
    return x[..., :LANES], x[..., LANES:]


def block_kernel(g, *refs):
    refs = list(refs)
    r = Inputs(*(refs.pop(0) for _ in Inputs._fields))
    block_out, tokens_grad, ct_out, ps_out, in_recv, up_recv, down_recv, out_recv = (refs.pop(0) for _ in range(8))
    w = types.SimpleNamespace(**{name: refs.pop(0) for name in scratch_buffers(g)})
    sems = types.SimpleNamespace(**{name: (refs.pop(0), refs.pop(0)) for name in semaphore_counts(g)})
    local_sem = refs.pop(0)
    net = Net(g)
    local_count = [0]

    def to_local(src, dst):
        copy = pltpu.make_async_copy(src, dst, local_sem.at[local_count[0]])
        local_count[0] += 1
        copy.start()
        return copy

    def to_output(src, dst):
        net.ends.append(to_local(src, dst).wait)

    coming = {
        name: to_local(getattr(r, name), getattr(w, name))
        for name in w.__dict__
        if name in Inputs._fields
    }
    r = r._replace(**{name: getattr(w, name) for name in coming})

    def arrive(*refs):
        for name in list(coming):
            if any(getattr(w, name) is ref for ref in refs):
                coming.pop(name).wait()
    tok, width, pt, ch, ff = g.tok, g.width, g.plane_tokens, g.chan, g.ff_part
    rows, planes, members, chips, blocks = g.rows, g.planes, g.members, g.chips, g.blocks
    part = g.down_rows
    exact = lax.Precision.HIGHEST

    barrier = pltpu.get_barrier_semaphore()
    partners = [net.member(lax.rem(net.m + j, members)) for j in range(1, members)]
    partners += [net.in_plane(lax.rem(net.z + j, planes)) for j in range(1, planes)]
    for there in partners:
        pl.semaphore_signal(barrier, inc=1, device_id=there, device_id_type=ON_MESH)

    for m in range(members):
        for b in range(3):
            at = b * width + m * LANES
            w.w_in_send[m * rows : (m + 1) * rows, b * LANES : (b + 1) * LANES] = r.input_weight[:, at : at + LANES]

    own_rows = step_at(net.flat, rows)

    def plane_rows(ref, z):
        return [ref.at[step_at(x * planes + z, INNER * rows)] for x in range(g.n_dp)]

    move_in = ToMembers(net, sems.w_in, lambda m: w.w_in_send.at[step_at(m, rows)], w.w_in.at[own_rows])
    line_in = LineGather(net, sems.w_in_line, lambda z: plane_rows(w.w_in, z))
    arrive(r.down_weight)
    w.w_down[step_at(net.z, part), :] = r.down_weight[...]
    w.w_out[step_at(net.m * planes + net.z, rows), :] = r.output_weight[...]
    line_down = LineGather(net, sems.w_down, lambda z: [w.w_down.at[step_at(z, part)]])
    line_out = LineGather(net, sems.w_out_line, lambda z: [w.w_out.at[step_at(net.m * planes + z, rows)]])
    pl.semaphore_wait(barrier, len(partners))
    move_in.start()
    line_out.start(far=False)
    line_down.start(far=False)

    xhat_one, inverse_one = normalized(r.tokens[...].astype(f32))
    w.xhat_one[...] = xhat_one
    mine = step_at(net.m, tok)
    w.act_one[mine, :] = (xhat_one * r.first_gain[...] + r.first_shift[...]).astype(bf16)
    gather_one = PlaneGather(net, sems.act_one, lambda m: w.act_one.at[step_at(m, tok)])
    gather_one.start()

    arrive(r.up_weight)
    for m in range(members):
        for z in range(planes):
            at = ((m // INNER) * g.n_seq + z * INNER + m % INNER) * part
            w.w_up_send[m * rows : (m + 1) * rows, z * part : (z + 1) * part] = r.up_weight[:, at : at + part]
    w.w_in[own_rows, :] = w.w_in_send[step_at(net.m, rows), :]
    w.w_up[own_rows, :] = w.w_up_send[step_at(net.m, rows), :]
    arrive(r.cotangent)
    w.cotan[mine, :] = r.cotangent[...]
    move_up = ToMembers(net, sems.w_up, lambda m: w.w_up_send.at[step_at(m, rows)], w.w_up.at[own_rows])
    line_up = LineGather(net, sems.w_up_line, lambda z: plane_rows(w.w_up, z))
    gather_cotan = PlaneGather(net, sems.cotan, lambda m: w.cotan.at[step_at(m, tok)])

    gather_out = PlaneGather(net, sems.w_out, lambda m: w.w_out.at[step_at(m, LANES)])
    move_up.start()
    line_out.start(far=True)
    move_in.wait()
    line_in.start(far=False)
    line_in.start(far=True)

    w.square[...] = jnp.zeros_like(w.square)
    lane_of = step_at(net.m, LANES)

    def param(row, ref, k, at):
        w.square[row : row + 1, :] = ref[k : k + 1, pl.ds(pl.multiple_of(at + net.m * LANES, LANES), LANES)]

    for b in range(3):
        param(b, r.input_bias, 0, b * width)
        for i in range(3):
            param(3 + 3 * i + b, r.short_weight, i, b * width)
        param(12 + b, r.short_bias, 0, b * width)
    param(15, r.skip_gain, 0, 0)
    param(16, r.decay_rates, 0, 0)
    w.param_cols[...] = w.square[...].T
    here = step_at(net.z, ch)

    def spread(col, rows=slice(None)):
        cols = w.param_cols[rows, col : col + 1]
        return jnp.broadcast_to(cols, (cols.shape[0], LANES))

    for b in range(3):
        for i in range(3):
            w.taps[i, b * LANES : (b + 1) * LANES, :] = spread(3 + 3 * i + b)
        w.taps[3, b * LANES : (b + 1) * LANES, :] = spread(12 + b)
    w.skip[...] = spread(15)
    w.decay[...] = spread(16, here)

    arrive(r.filter_weight, r.features, r.forth_high, r.forth_low, r.back_high, r.back_low)
    w.square[...] = jnp.zeros_like(w.square)
    for k, ref in enumerate((r.feat_bias, r.feat_freq, r.inner_bias, r.inner_freq)):
        w.square[k : k + 1, :FILT] = ref[...]
    w.net_cols[...] = w.square[...].T
    w.square[...] = jnp.zeros_like(w.square)
    w.square[:FEAT, :FILT] = r.feat_weight[...]
    w.net_weights[0] = w.square[...].T
    w.square[...] = jnp.zeros_like(w.square)
    w.square[:FILT, :FILT] = r.inner_weight[...]
    w.net_weights[1] = w.square[...].T
    w.square[...] = jnp.zeros_like(w.square)
    w.square[:FILT, :] = r.filter_weight[:, lane_of]
    w.net_weights[3] = w.square[...].T
    w.square[...] = jnp.zeros_like(w.square)
    w.square[:ch, :] = w.net_weights[3, here, :]
    w.net_weights[2] = w.square[...]
    w.net_weights[3] = w.square[...].T
    w.hid_two[...] = jnp.zeros_like(w.hid_two)

    span = 4 * LANES
    col = lambda k: w.net_cols[:FILT, k : k + 1]
    features_rows = r.features.shape[0]

    @pl.loop(0, g.length // span)
    def _(step):
        at = step_at(step, span)
        feats = r.features[:, at]
        p_one = dot_nn(w.net_weights[0, :FILT, :features_rows], feats, exact) + col(0)
        hid_one, cos_one = sin_cos(col(1) * p_one)
        p_two = dot_nn(w.net_weights[1, :FILT, :FILT], hid_one, exact) + col(2)
        hid_two, cos_two = sin_cos(col(3) * p_two)
        w.p_one[:, at], w.hid_one[:, at], w.cos_one[:, at] = p_one, hid_one, cos_one
        w.p_two[:, at], w.hid_two[:FILT, at], w.cos_two[:, at] = p_two, hid_two, cos_two
        filters = dot_nn(w.net_weights[2, :ch, :FILT], hid_two, exact)
        for k in range(span // LANES):
            cut = slice(k * LANES, (k + 1) * LANES)
            w.filt[step * (span // LANES) + k] = filters[:, cut] * jnp.exp(-w.decay[...] * feats[:1, cut])

    to_spectrum(g, lambda n, step: w.filt[n, step_at(step, 16), :], ch, w.stage_filt, r.turns, r.forth_high, r.forth_low, w.spec_filt)

    line_out.hand_on()
    line_in.hand_on()
    gather_one.forward_all()
    line_out.wait()
    gather_out.start()
    line_in.wait()
    move_up.wait()
    for b in range(3):
        turned = w.w_in[:, b * LANES : (b + 1) * LANES].astype(f32).T.astype(bf16)
        w.w_in_t[b * LANES : (b + 1) * LANES, :] = turned
    gather_one.wait_all()
    biases = jnp.concatenate([w.param_cols[:, b : b + 1] for b in range(3)], 0)

    def project(step):
        at = slice(step * 2 * tok, (step + 1) * 2 * tok)
        w.proj[:, at] = (dot_nt(w.w_in_t[...], w.act_one[at, :]) + biases).astype(bf16)

    def columns(a, n):
        return slice((a * INNER + n) * tok, (a * INNER + n + 1) * tok)

    def share_edge(values, n, rows, to_plane, from_plane, send, recv, sem, edge):
        for a in range(2):
            for b in range(3):
                block = values[b * LANES : (b + 1) * LANES, columns(a, n)].astype(f32)
                send[a * 8 : (a + 1) * 8, b * LANES : (b + 1) * LANES] = block.T[rows, :]
        there = lax.rem(to_plane + planes, planes)
        has_next = (to_plane >= 0) & (to_plane < planes)
        has_before = (from_plane >= 0) & (from_plane < planes)

        def copy():
            return net.copy(send, recv, sem, 0, net.in_plane(there))

        @pl.when(has_next)
        def _():
            copy().start()

        @pl.when(jnp.logical_not(has_before))
        def _():
            recv[...] = jnp.zeros_like(recv)

        def end():
            @pl.when(has_next)
            def _():
                copy().wait_send()

        net.ends.append(end)

        def wait():
            @pl.when(has_before)
            def _():
                copy().wait_recv()

            w.square[...] = jnp.zeros_like(w.square)
            for a in range(2):
                for b in range(3):
                    w.square[rows, :] = recv[a * 8 : (a + 1) * 8, b * LANES : (b + 1) * LANES]
                    edge[a, b * LANES : (b + 1) * LANES, :] = w.square[...].T

        return wait

    for half in range(INNER // 2)[::-1]:
        for a in range(2):
            project(a * INNER // 2 + half)
        if half == INNER // 2 - 1:
            wait_edge = share_edge(
                w.proj, INNER - 1, slice(LANES - 8, LANES), net.z + 1, net.z - 1, w.edge_send, w.edge_recv, sems.edge, w.edge
            )
            line_up.start(far=False)

    net.sent(move_in, line_in, line_out, move_up, gather_one)

    group = 32
    lane = lax.broadcasted_iota(jnp.int32, (group, LANES), 1)

    def rows_of(b, step):
        return pl.ds(pl.multiple_of(b * LANES + step * group, group), group)

    def rolled(x, by):
        return pltpu.roll(x, by, 1), pltpu.roll(x, (2 * by) % LANES, 1)

    def shifted(here, there, edge):
        return jnp.where(edge(1), there[0], here[0]), jnp.where(edge(2), there[1], here[1])

    from_left, from_right = (lambda k: lane < k), (lambda k: lane >= LANES - k)

    def filter_blocks(step, which):
        for a in range(2):
            conv = {}
            for b in range(3):
                at = rows_of(b, step)
                taps = [w.taps[i, at, :] for i in range(4)]
                before = rolled(w.edge[a, at, :], 1) if 0 in which else None
                for n in range(max(which) + 1):
                    now = w.proj[at, columns(a, n)].astype(f32)
                    turned = rolled(now, 1)
                    if n in which:
                        one, two = shifted(turned, before, from_left)
                        conv[b, n] = taps[3] + taps[2] * now + taps[1] * one + taps[0] * two
                        w.conv[at, columns(a, n)] = conv[b, n]
                    before = turned
            for n in which:
                carried = conv[0, n] * conv[2, n]
                w.carried[rows_of(0, step), columns(a, n)] = carried
                w.car_send[rows_of(0, step), columns(a, n)] = carried.astype(bf16)

    @pl.loop(0, LANES // group)
    def _(step):
        filter_blocks(step, range(1, INNER))

    wait_edge()

    @pl.loop(0, LANES // group)
    def _(step):
        filter_blocks(step, range(1))

    own_z = step_at(net.z, ch)

    def along(sem, send, recv):
        move = AlongPlanes(net, sem, lambda z: send.at[step_at(z, ch)], recv.at[own_z])
        move.start()
        recv[own_z, :] = send[own_z, :]
        return move

    def piece_of(n, step):
        a, part_rows = step * 16 // ch, step * 16 % ch
        return (
            pl.ds(pl.multiple_of(n // INNER * ch + part_rows, 16), 16),
            pl.ds(pl.multiple_of((a * INNER + n % INNER) * tok, tok), tok),
        )

    def received(recv):
        return lambda n, step: recv[piece_of(n, step)].astype(f32)

    def to_planes(send):
        def store(n, step, value):
            send[piece_of(n, step)] = value.astype(bf16)

        return store

    move_car = along(sems.car, w.car_send, w.car_recv)
    gather_cotan.start()
    line_up.hand_on()
    move_car.wait()

    def both(filt):
        return jnp.concatenate([filt, filt], 1)

    to_spectrum(g, received(w.car_recv), 2 * ch, w.stage, r.turns, r.forth_high, r.forth_low, w.spec_car)

    def forth_product(at):
        (hr, hi), (xr, xi) = halves(both(w.spec_filt[at])), halves(w.spec_car[at])
        return xr * hr - xi * hi, xr * hi + xi * hr

    from_spectrum(g, forth_product, 2 * ch, w.stage, r.turns, r.back_high, r.back_low, to_planes(w.y_send))
    move_y = along(sems.y, w.y_send, w.y_recv)
    gather_out.forward_all()
    move_y.wait()
    line_up.start(far=True)
    line_down.hand_on()
    line_down.start(far=True)

    @pl.loop(0, LANES // group)
    def _(step):
        at = rows_of(0, step)
        long_out = w.y_recv[at, :].astype(f32) + jnp.tile(w.skip[at, :], (1, members)) * w.carried[at, :]
        w.long[at, :] = long_out
        w.act_pre[at, :] = (w.conv[rows_of(1, step), :] * long_out).astype(bf16)

    own_block = step_at(net.m, LANES)
    move_pre = ToMembers(net, sems.pre, lambda m: w.act_pre.at[:, step_at(m, tok)], w.pre_recv.at[own_block])
    move_pre.start()
    w.pre_recv[own_block, :] = w.act_pre[:, mine]
    gather_cotan.forward_all()
    gather_out.wait_all()
    move_pre.wait()

    def by_line(piece):
        m, z = divmod(piece, planes)
        return (m // INNER) * g.n_seq + z * INNER + m % INNER

    for k in range(members * planes):
        at = by_line(k) * rows
        w.pre_line[k * rows : (k + 1) * rows, :] = w.pre_recv[at : at + rows, :]
    pre_rows = w.pre_line[...].astype(f32).T.astype(bf16)
    branch = dot_nn(pre_rows, w.w_out[...])
    residual = r.tokens[...].astype(f32) + branch + r.output_bias[...]
    w.residual[...] = residual
    xhat_two, inverse_two = normalized(residual)
    w.xhat_two[...] = xhat_two
    w.act_two[mine, :] = (xhat_two * r.second_gain[...] + r.second_shift[...]).astype(bf16)
    gather_two = PlaneGather(net, sems.act_two, lambda m: w.act_two.at[step_at(m, tok)])
    gather_two.start()
    net.sent(move_car, move_y, move_pre)

    gather_cotan.wait_all()
    line_up.wait()
    sum_two = PlaneSum(net, sems.gn_two, w.gn_two_sib, w.gn_two_recv, w.gn_two_own, w.gn_two_send)
    w.ps[...] = jnp.zeros_like(w.ps)
    hidden_block = [net.x * g.n_seq + z * INNER + net.q for z in range(planes)]
    up_bias = jnp.concatenate([r.up_bias[:, step_at(k, part)] for k in hidden_block], 1)
    bias_sum = jnp.zeros((1, ff), f32)
    slopes = []
    for j in range(chips):
        if j == 1:
            gather_two.forward_all()
        gather_two.wait(j)
        at = step_at(lax.rem(net.p + chips - j, chips), 2 * tok)
        gelu, slope = gelu_pair(dot_nn(w.act_two[at, :], w.w_up[...]) + up_bias)
        w.act_three[at, :] = gelu.astype(bf16)
        slopes.append(slope)
    plane_part = INNER * rows

    def parts_of(ref, z):
        at = z * g.n_dp * plane_part
        return [ref.at[pl.ds(at + x * plane_part, plane_part)] for x in range(g.n_dp)]

    def added(ref):
        group_rows = g.n_dp * plane_part
        return sum(ref[z * group_rows : (z + 1) * group_rows, :].astype(f32) for z in range(planes)).astype(bf16)

    def to_owners(sem, mid, out):
        move = ToMembers(net, sem, lambda m: mid.at[step_at(m, rows)], out.at[step_at(net.m, rows)])
        move.start()
        to_output(mid.at[step_at(net.m, rows)], out.at[step_at(net.m, rows)])
        return move

    sum_up = LineSum(
        net,
        sems.w_in_line,
        lambda z: plane_rows(w.up_send, z),
        lambda z: parts_of(w.up_parts, z),
        [w.up_pre.at[x * plane_part : (x + 1) * plane_part] for x in range(g.n_dp)],
    )
    half = part // 2

    def halves_of(ref, z):
        return [ref.at[step_at(2 * z + k, half)] for k in range(2)]

    sum_down = LineSum(
        net,
        sems.w_out_line,
        lambda z: halves_of(w.down_send, z),
        lambda z: halves_of(w.down_parts, z),
        [w.down_pre.at[k * half : (k + 1) * half] for k in range(2)],
    )
    @pl.loop(0, ff // 256)
    def _(step):
        at = step_at(step, 256)
        turned = w.act_three[:, at].astype(f32).T.astype(bf16)
        w.down_send[at, :] = dot_nn(turned, w.cotan[...]).astype(bf16)

    sum_down.start_early()
    line_down.wait()
    sum_down.start(far=False)
    sum_down.clear()
    w.down_parts[step_at(net.z, part), :] = w.down_send[step_at(net.z, part), :]
    for j in range(1, chips + 1):
        chip = lax.rem(net.p + j, chips)
        at = step_at(chip, 2 * tok)
        grad_upper = (dot_nt(w.cotan[at, :], w.w_down[...]) * slopes[-j]).astype(bf16)
        w.grad_up[at, :] = grad_upper
        bias_sum = bias_sum + column_sum(grad_upper.astype(f32))
        sum_two.own[at, :] = dot_nt(grad_upper, w.w_up[...]).astype(bf16)
        sum_two.start(chip)
        if j > 1:
            sum_two.relay(j - 1)
    for z, k in enumerate(hidden_block):
        w.ps[pl.ds(AT_UP_BIAS + k, 1), :] = bias_sum[:, z * part : (z + 1) * part]

    @pl.loop(0, width // 256)
    def _(step):
        at = step_at(step, 256)
        turned = w.act_two[:, at].astype(f32).T.astype(bf16)
        w.up_send[at, :] = dot_nn(turned, w.grad_up[...]).astype(bf16)

    sum_up.start_early()
    sum_down.add_up()
    sum_down.start(far=True)
    for slot, piece in zip(parts_of(w.up_parts, net.z), plane_rows(w.up_send, net.z)):
        slot[...] = piece[...]
    net.sent(gather_cotan, gather_two, line_up, line_down)
    sum_result = PlaneSum(net, sems.cotan, w.result_sib, w.result_recv, w.cotan, w.result_send)
    for j in range(1, chips + 1):
        chip = lax.rem(net.p + j, chips)
        at = step_at(chip, 2 * tok)
        sum_result.own[at, :] = dot_nn(w.act_three[at, :], w.w_down[...]).astype(bf16)
    sum_up.clear()
    grad_two = sum_two.result()

    xhat_two = w.xhat_two[...]
    to_rows(w.ps, AT_SECOND_GAIN, column_sum(grad_two * xhat_two))
    to_rows(w.ps, AT_SECOND_SHIFT, column_sum(grad_two))
    cotan = r.cotangent[...].astype(f32)
    to_rows(w.ps, AT_DOWN_BIAS, column_sum(cotan))
    grad_res = cotan + norm_back(grad_two, xhat_two, inverse_two, r.second_gain[...])
    w.grad_res[...] = grad_res
    grad_branch = grad_res.astype(bf16)
    w.grad_branch[...] = grad_branch
    to_rows(w.ps, AT_OUTPUT_BIAS, column_sum(grad_branch.astype(f32)))

    per_step = 256 // rows
    for step in range(width // 256):
        grad = dot_nt(w.w_out[step * 256 : (step + 1) * 256, :], w.grad_branch[...]).astype(bf16)
        for k in range(per_step):
            at = by_line(step * per_step + k) * rows
            w.gpre_send[at : at + rows, :] = grad[k * rows : (k + 1) * rows, :]

    move_gpre = ToMembers(net, sems.w_in, lambda m: w.gpre_send.at[step_at(m, LANES)], w.gpre.at[:, mine])
    move_gpre.start()
    w.gpre[:, mine] = w.gpre_send[own_block, :]

    sum_out = PlaneSum(net, sems.act_two, w.w_out_grad_sib, w.w_out_grad_recv, after=sum_two)
    for m in range(members):
        at = slice(m * LANES, (m + 1) * LANES)
        sum_out.own[at, :] = dot_nn(w.pre_line[at, :], w.grad_branch[...]).astype(bf16)
    sum_up.add_up()
    move_gpre.wait()
    for total in (sum_out, sum_result):
        for j in range(1, chips + 1):
            total.start(lax.rem(net.p + j, chips))

    @pl.loop(0, LANES // group)
    def _(step):
        at, second = rows_of(0, step), rows_of(1, step)
        grad_pre = w.gpre[at, :].astype(f32)
        grad_long = grad_pre * w.conv[second, :]
        w.grad_long[at, :] = grad_long
        w.gl_send[at, :] = grad_long.astype(bf16)
        w.grad_conv[second, :] = grad_pre * w.long[at, :]

    move_gl = along(sems.car, w.gl_send, w.gl_recv)
    sum_up.start(far=False)
    for j in range(1, chips):
        sum_out.relay(j)
    move_gl.wait()
    to_spectrum(g, received(w.gl_recv), 2 * ch, w.stage, r.turns, r.forth_high, r.forth_low, w.spec_grad)

    def back_product(at):
        (hr, hi), (gr, gi) = halves(both(w.spec_filt[at])), halves(w.spec_grad[at])
        return hr * gr + hi * gi, hr * gi - hi * gr

    from_spectrum(g, back_product, 2 * ch, w.stage, r.turns, r.back_high, r.back_low, to_planes(w.gc_send))
    move_gc = along(sems.y, w.gc_send, w.gc_recv)
    for j in range(1, chips):
        sum_result.relay(j)

    def filt_product(at):
        out = []
        for a in range(2):
            cut = slice(a * ch, (a + 1) * ch)
            (xr, xi), (gr, gi) = halves(w.spec_car[at, cut, :]), halves(w.spec_grad[at, cut, :])
            out.append((xr * gr + xi * gi, xr * gi - xi * gr))
        return out[0][0] + out[1][0], out[0][1] + out[1][1]

    def keep_filter(n, step, value):
        w.back_filt[n, step_at(step, 16), :] = value

    from_spectrum(g, filt_product, ch, w.stage_filt, r.turns, r.back_high, r.back_low, keep_filter)

    ones = jnp.ones((8, span), f32)
    chan_rows = step_at(net.chan_block, ch)
    w.ct[chan_rows, :] = jnp.zeros((ch, LANES), f32)

    @pl.loop(0, g.length // span)
    def _(step):
        at = step_at(step, span)
        feats = r.features[:, at]
        gate = []
        for k in range(span // LANES):
            fade = jnp.exp(-w.decay[...] * feats[:1, k * LANES : (k + 1) * LANES])
            gate.append(w.back_filt[step * (span // LANES) + k] * fade)
        gate = jnp.concatenate(gate, 1)
        w.ct[chan_rows, :] += dot_nt(gate, w.hid_two[:, at], exact)
        q_two = dot_nn(w.net_weights[3, :FILT, :ch], gate, exact)
        slope_two = q_two * w.cos_two[:, at]
        r_two = slope_two * col(3)
        w.ps[:FILT, :FILT] += dot_nt(w.hid_one[:, at], r_two, exact)
        q_one = dot_nn(r.inner_weight[...], r_two, exact)
        slope_one = q_one * w.cos_one[:, at]
        r_one = slope_one * col(1)
        w.ps[AT_FEAT : AT_FEAT + features_rows, :FILT] += dot_nt(feats, r_one, exact)
        for k, x in enumerate((r_one, slope_one * w.p_one[:, at], r_two, slope_two * w.p_two[:, at])):
            w.ps[AT_VECTOR + k : AT_VECTOR + k + 1, :FILT] += dot_nt(ones, x, exact)[:1, :]

    ct_z = AlongPlanes(net, sems.ct_z, lambda z: w.ct.at[chan_rows], w.ct.at[chan_rows])
    ct_z.start()
    move_gc.wait()

    @pl.loop(0, LANES // group)
    def _(step):
        at, last = rows_of(0, step), rows_of(2, step)
        grad = w.gc_recv[at, :].astype(f32) + jnp.tile(w.skip[at, :], (1, members)) * w.grad_long[at, :]
        w.grad_conv[at, :] = grad * w.conv[last, :]
        w.grad_conv[last, :] = grad * w.conv[at, :]

    wait_back_edge = share_edge(
        w.grad_conv, 0, slice(0, 8), net.z - 1, net.z + 1, w.back_edge_send, w.back_edge_recv, sems.back_edge, w.back_edge
    )
    sum_up.start(far=True)

    line_out_grad = LineSum(
        net,
        sems.w_down,
        lambda z: [w.out_sum.at[step_at(z, rows)]],
        lambda z: [w.out_parts.at[step_at(z, rows)]],
    )
    w.out_sum[...] = sum_out.result().astype(bf16)
    def filter_blocks_back(step, which):
        for a in range(2):
            for b in range(3):
                at = rows_of(b, step)
                taps = [w.taps[i, at, :] for i in range(3)]
                after = rolled(w.back_edge[a, at, :], LANES - 1) if INNER - 1 in which else None
                for n in range(min(which), INNER)[::-1]:
                    now = w.grad_conv[at, columns(a, n)]
                    turned = rolled(now, LANES - 1)
                    if n in which:
                        one, two = shifted(turned, after, from_right)
                        w.gproj[at, columns(a, n)] = (taps[2] * now + taps[1] * one + taps[0] * two).astype(bf16)
                    after = turned

    @pl.loop(0, LANES // group)
    def _(step):
        filter_blocks_back(step, range(INNER - 1))

    wait_back_edge()

    @pl.loop(0, LANES // group)
    def _(step):
        filter_blocks_back(step, range(INNER - 1, INNER))

    @pl.loop(0, width // 256)
    def _(step):
        at = step_at(step, 256)
        grad = dot_nn(w.gproj[...], w.act_one[:, at])
        w.gain_sum[:, at] = column_sum(grad * w.w_in_t[:, at].astype(f32))
        for b in range(3):
            cut = slice(b * LANES, (b + 1) * LANES)
            w.in_send[at, cut] = grad[cut].T.astype(bf16)

    sum_in = LineSum(
        net,
        sems.w_up_line,
        lambda z: plane_rows(w.in_send, z),
        lambda z: parts_of(w.w_in, z),
    )
    sum_in.start(far=False)
    for slot, piece in zip(parts_of(w.w_in, net.z), plane_rows(w.in_send, net.z)):
        slot[...] = piece[...]
    ct_z.wait()
    gather_ct = PlaneGather(net, sems.act_one, lambda m: w.ct.at[step_at(m, LANES)])
    gather_ct.start()
    w.block_out[...] = (w.residual[...] + sum_result.result() + r.down_bias[...]).astype(bf16)
    to_output(w.block_out, block_out)
    kept = w.conv

    @pl.loop(0, LANES // group)
    def _(step):
        for b in range(3):
            at = rows_of(b, step)
            sums = [jnp.zeros((group, LANES), f32)] * 5
            for a in range(2):
                before = rolled(w.edge[a, at, :], 1)
                for n in range(INNER):
                    grad, now = w.grad_conv[at, columns(a, n)], w.proj[at, columns(a, n)].astype(f32)
                    turned = rolled(now, 1)
                    one, two = shifted(turned, before, from_left)
                    terms = (grad * two, grad * one, grad * now, grad, w.gproj[at, columns(a, n)].astype(f32))
                    sums = [x + y for x, y in zip(sums, terms)]
                    before = turned
            for k in range(5):
                kept[at, k * LANES : (k + 1) * LANES] = sums[k]
        at = rows_of(0, step)
        product = w.grad_long[at, :] * w.carried[at, :]
        kept[at, 5 * LANES : 6 * LANES] = sum(product[:, k * LANES : (k + 1) * LANES] for k in range(members))

    which_lane = lax.broadcasted_iota(jnp.int32, (LANES, LANES), 1)
    tile = jnp.zeros((LANES, LANES), f32)
    for k, (kind, b) in enumerate(
        [(4, b) for b in range(3)] + [(i, b) for i in range(3) for b in range(3)] + [(3, b) for b in range(3)] + [(5, 0)]
    ):
        part_sums = kept[b * LANES : (b + 1) * LANES, kind * LANES : (kind + 1) * LANES]
        tile = jnp.where(which_lane == k, jnp.sum(part_sums, 1, keepdims=True), tile)
    channel_sum = jnp.sum(kept[:, 4 * LANES : 5 * LANES], 1, keepdims=True)
    shift_sum = column_sum(channel_sum * w.w_in_t[...].astype(f32))
    to_rows(w.ps, AT_FIRST_GAIN, (w.gain_sum[...] - r.first_shift[...] * shift_sum) / r.first_gain[...])
    to_rows(w.ps, AT_FIRST_SHIFT, shift_sum)
    w.ps[pl.ds(pl.multiple_of(AT_CHANNEL + net.m * 16, 16), 16), :] = tile.T[:16, :]

    share = PS_ROWS // members
    own_share = step_at(net.m, share)
    move_ps = ToMembers(net, sems.w_in, lambda m: w.ps.at[step_at(m, share)], w.ps_recv.at[own_share])
    net.sent(move_gpre)
    move_ps.start()
    w.ps_recv[own_share, :] = w.ps[own_share, :]
    sum_one = PlaneSum(net, sems.gn_two, w.gn_one_sib, w.gn_one_recv, after=sum_result)
    for j in range(1, chips + 1):
        chip = lax.rem(net.p + j, chips)
        at = step_at(chip, 2 * tok)
        turned = w.gproj[:, at].astype(f32).T.astype(bf16)
        sum_one.own[at, :] = dot_nn(turned, w.w_in_t[...]).astype(bf16)
        sum_one.start(chip)
        if j > 1:
            sum_one.relay(j - 1)
    move_ps.wait()

    def shares_added(ref, count):
        return sum(ref[k * share : (k + 1) * share, :] for k in range(count))

    own_line = step_at(net.z, share)
    w.ps_line[own_line, :] = shares_added(w.ps_recv, members)
    line_ps = AlongPlanes(net, sems.ps_line, lambda z: w.ps_line.at[own_line], w.ps_line.at[own_line])
    line_ps.start()
    sum_in.start(far=True)
    line_out_grad.start(far=False)
    line_out_grad.start(far=True)
    w.out_parts[step_at(net.z, rows), :] = w.out_sum[step_at(net.z, rows), :]
    sum_up.wait()
    w.up_mid[...] = added(w.up_parts)
    move_up_grad = to_owners(sems.w_up, w.up_mid, up_recv)
    sum_down.wait()
    w.down_total[...] = sum(w.down_parts[z * part : (z + 1) * part, :].astype(f32) for z in range(planes))
    to_output(w.down_total, down_recv)
    gather_ct.forward_all()
    line_ps.wait()
    w.ps_all[own_share, :] = shares_added(w.ps_line, planes)
    move_back = ToMembers(net, sems.ps_back, lambda m: w.ps_all.at[own_share], w.ps_all.at[own_share])
    move_back.start()
    sum_in.wait()
    w.in_mid[...] = added(w.w_in)
    move_in_grad = to_owners(sems.pre, w.in_mid, in_recv)
    grad_one = sum_one.result()

    grad_tokens = norm_back(grad_one, w.xhat_one[...], inverse_one, r.first_gain[...])
    w.tokens_grad[...] = (w.grad_res[...] + grad_tokens).astype(bf16)
    to_output(w.tokens_grad, tokens_grad)
    gather_ct.wait_all()
    to_output(w.ct, ct_out)
    line_out_grad.wait()
    w.out_total[...] = sum(w.out_parts[z * rows : (z + 1) * rows, :].astype(f32) for z in range(planes))
    to_output(w.out_total, out_recv)
    move_back.wait()
    to_output(w.ps_all, ps_out)
    move_in_grad.wait()
    move_up_grad.wait()
    net.finish()


def finish_kernel(g, *refs):
    ins, outs = refs[:8], refs[8:]
    block_in, tokens_in, ct, ps, in_recv, up_recv, down_recv, out_recv = ins
    (
        block_out, tokens_grad, first_gain, first_shift, input_weight, input_bias, short_weight, short_bias, feat_weight,
        feat_bias, feat_freq, inner_weight, inner_bias, inner_freq, filter_weight, skip_gain, output_weight, output_bias,
        second_gain, second_shift, up_weight, up_bias, down_weight, down_bias,
    ) = outs
    rows, planes, width, ff = g.rows, g.planes, g.width, g.ff_part
    for src, dst in ((block_in, block_out), (tokens_in, tokens_grad), (down_recv, down_weight), (out_recv, output_weight)):
        dst[...] = src[...]
    for m in range(g.members):
        x, q = m // INNER, m % INNER
        parts = [x * g.n_seq + z * INNER + q for z in range(planes)]
        total = in_recv[m * rows : (m + 1) * rows, :].astype(f32)
        for b in range(3):
            input_weight[:, b * width + m * LANES : b * width + (m + 1) * LANES] = total[:, b * LANES : (b + 1) * LANES]
        total = up_recv[m * rows : (m + 1) * rows, :].astype(f32)
        for z, k in enumerate(parts):
            cut = slice(z * g.down_rows, (z + 1) * g.down_rows)
            up_weight[:, k * g.down_rows : (k + 1) * g.down_rows] = total[:, cut]
    for m in range(g.members):
        cut = slice(m * LANES, (m + 1) * LANES)
        turned = ct[cut, :].T
        filter_weight[:, cut] = turned[:FILT, :]
        line = lambda k: ps[AT_CHANNEL + 16 * m + k : AT_CHANNEL + 16 * m + k + 1, :]
        for b in range(3):
            at = b * g.members + m
            input_bias[at : at + 1, :] = line(b)
            for i in range(3):
                short_weight[i : i + 1, b * width + m * LANES : b * width + (m + 1) * LANES] = line(3 + 3 * i + b)
            short_bias[at : at + 1, :] = line(12 + b)
        skip_gain[m : m + 1, :] = line(15)
    for out, at in (
        (first_gain, AT_FIRST_GAIN), (first_shift, AT_FIRST_SHIFT), (second_gain, AT_SECOND_GAIN), (up_bias, AT_UP_BIAS),
        (second_shift, AT_SECOND_SHIFT), (output_bias, AT_OUTPUT_BIAS), (down_bias, AT_DOWN_BIAS),
    ):
        out[...] = ps[at : at + out.shape[0], :]
    feat_weight[...] = ps[AT_FEAT : AT_FEAT + FEAT, :FILT]
    inner_weight[...] = ps[:FILT, :FILT]
    for k, out in enumerate((feat_bias, feat_freq, inner_bias, inner_freq)):
        out[...] = ps[AT_VECTOR + k : AT_VECTOR + k + 1, :FILT]


def on_device_in_kernels(g, *args):
    operands = [a[0] if a.ndim == 3 else a[None] if a.ndim == 1 else a for a in args]
    operands += [jnp.asarray(table) for table in constant_tables(g.blocks, LANES)]
    tok, width = g.tok, g.width
    in_vmem = pl.BlockSpec(memory_space=pltpu.VMEM)
    anywhere = pl.BlockSpec(memory_space=pl.ANY)
    S = jax.ShapeDtypeStruct
    buffers = scratch_buffers(g)
    parts = pl.pallas_call(
        functools.partial(block_kernel, g),
        out_shape=[
            S((tok, width), bf16),
            S((tok, width), bf16),
            S((width, LANES), f32),
            S((PS_ROWS, LANES), f32),
            S((g.members * g.rows, 3 * LANES), bf16),
            S((g.members * g.rows, g.ff_part), bf16),
            S((g.down_rows, width), f32),
            S((g.rows, width), f32),
        ],
        in_specs=[anywhere if name in buffers else in_vmem for name in Inputs._fields],
        out_specs=[anywhere] * 8,
        scratch_shapes=[pltpu.VMEM(shape, dtype) for shape, dtype in buffers.values()]
        + [pltpu.SemaphoreType.DMA((count,)) for pair in semaphore_counts(g).values() for count in pair]
        + [pltpu.SemaphoreType.DMA((len(set(Inputs._fields) & set(buffers)) + 8,))],
        compiler_params=pltpu.CompilerParams(
            collective_id=0, has_side_effects=True, vmem_limit_bytes=63 * 1024 * 1024
        ),
        name="block",
    )(*operands)

    def out_shape(a):
        if a.ndim == 3:
            return S(a.shape[1:], bf16)
        if a.ndim == 1:
            return S((a.shape[0] // LANES, LANES) if a.shape[0] % LANES == 0 else (1, a.shape[0]), f32)
        return S(a.shape, f32)

    named = Inputs(*args, *operands[len(args) :])
    wanted = [a for a in args if a is not named.cotangent and a is not named.decay_rates]
    wanted = [named.tokens] + wanted
    outs = pl.pallas_call(
        functools.partial(finish_kernel, g),
        out_shape=[out_shape(a) for a in wanted],
        in_specs=[in_vmem] * 8,
        out_specs=[in_vmem] * len(wanted),
        compiler_params=pltpu.CompilerParams(vmem_limit_bytes=63 * 1024 * 1024),
        name="finish",
    )(*parts)
    return tuple(o.reshape(a.shape) for o, a in zip(outs, wanted))


def on_device_by_size(tokens, cotangent, *args):
    named = Inputs(tokens, cotangent, *args, *[None] * 6)
    g = Geometry(
        lax.axis_size("dp"),
        lax.axis_size("seq"),
        tokens.shape[1],
        tokens.shape[2],
        named.up_weight.shape[1],
        named.input_weight.shape[0],
        named.down_weight.shape[0],
    )
    if g.fits():
        return on_device_in_kernels(g, tokens, cotangent, *args)
    return on_device(tokens, cotangent, *args)


def solution(mesh):
    placed = (
        P("dp", "seq", None),
        P("dp", "seq", None),
        P(),
        P(),
        P(("dp", "seq"), None),
        P(),
        P(),
        P(),
        P(),
        P(),
        P(),
        P(),
        P(),
        P(),
        P(),
        P(),
        P(),
        P(("dp", "seq"), None),
        P(),
        P(),
        P(),
        P(("dp", "seq"), None),
        P(),
        P(("dp", "seq"), None),
        P(),
    )
    return jax.shard_map(
        on_device_by_size,
        mesh=mesh,
        in_specs=placed,
        out_specs=(
            P("dp", "seq", None),
            P("dp", "seq", None),
            P(),
            P(),
            P(("dp", "seq"), None),
            P(),
            P(),
            P(),
            P(),
            P(),
            P(),
            P(),
            P(),
            P(),
            P(),
            P(),
            P(("dp", "seq"), None),
            P(),
            P(),
            P(),
            P(("dp", "seq"), None),
            P(),
            P(("dp", "seq"), None),
            P(),
        ),
        check_vma=False,
    )
```

```python
import functools
import math
import types
from typing import NamedTuple

import jax
import jax.numpy as jnp
import ml_dtypes
import numpy as np
from jax import lax
from jax.experimental import pallas as pl
from jax.experimental.pallas import tpu as pltpu
from jax.sharding import PartitionSpec as P

FEAT = 33
FILT = 64


exact_precision = lax.Precision.HIGHEST


def from_behind(x, axis, by):
    size = lax.axis_size(axis)
    pairs = [(i, i + by) for i in range(size) if 0 <= i + by < size]
    return lax.ppermute(x, axis, pairs)


def layer_norm(values, gain_vec, offset):
    center = values - jnp.mean(values, -1, keepdims=True)
    spread = jnp.mean(center * center, -1, keepdims=True)
    return center * lax.rsqrt(spread + 1e-05) * gain_vec + offset


def position_features(stamps, length):
    stamp_float = stamps.astype(jnp.float32)
    linear_ramp = stamp_float / (length - 1)
    band_rates = 0.0001 + jnp.arange((FEAT - 1) // 2).astype(jnp.float32) * ((15.0 - 0.0001) / 15.0)
    phase_angle = (stamp_float * (2.0 * math.pi / length))[:, None] * band_rates[None, :]
    return jnp.concatenate([linear_ramp[:, None], jnp.cos(phase_angle), -jnp.sin(phase_angle)], 1)


def filter_net(
    feat_weight,
    feat_bias,
    feat_freq,
    inner_weight,
    inner_bias,
    inner_freq,
    filter_weight,
    feature_rows,
    modulate,
):
    hidden = jnp.sin(
        feat_freq * (jnp.dot(feature_rows, feat_weight, precision=exact_precision) + feat_bias)
    )
    hidden = jnp.sin(
        inner_freq * (jnp.dot(hidden, inner_weight, precision=exact_precision) + inner_bias)
    )
    raw_filter = lax.dot_general(
        filter_weight, hidden, (((0,), (1,)), ((), ())), precision=exact_precision
    )
    return raw_filter * modulate


def short_conv(padded, kernel, offset):
    col_count = padded.shape[1] - 2
    return (
        offset[:, None]
        + kernel[0][:, None] * padded[:, :col_count]
        + kernel[1][:, None] * padded[:, 1 : col_count + 1]
        + kernel[2][:, None] * padded[:, 2:]
    )


def unit_angles(rows, cols, period):
    row_index = lax.broadcasted_iota(jnp.int32, (rows, cols), 0)
    col_index = lax.broadcasted_iota(jnp.int32, (rows, cols), 1)
    phase_angle = (row_index * col_index % period).astype(jnp.float32) * (2.0 * math.pi / period)
    return (jnp.cos(phase_angle), jnp.sin(phase_angle))


def forward_frequency_domain(signal, outer_size, period):
    block_count = signal.shape[1]
    row_count = signal.shape[2]
    cos_first, sin_first = unit_angles(outer_size, block_count, outer_size)
    real_first = jnp.einsum("dn,cnt->cdt", cos_first, signal, precision=exact_precision)
    imag_first = -jnp.einsum("dn,cnt->cdt", sin_first, signal, precision=exact_precision)
    cos_turn, sin_turn = unit_angles(outer_size, row_count, period)
    real_turned = real_first * cos_turn + imag_first * sin_turn
    imag_turned = imag_first * cos_turn - real_first * sin_turn
    cos_last, sin_last = unit_angles(row_count, row_count, row_count)
    real_out = jnp.einsum(
        "cdb,bk->cdk", real_turned, cos_last, precision=exact_precision
    ) + jnp.einsum("cdb,bk->cdk", imag_turned, sin_last, precision=exact_precision)
    imag_out = jnp.einsum(
        "cdb,bk->cdk", imag_turned, cos_last, precision=exact_precision
    ) - jnp.einsum("cdb,bk->cdk", real_turned, sin_last, precision=exact_precision)
    return (real_out, imag_out)


def inverse_spectrum(real_part, imag_part, block_count, period):
    outer_size = real_part.shape[1]
    row_count = real_part.shape[2]
    cos_last, sin_last = unit_angles(row_count, row_count, row_count)
    real_back = jnp.einsum(
        "cdk,kb->cdb", real_part, cos_last, precision=exact_precision
    ) - jnp.einsum("cdk,kb->cdb", imag_part, sin_last, precision=exact_precision)
    imag_back = jnp.einsum(
        "cdk,kb->cdb", real_part, sin_last, precision=exact_precision
    ) + jnp.einsum("cdk,kb->cdb", imag_part, cos_last, precision=exact_precision)
    cos_turn, sin_turn = unit_angles(outer_size, row_count, period)
    real_turned = real_back * cos_turn - imag_back * sin_turn
    imag_turned = real_back * sin_turn + imag_back * cos_turn
    cos_first, sin_first = unit_angles(block_count, outer_size, outer_size)
    summed = jnp.einsum(
        "nd,cdt->cnt", cos_first, real_turned, precision=exact_precision
    ) - jnp.einsum("nd,cdt->cnt", sin_first, imag_turned, precision=exact_precision)
    return summed / period


def on_device(
    tokens,
    cotangent,
    first_gain,
    first_shift,
    input_weight,
    input_bias,
    short_weight,
    short_bias,
    feat_weight,
    feat_bias,
    feat_freq,
    inner_weight,
    inner_bias,
    inner_freq,
    filter_weight,
    skip_gain,
    decay_rates,
    output_weight,
    output_bias,
    second_gain,
    second_shift,
    up_weight,
    up_bias,
    down_weight,
    down_bias,
):
    sequence_count = lax.axis_size("seq")
    seq_index = lax.axis_index("seq")
    row_count = tokens.shape[1]
    model_width = tokens.shape[2]
    length = row_count * sequence_count
    period = 2 * length
    outer_size = 2 * sequence_count
    narrow = model_width // sequence_count
    inputs = tokens[0].astype(jnp.float32)
    cotan_rows = cotangent[0].astype(jnp.float32)
    w_in, w_out, w_up, w_down = (
        lax.all_gather(input_weight, ("dp", "seq"), axis=0, tiled=True),
        lax.all_gather(output_weight, ("dp", "seq"), axis=0, tiled=True),
        lax.all_gather(up_weight, ("dp", "seq"), axis=0, tiled=True),
        lax.all_gather(down_weight, ("dp", "seq"), axis=0, tiled=True),
    )
    normed_one, norm_one_back = jax.vjp(layer_norm, inputs, first_gain, first_shift)
    act_one = normed_one.astype(jnp.bfloat16)
    projected = lax.dot_general(
        w_in, act_one, (((0,), (1,)), ((), ())), preferred_element_type=jnp.float32
    )
    projected = projected + input_bias[:, None]
    rim_rows = from_behind(projected[:, row_count - 2 :], "seq", 1)
    padded = jnp.concatenate([rim_rows, projected], 1)
    conv_out, short_back = jax.vjp(short_conv, padded, short_weight, short_bias)
    leading_gate = conv_out[:model_width]
    second_gate = conv_out[model_width : 2 * model_width]
    value_part = conv_out[2 * model_width :]
    carried = leading_gate * value_part
    stamps = seq_index * row_count + lax.iota(jnp.int32, row_count)
    modulate = jnp.exp(-decay_rates[:, None] * (stamps.astype(jnp.float32) / (length - 1))[None, :])
    filter_fixed = functools.partial(
        filter_net, feature_rows=position_features(stamps, length), modulate=modulate
    )
    filters, filter_back = jax.vjp(
        filter_fixed,
        feat_weight,
        feat_bias,
        feat_freq,
        inner_weight,
        inner_bias,
        inner_freq,
        filter_weight,
    )
    carried_blocks = carried.reshape(sequence_count, narrow, row_count)
    filter_blocks = filters.reshape(sequence_count, narrow, row_count)
    carried_chan, filter_chan = (
        lax.all_to_all(
            carried_blocks.astype(jnp.bfloat16), "seq", split_axis=0, concat_axis=2, tiled=True
        ).astype(carried_blocks.dtype),
        lax.all_to_all(
            filter_blocks.astype(jnp.bfloat16), "seq", split_axis=0, concat_axis=2, tiled=True
        ).astype(filter_blocks.dtype),
    )
    carried_chan = carried_chan.reshape(narrow, sequence_count, row_count)
    filter_chan = filter_chan.reshape(narrow, sequence_count, row_count)
    carried_real, carried_imag = forward_frequency_domain(carried_chan, outer_size, period)
    filter_real, filter_imag = forward_frequency_domain(filter_chan, outer_size, period)
    conv_chan = inverse_spectrum(
        carried_real * filter_real - carried_imag * filter_imag,
        carried_real * filter_imag + carried_imag * filter_real,
        sequence_count,
        period,
    )
    conv_rows = lax.all_to_all(
        conv_chan.reshape(1, narrow, length).astype(jnp.bfloat16),
        "seq",
        split_axis=2,
        concat_axis=0,
        tiled=True,
    ).astype(jnp.float32)
    long_out = conv_rows.reshape(model_width, row_count) + skip_gain[:, None] * carried
    act_pre = (second_gate * long_out).astype(jnp.bfloat16)
    branch_out = lax.dot_general(
        act_pre, w_out, (((0,), (0,)), ((), ())), preferred_element_type=jnp.float32
    )
    residual = inputs + branch_out + output_bias
    normed_two, norm_two_back = jax.vjp(layer_norm, residual, second_gain, second_shift)
    act_two = normed_two.astype(jnp.bfloat16)
    upper = jnp.dot(act_two, w_up, preferred_element_type=jnp.float32) + up_bias
    gelu_out, gelu_back = jax.vjp(jax.nn.gelu, upper)
    act_three = gelu_out.astype(jnp.bfloat16)
    result = residual + jnp.dot(act_three, w_down, preferred_element_type=jnp.float32) + down_bias
    block_out = result.astype(jnp.bfloat16)[None]
    grad_final = cotan_rows.astype(jnp.bfloat16)
    down_grad = lax.dot_general(
        act_three, grad_final, (((0,), (0,)), ((), ())), preferred_element_type=jnp.float32
    )
    down_bias_grad = jnp.sum(grad_final, 0, dtype=jnp.float32)
    grad_act_three = lax.dot_general(
        grad_final, w_down, (((1,), (1,)), ((), ())), preferred_element_type=jnp.float32
    )
    (grad_upper,) = gelu_back(grad_act_three)
    grad_upper = grad_upper.astype(jnp.bfloat16)
    up_grad = lax.dot_general(
        act_two, grad_upper, (((0,), (0,)), ((), ())), preferred_element_type=jnp.float32
    )
    up_bias_grad = jnp.sum(grad_upper, 0, dtype=jnp.float32)
    grad_norm_two = lax.dot_general(
        grad_upper, w_up, (((1,), (1,)), ((), ())), preferred_element_type=jnp.float32
    )
    grad_resid_norm, second_gain_grad, second_shift_grad = norm_two_back(grad_norm_two)
    grad_residual = cotan_rows + grad_resid_norm
    grad_branch = grad_residual.astype(jnp.bfloat16)
    output_grad = jnp.dot(act_pre, grad_branch, preferred_element_type=jnp.float32)
    output_bias_grad = jnp.sum(grad_branch, 0, dtype=jnp.float32)
    grad_pre = lax.dot_general(
        w_out, grad_branch, (((1,), (1,)), ((), ())), preferred_element_type=jnp.float32
    )
    grad_second = grad_pre * long_out
    grad_long = grad_pre * second_gate
    skip_gain_grad = jnp.sum(grad_long * carried, 1)
    grad_long_blocks = grad_long.reshape(sequence_count, narrow, row_count)
    grad_chan, carried_again, filter_again = (
        lax.all_to_all(
            grad_long_blocks.astype(jnp.bfloat16), "seq", split_axis=0, concat_axis=2, tiled=True
        ).astype(grad_long_blocks.dtype),
        lax.all_to_all(
            carried_blocks.astype(jnp.bfloat16), "seq", split_axis=0, concat_axis=2, tiled=True
        ).astype(carried_blocks.dtype),
        lax.all_to_all(
            filter_blocks.astype(jnp.bfloat16), "seq", split_axis=0, concat_axis=2, tiled=True
        ).astype(filter_blocks.dtype),
    )
    carried_real, carried_imag = forward_frequency_domain(
        carried_again.reshape(narrow, sequence_count, row_count), outer_size, period
    )
    filter_real, filter_imag = forward_frequency_domain(
        filter_again.reshape(narrow, sequence_count, row_count), outer_size, period
    )
    grad_real, grad_imag = forward_frequency_domain(
        grad_chan.reshape(narrow, sequence_count, row_count), outer_size, period
    )
    carried_back = inverse_spectrum(
        filter_real * grad_real + filter_imag * grad_imag,
        filter_real * grad_imag - filter_imag * grad_real,
        sequence_count,
        period,
    )
    filter_grad_chan = inverse_spectrum(
        carried_real * grad_real + carried_imag * grad_imag,
        carried_real * grad_imag - carried_imag * grad_real,
        sequence_count,
        period,
    )
    carried_got, filters_got = (
        lax.all_to_all(
            carried_back.reshape(1, narrow, length).astype(jnp.bfloat16),
            "seq",
            split_axis=2,
            concat_axis=0,
            tiled=True,
        ).astype(jnp.float32),
        lax.all_to_all(
            filter_grad_chan.reshape(1, narrow, length).astype(jnp.bfloat16),
            "seq",
            split_axis=2,
            concat_axis=0,
            tiled=True,
        ).astype(jnp.float32),
    )
    grad_carried = carried_got.reshape(model_width, row_count) + skip_gain[:, None] * grad_long
    grad_filters = filters_got.reshape(model_width, row_count)
    (
        feat_weight_grad,
        feat_bias_grad,
        feat_freq_grad,
        inner_weight_grad,
        inner_bias_grad,
        inner_freq_grad,
        filter_weight_grad,
    ) = filter_back(grad_filters)
    grad_conv = jnp.concatenate(
        [grad_carried * value_part, grad_second, grad_carried * leading_gate], 0
    )
    grad_padded, short_weight_grad, short_bias_grad = short_back(grad_conv)
    rim_grad = from_behind(grad_padded[:, :2], "seq", -1)
    grad_projected = jnp.concatenate(
        [grad_padded[:, 2:row_count], grad_padded[:, row_count:] + rim_grad], 1
    )
    grad_projected = grad_projected.astype(jnp.bfloat16)
    input_grad = lax.dot_general(
        act_one, grad_projected, (((0,), (1,)), ((), ())), preferred_element_type=jnp.float32
    )
    input_bias_grad = jnp.sum(grad_projected, 1, dtype=jnp.float32)
    first_norm_gradient = lax.dot_general(
        grad_projected, w_in, (((0,), (1,)), ((), ())), preferred_element_type=jnp.float32
    )
    grad_inputs, first_gain_grad, first_shift_grad = norm_one_back(first_norm_gradient)
    tokens_grad = (grad_inputs + grad_residual).astype(jnp.bfloat16)[None]
    input_weight_grad, output_weight_grad, up_weight_grad, down_weight_grad = (
        lax.psum_scatter(input_grad, ("dp", "seq"), scatter_dimension=0, tiled=True),
        lax.psum_scatter(output_grad, ("dp", "seq"), scatter_dimension=0, tiled=True),
        lax.psum_scatter(up_grad, ("dp", "seq"), scatter_dimension=0, tiled=True),
        lax.psum_scatter(down_grad, ("dp", "seq"), scatter_dimension=0, tiled=True),
    )
    (
        first_gain_grad,
        first_shift_grad,
        input_bias_grad,
        short_weight_grad,
        short_bias_grad,
        feat_weight_grad,
        feat_bias_grad,
        feat_freq_grad,
        inner_weight_grad,
        inner_bias_grad,
        inner_freq_grad,
        filter_weight_grad,
        skip_gain_grad,
        output_bias_grad,
        second_gain_grad,
        second_shift_grad,
        up_bias_grad,
        down_bias_grad,
    ) = lax.psum(
        (
            first_gain_grad,
            first_shift_grad,
            input_bias_grad,
            short_weight_grad,
            short_bias_grad,
            feat_weight_grad,
            feat_bias_grad,
            feat_freq_grad,
            inner_weight_grad,
            inner_bias_grad,
            inner_freq_grad,
            filter_weight_grad,
            skip_gain_grad,
            output_bias_grad,
            second_gain_grad,
            second_shift_grad,
            up_bias_grad,
            down_bias_grad,
        ),
        ("dp", "seq"),
    )
    return (
        block_out,
        tokens_grad,
        first_gain_grad,
        first_shift_grad,
        input_weight_grad,
        input_bias_grad,
        short_weight_grad,
        short_bias_grad,
        feat_weight_grad,
        feat_bias_grad,
        feat_freq_grad,
        inner_weight_grad,
        inner_bias_grad,
        inner_freq_grad,
        filter_weight_grad,
        skip_gain_grad,
        output_weight_grad,
        output_bias_grad,
        second_gain_grad,
        second_shift_grad,
        up_weight_grad,
        up_bias_grad,
        down_weight_grad,
        down_bias_grad,
    )


f32 = jnp.float32
bf16 = jnp.bfloat16
ON_MESH = pl.DeviceIdType.MESH
INNER = 4
LANES = 128
PS_ROWS = 320
AT_VECTOR = 64
AT_SECOND_GAIN = 72
AT_SECOND_SHIFT = 80
AT_OUTPUT_BIAS = 88
AT_DOWN_BIAS = 96
AT_FIRST_GAIN = 104
AT_FIRST_SHIFT = 112
AT_UP_BIAS = 120
AT_FEAT = 152
AT_CHANNEL = 192


def dot_nn(a, b, precision=None):
    return lax.dot_general(
        a, b, (((1,), (0,)), ((), ())), precision=precision, preferred_element_type=f32
    )


def dot_nt(a, b, precision=None):
    return lax.dot_general(
        a, b, (((1,), (1,)), ((), ())), precision=precision, preferred_element_type=f32
    )


def step_at(index, size):
    return pl.ds(pl.multiple_of(index * size, size), size)


def times_unit(value, turns):
    re, im = value
    c, s = math.cos(2 * math.pi * turns), math.sin(2 * math.pi * turns)
    if abs(s) < 1e-12:
        return (re, im) if c > 0 else (-re, -im)
    if abs(c) < 1e-12:
        return (-im, re) if s > 0 else (im, -re)
    return re * c - im * s, re * s + im * c


def small_transform(values, sign):
    size = len(values)
    if size == 1:
        return values
    even = small_transform(values[0::2], sign)
    odd = small_transform(values[1::2], sign)
    turned = [times_unit(odd[k], sign * k / size) for k in range(size // 2)]
    return [(e[0] + t[0], e[1] + t[1]) for e, t in zip(even, turned)] + [
        (e[0] - t[0], e[1] - t[1]) for e, t in zip(even, turned)
    ]


@functools.lru_cache(None)
def constant_tables(blocks, lanes):
    length = blocks * lanes
    n2 = np.arange(lanes)
    angle = 2 * np.pi * np.outer(n2, n2) / lanes
    c, s = np.cos(angle), np.sin(angle)
    forth = np.block([[c, -s], [s, c]])
    back = np.block([[c, s], [-s, c]])

    def split(x):
        high = x.astype(ml_dtypes.bfloat16)
        return high, (x - high.astype(np.float64)).astype(ml_dtypes.bfloat16)

    turn = 2 * np.pi * np.outer(np.arange(blocks) + 0.25, n2) / length
    turns = np.concatenate([np.cos(turn), np.sin(turn)], 1).astype(np.float32)
    rates = 1e-4 + np.arange((FEAT - 1) // 2) * ((15.0 - 1e-4) / 15.0)
    phase = (2 * np.pi * np.arange(length) / length)[None, :] * rates[:, None]
    ramp = (np.arange(length) / (length - 1))[None, :]
    features = np.concatenate([ramp, np.cos(phase), -np.sin(phase)], 0)
    features = np.pad(features, ((0, -FEAT % 8), (0, 0))).astype(np.float32)
    return split(forth) + split(back) + (turns, features)


def split_dot(x, high, low):
    head = x.astype(bf16)
    tail = (x - head.astype(f32)).astype(bf16)
    return dot_nn(jnp.concatenate([head, tail, head], 1), jnp.concatenate([high, high, low], 0))


def sin_cos(x):
    count = jnp.floor(x * (2 / math.pi) + 0.5)
    r = x - count * 1.5703125
    r = r - count * 4.837512969970703e-4
    r = r - count * 7.549789948768648e-8
    r2 = r * r
    s = r + r * r2 * (-1.6666654611e-1 + r2 * (8.3321608736e-3 + r2 * -1.9515295891e-4))
    c = 1.0 - 0.5 * r2 + r2 * r2 * (
        4.166664568298827e-2 + r2 * (-1.388731625493765e-3 + r2 * 2.443315711809948e-5)
    )
    quarter = count - 4.0 * jnp.floor(count * 0.25)
    odd = (quarter == 1.0) | (quarter == 3.0)
    sine = jnp.where(odd, c, s)
    cosine = jnp.where(odd, s, c)
    sine = jnp.where(quarter >= 2.0, -sine, sine)
    cosine = jnp.where((quarter == 1.0) | (quarter == 2.0), -cosine, cosine)
    return sine, cosine


class Inputs(NamedTuple):
    tokens: jax.Array
    cotangent: jax.Array
    first_gain: jax.Array
    first_shift: jax.Array
    input_weight: jax.Array
    input_bias: jax.Array
    short_weight: jax.Array
    short_bias: jax.Array
    feat_weight: jax.Array
    feat_bias: jax.Array
    feat_freq: jax.Array
    inner_weight: jax.Array
    inner_bias: jax.Array
    inner_freq: jax.Array
    filter_weight: jax.Array
    skip_gain: jax.Array
    decay_rates: jax.Array
    output_weight: jax.Array
    output_bias: jax.Array
    second_gain: jax.Array
    second_shift: jax.Array
    up_weight: jax.Array
    up_bias: jax.Array
    down_weight: jax.Array
    down_bias: jax.Array
    forth_high: jax.Array
    forth_low: jax.Array
    back_high: jax.Array
    back_low: jax.Array
    turns: jax.Array
    features: jax.Array


def scratch_buffers(g):
    tok, width, pt, ch = g.tok, g.width, g.plane_tokens, g.chan
    ff, blocks = g.ff_part, g.blocks
    return dict(
        up_weight=((g.rows, g.hidden), bf16),
        down_weight=((g.down_rows, width), bf16),
        cotangent=((tok, width), bf16),
        filter_weight=((FILT, width), f32),
        features=((FEAT + -FEAT % 8, g.length), f32),
        forth_high=((2 * LANES, 2 * LANES), bf16),
        forth_low=((2 * LANES, 2 * LANES), bf16),
        back_high=((2 * LANES, 2 * LANES), bf16),
        back_low=((2 * LANES, 2 * LANES), bf16),
        block_out=((tok, width), bf16),
        tokens_grad=((tok, width), bf16),
        w_in=((width, 3 * LANES), bf16),
        w_in_send=((g.members * g.rows, 3 * LANES), bf16),
        w_up_send=((g.members * g.rows, ff), bf16),
        w_in_t=((3 * LANES, width), bf16),
        w_out=((width, width), bf16),
        w_up=((width, ff), bf16),
        w_down=((ff, width), bf16),
        act_one=((pt, width), bf16),
        act_two=((pt, width), bf16),
        cotan=((pt, width), bf16),
        proj=((3 * LANES, pt), bf16),
        conv=((3 * LANES, pt), f32),
        grad_conv=((3 * LANES, pt), f32),
        carried=((LANES, pt), f32),
        long=((LANES, pt), f32),
        grad_long=((LANES, pt), f32),
        car_send=((LANES, pt), bf16),
        car_recv=((LANES, pt), bf16),
        y_send=((LANES, pt), bf16),
        y_recv=((LANES, pt), bf16),
        gl_send=((LANES, pt), bf16),
        gl_recv=((LANES, pt), bf16),
        gc_send=((LANES, pt), bf16),
        gc_recv=((LANES, pt), bf16),
        act_pre=((LANES, pt), bf16),
        gpre=((LANES, pt), bf16),
        gproj=((3 * LANES, pt), bf16),
        taps=((4, 3 * LANES, LANES), f32),
        skip=((LANES, LANES), f32),
        edge_send=((16, 3 * LANES), f32),
        edge_recv=((16, 3 * LANES), f32),
        back_edge_send=((16, 3 * LANES), f32),
        back_edge_recv=((16, 3 * LANES), f32),
        edge=((2, 3 * LANES, LANES), f32),
        back_edge=((2, 3 * LANES, LANES), f32),
        ps_recv=((PS_ROWS, LANES), f32),
        ps_line=((PS_ROWS // g.members * g.planes, LANES), f32),
        square=((LANES, LANES), f32),
        param_cols=((LANES, LANES), f32),
        decay=((ch, LANES), f32),
        net_weights=((4, LANES, LANES), f32),
        net_cols=((LANES, LANES), f32),
        p_one=((FILT, g.length), f32),
        hid_one=((FILT, g.length), f32),
        cos_one=((FILT, g.length), f32),
        p_two=((FILT, g.length), f32),
        hid_two=((LANES, g.length), f32),
        cos_two=((FILT, g.length), f32),
        filt=((blocks, ch, LANES), f32),
        stage=((blocks, 2 * ch, 2 * LANES), f32),
        stage_filt=((blocks, ch, 2 * LANES), f32),
        spec_filt=((blocks, ch, 2 * LANES), f32),
        spec_car=((blocks, 2 * ch, 2 * LANES), f32),
        spec_grad=((blocks, 2 * ch, 2 * LANES), f32),
        back_filt=((blocks, ch, LANES), f32),
        pre_recv=((width, tok), bf16),
        pre_line=((width, tok), bf16),
        gpre_send=((width, tok), bf16),
        residual=((tok, width), f32),
        xhat_two=((tok, width), f32),
        xhat_one=((tok, width), f32),
        grad_res=((tok, width), f32),
        grad_branch=((tok, width), bf16),
        act_three=((pt, ff), bf16),
        grad_up=((pt, ff), bf16),
        up_send=((width, ff), bf16),
        up_parts=((width, ff), bf16),
        up_pre=((width // g.planes, ff), bf16),
        up_mid=((width // g.planes, ff), bf16),
        down_parts=((ff, width), bf16),
        down_pre=((g.down_rows, width), bf16),
        down_total=((g.down_rows, width), f32),
        down_send=((ff, width), bf16),
        in_mid=((width // g.planes, 3 * LANES), bf16),
        in_send=((width, 3 * LANES), bf16),
        out_sum=((LANES, width), bf16),
        out_parts=((LANES, width), bf16),
        out_total=((g.rows, width), f32),
        ct=((width, LANES), f32),
        gain_sum=((1, width), f32),
        ps=((PS_ROWS, LANES), f32),
        ps_all=((PS_ROWS, LANES), f32),
        gn_two_own=((pt, width), bf16),
        gn_two_send=((pt // 2, width), bf16),
        gn_two_sib=((pt // 2, width), bf16),
        gn_two_recv=((3 * tok, width), bf16),
        result_send=((pt // 2, width), bf16),
        result_sib=((pt // 2, width), bf16),
        result_recv=((3 * tok, width), bf16),
        w_out_grad_sib=((pt // 2, width), bf16),
        w_out_grad_recv=((3 * tok, width), bf16),
        gn_one_sib=((pt // 2, width), bf16),
        gn_one_recv=((3 * tok, width), bf16),
    )


def semaphore_counts(g):
    plane, line = (g.members - 1,) * 2, (g.planes - 1,) * 2
    chips = (2 * g.chips - 1,) * 2
    along, along_twice = (g.planes + 1,) * 2, (2 * g.planes + 2,) * 2
    return dict(
        w_in=plane,
        w_up=plane,
        pre=plane,
        ps_back=plane,
        car=line,
        y=line,
        ps_line=line,
        ct_z=line,
        edge=(1, 1),
        back_edge=(1, 1),
        act_one=chips,
        act_two=chips,
        cotan=chips,
        w_out=chips,
        gn_two=chips,
        w_in_line=along_twice,
        w_up_line=along_twice,
        w_out_line=along_twice,
        w_down=along,
    )


class Geometry:
    def __init__(self, n_dp, n_seq, tok, width, hidden, rows, down_rows):
        self.n_dp, self.n_seq = n_dp, n_seq
        self.devices = n_dp * n_seq
        self.planes = n_seq // INNER
        self.members = n_dp * INNER
        self.chips = self.members // 2
        self.tok, self.width, self.hidden = tok, width, hidden
        self.rows, self.down_rows = rows, down_rows
        self.plane_tokens = self.members * tok
        self.length = n_seq * tok
        self.blocks = n_seq
        self.ff_part = hidden // self.members
        self.chan = LANES // max(self.planes, 1)

    def fits(self):
        return (
            self.n_dp == 2
            and self.n_seq % INNER == 0
            and self.tok == LANES
            and self.width == self.members * LANES
            and self.down_rows % LANES == 0
            and self.rows % 16 == 0
            and self.chan % 16 == 0
            and self.down_rows * self.planes == self.ff_part
        )


class Net:
    def __init__(self, g):
        self.g = g
        self.x, self.s = lax.axis_index("dp"), lax.axis_index("seq")
        self.z, self.q = self.s // INNER, self.s % INNER
        self.m = self.x * INNER + self.q
        self.p, self.c = self.m // 2, self.m % 2
        self.flat = self.x * g.n_seq + self.s
        self.sib = 2 * self.p + 1 - self.c
        self.chan_block = self.m * g.planes + self.z
        self.ends = []

    def device(self, flat):
        return (flat // self.g.n_seq, flat % self.g.n_seq)

    def member(self, m):
        return (m // INNER, self.z * INNER + m % INNER)

    def in_plane(self, z):
        return (self.x, z * INNER + self.q)

    def copy(self, src, dst, sems, k, device, sent=None):
        send, recv = sems
        return pltpu.make_async_remote_copy(
            src_ref=src,
            dst_ref=dst,
            send_sem=send.at[k if sent is None else sent],
            recv_sem=recv.at[k],
            device_id=device,
            device_id_type=ON_MESH,
        )

    def sent(self, *moves):
        for move in moves:
            move.wait_send()
            self.ends.remove(move.wait_send)

    def finish(self):
        for end in self.ends:
            end()


class AlongPlanes:
    def __init__(self, net, sems, src, dst):
        self.net, self.sems, self.src, self.dst = net, sems, src, dst
        net.ends.append(self.wait_send)

    def each(self, act):
        net = self.net
        for j in range(1, net.g.planes):
            z = lax.rem(net.z + j, net.g.planes)
            act(net.copy(self.src(z), self.dst, self.sems, j - 1, net.in_plane(z)))

    def start(self):
        self.each(lambda copy: copy.start())

    def wait(self):
        self.each(lambda copy: copy.wait_recv())

    def wait_send(self):
        self.each(lambda copy: copy.wait_send())


class ToMembers:
    def __init__(self, net, sems, src, dst):
        self.net, self.sems, self.src, self.dst = net, sems, src, dst
        net.ends.append(self.wait_send)

    def each(self, act):
        net = self.net
        for j in range(1, net.g.members):
            m = lax.rem(net.m + j, net.g.members)
            act(net.copy(self.src(m), self.dst, self.sems, j - 1, net.member(m)))

    def start(self):
        self.each(lambda copy: copy.start())

    def wait(self):
        self.each(lambda copy: copy.wait_recv())

    def wait_send(self):
        self.each(lambda copy: copy.wait_send())


def relays(planes):
    return [(2, 1, 0), (planes - 3, planes - 2, planes - 1)] if planes > 3 else []


class LineGather:
    def __init__(self, net, sems, pieces):
        self.net, self.sems, self.pieces = net, sems, pieces
        net.ends.append(self.wait_send)

    def copies(self, source, target, handed):
        n = len(self.pieces(0))
        for k, piece in enumerate(self.pieces(source)):
            sent = (self.net.g.planes if handed else target) * n + k
            yield self.net.copy(piece, piece, self.sems, source * n + k, self.net.in_plane(target), sent)

    def to_plane(self, target, act):
        z = self.net.z
        away = z != target
        for source, _, end in relays(self.net.g.planes):
            if end == target:
                away = away & (z != source)

        @pl.when(away)
        def _():
            for copy in self.copies(z, target, 0):
                act(copy)

    def start(self, far):
        for target in range(self.net.g.planes):
            near = (self.net.z == target - 1) | (self.net.z == target + 1)

            @pl.when((near if not far else jnp.logical_not(near)))
            def _():
                self.to_plane(target, lambda copy: copy.start())

    def hand_on(self):
        for source, through, target in relays(self.net.g.planes):

            @pl.when(self.net.z == through)
            def _():
                for copy in self.copies(source, target, 1):
                    copy.wait_recv()
                    copy.start()

    def wait(self):
        for source in range(self.net.g.planes):
            due = self.net.z != source
            for held, through, _ in relays(self.net.g.planes):
                if held == source:
                    due = due & (self.net.z != through)

            @pl.when(due)
            def _():
                for copy in self.copies(source, 0, 0):
                    copy.wait_recv()

    def wait_send(self):
        for target in range(self.net.g.planes):
            self.to_plane(target, lambda copy: copy.wait_send())
        for source, through, target in relays(self.net.g.planes):

            @pl.when(self.net.z == through)
            def _():
                for copy in self.copies(source, target, 1):
                    copy.wait_send()


class LineSum:
    def __init__(self, net, sems, own, slots, pre=()):
        self.net, self.sems, self.own, self.slots, self.pre = net, sems, own, slots, pre
        passing = relays(net.g.planes) if pre else []
        self.ends = [(t, through, 0 if t else net.g.planes - 1) for _, through, t in passing]
        net.ends.append(self.wait_send)

    def copies(self, target):
        for k, (piece, slot) in enumerate(zip(self.own(target), self.slots(self.net.z))):
            n = len(self.own(0))
            yield self.net.copy(piece, slot, self.sems, self.net.z * n + k, self.net.in_plane(target), target * n + k)

    def early(self, target, through):
        n = len(self.own(0))
        for k, (piece, held) in enumerate(zip(self.own(target), self.pre)):
            at = self.net.g.planes * n + k
            yield self.net.copy(piece, held, self.sems, at, self.net.in_plane(through), target * n + k)

    def direct(self, target, act):
        away = self.net.z != target
        for end, through, far in self.ends:
            if end == target:
                away = away & (self.net.z != through) & (self.net.z != far)

        @pl.when(away)
        def _():
            for copy in self.copies(target):
                act(copy)

    def start_early(self):
        for target, through, far in self.ends:

            @pl.when(self.net.z == far)
            def _():
                for copy in self.early(target, through):
                    copy.start()

    def start(self, far):
        for target in range(self.net.g.planes):
            near = (self.net.z == target - 1) | (self.net.z == target + 1)

            @pl.when(jnp.logical_not(near) if far else near)
            def _():
                self.direct(target, lambda copy: copy.start())

    def clear(self):
        for target, _, far in self.ends:

            @pl.when(self.net.z == target)
            def _():
                for slot in self.slots(far):
                    slot[...] = jnp.zeros(slot.shape, slot.dtype)

    def add_up(self):
        for target, through, _ in self.ends:

            @pl.when(self.net.z == through)
            def _():
                arriving, leaving = self.early(target, through), self.copies(target)
                for piece, held, come, go in zip(self.own(target), self.pre, arriving, leaving):
                    come.wait_recv()
                    piece[...] = (piece[...].astype(f32) + held[...].astype(f32)).astype(bf16)
                    go.start()

    def wait(self):
        for source in range(self.net.g.planes):
            due = self.net.z != source
            for target, _, far in self.ends:
                if far == source:
                    due = due & (self.net.z != target)

            @pl.when(due)
            def _():
                n = len(self.own(0))
                for k, slot in enumerate(self.slots(source)):
                    self.net.copy(slot, slot, self.sems, source * n + k, self.net.in_plane(source)).wait_recv()

    def wait_send(self):
        for target, through, far in self.ends:

            @pl.when(self.net.z == far)
            def _():
                for copy in self.early(target, through):
                    copy.wait_send()

            @pl.when(self.net.z == through)
            def _():
                for copy in self.copies(target):
                    copy.wait_send()

        for target in range(self.net.g.planes):
            self.direct(target, lambda copy: copy.wait_send())


class PlaneGather:
    def __init__(self, net, sems, piece):
        self.net, self.sems, self.piece = net, sems, piece
        net.ends.append(self.wait_send)

    def peer(self, j):
        return 2 * lax.rem(self.net.p + j, self.net.g.chips) + self.net.c

    def source(self, j):
        return 2 * lax.rem(self.net.p + self.net.g.chips - j, self.net.g.chips) + self.net.c

    def across(self, j):
        net = self.net
        mine = self.piece(net.m)
        return net.copy(mine, mine, self.sems, j - 1, net.member(self.peer(j)))

    def beside(self, j):
        net = self.net
        held = self.piece(self.source(j) if j else net.m)
        return net.copy(held, held, self.sems, net.g.chips - 1 + j, net.member(net.sib))

    def start(self):
        for j in range(1, self.net.g.chips):
            self.across(j).start()
        self.beside(0).start()

    def forward(self, j):
        self.across(j).wait_recv()
        self.beside(j).start()

    def wait(self, j):
        self.beside(j).wait_recv()

    def forward_all(self):
        for j in range(1, self.net.g.chips):
            self.forward(j)

    def wait_all(self):
        for j in range(self.net.g.chips):
            self.wait(j)

    def wait_send(self):
        for j in range(1, self.net.g.chips):
            self.across(j).wait_send()
        for j in range(self.net.g.chips):
            self.beside(j).wait_send()


class PlaneSum:
    def __init__(self, net, sems, sib, recv, own=None, send=None, after=None):
        self.net, self.sems, self.sib, self.recv = net, sems, sib, recv
        if after is None:
            self.own, self.send = own, send
        else:
            self.own, self.send = after.own, after.send
            net.sent(after)
        net.ends.append(self.wait_send)

    def block(self, ref, k):
        return ref.at[step_at(k, self.net.g.tok)]

    def beside(self, chip):
        net = self.net
        return net.copy(
            self.block(self.own, 2 * chip + 1 - net.c), self.block(self.sib, chip), self.sems, chip, net.member(net.sib)
        )

    def across(self, j):
        net = self.net
        chip = lax.rem(net.p + j, net.g.chips)
        return net.copy(
            self.block(self.send, chip),
            self.block(self.recv, j - 1),
            self.sems,
            net.g.chips - 1 + j,
            net.member(2 * chip + net.c),
        )

    def start(self, chip):
        self.beside(chip).start()

    def pair(self, chip):
        self.beside(chip).wait_recv()
        mine = self.own[step_at(2 * chip + self.net.c, self.net.g.tok), :].astype(f32)
        return mine + self.sib[step_at(chip, self.net.g.tok), :].astype(f32)

    def relay(self, j):
        chip = lax.rem(self.net.p + j, self.net.g.chips)
        self.send[step_at(chip, self.net.g.tok), :] = self.pair(chip).astype(bf16)
        self.across(j).start()

    def result(self):
        total = self.pair(self.net.p)
        tok = self.net.g.tok
        for j in range(1, self.net.g.chips):
            self.across(j).wait_recv()
            total = total + self.recv[(j - 1) * tok : j * tok, :].astype(f32)
        return total

    def wait_send(self):
        for chip in range(self.net.g.chips):
            self.beside(chip).wait_send()
        for j in range(1, self.net.g.chips):
            self.across(j).wait_send()


def to_rows(ref, at, row):
    for k in range(row.shape[1] // LANES):
        ref[at + k : at + k + 1, :] = row[:, k * LANES : (k + 1) * LANES]


def column_sum(x):
    return jnp.sum(x, 0, keepdims=True)


def normalized(x):
    center = x - jnp.mean(x, -1, keepdims=True)
    inverse = lax.rsqrt(jnp.mean(center * center, -1, keepdims=True) + 1e-5)
    return center * inverse, inverse


def norm_back(grad, xhat, inverse, gain):
    e = grad * gain
    return (e - jnp.mean(e, -1, keepdims=True) - xhat * jnp.mean(e * xhat, -1, keepdims=True)) * inverse


def gelu_pair(v):
    scale = math.sqrt(2 / math.pi)
    v2 = v * v
    t = jnp.tanh(scale * v * (1.0 + 0.044715 * v2))
    half = 0.5 * (1.0 + t)
    return v * half, half + 0.5 * v * (1.0 - t * t) * (scale * (1.0 + 3 * 0.044715 * v2))


def to_spectrum(g, load, rows, stage, turns, high, low, out):
    @pl.loop(0, rows // 16)
    def _(step):
        at = step_at(step, 16)
        first = []
        for n in range(g.blocks):
            block = load(n, step)
            angle = -2 * math.pi * n / (4 * g.blocks)
            first.append((block * math.cos(angle), block * math.sin(angle)))
        for k, (re, im) in enumerate(small_transform(first, -1)):
            c, s = turns[k : k + 1, :LANES], turns[k : k + 1, LANES:]
            stage[k, at, :LANES] = re * c + im * s
            stage[k, at, LANES:] = im * c - re * s

    group = 256 // rows

    @pl.loop(0, g.blocks // group)
    def _(step):
        at = step_at(step, group)
        x = stage[at].reshape(group * rows, 2 * LANES)
        out[at] = split_dot(x, high[...], low[...]).reshape(group, rows, 2 * LANES)


def from_spectrum(g, product, rows, stage, turns, high, low, store):
    group = 256 // rows

    @pl.loop(0, g.blocks // group)
    def _(step):
        at = step_at(step, group)
        re, im = product(at)
        x = jnp.concatenate([re, im], -1).reshape(group * rows, 2 * LANES)
        stage[at] = split_dot(x, high[...], low[...]).reshape(group, rows, 2 * LANES)

    @pl.loop(0, rows // 16)
    def _(step):
        at = step_at(step, 16)
        values = []
        for k in range(g.blocks):
            re, im = stage[k, at, :LANES], stage[k, at, LANES:]
            c, s = turns[k : k + 1, :LANES], turns[k : k + 1, LANES:]
            values.append((re * c - im * s, re * s + im * c))
        for n, (re, im) in enumerate(small_transform(values, 1)):
            angle = 2 * math.pi * n / (4 * g.blocks)
            store(n, step, (re * math.cos(angle) - im * math.sin(angle)) * (1.0 / g.length))


def halves(x):
    return x[..., :LANES], x[..., LANES:]


def block_kernel(g, *refs):
    refs = list(refs)
    r = Inputs(*(refs.pop(0) for _ in Inputs._fields))
    block_out, tokens_grad, ct_out, ps_out, in_recv, up_recv, down_recv, out_recv = (refs.pop(0) for _ in range(8))
    w = types.SimpleNamespace(**{name: refs.pop(0) for name in scratch_buffers(g)})
    sems = types.SimpleNamespace(**{name: (refs.pop(0), refs.pop(0)) for name in semaphore_counts(g)})
    local_sem = refs.pop(0)
    net = Net(g)
    local_count = [0]

    def to_local(src, dst):
        copy = pltpu.make_async_copy(src, dst, local_sem.at[local_count[0]])
        local_count[0] += 1
        copy.start()
        return copy

    def to_output(src, dst):
        net.ends.append(to_local(src, dst).wait)

    coming = {
        name: to_local(getattr(r, name), getattr(w, name))
        for name in w.__dict__
        if name in Inputs._fields
    }
    r = r._replace(**{name: getattr(w, name) for name in coming})

    def arrive(*refs):
        for name in list(coming):
            if any(getattr(w, name) is ref for ref in refs):
                coming.pop(name).wait()
    tok, width, pt, ch, ff = g.tok, g.width, g.plane_tokens, g.chan, g.ff_part
    rows, planes, members, chips, blocks = g.rows, g.planes, g.members, g.chips, g.blocks
    part = g.down_rows
    exact = lax.Precision.HIGHEST

    barrier = pltpu.get_barrier_semaphore()
    partners = [net.member(lax.rem(net.m + j, members)) for j in range(1, members)]
    partners += [net.in_plane(lax.rem(net.z + j, planes)) for j in range(1, planes)]
    for there in partners:
        pl.semaphore_signal(barrier, inc=1, device_id=there, device_id_type=ON_MESH)

    for m in range(members):
        for b in range(3):
            at = b * width + m * LANES
            w.w_in_send[m * rows : (m + 1) * rows, b * LANES : (b + 1) * LANES] = r.input_weight[:, at : at + LANES]

    own_rows = step_at(net.flat, rows)

    def plane_rows(ref, z):
        return [ref.at[step_at(x * planes + z, INNER * rows)] for x in range(g.n_dp)]

    move_in = ToMembers(net, sems.w_in, lambda m: w.w_in_send.at[step_at(m, rows)], w.w_in.at[own_rows])
    line_in = LineGather(net, sems.w_in_line, lambda z: plane_rows(w.w_in, z))
    arrive(r.down_weight)
    w.w_down[step_at(net.z, part), :] = r.down_weight[...]
    w.w_out[step_at(net.m * planes + net.z, rows), :] = r.output_weight[...]
    line_down = LineGather(net, sems.w_down, lambda z: [w.w_down.at[step_at(z, part)]])
    line_out = LineGather(net, sems.w_out_line, lambda z: [w.w_out.at[step_at(net.m * planes + z, rows)]])
    pl.semaphore_wait(barrier, len(partners))
    move_in.start()
    line_out.start(far=False)
    line_down.start(far=False)

    xhat_one, inverse_one = normalized(r.tokens[...].astype(f32))
    w.xhat_one[...] = xhat_one
    mine = step_at(net.m, tok)
    w.act_one[mine, :] = (xhat_one * r.first_gain[...] + r.first_shift[...]).astype(bf16)
    gather_one = PlaneGather(net, sems.act_one, lambda m: w.act_one.at[step_at(m, tok)])
    gather_one.start()

    arrive(r.up_weight)
    for m in range(members):
        for z in range(planes):
            at = ((m // INNER) * g.n_seq + z * INNER + m % INNER) * part
            w.w_up_send[m * rows : (m + 1) * rows, z * part : (z + 1) * part] = r.up_weight[:, at : at + part]
    w.w_in[own_rows, :] = w.w_in_send[step_at(net.m, rows), :]
    w.w_up[own_rows, :] = w.w_up_send[step_at(net.m, rows), :]
    arrive(r.cotangent)
    w.cotan[mine, :] = r.cotangent[...]
    move_up = ToMembers(net, sems.w_up, lambda m: w.w_up_send.at[step_at(m, rows)], w.w_up.at[own_rows])
    line_up = LineGather(net, sems.w_up_line, lambda z: plane_rows(w.w_up, z))
    gather_cotan = PlaneGather(net, sems.cotan, lambda m: w.cotan.at[step_at(m, tok)])

    gather_out = PlaneGather(net, sems.w_out, lambda m: w.w_out.at[step_at(m, LANES)])
    move_up.start()
    line_out.start(far=True)
    move_in.wait()
    line_in.start(far=False)
    line_in.start(far=True)

    w.square[...] = jnp.zeros_like(w.square)
    lane_of = step_at(net.m, LANES)

    def param(row, ref, k, at):
        w.square[row : row + 1, :] = ref[k : k + 1, pl.ds(pl.multiple_of(at + net.m * LANES, LANES), LANES)]

    for b in range(3):
        param(b, r.input_bias, 0, b * width)
        for i in range(3):
            param(3 + 3 * i + b, r.short_weight, i, b * width)
        param(12 + b, r.short_bias, 0, b * width)
    param(15, r.skip_gain, 0, 0)
    param(16, r.decay_rates, 0, 0)
    w.param_cols[...] = w.square[...].T
    here = step_at(net.z, ch)

    def spread(col, rows=slice(None)):
        cols = w.param_cols[rows, col : col + 1]
        return jnp.broadcast_to(cols, (cols.shape[0], LANES))

    for b in range(3):
        for i in range(3):
            w.taps[i, b * LANES : (b + 1) * LANES, :] = spread(3 + 3 * i + b)
        w.taps[3, b * LANES : (b + 1) * LANES, :] = spread(12 + b)
    w.skip[...] = spread(15)
    w.decay[...] = spread(16, here)

    arrive(r.filter_weight, r.features, r.forth_high, r.forth_low, r.back_high, r.back_low)
    w.square[...] = jnp.zeros_like(w.square)
    for k, ref in enumerate((r.feat_bias, r.feat_freq, r.inner_bias, r.inner_freq)):
        w.square[k : k + 1, :FILT] = ref[...]
    w.net_cols[...] = w.square[...].T
    w.square[...] = jnp.zeros_like(w.square)
    w.square[:FEAT, :FILT] = r.feat_weight[...]
    w.net_weights[0] = w.square[...].T
    w.square[...] = jnp.zeros_like(w.square)
    w.square[:FILT, :FILT] = r.inner_weight[...]
    w.net_weights[1] = w.square[...].T
    w.square[...] = jnp.zeros_like(w.square)
    w.square[:FILT, :] = r.filter_weight[:, lane_of]
    w.net_weights[3] = w.square[...].T
    w.square[...] = jnp.zeros_like(w.square)
    w.square[:ch, :] = w.net_weights[3, here, :]
    w.net_weights[2] = w.square[...]
    w.net_weights[3] = w.square[...].T
    w.hid_two[...] = jnp.zeros_like(w.hid_two)

    span = 4 * LANES
    col = lambda k: w.net_cols[:FILT, k : k + 1]
    features_rows = r.features.shape[0]

    @pl.loop(0, g.length // span)
    def _(step):
        at = step_at(step, span)
        feats = r.features[:, at]
        p_one = dot_nn(w.net_weights[0, :FILT, :features_rows], feats, exact) + col(0)
        hid_one, cos_one = sin_cos(col(1) * p_one)
        p_two = dot_nn(w.net_weights[1, :FILT, :FILT], hid_one, exact) + col(2)
        hid_two, cos_two = sin_cos(col(3) * p_two)
        w.p_one[:, at], w.hid_one[:, at], w.cos_one[:, at] = p_one, hid_one, cos_one
        w.p_two[:, at], w.hid_two[:FILT, at], w.cos_two[:, at] = p_two, hid_two, cos_two
        filters = dot_nn(w.net_weights[2, :ch, :FILT], hid_two, exact)
        for k in range(span // LANES):
            cut = slice(k * LANES, (k + 1) * LANES)
            w.filt[step * (span // LANES) + k] = filters[:, cut] * jnp.exp(-w.decay[...] * feats[:1, cut])

    to_spectrum(g, lambda n, step: w.filt[n, step_at(step, 16), :], ch, w.stage_filt, r.turns, r.forth_high, r.forth_low, w.spec_filt)

    line_out.hand_on()
    line_in.hand_on()
    gather_one.forward_all()
    line_out.wait()
    gather_out.start()
    line_in.wait()
    move_up.wait()
    for b in range(3):
        turned = w.w_in[:, b * LANES : (b + 1) * LANES].astype(f32).T.astype(bf16)
        w.w_in_t[b * LANES : (b + 1) * LANES, :] = turned
    gather_one.wait_all()
    biases = jnp.concatenate([w.param_cols[:, b : b + 1] for b in range(3)], 0)

    def project(step):
        at = slice(step * 2 * tok, (step + 1) * 2 * tok)
        w.proj[:, at] = (dot_nt(w.w_in_t[...], w.act_one[at, :]) + biases).astype(bf16)

    def columns(a, n):
        return slice((a * INNER + n) * tok, (a * INNER + n + 1) * tok)

    def share_edge(values, n, rows, to_plane, from_plane, send, recv, sem, edge):
        for a in range(2):
            for b in range(3):
                block = values[b * LANES : (b + 1) * LANES, columns(a, n)].astype(f32)
                send[a * 8 : (a + 1) * 8, b * LANES : (b + 1) * LANES] = block.T[rows, :]
        there = lax.rem(to_plane + planes, planes)
        has_next = (to_plane >= 0) & (to_plane < planes)
        has_before = (from_plane >= 0) & (from_plane < planes)

        def copy():
            return net.copy(send, recv, sem, 0, net.in_plane(there))

        @pl.when(has_next)
        def _():
            copy().start()

        @pl.when(jnp.logical_not(has_before))
        def _():
            recv[...] = jnp.zeros_like(recv)

        def end():
            @pl.when(has_next)
            def _():
                copy().wait_send()

        net.ends.append(end)

        def wait():
            @pl.when(has_before)
            def _():
                copy().wait_recv()

            w.square[...] = jnp.zeros_like(w.square)
            for a in range(2):
                for b in range(3):
                    w.square[rows, :] = recv[a * 8 : (a + 1) * 8, b * LANES : (b + 1) * LANES]
                    edge[a, b * LANES : (b + 1) * LANES, :] = w.square[...].T

        return wait

    for half in range(INNER // 2)[::-1]:
        for a in range(2):
            project(a * INNER // 2 + half)
        if half == INNER // 2 - 1:
            wait_edge = share_edge(
                w.proj, INNER - 1, slice(LANES - 8, LANES), net.z + 1, net.z - 1, w.edge_send, w.edge_recv, sems.edge, w.edge
            )
            line_up.start(far=False)

    net.sent(move_in, line_in, line_out, move_up, gather_one)

    group = 32
    lane = lax.broadcasted_iota(jnp.int32, (group, LANES), 1)

    def rows_of(b, step):
        return pl.ds(pl.multiple_of(b * LANES + step * group, group), group)

    def rolled(x, by):
        return pltpu.roll(x, by, 1), pltpu.roll(x, (2 * by) % LANES, 1)

    def shifted(here, there, edge):
        return jnp.where(edge(1), there[0], here[0]), jnp.where(edge(2), there[1], here[1])

    from_left, from_right = (lambda k: lane < k), (lambda k: lane >= LANES - k)

    def filter_blocks(step, which):
        for a in range(2):
            conv = {}
            for b in range(3):
                at = rows_of(b, step)
                taps = [w.taps[i, at, :] for i in range(4)]
                before = rolled(w.edge[a, at, :], 1) if 0 in which else None
                for n in range(max(which) + 1):
                    now = w.proj[at, columns(a, n)].astype(f32)
                    turned = rolled(now, 1)
                    if n in which:
                        one, two = shifted(turned, before, from_left)
                        conv[b, n] = taps[3] + taps[2] * now + taps[1] * one + taps[0] * two
                        w.conv[at, columns(a, n)] = conv[b, n]
                    before = turned
            for n in which:
                carried = conv[0, n] * conv[2, n]
                w.carried[rows_of(0, step), columns(a, n)] = carried
                w.car_send[rows_of(0, step), columns(a, n)] = carried.astype(bf16)

    @pl.loop(0, LANES // group)
    def _(step):
        filter_blocks(step, range(1, INNER))

    wait_edge()

    @pl.loop(0, LANES // group)
    def _(step):
        filter_blocks(step, range(1))

    own_z = step_at(net.z, ch)

    def along(sem, send, recv):
        move = AlongPlanes(net, sem, lambda z: send.at[step_at(z, ch)], recv.at[own_z])
        move.start()
        recv[own_z, :] = send[own_z, :]
        return move

    def piece_of(n, step):
        a, part_rows = step * 16 // ch, step * 16 % ch
        return (
            pl.ds(pl.multiple_of(n // INNER * ch + part_rows, 16), 16),
            pl.ds(pl.multiple_of((a * INNER + n % INNER) * tok, tok), tok),
        )

    def received(recv):
        return lambda n, step: recv[piece_of(n, step)].astype(f32)

    def to_planes(send):
        def store(n, step, value):
            send[piece_of(n, step)] = value.astype(bf16)

        return store

    move_car = along(sems.car, w.car_send, w.car_recv)
    gather_cotan.start()
    line_up.hand_on()
    move_car.wait()

    def both(filt):
        return jnp.concatenate([filt, filt], 1)

    to_spectrum(g, received(w.car_recv), 2 * ch, w.stage, r.turns, r.forth_high, r.forth_low, w.spec_car)

    def forth_product(at):
        (hr, hi), (xr, xi) = halves(both(w.spec_filt[at])), halves(w.spec_car[at])
        return xr * hr - xi * hi, xr * hi + xi * hr

    from_spectrum(g, forth_product, 2 * ch, w.stage, r.turns, r.back_high, r.back_low, to_planes(w.y_send))
    move_y = along(sems.y, w.y_send, w.y_recv)
    gather_out.forward_all()
    move_y.wait()
    line_up.start(far=True)
    line_down.hand_on()
    line_down.start(far=True)

    @pl.loop(0, LANES // group)
    def _(step):
        at = rows_of(0, step)
        long_out = w.y_recv[at, :].astype(f32) + jnp.tile(w.skip[at, :], (1, members)) * w.carried[at, :]
        w.long[at, :] = long_out
        w.act_pre[at, :] = (w.conv[rows_of(1, step), :] * long_out).astype(bf16)

    own_block = step_at(net.m, LANES)
    move_pre = ToMembers(net, sems.pre, lambda m: w.act_pre.at[:, step_at(m, tok)], w.pre_recv.at[own_block])
    move_pre.start()
    w.pre_recv[own_block, :] = w.act_pre[:, mine]
    gather_cotan.forward_all()
    gather_out.wait_all()
    move_pre.wait()

    def by_line(piece):
        m, z = divmod(piece, planes)
        return (m // INNER) * g.n_seq + z * INNER + m % INNER

    for k in range(members * planes):
        at = by_line(k) * rows
        w.pre_line[k * rows : (k + 1) * rows, :] = w.pre_recv[at : at + rows, :]
    pre_rows = w.pre_line[...].astype(f32).T.astype(bf16)
    branch = dot_nn(pre_rows, w.w_out[...])
    residual = r.tokens[...].astype(f32) + branch + r.output_bias[...]
    w.residual[...] = residual
    xhat_two, inverse_two = normalized(residual)
    w.xhat_two[...] = xhat_two
    w.act_two[mine, :] = (xhat_two * r.second_gain[...] + r.second_shift[...]).astype(bf16)
    gather_two = PlaneGather(net, sems.act_two, lambda m: w.act_two.at[step_at(m, tok)])
    gather_two.start()
    net.sent(move_car, move_y, move_pre)

    gather_cotan.wait_all()
    line_up.wait()
    sum_two = PlaneSum(net, sems.gn_two, w.gn_two_sib, w.gn_two_recv, w.gn_two_own, w.gn_two_send)
    w.ps[...] = jnp.zeros_like(w.ps)
    hidden_block = [net.x * g.n_seq + z * INNER + net.q for z in range(planes)]
    up_bias = jnp.concatenate([r.up_bias[:, step_at(k, part)] for k in hidden_block], 1)
    bias_sum = jnp.zeros((1, ff), f32)
    slopes = []
    for j in range(chips):
        if j == 1:
            gather_two.forward_all()
        gather_two.wait(j)
        at = step_at(lax.rem(net.p + chips - j, chips), 2 * tok)
        gelu, slope = gelu_pair(dot_nn(w.act_two[at, :], w.w_up[...]) + up_bias)
        w.act_three[at, :] = gelu.astype(bf16)
        slopes.append(slope)
    plane_part = INNER * rows

    def parts_of(ref, z):
        at = z * g.n_dp * plane_part
        return [ref.at[pl.ds(at + x * plane_part, plane_part)] for x in range(g.n_dp)]

    def added(ref):
        group_rows = g.n_dp * plane_part
        return sum(ref[z * group_rows : (z + 1) * group_rows, :].astype(f32) for z in range(planes)).astype(bf16)

    def to_owners(sem, mid, out):
        move = ToMembers(net, sem, lambda m: mid.at[step_at(m, rows)], out.at[step_at(net.m, rows)])
        move.start()
        to_output(mid.at[step_at(net.m, rows)], out.at[step_at(net.m, rows)])
        return move

    sum_up = LineSum(
        net,
        sems.w_in_line,
        lambda z: plane_rows(w.up_send, z),
        lambda z: parts_of(w.up_parts, z),
        [w.up_pre.at[x * plane_part : (x + 1) * plane_part] for x in range(g.n_dp)],
    )
    half = part // 2

    def halves_of(ref, z):
        return [ref.at[step_at(2 * z + k, half)] for k in range(2)]

    sum_down = LineSum(
        net,
        sems.w_out_line,
        lambda z: halves_of(w.down_send, z),
        lambda z: halves_of(w.down_parts, z),
        [w.down_pre.at[k * half : (k + 1) * half] for k in range(2)],
    )
    @pl.loop(0, ff // 256)
    def _(step):
        at = step_at(step, 256)
        turned = w.act_three[:, at].astype(f32).T.astype(bf16)
        w.down_send[at, :] = dot_nn(turned, w.cotan[...]).astype(bf16)

    sum_down.start_early()
    line_down.wait()
    sum_down.start(far=False)
    sum_down.clear()
    w.down_parts[step_at(net.z, part), :] = w.down_send[step_at(net.z, part), :]
    for j in range(1, chips + 1):
        chip = lax.rem(net.p + j, chips)
        at = step_at(chip, 2 * tok)
        grad_upper = (dot_nt(w.cotan[at, :], w.w_down[...]) * slopes[-j]).astype(bf16)
        w.grad_up[at, :] = grad_upper
        bias_sum = bias_sum + column_sum(grad_upper.astype(f32))
        sum_two.own[at, :] = dot_nt(grad_upper, w.w_up[...]).astype(bf16)
        sum_two.start(chip)
        if j > 1:
            sum_two.relay(j - 1)
    for z, k in enumerate(hidden_block):
        w.ps[pl.ds(AT_UP_BIAS + k, 1), :] = bias_sum[:, z * part : (z + 1) * part]

    @pl.loop(0, width // 256)
    def _(step):
        at = step_at(step, 256)
        turned = w.act_two[:, at].astype(f32).T.astype(bf16)
        w.up_send[at, :] = dot_nn(turned, w.grad_up[...]).astype(bf16)

    sum_up.start_early()
    sum_down.add_up()
    sum_down.start(far=True)
    for slot, piece in zip(parts_of(w.up_parts, net.z), plane_rows(w.up_send, net.z)):
        slot[...] = piece[...]
    net.sent(gather_cotan, gather_two, line_up, line_down)
    sum_result = PlaneSum(net, sems.cotan, w.result_sib, w.result_recv, w.cotan, w.result_send)
    for j in range(1, chips + 1):
        chip = lax.rem(net.p + j, chips)
        at = step_at(chip, 2 * tok)
        sum_result.own[at, :] = dot_nn(w.act_three[at, :], w.w_down[...]).astype(bf16)
    sum_up.clear()
    grad_two = sum_two.result()

    xhat_two = w.xhat_two[...]
    to_rows(w.ps, AT_SECOND_GAIN, column_sum(grad_two * xhat_two))
    to_rows(w.ps, AT_SECOND_SHIFT, column_sum(grad_two))
    cotan = r.cotangent[...].astype(f32)
    to_rows(w.ps, AT_DOWN_BIAS, column_sum(cotan))
    grad_res = cotan + norm_back(grad_two, xhat_two, inverse_two, r.second_gain[...])
    w.grad_res[...] = grad_res
    grad_branch = grad_res.astype(bf16)
    w.grad_branch[...] = grad_branch
    to_rows(w.ps, AT_OUTPUT_BIAS, column_sum(grad_branch.astype(f32)))

    per_step = 256 // rows
    for step in range(width // 256):
        grad = dot_nt(w.w_out[step * 256 : (step + 1) * 256, :], w.grad_branch[...]).astype(bf16)
        for k in range(per_step):
            at = by_line(step * per_step + k) * rows
            w.gpre_send[at : at + rows, :] = grad[k * rows : (k + 1) * rows, :]

    move_gpre = ToMembers(net, sems.w_in, lambda m: w.gpre_send.at[step_at(m, LANES)], w.gpre.at[:, mine])
    move_gpre.start()
    w.gpre[:, mine] = w.gpre_send[own_block, :]

    sum_out = PlaneSum(net, sems.act_two, w.w_out_grad_sib, w.w_out_grad_recv, after=sum_two)
    for m in range(members):
        at = slice(m * LANES, (m + 1) * LANES)
        sum_out.own[at, :] = dot_nn(w.pre_line[at, :], w.grad_branch[...]).astype(bf16)
    sum_up.add_up()
    move_gpre.wait()
    for total in (sum_out, sum_result):
        for j in range(1, chips + 1):
            total.start(lax.rem(net.p + j, chips))

    @pl.loop(0, LANES // group)
    def _(step):
        at, second = rows_of(0, step), rows_of(1, step)
        grad_pre = w.gpre[at, :].astype(f32)
        grad_long = grad_pre * w.conv[second, :]
        w.grad_long[at, :] = grad_long
        w.gl_send[at, :] = grad_long.astype(bf16)
        w.grad_conv[second, :] = grad_pre * w.long[at, :]

    move_gl = along(sems.car, w.gl_send, w.gl_recv)
    sum_up.start(far=False)
    for j in range(1, chips):
        sum_out.relay(j)
    move_gl.wait()
    to_spectrum(g, received(w.gl_recv), 2 * ch, w.stage, r.turns, r.forth_high, r.forth_low, w.spec_grad)

    def back_product(at):
        (hr, hi), (gr, gi) = halves(both(w.spec_filt[at])), halves(w.spec_grad[at])
        return hr * gr + hi * gi, hr * gi - hi * gr

    from_spectrum(g, back_product, 2 * ch, w.stage, r.turns, r.back_high, r.back_low, to_planes(w.gc_send))
    move_gc = along(sems.y, w.gc_send, w.gc_recv)
    for j in range(1, chips):
        sum_result.relay(j)

    def filt_product(at):
        out = []
        for a in range(2):
            cut = slice(a * ch, (a + 1) * ch)
            (xr, xi), (gr, gi) = halves(w.spec_car[at, cut, :]), halves(w.spec_grad[at, cut, :])
            out.append((xr * gr + xi * gi, xr * gi - xi * gr))
        return out[0][0] + out[1][0], out[0][1] + out[1][1]

    def keep_filter(n, step, value):
        w.back_filt[n, step_at(step, 16), :] = value

    from_spectrum(g, filt_product, ch, w.stage_filt, r.turns, r.back_high, r.back_low, keep_filter)

    ones = jnp.ones((8, span), f32)
    chan_rows = step_at(net.chan_block, ch)
    w.ct[chan_rows, :] = jnp.zeros((ch, LANES), f32)

    @pl.loop(0, g.length // span)
    def _(step):
        at = step_at(step, span)
        feats = r.features[:, at]
        gate = []
        for k in range(span // LANES):
            fade = jnp.exp(-w.decay[...] * feats[:1, k * LANES : (k + 1) * LANES])
            gate.append(w.back_filt[step * (span // LANES) + k] * fade)
        gate = jnp.concatenate(gate, 1)
        w.ct[chan_rows, :] += dot_nt(gate, w.hid_two[:, at], exact)
        q_two = dot_nn(w.net_weights[3, :FILT, :ch], gate, exact)
        slope_two = q_two * w.cos_two[:, at]
        r_two = slope_two * col(3)
        w.ps[:FILT, :FILT] += dot_nt(w.hid_one[:, at], r_two, exact)
        q_one = dot_nn(r.inner_weight[...], r_two, exact)
        slope_one = q_one * w.cos_one[:, at]
        r_one = slope_one * col(1)
        w.ps[AT_FEAT : AT_FEAT + features_rows, :FILT] += dot_nt(feats, r_one, exact)
        for k, x in enumerate((r_one, slope_one * w.p_one[:, at], r_two, slope_two * w.p_two[:, at])):
            w.ps[AT_VECTOR + k : AT_VECTOR + k + 1, :FILT] += dot_nt(ones, x, exact)[:1, :]

    ct_z = AlongPlanes(net, sems.ct_z, lambda z: w.ct.at[chan_rows], w.ct.at[chan_rows])
    ct_z.start()
    move_gc.wait()

    @pl.loop(0, LANES // group)
    def _(step):
        at, last = rows_of(0, step), rows_of(2, step)
        grad = w.gc_recv[at, :].astype(f32) + jnp.tile(w.skip[at, :], (1, members)) * w.grad_long[at, :]
        w.grad_conv[at, :] = grad * w.conv[last, :]
        w.grad_conv[last, :] = grad * w.conv[at, :]

    wait_back_edge = share_edge(
        w.grad_conv, 0, slice(0, 8), net.z - 1, net.z + 1, w.back_edge_send, w.back_edge_recv, sems.back_edge, w.back_edge
    )
    sum_up.start(far=True)

    line_out_grad = LineSum(
        net,
        sems.w_down,
        lambda z: [w.out_sum.at[step_at(z, rows)]],
        lambda z: [w.out_parts.at[step_at(z, rows)]],
    )
    w.out_sum[...] = sum_out.result().astype(bf16)
    def filter_blocks_back(step, which):
        for a in range(2):
            for b in range(3):
                at = rows_of(b, step)
                taps = [w.taps[i, at, :] for i in range(3)]
                after = rolled(w.back_edge[a, at, :], LANES - 1) if INNER - 1 in which else None
                for n in range(min(which), INNER)[::-1]:
                    now = w.grad_conv[at, columns(a, n)]
                    turned = rolled(now, LANES - 1)
                    if n in which:
                        one, two = shifted(turned, after, from_right)
                        w.gproj[at, columns(a, n)] = (taps[2] * now + taps[1] * one + taps[0] * two).astype(bf16)
                    after = turned

    @pl.loop(0, LANES // group)
    def _(step):
        filter_blocks_back(step, range(INNER - 1))

    wait_back_edge()

    @pl.loop(0, LANES // group)
    def _(step):
        filter_blocks_back(step, range(INNER - 1, INNER))

    @pl.loop(0, width // 256)
    def _(step):
        at = step_at(step, 256)
        grad = dot_nn(w.gproj[...], w.act_one[:, at])
        w.gain_sum[:, at] = column_sum(grad * w.w_in_t[:, at].astype(f32))
        for b in range(3):
            cut = slice(b * LANES, (b + 1) * LANES)
            w.in_send[at, cut] = grad[cut].T.astype(bf16)

    sum_in = LineSum(
        net,
        sems.w_up_line,
        lambda z: plane_rows(w.in_send, z),
        lambda z: parts_of(w.w_in, z),
    )
    sum_in.start(far=False)
    for slot, piece in zip(parts_of(w.w_in, net.z), plane_rows(w.in_send, net.z)):
        slot[...] = piece[...]
    ct_z.wait()
    gather_ct = PlaneGather(net, sems.act_one, lambda m: w.ct.at[step_at(m, LANES)])
    gather_ct.start()
    w.block_out[...] = (w.residual[...] + sum_result.result() + r.down_bias[...]).astype(bf16)
    to_output(w.block_out, block_out)
    kept = w.conv

    @pl.loop(0, LANES // group)
    def _(step):
        for b in range(3):
            at = rows_of(b, step)
            sums = [jnp.zeros((group, LANES), f32)] * 5
            for a in range(2):
                before = rolled(w.edge[a, at, :], 1)
                for n in range(INNER):
                    grad, now = w.grad_conv[at, columns(a, n)], w.proj[at, columns(a, n)].astype(f32)
                    turned = rolled(now, 1)
                    one, two = shifted(turned, before, from_left)
                    terms = (grad * two, grad * one, grad * now, grad, w.gproj[at, columns(a, n)].astype(f32))
                    sums = [x + y for x, y in zip(sums, terms)]
                    before = turned
            for k in range(5):
                kept[at, k * LANES : (k + 1) * LANES] = sums[k]
        at = rows_of(0, step)
        product = w.grad_long[at, :] * w.carried[at, :]
        kept[at, 5 * LANES : 6 * LANES] = sum(product[:, k * LANES : (k + 1) * LANES] for k in range(members))

    which_lane = lax.broadcasted_iota(jnp.int32, (LANES, LANES), 1)
    tile = jnp.zeros((LANES, LANES), f32)
    for k, (kind, b) in enumerate(
        [(4, b) for b in range(3)] + [(i, b) for i in range(3) for b in range(3)] + [(3, b) for b in range(3)] + [(5, 0)]
    ):
        part_sums = kept[b * LANES : (b + 1) * LANES, kind * LANES : (kind + 1) * LANES]
        tile = jnp.where(which_lane == k, jnp.sum(part_sums, 1, keepdims=True), tile)
    channel_sum = jnp.sum(kept[:, 4 * LANES : 5 * LANES], 1, keepdims=True)
    shift_sum = column_sum(channel_sum * w.w_in_t[...].astype(f32))
    to_rows(w.ps, AT_FIRST_GAIN, (w.gain_sum[...] - r.first_shift[...] * shift_sum) / r.first_gain[...])
    to_rows(w.ps, AT_FIRST_SHIFT, shift_sum)
    w.ps[pl.ds(pl.multiple_of(AT_CHANNEL + net.m * 16, 16), 16), :] = tile.T[:16, :]

    share = PS_ROWS // members
    own_share = step_at(net.m, share)
    move_ps = ToMembers(net, sems.w_in, lambda m: w.ps.at[step_at(m, share)], w.ps_recv.at[own_share])
    net.sent(move_gpre)
    move_ps.start()
    w.ps_recv[own_share, :] = w.ps[own_share, :]
    sum_one = PlaneSum(net, sems.gn_two, w.gn_one_sib, w.gn_one_recv, after=sum_result)
    for j in range(1, chips + 1):
        chip = lax.rem(net.p + j, chips)
        at = step_at(chip, 2 * tok)
        turned = w.gproj[:, at].astype(f32).T.astype(bf16)
        sum_one.own[at, :] = dot_nn(turned, w.w_in_t[...]).astype(bf16)
        sum_one.start(chip)
        if j > 1:
            sum_one.relay(j - 1)
    move_ps.wait()

    def shares_added(ref, count):
        return sum(ref[k * share : (k + 1) * share, :] for k in range(count))

    own_line = step_at(net.z, share)
    w.ps_line[own_line, :] = shares_added(w.ps_recv, members)
    line_ps = AlongPlanes(net, sems.ps_line, lambda z: w.ps_line.at[own_line], w.ps_line.at[own_line])
    line_ps.start()
    sum_in.start(far=True)
    line_out_grad.start(far=False)
    line_out_grad.start(far=True)
    w.out_parts[step_at(net.z, rows), :] = w.out_sum[step_at(net.z, rows), :]
    sum_up.wait()
    w.up_mid[...] = added(w.up_parts)
    move_up_grad = to_owners(sems.w_up, w.up_mid, up_recv)
    sum_down.wait()
    w.down_total[...] = sum(w.down_parts[z * part : (z + 1) * part, :].astype(f32) for z in range(planes))
    to_output(w.down_total, down_recv)
    gather_ct.forward_all()
    line_ps.wait()
    w.ps_all[own_share, :] = shares_added(w.ps_line, planes)
    move_back = ToMembers(net, sems.ps_back, lambda m: w.ps_all.at[own_share], w.ps_all.at[own_share])
    move_back.start()
    sum_in.wait()
    w.in_mid[...] = added(w.w_in)
    move_in_grad = to_owners(sems.pre, w.in_mid, in_recv)
    grad_one = sum_one.result()

    grad_tokens = norm_back(grad_one, w.xhat_one[...], inverse_one, r.first_gain[...])
    w.tokens_grad[...] = (w.grad_res[...] + grad_tokens).astype(bf16)
    to_output(w.tokens_grad, tokens_grad)
    gather_ct.wait_all()
    to_output(w.ct, ct_out)
    line_out_grad.wait()
    w.out_total[...] = sum(w.out_parts[z * rows : (z + 1) * rows, :].astype(f32) for z in range(planes))
    to_output(w.out_total, out_recv)
    move_back.wait()
    to_output(w.ps_all, ps_out)
    move_in_grad.wait()
    move_up_grad.wait()
    net.finish()


def finish_kernel(g, *refs):
    ins, outs = refs[:8], refs[8:]
    block_in, tokens_in, ct, ps, in_recv, up_recv, down_recv, out_recv = ins
    (
        block_out, tokens_grad, first_gain, first_shift, input_weight, input_bias, short_weight, short_bias, feat_weight,
        feat_bias, feat_freq, inner_weight, inner_bias, inner_freq, filter_weight, skip_gain, output_weight, output_bias,
        second_gain, second_shift, up_weight, up_bias, down_weight, down_bias,
    ) = outs
    rows, planes, width, ff = g.rows, g.planes, g.width, g.ff_part
    for src, dst in ((block_in, block_out), (tokens_in, tokens_grad), (down_recv, down_weight), (out_recv, output_weight)):
        dst[...] = src[...]
    for m in range(g.members):
        x, q = m // INNER, m % INNER
        parts = [x * g.n_seq + z * INNER + q for z in range(planes)]
        total = in_recv[m * rows : (m + 1) * rows, :].astype(f32)
        for b in range(3):
            input_weight[:, b * width + m * LANES : b * width + (m + 1) * LANES] = total[:, b * LANES : (b + 1) * LANES]
        total = up_recv[m * rows : (m + 1) * rows, :].astype(f32)
        for z, k in enumerate(parts):
            cut = slice(z * g.down_rows, (z + 1) * g.down_rows)
            up_weight[:, k * g.down_rows : (k + 1) * g.down_rows] = total[:, cut]
    for m in range(g.members):
        cut = slice(m * LANES, (m + 1) * LANES)
        turned = ct[cut, :].T
        filter_weight[:, cut] = turned[:FILT, :]
        line = lambda k: ps[AT_CHANNEL + 16 * m + k : AT_CHANNEL + 16 * m + k + 1, :]
        for b in range(3):
            at = b * g.members + m
            input_bias[at : at + 1, :] = line(b)
            for i in range(3):
                short_weight[i : i + 1, b * width + m * LANES : b * width + (m + 1) * LANES] = line(3 + 3 * i + b)
            short_bias[at : at + 1, :] = line(12 + b)
        skip_gain[m : m + 1, :] = line(15)
    for out, at in (
        (first_gain, AT_FIRST_GAIN), (first_shift, AT_FIRST_SHIFT), (second_gain, AT_SECOND_GAIN), (up_bias, AT_UP_BIAS),
        (second_shift, AT_SECOND_SHIFT), (output_bias, AT_OUTPUT_BIAS), (down_bias, AT_DOWN_BIAS),
    ):
        out[...] = ps[at : at + out.shape[0], :]
    feat_weight[...] = ps[AT_FEAT : AT_FEAT + FEAT, :FILT]
    inner_weight[...] = ps[:FILT, :FILT]
    for k, out in enumerate((feat_bias, feat_freq, inner_bias, inner_freq)):
        out[...] = ps[AT_VECTOR + k : AT_VECTOR + k + 1, :FILT]


def on_device_in_kernels(g, *args):
    operands = [a[0] if a.ndim == 3 else a[None] if a.ndim == 1 else a for a in args]
    operands += [jnp.asarray(table) for table in constant_tables(g.blocks, LANES)]
    tok, width = g.tok, g.width
    in_vmem = pl.BlockSpec(memory_space=pltpu.VMEM)
    anywhere = pl.BlockSpec(memory_space=pl.ANY)
    S = jax.ShapeDtypeStruct
    buffers = scratch_buffers(g)
    parts = pl.pallas_call(
        functools.partial(block_kernel, g),
        out_shape=[
            S((tok, width), bf16),
            S((tok, width), bf16),
            S((width, LANES), f32),
            S((PS_ROWS, LANES), f32),
            S((g.members * g.rows, 3 * LANES), bf16),
            S((g.members * g.rows, g.ff_part), bf16),
            S((g.down_rows, width), f32),
            S((g.rows, width), f32),
        ],
        in_specs=[anywhere if name in buffers else in_vmem for name in Inputs._fields],
        out_specs=[anywhere] * 8,
        scratch_shapes=[pltpu.VMEM(shape, dtype) for shape, dtype in buffers.values()]
        + [pltpu.SemaphoreType.DMA((count,)) for pair in semaphore_counts(g).values() for count in pair]
        + [pltpu.SemaphoreType.DMA((len(set(Inputs._fields) & set(buffers)) + 8,))],
        compiler_params=pltpu.CompilerParams(
            collective_id=0, has_side_effects=True, vmem_limit_bytes=63 * 1024 * 1024
        ),
        name="block",
    )(*operands)

    def out_shape(a):
        if a.ndim == 3:
            return S(a.shape[1:], bf16)
        if a.ndim == 1:
            return S((a.shape[0] // LANES, LANES) if a.shape[0] % LANES == 0 else (1, a.shape[0]), f32)
        return S(a.shape, f32)

    named = Inputs(*args, *operands[len(args) :])
    wanted = [a for a in args if a is not named.cotangent and a is not named.decay_rates]
    wanted = [named.tokens] + wanted
    outs = pl.pallas_call(
        functools.partial(finish_kernel, g),
        out_shape=[out_shape(a) for a in wanted],
        in_specs=[in_vmem] * 8,
        out_specs=[in_vmem] * len(wanted),
        compiler_params=pltpu.CompilerParams(vmem_limit_bytes=63 * 1024 * 1024),
        name="finish",
    )(*parts)
    return tuple(o.reshape(a.shape) for o, a in zip(outs, wanted))


def on_device_by_size(tokens, cotangent, *args):
    named = Inputs(tokens, cotangent, *args, *[None] * 6)
    g = Geometry(
        lax.axis_size("dp"),
        lax.axis_size("seq"),
        tokens.shape[1],
        tokens.shape[2],
        named.up_weight.shape[1],
        named.input_weight.shape[0],
        named.down_weight.shape[0],
    )
    if g.fits():
        return on_device_in_kernels(g, tokens, cotangent, *args)
    return on_device(tokens, cotangent, *args)


def solution(mesh):
    placed = (
        P("dp", "seq", None),
        P("dp", "seq", None),
        P(),
        P(),
        P(("dp", "seq"), None),
        P(),
        P(),
        P(),
        P(),
        P(),
        P(),
        P(),
        P(),
        P(),
        P(),
        P(),
        P(),
        P(("dp", "seq"), None),
        P(),
        P(),
        P(),
        P(("dp", "seq"), None),
        P(),
        P(("dp", "seq"), None),
        P(),
    )
    return jax.shard_map(
        on_device_by_size,
        mesh=mesh,
        in_specs=placed,
        out_specs=(
            P("dp", "seq", None),
            P("dp", "seq", None),
            P(),
            P(),
            P(("dp", "seq"), None),
            P(),
            P(),
            P(),
            P(),
            P(),
            P(),
            P(),
            P(),
            P(),
            P(),
            P(),
            P(("dp", "seq"), None),
            P(),
            P(),
            P(),
            P(("dp", "seq"), None),
            P(),
            P(("dp", "seq"), None),
            P(),
        ),
        check_vma=False,
    )
```
